32 devices in a mesh: exp: 8 (over z, x), hid: 4 (over y, core).
Axes of the slice: x: 2, y: 2, z: 4, core: 2. Of those that a mesh axis runs over, the one named last changes fastest.
Arguments:
- tokens: bfloat16 [16384, 1024], P(('exp', 'hid')), may hold values from -6 to 6
- token_ids: int32 [16384], P(('exp', 'hid')), may hold values from 0 to 8007
- lengths: int32 [32, 2], P(('exp', 'hid')), may hold values from 0 to 512, as said below
- hash_table: int32 [8008], replicated, may hold values from 0 to 31
- capacity: int32 [32], replicated, may hold values from 16 to 32, as said below
- gain_one: float32 [1024], replicated, may hold values from 0.5 to 1.5
- shift_one: float32 [1024], replicated, may hold values from -0.6 to 0.6
- w_qkv: bfloat16 [1024, 3072], replicated, may hold values from -0.1875 to 0.1875
- w_out: bfloat16 [1024, 1024], replicated, may hold values from -1.5 to 1.5
- gain_two: float32 [1024], replicated, may hold values from 0.5 to 1.5
- shift_two: float32 [1024], replicated, may hold values from -0.6 to 0.6
- w_in: bfloat16 [32, 1024, 4096], P('exp', None, 'hid'), may hold values from -0.1875 to 0.1875
- bias_in: float32 [32, 4096], P('exp', 'hid'), may hold values from -0.6 to 0.6
- w_back: bfloat16 [32, 4096, 1024], P('exp', 'hid'), may hold values from -0.125 to 0.125
- bias_back: float32 [32, 1024], P('exp'), may hold values from -0.6 to 0.6
- cotangent: bfloat16 [16384, 1024], P(('exp', 'hid')), may hold values from -15 to 15, as said below
Outputs:
- output: bfloat16 [16384, 1024], P(('exp', 'hid'))
- grad_tokens: float32 [16384, 1024], P(('exp', 'hid'))
- grad_gain_one: float32 [1024], replicated
- grad_shift_one: float32 [1024], replicated
- grad_qkv: float32 [1024, 3072], replicated
- grad_out: float32 [1024, 1024], replicated
- grad_gain_two: float32 [1024], replicated
- grad_shift_two: float32 [1024], replicated
- grad_in: float32 [32, 1024, 4096], P('exp', None, 'hid')
- grad_bias_in: float32 [32, 4096], P('exp', 'hid')
- grad_back: float32 [32, 4096, 1024], P('exp', 'hid')
- grad_bias_back: float32 [32, 1024], P('exp')
The draws below stay inside these ranges and needn't reach their ends.
Inputs may be any that keep to these rules, and one draw needn't show every extreme that they name: `cotangent`: cotangent of the block's output. `capacity`: some experts take 32, some 32 // 2. `lengths`: each row is either one sequence of 512 followed by zeros, or 2 sequences of 256; some rows are of each kind.
All inputs are finite; a program needn't handle non-finite values.
Results may differ from the reference program's by a relative error of at most 0.011.
Values may be sent and summed in bfloat16 or wider, within the bound.
A program may use at most 320 MiB of HBM per device.

```python
import math
import jax
import jax.numpy as jnp
import numpy as np
from jax import lax

D = 1024
HEADS = 16
HEAD_DIM = 64
FF = 4096
VOCAB = 8008
TOK_DEV = 512
SHORT = 256
DOCS = 2
EXPERTS = 32
CAP = 32
TOKENS = 16384
DEVICES = 32


def draw_capacity(key, part):
    first_key, second_key, third_key = jax.random.split(key, 3)
    lower_cap = jax.random.randint(first_key, (EXPERTS,), CAP // 2, CAP + 1)
    at_full = jax.random.randint(second_key, (EXPERTS,), 0, 4) > 0
    forced = jax.random.randint(third_key, (), 0, EXPERTS)
    expert_range = jnp.arange(EXPERTS)
    at_full = at_full | (expert_range == forced)
    values = jnp.where(at_full, CAP, lower_cap)
    values = jnp.where(expert_range == (forced + 1) % EXPERTS, CAP // 2, values)
    return values.astype(jnp.int32)


def draw_lengths(key, part):
    first_key, second_key = jax.random.split(jax.random.fold_in(key, 17))
    long_rows = jax.random.randint(first_key, (DEVICES,), 0, 2) > 0
    forced = jax.random.randint(second_key, (), 0, DEVICES)
    device_range = jnp.arange(DEVICES)
    long_rows = (long_rows | (device_range == forced)) & (device_range != (forced + 1) % DEVICES)
    doc_range = jnp.arange(DOCS)
    long_row = jnp.where(doc_range == 0, TOK_DEV, 0)
    short_row = jnp.full((DOCS,), SHORT)
    return jnp.where(long_rows[:, None], long_row[None, :], short_row[None, :]).astype(jnp.int32)


def draw_cotangent(key, part):
    places = jnp.arange(TOKENS, dtype=jnp.float32)
    rising = jnp.exp(jnp.log(3.0) * places / (TOKENS - 1))[:, None]
    values = jnp.clip(jax.random.normal(key, (TOKENS, D), jnp.float32), -5.0, 5.0)
    return (values * rising).astype(jnp.bfloat16)


def touch_ends(values, rng, low, top_value):
    longest = values.shape.index(max(values.shape))
    spots = []
    for shift in (0, 1):
        where = [jax.random.randint(jax.random.fold_in(rng, axis), (), 0, length) for axis, length in enumerate(values.shape)]
        where[longest] = (where[longest] + shift) % values.shape[longest]
        spots.append(tuple(where))
    return values.at[spots[0]].set(low).at[spots[1]].set(top_value)


def block_scale(rng, extent, shards, least, top_value):
    gain = 1.0
    for dim, parts in shards:
        steps = jax.random.uniform(jax.random.fold_in(jax.random.fold_in(rng, 6), dim), (parts,), jnp.float32, least / len(shards), top_value / len(shards))
        gain = gain * jnp.repeat(jnp.exp(steps), extent[dim] // parts).reshape((-1,) + (1,) * (len(extent) - 1 - dim))
    return gain


def cumulative_ranks(count, lean):
    loads = [(1 << 20) // math.isqrt(rank ** lean) + 1 for rank in range(1, count + 1)]
    deviation = 1 + sum(loads) // (1 << 30)
    return np.cumsum(np.array([max(1, weight // deviation) for weight in loads]))


def skewed_ids(own_key, dims, number_of, lean):
    listing = cumulative_ranks(number_of, lean)
    pick = jax.random.randint(jax.random.fold_in(own_key, 1), dims, 0, int(listing[number_of - 1]))
    standing = jnp.searchsorted(jnp.asarray(listing, jnp.int32), pick, side="right")
    return jax.random.permutation(jax.random.fold_in(own_key, 2), number_of)[standing].astype(jnp.int32)


def gaussian(rng, shape, scale, reach, pieces=(), held_as=jnp.bfloat16):
    factor_of = block_scale(rng, shape, pieces, -0.22, 0.18) if pieces else 1.0
    values = jax.random.normal(rng, shape, jnp.float32) * scale * factor_of
    return jnp.minimum(jnp.maximum(values, -reach), reach).astype(held_as)


def setup_inputs(seed: int = 0) -> dict:
    key_list = jax.random.split(jax.random.key(seed), 17)
    return {
        "tokens": gaussian(key_list[0], (TOKENS, D), 1.0, 6.0, ((0, 32),)),
        "token_ids": touch_ends(skewed_ids(key_list[1], (TOKENS,), VOCAB, 2), jax.random.fold_in(key_list[1], 3), 0, VOCAB - 1).astype(jnp.int32),
        "lengths": draw_lengths(jax.random.fold_in(key_list[16], 71), 0),
        "hash_table": touch_ends(jax.random.randint(key_list[3], (VOCAB,), 0, EXPERTS), jax.random.fold_in(key_list[3], 1), 0, EXPERTS - 1).astype(jnp.int32),
        "capacity": draw_capacity(jax.random.fold_in(key_list[16], 71), 0),
        "gain_one": jnp.clip(1.0 + 0.1 * jax.random.normal(key_list[5], (D,), jnp.float32), 0.5, 1.5),
        "shift_one": gaussian(key_list[6], (D,), 0.1, 0.6, (), jnp.float32),
        "w_qkv": gaussian(key_list[7], (D, 3 * D), D ** -0.5, 0.1875),
        "w_out": gaussian(key_list[8], (D, D), (D // 64) ** -0.5, 1.5),
        "gain_two": jnp.clip(1.0 + 0.1 * jax.random.normal(key_list[9], (D,), jnp.float32), 0.5, 1.5),
        "shift_two": gaussian(key_list[10], (D,), 0.1, 0.6, (), jnp.float32),
        "w_in": gaussian(key_list[11], (EXPERTS, D, FF), D ** -0.5, 0.1875, ((0, 8), (2, 4))),
        "bias_in": gaussian(key_list[12], (EXPERTS, FF), 0.1, 0.6, ((0, 8), (1, 4)), jnp.float32),
        "w_back": gaussian(key_list[13], (EXPERTS, FF, D), (FF // 2) ** -0.5, 0.125, ((0, 8), (1, 4))),
        "bias_back": gaussian(key_list[14], (EXPERTS, D), 0.1, 0.6, ((0, 8),), jnp.float32),
        "cotangent": draw_cotangent(jax.random.fold_in(key_list[16], 71), 0),
    }


@jax.custom_vjp
def low(v):
    return lax.optimization_barrier(v.astype(jnp.bfloat16)).astype(jnp.float32)

@jax.custom_vjp
def low_back(v):
    return v

def low_keep(v):
    return (low(v), None)

def low_pass(kept, grad):
    return (grad,)

def back_keep(v):
    return (v, None)

def back_low(kept, grad):
    return (low(grad),)
low.defvjp(low_keep, low_pass)
low_back.defvjp(back_keep, back_low)
highest = lax.Precision.HIGHEST
epsilon = 1e-05
masked_score = -1e+30

def layer_norm(tok_rows, norm_gain, norm_shift):
    row_mean = lax.optimization_barrier(jnp.mean(tok_rows, axis=-1, keepdims=True))
    centred = tok_rows - row_mean
    row_var = lax.optimization_barrier(jnp.mean(centred * centred, axis=-1, keepdims=True))
    return centred * lax.rsqrt(row_var + epsilon) * norm_gain + norm_shift

def documents(length_row):
    doc_ends = jnp.cumsum(length_row)
    places = jnp.arange(TOK_DEV, dtype=jnp.int32)
    return lax.optimization_barrier(jnp.sum((places[:, None] >= doc_ends[None, :]).astype(jnp.int32), axis=1))

def routing(id_row, hash_table, capacity):
    chosen = jnp.take(hash_table, id_row)
    onehot = (chosen[:, None] == jnp.arange(EXPERTS, dtype=jnp.int32)[None, :]).astype(jnp.int32)
    before = jnp.cumsum(onehot, axis=0) - onehot
    rank_in = lax.optimization_barrier(jnp.sum(before * onehot, axis=1))
    kept_rows = rank_in < jnp.take(capacity, chosen)
    slot_ids = chosen * CAP + rank_in
    slot_range = jnp.arange(EXPERTS * CAP, dtype=jnp.int32)
    matches = (slot_ids[None, :] == slot_range[:, None]) & kept_rows[None, :]
    source_row = lax.optimization_barrier(jnp.sum(matches.astype(jnp.int32) * jnp.arange(TOK_DEV, dtype=jnp.int32)[None, :], axis=1))
    filled = jnp.any(matches, axis=1)
    return (jnp.minimum(slot_ids, EXPERTS * CAP - 1).astype(jnp.int32), kept_rows, source_row.astype(jnp.int32), filled)

def attend(tok_rows, doc_ids, gain_one, shift_one, w_qkv, w_out):
    normed = low(layer_norm(tok_rows, gain_one, shift_one))
    mixed = low(low_back(jnp.dot(normed, w_qkv, precision=highest)))
    qkv_parts = mixed.reshape(TOK_DEV, 3, HEADS, HEAD_DIM)
    raw_scores = low_back(jnp.einsum('qhd,khd->hqk', qkv_parts[:, 0], qkv_parts[:, 1], precision=highest))
    scores = raw_scores * HEAD_DIM ** (-0.5)
    places = jnp.arange(TOK_DEV, dtype=jnp.int32)
    allowed = (doc_ids[:, None] == doc_ids[None, :]) & (places[:, None] >= places[None, :])
    scores = jnp.where(allowed[None], scores, masked_score)
    row_max = lax.optimization_barrier(jnp.max(scores, axis=-1, keepdims=True))
    exponent = jnp.exp(scores - row_max)
    attn_probs = low(exponent / lax.optimization_barrier(jnp.sum(exponent, axis=-1, keepdims=True)))
    context = jnp.einsum('hqk,khd->qhd', attn_probs, qkv_parts[:, 2], precision=highest)
    context = low(low_back(context.reshape(TOK_DEV, D)))
    return tok_rows + low_back(jnp.dot(context, w_out, precision=highest))

def expert_ffn(members):
    rows_in, weight_in, shift_in, weight_back, shift_back = members
    hidden_pre = low_back(jnp.einsum('ncd,df->ncf', rows_in, weight_in, precision=highest) + shift_in)
    hidden = low(jax.nn.silu(hidden_pre))
    return low(low_back(jnp.einsum('ncf,fd->ncd', hidden, weight_back, precision=highest) + shift_back))

def pick_rows(normed_rows, source_row, filled):
    return jnp.where(filled[:, None], jnp.take(normed_rows, source_row, axis=0), 0.0)

def place_rows(expert_rows, slot_ids, kept_rows):
    return jnp.where(kept_rows[:, None], jnp.take(expert_rows, slot_ids, axis=0), 0.0)

def reference(tokens, token_ids, lengths, hash_table, capacity, gain_one, shift_one, w_qkv, w_out, gain_two, shift_two, w_in, bias_in, w_back, bias_back, cotangent):
    doc_ids = jax.vmap(documents)(lengths)
    id_rows = token_ids.reshape(DEVICES, TOK_DEV)
    slot_ids, kept_rows, source_row, filled = jax.vmap(routing, in_axes=(0, None, None))(id_rows, hash_table, capacity)

    def forward(tok_in, gain_a, shift_a, weight_qkv, weight_out, gain_b, shift_b, weight_in, shift_in, weight_back, shift_back):
        blocks = tok_in.reshape(DEVICES, TOK_DEV, D)

        def attend_block(pair):
            return attend(pair[0], pair[1], gain_a, shift_a, weight_qkv, weight_out)
        middle = lax.map(jax.checkpoint(attend_block), (blocks, doc_ids))
        normed_two = low(layer_norm(middle, gain_b, shift_b))
        dispatched = jax.vmap(pick_rows)(normed_two, source_row, filled)
        dispatched = low_back(dispatched.reshape(DEVICES, EXPERTS, CAP, D).transpose(1, 0, 2, 3))
        expert_out = lax.map(jax.checkpoint(expert_ffn), (dispatched, weight_in, shift_in[:, None, None, :], weight_back, shift_back[:, None, None, :]))
        expert_out = expert_out.transpose(1, 0, 2, 3).reshape(DEVICES, EXPERTS * CAP, D)
        combined = jax.vmap(place_rows)(expert_out, slot_ids, kept_rows)
        return (middle + combined).reshape(TOKENS, D)
    floats = (tokens.astype(jnp.float32), gain_one.astype(jnp.float32), shift_one.astype(jnp.float32), w_qkv.astype(jnp.float32), w_out.astype(jnp.float32), gain_two.astype(jnp.float32), shift_two.astype(jnp.float32), w_in.astype(jnp.float32), bias_in.astype(jnp.float32), w_back.astype(jnp.float32), bias_back.astype(jnp.float32))
    result, pullback = jax.vjp(forward, *floats)
    grads = pullback(cotangent.astype(jnp.float32))
    return (result.astype(jnp.bfloat16), grads[0], grads[1], grads[2], grads[3], grads[4], grads[5], grads[6], grads[7], grads[8], grads[9], grads[10])
```

```python
import functools

import jax
import jax.numpy as jnp
from jax import lax
from jax.experimental import pallas as pl
from jax.experimental.pallas import tpu as pltpu
from jax.sharding import PartitionSpec as P

HEADS = 16
MESH = pl.DeviceIdType.MESH
BF = jnp.bfloat16
F32 = jnp.float32
epsilon = 1e-05
masked_score = -1e30
DMA = pltpu.SemaphoreType.DMA
VM = pl.BlockSpec(memory_space=pltpu.VMEM)
SM = pl.BlockSpec(memory_space=pltpu.SMEM)
HB = pl.BlockSpec(memory_space=pl.ANY)
MIB = 1 << 20


def mm(a, b):
    return lax.dot_general(a, b, (((1,), (0,)), ((), ())), preferred_element_type=F32)


def mm_nt(a, b):
    return lax.dot_general(a, b, (((1,), (1,)), ((), ())), preferred_element_type=F32)


def mm_tn(a, b):
    return lax.dot_general(a, b, (((0,), (0,)), ((), ())), preferred_element_type=F32)


def place():
    e = lax.axis_index("exp")
    h = lax.axis_index("hid")
    return e, h, lax.div(h, 2), lax.rem(h, 2)


def rcopy(src, dst, send, recv, dev):
    return pltpu.make_async_remote_copy(
        src_ref=src, dst_ref=dst, send_sem=send, recv_sem=recv, device_id=dev, device_id_type=MESH
    )


def greet(n_exp, n_y):
    e, h, y, c = place()
    sem = pltpu.get_barrier_semaphore()
    for k in range(1, n_exp):
        pl.semaphore_signal(sem, inc=1, device_id=(e ^ k, h), device_id_type=MESH)
    for d in range(1, n_y):
        pl.semaphore_signal(
            sem, inc=1, device_id=(e, lax.rem(y + d, n_y) * 2 + c), device_id_type=MESH
        )
    pl.semaphore_signal(sem, inc=1, device_id=(e, y * 2 + 1 - c), device_id_type=MESH)
    pl.semaphore_wait(sem, n_exp - 1 + n_y)


class Spread:
    def __init__(self, n_exp, n_y, rows, land, sems):
        self.n_exp, self.n_y, self.rows, self.land = n_exp, n_y, rows, land
        self.es, self.er, self.ys, self.yr, self.cs, self.cr = sems
        self.e, self.h, self.y, self.c = place()

    @staticmethod
    def sems(n_exp, n_y):
        return [DMA((n_exp,)), DMA((n_exp,))] + [DMA((n_exp, n_y))] * 4

    def over_exp(self, k):
        return rcopy(
            self.rows.at[self.e ^ k], self.land.at[:, self.e, self.h],
            self.es.at[k], self.er.at[k], (self.e ^ k, self.h),
        )

    def block(self, k, hid):
        return self.land.at[:, self.e ^ k, hid]

    def over_y(self, k, d):
        blk = self.block(k, self.h)
        dev = (self.e, lax.rem(self.y + d, self.n_y) * 2 + self.c)
        return rcopy(blk, blk, self.ys.at[k, d], self.yr.at[k, d], dev)

    def over_core(self, k, d):
        blk = self.block(k, lax.rem(self.y + self.n_y - d, self.n_y) * 2 + self.c)
        dev = (self.e, self.y * 2 + 1 - self.c)
        return rcopy(blk, blk, self.cs.at[k, d], self.cr.at[k, d], dev)

    def pass_on(self, k):
        @pl.when(k > 0)
        def _():
            self.over_exp(k).wait_recv()

        for d in range(1, self.n_y):
            self.over_y(k, d).start()
        self.over_core(k, 0).start()

    def pass_y(self, k):
        for d in range(1, self.n_y):
            self.over_y(k, d).wait_recv()
            self.over_core(k, d).start()

    def landed(self, k):
        for d in range(self.n_y):
            self.over_core(k, d).wait_recv()

    def sent(self, k):
        @pl.when(k > 0)
        def _():
            self.over_exp(k).wait_send()

        for d in range(1, self.n_y):
            self.over_y(k, d).wait_send()
        for d in range(self.n_y):
            self.over_core(k, d).wait_send()


class Gather:
    def __init__(self, n_exp, n_y, other, mine, pairs, from_y, back, sems):
        self.n_exp, self.n_y, self.other, self.mine = n_exp, n_y, other, mine
        self.pairs, self.from_y, self.back = pairs, from_y, back
        self.es, self.er, self.ys, self.yr, self.cs, self.cr = sems
        self.e, self.h, self.y, self.c = place()

    @staticmethod
    def sems(n_exp, n_y):
        return [DMA((n_exp,)), DMA((n_exp,)), DMA((n_exp, n_y)), DMA((n_exp, n_y)), DMA((n_exp,)), DMA((n_exp,))]

    @staticmethod
    def scratch(n_exp, n_y, lc, cap, d):
        return [
            pltpu.VMEM((n_exp, lc, n_y, cap, d), BF),
            pltpu.VMEM((n_exp, n_y - 1, lc, cap, d), BF),
        ]

    def over_core(self, k):
        t = self.e ^ k
        dev = (self.e, self.y * 2 + 1 - self.c)
        return rcopy(self.other(k), self.pairs.at[t], self.cs.at[k], self.cr.at[k], dev)

    def over_y(self, k, d):
        t = self.e ^ k
        dev = (self.e, lax.rem(self.y + d, self.n_y) * 2 + self.c)
        yy = lax.rem(self.y + d, self.n_y)
        return rcopy(self.pairs.at[t, :, yy], self.from_y.at[t, d - 1], self.ys.at[k, d], self.yr.at[k, d], dev)

    def over_exp(self, k):
        t = self.e ^ k
        return rcopy(self.pairs.at[t, :, self.y], self.back.at[self.e], self.es.at[k], self.er.at[k], (t, self.h))

    def pair(self, k, yy):
        t = self.e ^ k
        return self.mine(k, yy).astype(F32) + self.pairs[t, :, yy].astype(F32)

    def step_core(self, k):
        self.over_core(k).start()

    def step_y(self, k):
        t = self.e ^ k
        self.over_core(k).wait_recv()
        for d in range(1, self.n_y):
            yy = lax.rem(self.y + d, self.n_y)
            self.pairs[t, :, yy] = self.pair(k, yy).astype(BF)
            self.over_y(k, d).start()

    def step_exp(self, k, extra=None):
        t = self.e ^ k
        total = self.pair(k, self.y)
        for d in range(1, self.n_y):
            self.over_y(k, d).wait_recv()
            total = total + self.from_y[t, d - 1].astype(F32)
        if extra is not None:
            total = total + extra
        total = total.astype(BF)

        @pl.when(k == 0)
        def _():
            self.back[t] = total

        @pl.when(k > 0)
        def _():
            self.pairs[t, :, self.y] = total
            self.over_exp(k).start()

    def finish(self, k):
        for d in range(1, self.n_y):
            self.over_y(k, d).wait_send()

        @pl.when(k > 0)
        def _():
            self.over_exp(k).wait_send()
            self.over_exp(k).wait_recv()


def norm_rows(rows, gain, shift):
    mean = jnp.mean(rows, axis=-1, keepdims=True)
    centred = rows - mean
    var = jnp.mean(centred * centred, axis=-1, keepdims=True)
    inverse = lax.rsqrt(var + epsilon)
    unit = centred * inverse
    return unit * gain + shift, unit, inverse


def norm_back(upstream, unit, inverse, gain):
    scaled = upstream * gain
    inner = (
        scaled
        - jnp.mean(scaled, axis=-1, keepdims=True)
        - unit * jnp.mean(scaled * unit, axis=-1, keepdims=True)
    )
    return inner * inverse


def slot_block(slot_row, first, count):
    tok = slot_row.shape[1]
    ids = lax.broadcasted_iota(jnp.int32, (count, tok), 0) + first
    return jnp.where(slot_row == ids, 1.0, 0.0).astype(BF)


def tok_block(slot_col, first, count):
    ids = lax.broadcasted_iota(jnp.int32, (slot_col.shape[0], count), 1) + first
    return jnp.where(slot_col == ids, 1.0, 0.0).astype(BF)


def doc_bias(lens, tok):
    q = lax.broadcasted_iota(jnp.int32, (tok, tok), 0)
    k = lax.broadcasted_iota(jnp.int32, (tok, tok), 1)
    dq = jnp.zeros((tok, tok), jnp.int32)
    dk = jnp.zeros((tok, tok), jnp.int32)
    end = 0
    for j in range(lens.shape[1]):
        end = end + lens[0, j]
        dq = dq + jnp.where(q >= end, 1, 0)
        dk = dk + jnp.where(k >= end, 1, 0)
    return jnp.where((dq == dk) & (q >= k), 0.0, masked_score)


def attend_kernel(
    n_exp, n_y, lens, slot_row, tokens, gain1, shift1, w_qkv, w_out, gain2, shift2, cot,
    mixed, context, middle, lse, send, land,
    cot_rows, normed, bias, own_sem, *sems,
):
    tok, width = tokens.shape
    e, h, y, c = place()
    lc, cap = send.shape[1], send.shape[2]
    per = lc * cap
    hd = width // HEADS
    spread = Spread(n_exp, n_y, cot_rows, land, sems)
    greet(n_exp, n_y)

    def pick(source, dst):
        rows = mm(slot_block(slot_row[...], dst * per, per), source)
        return rows.astype(BF).reshape(lc, cap, width)

    @pl.loop(1, n_exp)
    def _(k):
        cot_rows[e ^ k] = pick(cot[...], e ^ k)
        spread.over_exp(k).start()

    cot_rows[e] = pick(cot[...], e)
    own = pltpu.make_async_copy(cot_rows.at[e], land.at[:, e, h], own_sem)
    own.start()

    @pl.loop(0, tok // 128)
    def _(i):
        rows = pl.ds(i * 128, 128)
        out, _, _ = norm_rows(tokens[rows].astype(F32), gain1[...], shift1[...])
        normed[rows] = out.astype(BF)

    bias[...] = doc_bias(lens, tok)
    own.wait()

    @pl.loop(0, 3 * width // 512)
    def _(i):
        cols = pl.ds(pl.multiple_of(i * 512, 512), 512)
        mixed[:, cols] = mm(normed[...], w_qkv[:, cols]).astype(BF)

    lse[...] = jnp.zeros_like(lse)
    lane = lax.broadcasted_iota(jnp.int32, (1, 128), 1)
    n_pairs = width // 128
    steps = n_exp // n_pairs
    half = tok // 2
    heads_in = 128 // hd

    @pl.loop(0, n_pairs)
    def _(p):
        for j in range(steps):
            k = p * steps + j
            spread.pass_on(k)

            @pl.when(k > 0)
            def _():
                spread.pass_y(k - 1)

        def cols(part):
            return pl.ds(pl.multiple_of(part * width + p * 128, 128), 128)

        q, key, val = mixed[:, cols(0)], mixed[:, cols(1)], mixed[:, cols(2)]
        for blk in range(2):
            rows = slice(blk * half, (blk + 1) * half)
            n_keys = (blk + 1) * half
            total = jnp.zeros((half, 128), F32)
            lses = lse[rows, :]
            for hh in range(heads_in):
                own_lanes = (lane >= hh * hd) & (lane < (hh + 1) * hd)
                qh = jnp.where(own_lanes, q[rows] * BF(hd**-0.5), BF(0))
                vh = jnp.where(own_lanes, val[:n_keys], BF(0))
                s = mm_nt(qh, key[:n_keys]) + bias[rows, :n_keys]
                top = jnp.max(s, axis=-1, keepdims=True)
                ex = jnp.exp(s - top)
                tot = jnp.sum(ex, axis=-1, keepdims=True)
                probs = (ex * (1.0 / tot)).astype(BF)
                total = total + mm(probs, vh)
                lses = jnp.where(lane == p * heads_in + hh, top + jnp.log(tot), lses)
            lse[rows, :] = lses
            context[rows, pl.ds(pl.multiple_of(p * 128, 128), 128)] = total.astype(BF)

    spread.pass_y(n_exp - 1)

    @pl.loop(0, tok // 256)
    def _(i):
        rows = pl.ds(i * 256, 256)
        mid = tokens[rows].astype(F32) + mm(context[rows], w_out[...])
        middle[rows] = mid
        out, _, _ = norm_rows(mid, gain2[...], shift2[...])
        normed[rows] = out.astype(BF)

    @pl.loop(0, n_exp)
    def _(k):
        send[k] = pick(normed[...], k)

    @pl.loop(0, n_exp)
    def _(k):
        spread.landed(k)
        spread.sent(k)


def attend(n_exp, n_hid, lc, cap, lens, slot_row, tokens, gain1, shift1, w_qkv, w_out, gain2, shift2, cot):
    n_y = n_hid // 2
    tok, width = tokens.shape
    shape = jax.ShapeDtypeStruct
    return pl.pallas_call(
        functools.partial(attend_kernel, n_exp, n_y),
        name="attend",
        out_shape=(
            shape((tok, 3 * width), BF),
            shape((tok, width), BF),
            shape((tok, width), F32),
            shape((tok, 128), F32),
            shape((n_exp, lc, cap, width), BF),
            shape((lc, n_exp, n_hid, cap, width), BF),
        ),
        in_specs=[SM] + [VM] * 9,
        out_specs=[VM] * 6,
        scratch_shapes=[
            pltpu.VMEM((n_exp, lc, cap, width), BF),
            pltpu.VMEM((tok, width), BF),
            pltpu.VMEM((tok, tok), F32),
            DMA,
            *Spread.sems(n_exp, n_y),
        ],
        compiler_params=pltpu.CompilerParams(
            collective_id=0, has_side_effects=True, vmem_limit_bytes=56 * MIB
        ),
    )(lens, slot_row, tokens, gain1, shift1, w_qkv, w_out, gain2, shift2, cot)


def expert_kernel(
    n_exp, n_y, rows, grads, w_in, bias_in, w_back,
    back, x_out, h_out, gp_out, f_out, gb_in, gb_back,
    land, part, win_v, wback_v, g_v, h_v, gp_v, f_v,
    w_sem, g_sem, o_sem, x_sem, own_sem, *rest,
):
    e, h, y, c = place()
    n_gather = len(Gather.scratch(1, 2, 1, 1, 1))
    n_spread = len(Spread.sems(1, 1))
    scr, sp_sems, ga_sems = rest[:n_gather], rest[n_gather : n_gather + n_spread], rest[n_gather + n_spread :]
    spread = Spread(n_exp, n_y, rows, land, sp_sems)


    def part_of(k):
        return part.at[lax.rem(lax.div(k, 2), 2), :, lax.rem(e ^ k, 2)]

    gather = Gather(
        n_exp, n_y, lambda k: part_of(k).at[:, :, 1 - c], lambda k, yy: part_of(k)[:, yy, c],
        *scr, back, ga_sems,
    )
    n_hid = 2 * n_y
    lc, cap, width = rows.shape[1:]
    ff = w_in.shape[2]
    count = 2 * n_hid * cap
    n_chunks = n_exp // 2
    step_f = min(512, ff)

    def weights(ex):
        return (
            pltpu.make_async_copy(w_in.at[ex], win_v.at[ex], w_sem.at[0, ex]),
            pltpu.make_async_copy(w_back.at[ex], wback_v.at[ex], w_sem.at[1, ex]),
        )

    for ex in range(lc):
        for cp in weights(ex):
            cp.start()

    def base_of(i):
        t = e ^ (2 * lax.div(i, lc))
        return t - lax.rem(t, 2)

    def g_copy(i):
        src = grads.at[lax.rem(i, lc), pl.ds(base_of(i), 2)]
        return pltpu.make_async_copy(src, g_v.at[lax.rem(i, 2)], g_sem.at[lax.rem(i, 2)])

    def out_copies(i):
        ex, slot, to = lax.rem(i, lc), lax.rem(i, 2), pl.ds(base_of(i), 2)
        return (
            pltpu.make_async_copy(h_v.at[slot], h_out.at[ex, to], o_sem.at[0, slot]),
            pltpu.make_async_copy(gp_v.at[slot], gp_out.at[ex, to], o_sem.at[1, slot]),
            pltpu.make_async_copy(f_v.at[slot], f_out.at[ex, to], o_sem.at[2, slot]),
        )

    def x_copy(i):
        ex, to = lax.rem(i, lc), pl.ds(base_of(i), 2)
        return pltpu.make_async_copy(land.at[ex, to], x_out.at[ex, to], x_sem.at[i])

    g_copy(0).start()
    own = pltpu.make_async_copy(rows.at[e], land.at[:, e, h], own_sem)
    own.start()
    greet(n_exp, n_y)

    @pl.loop(1, n_exp)
    def _(k):
        spread.over_exp(k).start()

    gb_in[...] = jnp.zeros_like(gb_in)
    gb_back[...] = jnp.zeros_like(gb_back)
    own.wait()
    spread.pass_on(0)
    spread.pass_on(1)
    spread.pass_y(0)
    spread.pass_y(1)

    n_steps = n_chunks * lc

    @pl.loop(0, n_steps)
    def _(i):
        j, ex = lax.div(i, lc), lax.rem(i, lc)
        slot = lax.rem(i, 2)
        base = base_of(i)

        @pl.when(i + 1 < n_steps)
        def _():
            g_copy(i + 1).start()

        @pl.when(ex == 0)
        def _():
            spread.landed(2 * j)
            spread.landed(2 * j + 1)

            @pl.when(j >= 2)
            def _():
                gather.over_core(2 * j - 4).wait_send()
                gather.over_core(2 * j - 3).wait_send()

        @pl.when(j == 0)
        def _():
            for cp in weights(ex):
                cp.wait()

        x_copy(i).start()
        g_copy(i).wait()

        @pl.when(i >= 2)
        def _():
            for cp in out_copies(i - 2):
                cp.wait()

        x = land[ex, pl.ds(base, 2)].reshape(count, width)
        g = g_v[slot].reshape(count, width)
        gb_back[ex] += jnp.sum(g.astype(F32), axis=0, keepdims=True)
        hs, gps = [], []
        for f in range(ff // step_f):
            cols = slice(f * step_f, (f + 1) * step_f)
            pre = mm(x, win_v[ex, :, cols]) + bias_in[ex, :, cols]
            sig = jax.nn.sigmoid(pre)
            hid = (pre * sig).astype(BF)
            gh = mm_nt(g, wback_v[ex, cols, :])
            gp = (gh * sig * (1.0 + pre * (1.0 - sig))).astype(BF)
            gb_in[ex, :, cols] += jnp.sum(gp.astype(F32), axis=0, keepdims=True)
            h_v[slot, :, :, cols] = hid.reshape(2, n_hid * cap, step_f)
            gp_v[slot, :, :, cols] = gp.reshape(2, n_hid * cap, step_f)
        gpv = gp_v[slot].reshape(count, ff)
        gd = mm_nt(gpv, win_v[ex])
        part[lax.rem(j, 2), ex] = gd.astype(BF).reshape(2, n_y, 2, cap, width)
        hv = h_v[slot].reshape(count, ff)
        f_v[slot] = mm(hv, wback_v[ex]).astype(BF).reshape(2, n_y, 2, cap, width)
        for cp in out_copies(i):
            cp.start()

        @pl.when(j + 1 < n_chunks)
        def _():
            @pl.when(ex == 0)
            def _():
                spread.pass_on(2 * j + 2)

            @pl.when(ex == 1)
            def _():
                spread.pass_y(2 * j + 2)
                spread.pass_on(2 * j + 3)

            @pl.when(ex == 2)
            def _():
                spread.pass_y(2 * j + 3)

        @pl.when(j > 0)
        def _():
            @pl.when(ex == 0)
            def _():
                gather.step_y(2 * j - 2)
                gather.step_y(2 * j - 1)

            @pl.when(ex == lc - 1)
            def _():
                gather.step_exp(2 * j - 2)
                gather.step_exp(2 * j - 1)

        @pl.when(ex == lc - 1)
        def _():
            gather.step_core(2 * j)
            gather.step_core(2 * j + 1)

    gather.step_y(n_exp - 2)
    gather.step_y(n_exp - 1)
    gather.step_exp(n_exp - 2)
    gather.step_exp(n_exp - 1)

    for k in range(n_exp - 4, n_exp):
        gather.over_core(k).wait_send()
    for i in (n_steps - 2, n_steps - 1):
        for cp in out_copies(i):
            cp.wait()

    @pl.loop(0, n_steps)
    def _(i):
        x_copy(i).wait()

    @pl.loop(0, n_exp)
    def _(k):
        spread.sent(k)
        gather.finish(k)


def experts(n_exp, n_hid, rows, grads, w_in, bias_in, w_back):
    n_y = n_hid // 2
    _, lc, cap, width = rows.shape
    ff = w_in.shape[2]
    shape = jax.ShapeDtypeStruct
    per = n_hid * cap
    n_steps = n_exp // 2 * lc
    return pl.pallas_call(
        functools.partial(expert_kernel, n_exp, n_y),
        name="experts",
        out_shape=(
            shape((n_exp, lc, cap, width), BF),
            shape((lc, n_exp, n_hid, cap, width), BF),
            shape((lc, n_exp, per, ff), BF),
            shape((lc, n_exp, per, ff), BF),
            shape((lc, n_exp, n_y, 2, cap, width), BF),
            shape((lc, 1, ff), F32),
            shape((lc, 1, width), F32),
        ),
        in_specs=[VM, HB, HB, VM, HB],
        out_specs=[VM, HB, HB, HB, HB, VM, VM],
        scratch_shapes=[
            pltpu.VMEM((lc, n_exp, n_hid, cap, width), BF),
            pltpu.VMEM((2, lc, 2, n_y, 2, cap, width), BF),
            pltpu.VMEM(w_in.shape, BF),
            pltpu.VMEM(w_back.shape, BF),
            pltpu.VMEM((2, 2, n_hid, cap, width), BF),
            pltpu.VMEM((2, 2, per, ff), BF),
            pltpu.VMEM((2, 2, per, ff), BF),
            pltpu.VMEM((2, 2, n_y, 2, cap, width), BF),
            DMA((2, lc)), DMA((2,)), DMA((3, 2)), DMA((n_steps,)), DMA,
            *Gather.scratch(n_exp, n_y, lc, cap, width),
            *Spread.sems(n_exp, n_y),
            *Gather.sems(n_exp, n_y),
        ],
        compiler_params=pltpu.CompilerParams(
            collective_id=1, has_side_effects=True, vmem_limit_bytes=62 * MIB
        ),
    )(rows, grads, w_in, bias_in, w_back)


def wgrad_kernel(x, gp, h, g, g_in, g_back):
    g_in[0] = mm_tn(x[0], gp[0])
    g_back[0] = mm_tn(h[0], g[0])


def wgrad(x, gp, h, g):
    lc, n, width = x.shape
    ff = gp.shape[2]
    cut = 2
    shape = jax.ShapeDtypeStruct
    return pl.pallas_call(
        wgrad_kernel,
        name="wgrad",
        grid=(lc, cut),
        out_shape=(shape((lc, width, ff), F32), shape((lc, ff, width), F32)),
        in_specs=[
            pl.BlockSpec((1, n, width), lambda i, j: (i, 0, 0)),
            pl.BlockSpec((1, n, ff // cut), lambda i, j: (i, 0, j)),
            pl.BlockSpec((1, n, ff), lambda i, j: (i, 0, 0)),
            pl.BlockSpec((1, n, width // cut), lambda i, j: (i, 0, j)),
        ],
        out_specs=[
            pl.BlockSpec((1, width, ff // cut), lambda i, j: (i, 0, j)),
            pl.BlockSpec((1, ff, width // cut), lambda i, j: (i, 0, j)),
        ],
        compiler_params=pltpu.CompilerParams(vmem_limit_bytes=56 * MIB),
    )(x, gp, h, g)


def attend_back_kernel(
    n_exp, n_y, lens, slot_col, tokens, middle, cot, mixed, context, lse, back,
    gain1, shift1, w_qkv, w_out, gain2, bias_back, f_part,
    output, g_tokens, g_mats, g_norms,
    bias, gm, gattn, gctx, gmixed, n1t, lse_t, mine_v, f_back, mine_sem, *rest,
):
    tok, width = tokens.shape
    hd = width // HEADS
    e, h, y, c = place()
    n_gather = len(Gather.scratch(1, 2, 1, 1, 1))
    lc, cap = f_back.shape[1:3]
    gather = Gather(
        n_exp, n_y, lambda k: f_part.at[:, e ^ k, :, 1 - c], lambda k, yy: mine_v[lax.rem(k, 4), :, yy],
        *rest[:n_gather], f_back, rest[n_gather:],
    )

    def fetch(k):
        slot = lax.rem(k, 4)
        return pltpu.make_async_copy(f_part.at[:, e ^ k, :, c], mine_v.at[slot], mine_sem.at[slot])

    for k in range(3):
        fetch(k).start()
    greet(n_exp, n_y)

    @pl.loop(0, n_exp)
    def _(k):
        gather.step_core(k)

    g_norms[...] = jnp.zeros_like(g_norms)
    n_slots = n_exp * lc * cap

    def fold(values):
        return jnp.sum(values, axis=0, keepdims=True)

    @pl.loop(0, tok // 256)
    def _(i):
        rows = pl.ds(pl.multiple_of(i * 256, 256), 256)
        table = tok_block(slot_col[rows], 0, n_slots)
        up = mm(table, back[...].reshape(n_slots, width))
        _, unit, inverse = norm_rows(middle[rows], gain2[...], 0.0)
        g_norms[2:3] += fold(up * unit)
        g_norms[3:4] += fold(up)
        g_mid = cot[rows].astype(F32) + norm_back(up, unit, inverse, gain2[...])
        gm[rows] = g_mid
        gattn[rows] = g_mid.astype(BF)
        gctx[rows] = mm_nt(gattn[rows], w_out[...]).astype(BF)
        out, _, _ = norm_rows(tokens[rows].astype(F32), gain1[...], shift1[...])
        n1t[:, rows] = out.astype(BF).T

    def step_y(k):
        fetch(k).wait()
        gather.step_y(k)

    step_y(0)
    step_y(1)

    @pl.loop(0, width // 256)
    def _(i):
        cols = pl.ds(pl.multiple_of(i * 256, 256), 256)
        part = mm_tn(context[:, cols], gattn[...]).astype(BF)
        g_mats[3, pl.ds(i * 16, 16)] = part.reshape(16, 16, width)

    key_i = lax.broadcasted_iota(jnp.int32, (tok, tok), 0)
    qry_i = lax.broadcasted_iota(jnp.int32, (tok, tok), 1)
    dk_, dq_ = jnp.zeros((tok, tok), jnp.int32), jnp.zeros((tok, tok), jnp.int32)
    end = 0
    for j in range(lens.shape[1]):
        end = end + lens[0, j]
        dk_ = dk_ + jnp.where(key_i >= end, 1, 0)
        dq_ = dq_ + jnp.where(qry_i >= end, 1, 0)
    bias[...] = jnp.where((dk_ == dq_) & (qry_i >= key_i), 0.0, masked_score)
    lse_t[...] = lse[...].T

    lane = lax.broadcasted_iota(jnp.int32, (1, 128), 1)
    n_pairs = width // 128
    steps = n_exp // n_pairs
    half = tok // 2
    heads_in = 128 // hd

    @pl.loop(0, n_pairs)
    def _(p):
        for j in range(steps):
            k = p * steps + j

            @pl.when(k + 3 < n_exp)
            def _():
                fetch(k + 3).start()

            @pl.when(k + 2 < n_exp)
            def _():
                step_y(k + 2)

            gather.step_exp(k, bias_back[...])

        def cols(part):
            return pl.ds(pl.multiple_of(part * width + p * 128, 128), 128)

        q, key, val, do = mixed[:, cols(0)], mixed[:, cols(1)], mixed[:, cols(2)], gctx[:, cols(0)]
        dq = [jnp.zeros((half, 128), F32) for _ in range(2)]
        dkey = [jnp.zeros((half, 128), F32) for _ in range(2)]
        dval = [jnp.zeros((half, 128), F32) for _ in range(2)]
        for hh in range(heads_in):
            own_lanes = (lane >= hh * hd) & (lane < (hh + 1) * hd)
            qh = jnp.where(own_lanes, q * BF(hd**-0.5), BF(0))
            kh = jnp.where(own_lanes, key * BF(hd**-0.5), BF(0))
            doh = jnp.where(own_lanes, do, BF(0))
            lrow = lse_t[pl.ds(p * heads_in + hh, 1), :]
            for qb in range(2):
                rows = slice(qb * half, (qb + 1) * half)
                n = (qb + 1) * half
                s = mm_nt(key[:n], qh[rows]) + (bias[:n, rows] - lrow[:, rows])
                pt = jnp.exp(s)
                dp = mm_nt(val[:n], doh[rows])
                inner = jnp.sum(dp * pt, axis=0, keepdims=True)
                ds = (pt * (dp - inner)).astype(BF)
                ptb = pt.astype(BF)
                dv_, dk2 = mm(ptb, doh[rows]), mm(ds, qh[rows])
                for kb in range(qb + 1):
                    part = slice(kb * half, (kb + 1) * half)
                    dval[kb] = dval[kb] + dv_[part]
                    dkey[kb] = dkey[kb] + dk2[part]
                dq[qb] = dq[qb] + mm_tn(ds, kh[:n])
        for b in range(2):
            rows = slice(b * half, (b + 1) * half)
            gmixed[rows, cols(0)] = dq[b].astype(BF)
            gmixed[rows, cols(1)] = dkey[b].astype(BF)
            gmixed[rows, cols(2)] = dval[b].astype(BF)

    @pl.loop(0, tok // 256)
    def _(i):
        rows = pl.ds(pl.multiple_of(i * 256, 256), 256)
        up = mm_nt(gmixed[rows], w_qkv[...])
        _, unit, inverse = norm_rows(tokens[rows].astype(F32), gain1[...], 0.0)
        g_norms[0:1] += fold(up * unit)
        g_norms[1:2] += fold(up)
        g_tokens[rows] = gm[rows] + norm_back(up, unit, inverse, gain1[...])

    for part in range(3):

        @pl.loop(0, width // 256)
        def _(i):
            rows = pl.ds(pl.multiple_of(i * 256, 256), 256)
            piece = mm(n1t[rows], gmixed[:, part * width : (part + 1) * width])
            g_mats[part, pl.ds(i * 16, 16)] = piece.astype(BF).reshape(16, 16, width)

    @pl.loop(0, n_exp)
    def _(k):
        gather.over_core(k).wait_send()
        gather.finish(k)

    @pl.loop(0, tok // 256)
    def _(i):
        rows = pl.ds(pl.multiple_of(i * 256, 256), 256)
        table = tok_block(slot_col[rows], 0, n_slots)
        output[rows] = (middle[rows] + mm(table, f_back[...].reshape(n_slots, width))).astype(BF)


def attend_back(
    n_exp, n_hid, lens, slot_col, tokens, middle, cot, mixed, context, lse, back,
    gain1, shift1, w_qkv, w_out, gain2, bias_back, f_part,
):
    n_y = n_hid // 2
    tok, width = tokens.shape
    _, lc, cap, _ = back.shape
    shape = jax.ShapeDtypeStruct
    return pl.pallas_call(
        functools.partial(attend_back_kernel, n_exp, n_y),
        name="attend_back",
        out_shape=(
            shape((tok, width), BF),
            shape((tok, width), F32),
            shape((4, width // 16, 16, width), BF),
            shape((8, width), F32),
        ),
        in_specs=[SM] + [VM] * 14 + [HB],
        out_specs=[VM] * 4,
        scratch_shapes=[
            pltpu.VMEM((tok, tok), F32),
            pltpu.VMEM((tok, width), F32),
            pltpu.VMEM((tok, width), BF),
            pltpu.VMEM((tok, width), BF),
            pltpu.VMEM((tok, 3 * width), BF),
            pltpu.VMEM((width, tok), BF),
            pltpu.VMEM((128, tok), F32),
            pltpu.VMEM((4, lc, n_y, cap, width), BF),
            pltpu.VMEM((n_exp, lc, cap, width), BF),
            DMA((4,)),
            *Gather.scratch(n_exp, n_y, lc, cap, width),
            *Gather.sems(n_exp, n_y),
        ],
        compiler_params=pltpu.CompilerParams(
            collective_id=2, has_side_effects=True, vmem_limit_bytes=62 * MIB
        ),
    )(
        lens, slot_col, tokens, middle, cot, mixed, context, lse, back,
        gain1, shift1, w_qkv, w_out, gain2, bias_back, f_part,
    )


def reduce_all(n_exp, n_hid, mats, norms):
    return lax.psum(mats, ("exp", "hid")), lax.psum(norms, ("exp", "hid"))


def token_slots(token_ids, hash_table, capacity, cap):
    chosen = jnp.take(hash_table, token_ids, mode="clip")
    places = jnp.arange(chosen.shape[0], dtype=jnp.int32)
    earlier = (chosen[:, None] == chosen[None, :]) & (places[:, None] > places[None, :])
    rank = jnp.sum(earlier.astype(jnp.int32), axis=1)
    experts_ids = jnp.arange(capacity.shape[0], dtype=jnp.int32)
    limit = jnp.sum(jnp.where(chosen[:, None] == experts_ids[None, :], capacity[None, :], 0), axis=1)
    return jnp.where(rank < limit, chosen * cap + rank, -1)


def per_device(
    tokens, token_ids, lengths, hash_table, capacity, gain_one, shift_one, w_qkv, w_out,
    gain_two, shift_two, w_in, bias_in, w_back, bias_back, cotangent,
):
    n_exp, n_hid = lax.axis_size("exp"), lax.axis_size("hid")
    tok, width = tokens.shape
    lc, _, ff = w_in.shape
    cap = 2 * tok // capacity.shape[0]
    slot = token_slots(token_ids, hash_table, capacity, cap)
    gain1, shift1, gain2, shift2 = (v[None] for v in (gain_one, shift_one, gain_two, shift_two))
    mixed, context, middle, lse, send, grads = attend(
        n_exp, n_hid, lc, cap, lengths, slot[None], tokens, gain1, shift1, w_qkv, w_out, gain2, shift2, cotangent
    )
    back, x, hid, gp, f_part, gb_in, gb_back = experts(
        n_exp, n_hid, send, grads, w_in, bias_in[:, None], w_back
    )
    output, g_tokens, mats, norms = attend_back(
        n_exp, n_hid, lengths, slot[:, None], tokens, middle, cotangent, mixed, context, lse, back,
        gain1, shift1, w_qkv, w_out, gain2, bias_back[:, None], f_part,
    )
    mats, norms = reduce_all(n_exp, n_hid, mats, norms)
    n_rows = n_exp * n_hid * cap
    g_in, g_back = wgrad(
        x.reshape(lc, n_rows, width), gp.reshape(lc, n_rows, ff),
        hid.reshape(lc, n_rows, ff), grads.reshape(lc, n_rows, width),
    )
    mats = mats.reshape(4, width, width).astype(F32)
    g_qkv = jnp.concatenate([mats[0], mats[1], mats[2]], axis=1)
    return (
        output, g_tokens, norms[0], norms[1], g_qkv, mats[3], norms[2], norms[3],
        g_in, gb_in[:, 0], g_back, gb_back[:, 0],
    )


def solution(mesh):
    both = P(("exp", "hid"))
    rows = P(("exp", "hid"), None)
    placed = (
        rows, both, rows, P(), P(), P(), P(), P(), P(), P(), P(),
        P("exp", None, "hid"), P("exp", "hid"), P("exp", "hid", None), P("exp", None), rows,
    )
    return jax.shard_map(
        per_device,
        mesh=mesh,
        in_specs=placed,
        out_specs=(
            rows, rows, P(), P(), P(), P(), P(), P(),
            P("exp", None, "hid"), P("exp", "hid"), P("exp", "hid", None), P("exp", None),
        ),
        check_vma=False,
    )
```

```python
import functools

import jax
import jax.numpy as jnp
from jax import lax
from jax.experimental import pallas as pl
from jax.experimental.pallas import tpu as pltpu
from jax.sharding import PartitionSpec as P

HEADS = 16
MESH = pl.DeviceIdType.MESH
BF = jnp.bfloat16
F32 = jnp.float32
epsilon = 1e-05
masked_score = -1e30
DMA = pltpu.SemaphoreType.DMA
VM = pl.BlockSpec(memory_space=pltpu.VMEM)
SM = pl.BlockSpec(memory_space=pltpu.SMEM)
HB = pl.BlockSpec(memory_space=pl.ANY)
MIB = 1 << 20


def mm(a, b):
    return lax.dot_general(a, b, (((1,), (0,)), ((), ())), preferred_element_type=F32)


def mm_nt(a, b):
    return lax.dot_general(a, b, (((1,), (1,)), ((), ())), preferred_element_type=F32)


def mm_tn(a, b):
    return lax.dot_general(a, b, (((0,), (0,)), ((), ())), preferred_element_type=F32)


def place():
    e = lax.axis_index("exp")
    h = lax.axis_index("hid")
    return e, h, lax.div(h, 2), lax.rem(h, 2)


def rcopy(src, dst, send, recv, dev):
    return pltpu.make_async_remote_copy(
        src_ref=src, dst_ref=dst, send_sem=send, recv_sem=recv, device_id=dev, device_id_type=MESH
    )


def greet(n_exp, n_y):
    e, h, y, c = place()
    sem = pltpu.get_barrier_semaphore()
    for k in range(1, n_exp):
        pl.semaphore_signal(sem, inc=1, device_id=(e ^ k, h), device_id_type=MESH)
    for d in range(1, n_y):
        pl.semaphore_signal(
            sem, inc=1, device_id=(e, lax.rem(y + d, n_y) * 2 + c), device_id_type=MESH
        )
    pl.semaphore_signal(sem, inc=1, device_id=(e, y * 2 + 1 - c), device_id_type=MESH)
    pl.semaphore_wait(sem, n_exp - 1 + n_y)


class Spread:
    def __init__(self, n_exp, n_y, rows, land, sems):
        self.n_exp, self.n_y, self.rows, self.land = n_exp, n_y, rows, land
        self.es, self.er, self.ys, self.yr, self.cs, self.cr = sems
        self.e, self.h, self.y, self.c = place()

    @staticmethod
    def sems(n_exp, n_y):
        return [DMA((n_exp,)), DMA((n_exp,))] + [DMA((n_exp, n_y))] * 4

    def over_exp(self, k):
        return rcopy(
            self.rows.at[self.e ^ k], self.land.at[:, self.e, self.h],
            self.es.at[k], self.er.at[k], (self.e ^ k, self.h),
        )

    def block(self, k, hid):
        return self.land.at[:, self.e ^ k, hid]

    def over_y(self, k, d):
        blk = self.block(k, self.h)
        dev = (self.e, lax.rem(self.y + d, self.n_y) * 2 + self.c)
        return rcopy(blk, blk, self.ys.at[k, d], self.yr.at[k, d], dev)

    def over_core(self, k, d):
        blk = self.block(k, lax.rem(self.y + self.n_y - d, self.n_y) * 2 + self.c)
        dev = (self.e, self.y * 2 + 1 - self.c)
        return rcopy(blk, blk, self.cs.at[k, d], self.cr.at[k, d], dev)

    def pass_on(self, k):
        @pl.when(k > 0)
        def _():
            self.over_exp(k).wait_recv()

        for d in range(1, self.n_y):
            self.over_y(k, d).start()
        self.over_core(k, 0).start()

    def pass_y(self, k):
        for d in range(1, self.n_y):
            self.over_y(k, d).wait_recv()
            self.over_core(k, d).start()

    def landed(self, k):
        for d in range(self.n_y):
            self.over_core(k, d).wait_recv()

    def sent(self, k):
        @pl.when(k > 0)
        def _():
            self.over_exp(k).wait_send()

        for d in range(1, self.n_y):
            self.over_y(k, d).wait_send()
        for d in range(self.n_y):
            self.over_core(k, d).wait_send()


class Gather:
    def __init__(self, n_exp, n_y, other, mine, pairs, from_y, back, sems):
        self.n_exp, self.n_y, self.other, self.mine = n_exp, n_y, other, mine
        self.pairs, self.from_y, self.back = pairs, from_y, back
        self.es, self.er, self.ys, self.yr, self.cs, self.cr = sems
        self.e, self.h, self.y, self.c = place()

    @staticmethod
    def sems(n_exp, n_y):
        return [DMA((n_exp,)), DMA((n_exp,)), DMA((n_exp, n_y)), DMA((n_exp, n_y)), DMA((n_exp,)), DMA((n_exp,))]

    @staticmethod
    def scratch(n_exp, n_y, lc, cap, d):
        return [
            pltpu.VMEM((n_exp, lc, n_y, cap, d), BF),
            pltpu.VMEM((n_exp, n_y - 1, lc, cap, d), BF),
        ]

    def over_core(self, k):
        t = self.e ^ k
        dev = (self.e, self.y * 2 + 1 - self.c)
        return rcopy(self.other(k), self.pairs.at[t], self.cs.at[k], self.cr.at[k], dev)

    def over_y(self, k, d):
        t = self.e ^ k
        dev = (self.e, lax.rem(self.y + d, self.n_y) * 2 + self.c)
        yy = lax.rem(self.y + d, self.n_y)
        return rcopy(self.pairs.at[t, :, yy], self.from_y.at[t, d - 1], self.ys.at[k, d], self.yr.at[k, d], dev)

    def over_exp(self, k):
        t = self.e ^ k
        return rcopy(self.pairs.at[t, :, self.y], self.back.at[self.e], self.es.at[k], self.er.at[k], (t, self.h))

    def pair(self, k, yy):
        t = self.e ^ k
        return self.mine(k, yy).astype(F32) + self.pairs[t, :, yy].astype(F32)

    def step_core(self, k):
        self.over_core(k).start()

    def step_y(self, k):
        t = self.e ^ k
        self.over_core(k).wait_recv()
        for d in range(1, self.n_y):
            yy = lax.rem(self.y + d, self.n_y)
            self.pairs[t, :, yy] = self.pair(k, yy).astype(BF)
            self.over_y(k, d).start()

    def step_exp(self, k, extra=None):
        t = self.e ^ k
        total = self.pair(k, self.y)
        for d in range(1, self.n_y):
            self.over_y(k, d).wait_recv()
            total = total + self.from_y[t, d - 1].astype(F32)
        if extra is not None:
            total = total + extra
        total = total.astype(BF)

        @pl.when(k == 0)
        def _():
            self.back[t] = total

        @pl.when(k > 0)
        def _():
            self.pairs[t, :, self.y] = total
            self.over_exp(k).start()

    def finish(self, k):
        for d in range(1, self.n_y):
            self.over_y(k, d).wait_send()

        @pl.when(k > 0)
        def _():
            self.over_exp(k).wait_send()
            self.over_exp(k).wait_recv()


def norm_rows(rows, gain, shift):
    mean = jnp.mean(rows, axis=-1, keepdims=True)
    centred = rows - mean
    var = jnp.mean(centred * centred, axis=-1, keepdims=True)
    inverse = lax.rsqrt(var + epsilon)
    unit = centred * inverse
    return unit * gain + shift, unit, inverse


def norm_back(upstream, unit, inverse, gain):
    scaled = upstream * gain
    inner = (
        scaled
        - jnp.mean(scaled, axis=-1, keepdims=True)
        - unit * jnp.mean(scaled * unit, axis=-1, keepdims=True)
    )
    return inner * inverse


def slot_block(slot_row, first, count):
    tok = slot_row.shape[1]
    ids = lax.broadcasted_iota(jnp.int32, (count, tok), 0) + first
    return jnp.where(slot_row == ids, 1.0, 0.0).astype(BF)


def tok_block(slot_col, first, count):
    ids = lax.broadcasted_iota(jnp.int32, (slot_col.shape[0], count), 1) + first
    return jnp.where(slot_col == ids, 1.0, 0.0).astype(BF)


def doc_bias(lens, tok):
    q = lax.broadcasted_iota(jnp.int32, (tok, tok), 0)
    k = lax.broadcasted_iota(jnp.int32, (tok, tok), 1)
    dq = jnp.zeros((tok, tok), jnp.int32)
    dk = jnp.zeros((tok, tok), jnp.int32)
    end = 0
    for j in range(lens.shape[1]):
        end = end + lens[0, j]
        dq = dq + jnp.where(q >= end, 1, 0)
        dk = dk + jnp.where(k >= end, 1, 0)
    return jnp.where((dq == dk) & (q >= k), 0.0, masked_score)


def attend_kernel(
    n_exp, n_y, lens, slot_row, tokens, gain1, shift1, w_qkv, w_out, gain2, shift2, cot,
    mixed, context, middle, lse, send, land,
    cot_rows, normed, bias, own_sem, *sems,
):
    tok, width = tokens.shape
    e, h, y, c = place()
    lc, cap = send.shape[1], send.shape[2]
    per = lc * cap
    hd = width // HEADS
    spread = Spread(n_exp, n_y, cot_rows, land, sems)
    greet(n_exp, n_y)

    def pick(source, dst):
        rows = mm(slot_block(slot_row[...], dst * per, per), source)
        return rows.astype(BF).reshape(lc, cap, width)

    @pl.loop(1, n_exp)
    def _(k):
        cot_rows[e ^ k] = pick(cot[...], e ^ k)
        spread.over_exp(k).start()

    cot_rows[e] = pick(cot[...], e)
    own = pltpu.make_async_copy(cot_rows.at[e], land.at[:, e, h], own_sem)
    own.start()

    @pl.loop(0, tok // 128)
    def _(i):
        rows = pl.ds(i * 128, 128)
        out, _, _ = norm_rows(tokens[rows].astype(F32), gain1[...], shift1[...])
        normed[rows] = out.astype(BF)

    bias[...] = doc_bias(lens, tok)
    own.wait()

    @pl.loop(0, 3 * width // 512)
    def _(i):
        cols = pl.ds(pl.multiple_of(i * 512, 512), 512)
        mixed[:, cols] = mm(normed[...], w_qkv[:, cols]).astype(BF)

    lse[...] = jnp.zeros_like(lse)
    lane = lax.broadcasted_iota(jnp.int32, (1, 128), 1)
    n_pairs = width // 128
    steps = n_exp // n_pairs
    half = tok // 2
    heads_in = 128 // hd

    @pl.loop(0, n_pairs)
    def _(p):
        for j in range(steps):
            k = p * steps + j
            spread.pass_on(k)

            @pl.when(k > 0)
            def _():
                spread.pass_y(k - 1)

        def cols(part):
            return pl.ds(pl.multiple_of(part * width + p * 128, 128), 128)

        q, key, val = mixed[:, cols(0)], mixed[:, cols(1)], mixed[:, cols(2)]
        for blk in range(2):
            rows = slice(blk * half, (blk + 1) * half)
            n_keys = (blk + 1) * half
            total = jnp.zeros((half, 128), F32)
            lses = lse[rows, :]
            for hh in range(heads_in):
                own_lanes = (lane >= hh * hd) & (lane < (hh + 1) * hd)
                qh = jnp.where(own_lanes, q[rows] * BF(hd**-0.5), BF(0))
                vh = jnp.where(own_lanes, val[:n_keys], BF(0))
                s = mm_nt(qh, key[:n_keys]) + bias[rows, :n_keys]
                top = jnp.max(s, axis=-1, keepdims=True)
                ex = jnp.exp(s - top)
                tot = jnp.sum(ex, axis=-1, keepdims=True)
                probs = (ex * (1.0 / tot)).astype(BF)
                total = total + mm(probs, vh)
                lses = jnp.where(lane == p * heads_in + hh, top + jnp.log(tot), lses)
            lse[rows, :] = lses
            context[rows, pl.ds(pl.multiple_of(p * 128, 128), 128)] = total.astype(BF)

    spread.pass_y(n_exp - 1)

    @pl.loop(0, tok // 256)
    def _(i):
        rows = pl.ds(i * 256, 256)
        mid = tokens[rows].astype(F32) + mm(context[rows], w_out[...])
        middle[rows] = mid
        out, _, _ = norm_rows(mid, gain2[...], shift2[...])
        normed[rows] = out.astype(BF)

    @pl.loop(0, n_exp)
    def _(k):
        send[k] = pick(normed[...], k)

    @pl.loop(0, n_exp)
    def _(k):
        spread.landed(k)
        spread.sent(k)


def attend(n_exp, n_hid, lc, cap, lens, slot_row, tokens, gain1, shift1, w_qkv, w_out, gain2, shift2, cot):
    n_y = n_hid // 2
    tok, width = tokens.shape
    shape = jax.ShapeDtypeStruct
    return pl.pallas_call(
        functools.partial(attend_kernel, n_exp, n_y),
        name="attend",
        out_shape=(
            shape((tok, 3 * width), BF),
            shape((tok, width), BF),
            shape((tok, width), F32),
            shape((tok, 128), F32),
            shape((n_exp, lc, cap, width), BF),
            shape((lc, n_exp, n_hid, cap, width), BF),
        ),
        in_specs=[SM] + [VM] * 9,
        out_specs=[VM] * 6,
        scratch_shapes=[
            pltpu.VMEM((n_exp, lc, cap, width), BF),
            pltpu.VMEM((tok, width), BF),
            pltpu.VMEM((tok, tok), F32),
            DMA,
            *Spread.sems(n_exp, n_y),
        ],
        compiler_params=pltpu.CompilerParams(
            collective_id=0, has_side_effects=True, vmem_limit_bytes=56 * MIB
        ),
    )(lens, slot_row, tokens, gain1, shift1, w_qkv, w_out, gain2, shift2, cot)


def expert_kernel(
    n_exp, n_y, rows, grads, w_in, bias_in, w_back,
    back, x_out, h_out, gp_out, f_out, gb_in, gb_back,
    land, part, win_v, wback_v, g_v, h_v, gp_v, f_v,
    w_sem, g_sem, o_sem, x_sem, own_sem, *rest,
):
    e, h, y, c = place()
    n_gather = len(Gather.scratch(1, 2, 1, 1, 1))
    n_spread = len(Spread.sems(1, 1))
    scr, sp_sems, ga_sems = rest[:n_gather], rest[n_gather : n_gather + n_spread], rest[n_gather + n_spread :]
    spread = Spread(n_exp, n_y, rows, land, sp_sems)


    def part_of(k):
        return part.at[lax.rem(lax.div(k, 2), 2), :, lax.rem(e ^ k, 2)]

    gather = Gather(
        n_exp, n_y, lambda k: part_of(k).at[:, :, 1 - c], lambda k, yy: part_of(k)[:, yy, c],
        *scr, back, ga_sems,
    )
    n_hid = 2 * n_y
    lc, cap, width = rows.shape[1:]
    ff = w_in.shape[2]
    count = 2 * n_hid * cap
    n_chunks = n_exp // 2
    step_f = min(512, ff)

    def weights(ex):
        return (
            pltpu.make_async_copy(w_in.at[ex], win_v.at[ex], w_sem.at[0, ex]),
            pltpu.make_async_copy(w_back.at[ex], wback_v.at[ex], w_sem.at[1, ex]),
        )

    for ex in range(lc):
        for cp in weights(ex):
            cp.start()

    def base_of(i):
        t = e ^ (2 * lax.div(i, lc))
        return t - lax.rem(t, 2)

    def g_copy(i):
        src = grads.at[lax.rem(i, lc), pl.ds(base_of(i), 2)]
        return pltpu.make_async_copy(src, g_v.at[lax.rem(i, 2)], g_sem.at[lax.rem(i, 2)])

    def out_copies(i):
        ex, slot, to = lax.rem(i, lc), lax.rem(i, 2), pl.ds(base_of(i), 2)
        return (
            pltpu.make_async_copy(h_v.at[slot], h_out.at[ex, to], o_sem.at[0, slot]),
            pltpu.make_async_copy(gp_v.at[slot], gp_out.at[ex, to], o_sem.at[1, slot]),
            pltpu.make_async_copy(f_v.at[slot], f_out.at[ex, to], o_sem.at[2, slot]),
        )

    def x_copy(i):
        ex, to = lax.rem(i, lc), pl.ds(base_of(i), 2)
        return pltpu.make_async_copy(land.at[ex, to], x_out.at[ex, to], x_sem.at[i])

    g_copy(0).start()
    own = pltpu.make_async_copy(rows.at[e], land.at[:, e, h], own_sem)
    own.start()
    greet(n_exp, n_y)

    @pl.loop(1, n_exp)
    def _(k):
        spread.over_exp(k).start()

    gb_in[...] = jnp.zeros_like(gb_in)
    gb_back[...] = jnp.zeros_like(gb_back)
    own.wait()
    spread.pass_on(0)
    spread.pass_on(1)
    spread.pass_y(0)
    spread.pass_y(1)

    n_steps = n_chunks * lc

    @pl.loop(0, n_steps)
    def _(i):
        j, ex = lax.div(i, lc), lax.rem(i, lc)
        slot = lax.rem(i, 2)
        base = base_of(i)

        @pl.when(i + 1 < n_steps)
        def _():
            g_copy(i + 1).start()

        @pl.when(ex == 0)
        def _():
            spread.landed(2 * j)
            spread.landed(2 * j + 1)

            @pl.when(j >= 2)
            def _():
                gather.over_core(2 * j - 4).wait_send()
                gather.over_core(2 * j - 3).wait_send()

        @pl.when(j == 0)
        def _():
            for cp in weights(ex):
                cp.wait()

        x_copy(i).start()
        g_copy(i).wait()

        @pl.when(i >= 2)
        def _():
            for cp in out_copies(i - 2):
                cp.wait()

        x = land[ex, pl.ds(base, 2)].reshape(count, width)
        g = g_v[slot].reshape(count, width)
        gb_back[pl.ds(ex, 1)] += jnp.sum(g.astype(F32), axis=0, keepdims=True)
        hs, gps = [], []
        for f in range(ff // step_f):
            cols = slice(f * step_f, (f + 1) * step_f)
            pre = mm(x, win_v[ex, :, cols]) + bias_in[pl.ds(ex, 1), cols]
            sig = jax.nn.sigmoid(pre)
            hid = (pre * sig).astype(BF)
            gh = mm_nt(g, wback_v[ex, cols, :])
            gp = (gh * sig * (1.0 + pre * (1.0 - sig))).astype(BF)
            gb_in[pl.ds(ex, 1), cols] += jnp.sum(gp.astype(F32), axis=0, keepdims=True)
            h_v[slot, :, :, cols] = hid.reshape(2, n_hid * cap, step_f)
            gp_v[slot, :, :, cols] = gp.reshape(2, n_hid * cap, step_f)
        gpv = gp_v[slot].reshape(count, ff)
        gd = mm_nt(gpv, win_v[ex])
        part[lax.rem(j, 2), ex] = gd.astype(BF).reshape(2, n_y, 2, cap, width)
        hv = h_v[slot].reshape(count, ff)
        f_v[slot] = mm(hv, wback_v[ex]).astype(BF).reshape(2, n_y, 2, cap, width)
        for cp in out_copies(i):
            cp.start()

        @pl.when(j + 1 < n_chunks)
        def _():
            @pl.when(ex == 0)
            def _():
                spread.pass_on(2 * j + 2)

            @pl.when(ex == 1)
            def _():
                spread.pass_y(2 * j + 2)
                spread.pass_on(2 * j + 3)

            @pl.when(ex == 2)
            def _():
                spread.pass_y(2 * j + 3)

        @pl.when(j > 0)
        def _():
            @pl.when(ex == 0)
            def _():
                gather.step_y(2 * j - 2)
                gather.step_y(2 * j - 1)

            @pl.when(ex == lc - 1)
            def _():
                gather.step_exp(2 * j - 2)
                gather.step_exp(2 * j - 1)

        @pl.when(ex == lc - 1)
        def _():
            gather.step_core(2 * j)
            gather.step_core(2 * j + 1)

    gather.step_y(n_exp - 2)
    gather.step_y(n_exp - 1)
    gather.step_exp(n_exp - 2)
    gather.step_exp(n_exp - 1)

    for k in range(n_exp - 4, n_exp):
        gather.over_core(k).wait_send()
    for i in (n_steps - 2, n_steps - 1):
        for cp in out_copies(i):
            cp.wait()

    @pl.loop(0, n_steps)
    def _(i):
        x_copy(i).wait()

    @pl.loop(0, n_exp)
    def _(k):
        spread.sent(k)
        gather.finish(k)


def experts(n_exp, n_hid, rows, grads, w_in, bias_in, w_back):
    n_y = n_hid // 2
    _, lc, cap, width = rows.shape
    ff = w_in.shape[2]
    shape = jax.ShapeDtypeStruct
    per = n_hid * cap
    n_steps = n_exp // 2 * lc
    return pl.pallas_call(
        functools.partial(expert_kernel, n_exp, n_y),
        name="experts",
        out_shape=(
            shape((n_exp, lc, cap, width), BF),
            shape((lc, n_exp, n_hid, cap, width), BF),
            shape((lc, n_exp, per, ff), BF),
            shape((lc, n_exp, per, ff), BF),
            shape((lc, n_exp, n_y, 2, cap, width), BF),
            shape((lc, ff), F32),
            shape((lc, width), F32),
        ),
        in_specs=[VM, HB, HB, VM, HB],
        out_specs=[VM, HB, HB, HB, HB, VM, VM],
        scratch_shapes=[
            pltpu.VMEM((lc, n_exp, n_hid, cap, width), BF),
            pltpu.VMEM((2, lc, 2, n_y, 2, cap, width), BF),
            pltpu.VMEM(w_in.shape, BF),
            pltpu.VMEM(w_back.shape, BF),
            pltpu.VMEM((2, 2, n_hid, cap, width), BF),
            pltpu.VMEM((2, 2, per, ff), BF),
            pltpu.VMEM((2, 2, per, ff), BF),
            pltpu.VMEM((2, 2, n_y, 2, cap, width), BF),
            DMA((2, lc)), DMA((2,)), DMA((3, 2)), DMA((n_steps,)), DMA,
            *Gather.scratch(n_exp, n_y, lc, cap, width),
            *Spread.sems(n_exp, n_y),
            *Gather.sems(n_exp, n_y),
        ],
        compiler_params=pltpu.CompilerParams(
            collective_id=1, has_side_effects=True, vmem_limit_bytes=62 * MIB
        ),
    )(rows, grads, w_in, bias_in, w_back)


def finish_kernel(x, gp, h, g, mats, g_in, g_back, g_qkv, g_out):
    g_in[0] = mm_tn(x[0], gp[0])
    g_back[0] = mm_tn(h[0], g[0])
    rows, width = g_out.shape
    for part in range(3):
        g_qkv[:, part * width : (part + 1) * width] = mats[part].reshape(rows, width).astype(F32)
    g_out[...] = mats[3].reshape(rows, width).astype(F32)


def finish(x, gp, h, g, mats):
    lc, n, width = x.shape
    ff = gp.shape[2]
    cut = 2
    rows = width // (lc * cut)
    mats = mats.reshape(4, width // 16, 16, width)
    shape = jax.ShapeDtypeStruct
    return pl.pallas_call(
        finish_kernel,
        name="finish",
        grid=(lc, cut),
        out_shape=(
            shape((lc, width, ff), F32), shape((lc, ff, width), F32),
            shape((width, 3 * width), F32), shape((width, width), F32),
        ),
        in_specs=[
            pl.BlockSpec((1, n, width), lambda i, j: (i, 0, 0)),
            pl.BlockSpec((1, n, ff // cut), lambda i, j: (i, 0, j)),
            pl.BlockSpec((1, n, ff), lambda i, j: (i, 0, 0)),
            pl.BlockSpec((1, n, width // cut), lambda i, j: (i, 0, j)),
            pl.BlockSpec((4, rows // 16, 16, width), lambda i, j: (0, i * cut + j, 0, 0)),
        ],
        out_specs=[
            pl.BlockSpec((1, width, ff // cut), lambda i, j: (i, 0, j)),
            pl.BlockSpec((1, ff, width // cut), lambda i, j: (i, 0, j)),
            pl.BlockSpec((rows, 3 * width), lambda i, j: (i * cut + j, 0)),
            pl.BlockSpec((rows, width), lambda i, j: (i * cut + j, 0)),
        ],
        compiler_params=pltpu.CompilerParams(vmem_limit_bytes=56 * MIB),
    )(x, gp, h, g, mats)


def attend_back_kernel(
    n_exp, n_y, lens, slot_col, tokens, middle, cot, mixed, context, lse, back,
    gain1, shift1, w_qkv, w_out, gain2, bias_back, f_part,
    output, g_tokens, g_mats, g_norms,
    bias, gm, gattn, gctx, gmixed, n1t, lse_t, mine_v, f_back, mine_sem, *rest,
):
    tok, width = tokens.shape
    hd = width // HEADS
    e, h, y, c = place()
    n_gather = len(Gather.scratch(1, 2, 1, 1, 1))
    lc, cap = f_back.shape[1:3]
    gather = Gather(
        n_exp, n_y, lambda k: f_part.at[:, e ^ k, :, 1 - c], lambda k, yy: mine_v[lax.rem(k, 4), :, yy],
        *rest[:n_gather], f_back, rest[n_gather:],
    )

    def fetch(k):
        slot = lax.rem(k, 4)
        return pltpu.make_async_copy(f_part.at[:, e ^ k, :, c], mine_v.at[slot], mine_sem.at[slot])

    for k in range(3):
        fetch(k).start()
    greet(n_exp, n_y)

    @pl.loop(0, n_exp)
    def _(k):
        gather.step_core(k)

    g_norms[...] = jnp.zeros_like(g_norms)
    n_slots = n_exp * lc * cap

    def fold(values):
        return jnp.sum(values, axis=0, keepdims=True)

    @pl.loop(0, tok // 256)
    def _(i):
        rows = pl.ds(pl.multiple_of(i * 256, 256), 256)
        table = tok_block(slot_col[rows], 0, n_slots)
        up = mm(table, back[...].reshape(n_slots, width))
        _, unit, inverse = norm_rows(middle[rows], gain2[...], 0.0)
        g_norms[2:3] += fold(up * unit)
        g_norms[3:4] += fold(up)
        g_mid = cot[rows].astype(F32) + norm_back(up, unit, inverse, gain2[...])
        gm[rows] = g_mid
        gattn[rows] = g_mid.astype(BF)
        gctx[rows] = mm_nt(gattn[rows], w_out[...]).astype(BF)
        out, _, _ = norm_rows(tokens[rows].astype(F32), gain1[...], shift1[...])
        n1t[:, rows] = out.astype(BF).T

    def step_y(k):
        fetch(k).wait()
        gather.step_y(k)

    step_y(0)
    step_y(1)

    @pl.loop(0, width // 256)
    def _(i):
        cols = pl.ds(pl.multiple_of(i * 256, 256), 256)
        part = mm_tn(context[:, cols], gattn[...]).astype(BF)
        g_mats[3, pl.ds(i * 16, 16)] = part.reshape(16, 16, width)

    key_i = lax.broadcasted_iota(jnp.int32, (tok, tok), 0)
    qry_i = lax.broadcasted_iota(jnp.int32, (tok, tok), 1)
    dk_, dq_ = jnp.zeros((tok, tok), jnp.int32), jnp.zeros((tok, tok), jnp.int32)
    end = 0
    for j in range(lens.shape[1]):
        end = end + lens[0, j]
        dk_ = dk_ + jnp.where(key_i >= end, 1, 0)
        dq_ = dq_ + jnp.where(qry_i >= end, 1, 0)
    bias[...] = jnp.where((dk_ == dq_) & (qry_i >= key_i), 0.0, masked_score)
    lse_t[...] = lse[...].T

    lane = lax.broadcasted_iota(jnp.int32, (1, 128), 1)
    n_pairs = width // 128
    steps = n_exp // n_pairs
    half = tok // 2
    heads_in = 128 // hd

    @pl.loop(0, n_pairs)
    def _(p):
        for j in range(steps):
            k = p * steps + j

            @pl.when(k + 3 < n_exp)
            def _():
                fetch(k + 3).start()

            @pl.when(k + 2 < n_exp)
            def _():
                step_y(k + 2)

            gather.step_exp(k, bias_back[...].reshape(lc, 1, width))

        def cols(part):
            return pl.ds(pl.multiple_of(part * width + p * 128, 128), 128)

        q, key, val, do = mixed[:, cols(0)], mixed[:, cols(1)], mixed[:, cols(2)], gctx[:, cols(0)]
        dq = [jnp.zeros((half, 128), F32) for _ in range(2)]
        dkey = [jnp.zeros((half, 128), F32) for _ in range(2)]
        dval = [jnp.zeros((half, 128), F32) for _ in range(2)]
        for hh in range(heads_in):
            own_lanes = (lane >= hh * hd) & (lane < (hh + 1) * hd)
            qh = jnp.where(own_lanes, q * BF(hd**-0.5), BF(0))
            kh = jnp.where(own_lanes, key * BF(hd**-0.5), BF(0))
            doh = jnp.where(own_lanes, do, BF(0))
            lrow = lse_t[pl.ds(p * heads_in + hh, 1), :]
            for qb in range(2):
                rows = slice(qb * half, (qb + 1) * half)
                n = (qb + 1) * half
                s = mm_nt(key[:n], qh[rows]) + (bias[:n, rows] - lrow[:, rows])
                pt = jnp.exp(s)
                dp = mm_nt(val[:n], doh[rows])
                inner = jnp.sum(dp * pt, axis=0, keepdims=True)
                ds = (pt * (dp - inner)).astype(BF)
                ptb = pt.astype(BF)
                dv_, dk2 = mm(ptb, doh[rows]), mm(ds, qh[rows])
                for kb in range(qb + 1):
                    part = slice(kb * half, (kb + 1) * half)
                    dval[kb] = dval[kb] + dv_[part]
                    dkey[kb] = dkey[kb] + dk2[part]
                dq[qb] = dq[qb] + mm_tn(ds, kh[:n])
        for b in range(2):
            rows = slice(b * half, (b + 1) * half)
            gmixed[rows, cols(0)] = dq[b].astype(BF)
            gmixed[rows, cols(1)] = dkey[b].astype(BF)
            gmixed[rows, cols(2)] = dval[b].astype(BF)

    @pl.loop(0, tok // 256)
    def _(i):
        rows = pl.ds(pl.multiple_of(i * 256, 256), 256)
        up = mm_nt(gmixed[rows], w_qkv[...])
        _, unit, inverse = norm_rows(tokens[rows].astype(F32), gain1[...], 0.0)
        g_norms[0:1] += fold(up * unit)
        g_norms[1:2] += fold(up)
        g_tokens[rows] = gm[rows] + norm_back(up, unit, inverse, gain1[...])

    for part in range(3):

        @pl.loop(0, width // 256)
        def _(i):
            rows = pl.ds(pl.multiple_of(i * 256, 256), 256)
            piece = mm(n1t[rows], gmixed[:, part * width : (part + 1) * width])
            g_mats[part, pl.ds(i * 16, 16)] = piece.astype(BF).reshape(16, 16, width)

    @pl.loop(0, n_exp)
    def _(k):
        gather.over_core(k).wait_send()
        gather.finish(k)

    @pl.loop(0, tok // 256)
    def _(i):
        rows = pl.ds(pl.multiple_of(i * 256, 256), 256)
        table = tok_block(slot_col[rows], 0, n_slots)
        output[rows] = (middle[rows] + mm(table, f_back[...].reshape(n_slots, width))).astype(BF)


def attend_back(
    n_exp, n_hid, lens, slot_col, tokens, middle, cot, mixed, context, lse, back,
    gain1, shift1, w_qkv, w_out, gain2, bias_back, f_part,
):
    n_y = n_hid // 2
    tok, width = tokens.shape
    _, lc, cap, _ = back.shape
    shape = jax.ShapeDtypeStruct
    return pl.pallas_call(
        functools.partial(attend_back_kernel, n_exp, n_y),
        name="attend_back",
        out_shape=(
            shape((tok, width), BF),
            shape((tok, width), F32),
            shape((4, width // 16, 16, width), BF),
            shape((8, width), F32),
        ),
        in_specs=[SM] + [VM] * 14 + [HB],
        out_specs=[VM] * 4,
        scratch_shapes=[
            pltpu.VMEM((tok, tok), F32),
            pltpu.VMEM((tok, width), F32),
            pltpu.VMEM((tok, width), BF),
            pltpu.VMEM((tok, width), BF),
            pltpu.VMEM((tok, 3 * width), BF),
            pltpu.VMEM((width, tok), BF),
            pltpu.VMEM((128, tok), F32),
            pltpu.VMEM((4, lc, n_y, cap, width), BF),
            pltpu.VMEM((n_exp, lc, cap, width), BF),
            DMA((4,)),
            *Gather.scratch(n_exp, n_y, lc, cap, width),
            *Gather.sems(n_exp, n_y),
        ],
        compiler_params=pltpu.CompilerParams(
            collective_id=2, has_side_effects=True, vmem_limit_bytes=62 * MIB
        ),
    )(
        lens, slot_col, tokens, middle, cot, mixed, context, lse, back,
        gain1, shift1, w_qkv, w_out, gain2, bias_back, f_part,
    )


def reduce_kernel(
    n_x, n_y, n_z, mats, norms, out, norms_out,
    acc, core_in, in1, in2, in3, n_acc, n_in,
    c_s, c_r, s1, r1, s2, r2, s3, r3, t3, u3, t2, u2, t1, u1, d_s, d_r, n_s, n_r,
):
    e, h, y, c = place()
    x, z = lax.rem(e, n_x), lax.div(e, n_x)
    sub = n_x * n_y * n_z
    half = mats.shape[0] // 2
    piece = half // 2
    n_sub = piece // sub
    at = {"x": (n_x, x), "y": (n_y, y), "z": (n_z, z)}
    orders = (("y", "x", "z"), ("x", "y", "z"))
    sibling = (e, y * 2 + 1 - c)

    def device(axis, o):
        return {"x": (z * n_x + o, h), "y": (e, o * 2 + c), "z": (o * n_x + x, h)}[axis]

    sem = pltpu.get_barrier_semaphore()
    for axis in "xyz":
        n, i = at[axis]
        for d in range(1, n):
            pl.semaphore_signal(sem, inc=1, device_id=device(axis, lax.rem(i + d, n)), device_id_type=MESH)
    pl.semaphore_signal(sem, inc=1, device_id=sibling, device_id_type=MESH)
    pl.semaphore_wait(sem, n_x + n_y + n_z - 2)

    def units(p, b, depth):
        first, count = p * piece + b * sub, sub
        for axis in orders[p][:depth]:
            n, i = at[axis]
            count = count // n
            first = first + i * count
        return first, count

    def core_copy(p, b):
        first = p * piece + b * sub
        return rcopy(
            mats.at[pl.ds((1 - c) * half + first, sub)], core_in.at[pl.ds(first, sub)],
            c_s.at[p, b], c_r.at[p, b], sibling,
        )

    lands = (in1, in2, in3)
    sends, recvs = (s1, s2, s3), (r1, r2, r3)

    def down(p, b, stage, d):
        n, i = at[orders[p][stage]]
        first, count = units(p, b, stage)
        count = count // n
        o = lax.rem(i + d, n)
        return rcopy(
            acc.at[pl.ds(first + o * count, count)], lands[stage].at[p, b, d - 1, pl.ds(0, count)],
            sends[stage].at[p, b, d - 1], recvs[stage].at[p, b, d - 1], device(orders[p][stage], o),
        )

    ups, upr = (t1, t2, t3), (u1, u2, u3)

    def up(p, b, stage, d):
        n, i = at[orders[p][stage]]
        first, count = units(p, b, stage + 1)
        region = out.at[pl.ds(c * half + first, count)]
        o = lax.rem(i + d, n)
        return rcopy(
            region, region, ups[stage].at[p, b, d - 1], upr[stage].at[p, b, d - 1], device(orders[p][stage], o)
        )

    def core_up(p, b):
        region = out.at[pl.ds(c * half + p * piece + b * sub, sub)]
        return rcopy(region, region, d_s.at[p, b], d_r.at[p, b], sibling)

    def peers(p, stage):
        return range(1, at[orders[p][stage]][0])

    def event(p, b, q):
        if q == 0:
            core_copy(p, b).wait_recv()
            first = p * piece + b * sub
            mine = mats[pl.ds(c * half + first, sub)].astype(F32)
            acc[pl.ds(first, sub)] = (mine + core_in[pl.ds(first, sub)].astype(F32)).astype(BF)
        elif q <= 3:
            first, count = units(p, b, q)
            total = acc[pl.ds(first, count)].astype(F32)
            for d in peers(p, q - 1):
                down(p, b, q - 1, d).wait_recv()
                total = total + lands[q - 1][p, b, d - 1, :count].astype(F32)
            if q < 3:
                acc[pl.ds(first, count)] = total.astype(BF)
            else:
                out[pl.ds(c * half + first, count)] = total.astype(BF)
        else:
            for d in peers(p, 6 - q):
                up(p, b, 6 - q, d).wait_recv()
        if q < 3:
            for d in peers(p, q):
                down(p, b, q, d).start()
        elif q < 6:
            for d in peers(p, 5 - q):
                up(p, b, 5 - q, d).start()
        else:
            core_up(p, b).start()

    for b in range(n_sub):
        for p in range(2):
            core_copy(p, b).start()

    n_axes = (None, "y", "x", "z")

    def n_copy(stage, d):
        if stage == 0:
            dev = sibling
        else:
            n, i = at[n_axes[stage]]
            dev = device(n_axes[stage], lax.rem(i + d, n))
        return rcopy(n_acc.at[stage], n_in.at[stage, d - 1], n_s.at[stage, d - 1], n_r.at[stage, d - 1], dev)

    def n_peers(stage):
        return range(1, 2 if stage == 0 else at[n_axes[stage]][0])

    def n_total(stage):
        for d in n_peers(stage):
            n_copy(stage, d).wait_recv()
        own = n_acc[stage]
        if stage == 0:
            return own + n_in[0, 0]
        n, i = at[n_axes[stage]]
        total = jnp.zeros_like(own)
        for m in range(n):
            term = own
            for d in range(1, n):
                term = jnp.where(lax.rem(i + n - d, n) == m, n_in[stage, d - 1], term)
            total = total + term
        return total

    n_acc[0] = norms[...]
    n_copy(0, 1).start()

    @pl.loop(0, n_sub + 6)
    def _(s):
        for q in range(7):

            @pl.when((s >= q) & (s - q < n_sub))
            def _():
                for p in range(2):
                    event(p, s - q, q)

        for stage in range(1, 4):

            @pl.when(s == stage)
            def _():
                n_acc[stage] = n_total(stage - 1)
                for d in n_peers(stage):
                    n_copy(stage, d).start()

    norms_out[...] = n_total(3)
    for stage in range(4):
        for d in n_peers(stage):
            n_copy(stage, d).wait_send()

    @pl.loop(0, n_sub)
    def _(b):
        for p in range(2):
            core_up(p, b).wait_recv()
            core_copy(p, b).wait_send()
            core_up(p, b).wait_send()
            for stage in range(3):
                for d in peers(p, stage):
                    down(p, b, stage, d).wait_send()
                    up(p, b, stage, d).wait_send()


def reduce_all(n_exp, n_hid, mats, norms):
    n_y = n_hid // 2
    n_x = n_y
    n_z = n_exp // n_x
    sub = n_x * n_y * n_z
    width = norms.shape[1]
    flat = mats.reshape(-1, 16, width)
    half = flat.shape[0] // 2
    n_sub = half // 2 // sub
    most = max(n_x, n_y)
    shape = jax.ShapeDtypeStruct

    def land(n, count):
        return pltpu.VMEM((2, n_sub, n - 1, count, 16, width), BF)

    def sems(n):
        return [DMA((2, n_sub, n - 1))] * 2

    mats, norms = pl.pallas_call(
        functools.partial(reduce_kernel, n_x, n_y, n_z),
        name="reduce_all",
        out_shape=(shape(flat.shape, BF), shape(norms.shape, F32)),
        in_specs=[VM] * 2,
        out_specs=[VM] * 2,
        scratch_shapes=[
            pltpu.VMEM((half, 16, width), BF),
            pltpu.VMEM((half, 16, width), BF),
            land(most, sub // min(n_x, n_y)),
            land(most, sub // (n_x * n_y)),
            land(n_z, 1),
            pltpu.VMEM((4, *norms.shape), F32),
            pltpu.VMEM((4, max(most, n_z) - 1, *norms.shape), F32),
            DMA((2, n_sub)), DMA((2, n_sub)),
            *sems(most), *sems(most), *sems(n_z), *sems(n_z), *sems(most), *sems(most),
            DMA((2, n_sub)), DMA((2, n_sub)),
            *[DMA((4, max(most, n_z) - 1))] * 2,
        ],
        compiler_params=pltpu.CompilerParams(
            collective_id=3, has_side_effects=True, vmem_limit_bytes=50 * MIB
        ),
    )(flat, norms)
    return mats, norms


def token_slots(token_ids, hash_table, capacity, cap):
    chosen = jnp.take(hash_table, token_ids, mode="clip")
    places = jnp.arange(chosen.shape[0], dtype=jnp.int32)
    earlier = (chosen[:, None] == chosen[None, :]) & (places[:, None] > places[None, :])
    rank = jnp.sum(earlier.astype(jnp.int32), axis=1)
    experts_ids = jnp.arange(capacity.shape[0], dtype=jnp.int32)
    limit = jnp.sum(jnp.where(chosen[:, None] == experts_ids[None, :], capacity[None, :], 0), axis=1)
    return jnp.where(rank < limit, chosen * cap + rank, -1)


def per_device(
    tokens, token_ids, lengths, hash_table, capacity, gain_one, shift_one, w_qkv, w_out,
    gain_two, shift_two, w_in, bias_in, w_back, bias_back, cotangent,
):
    n_exp, n_hid = lax.axis_size("exp"), lax.axis_size("hid")
    tok, width = tokens.shape
    lc, _, ff = w_in.shape
    cap = 2 * tok // capacity.shape[0]
    slot = token_slots(token_ids, hash_table, capacity, cap)
    gain1, shift1, gain2, shift2 = (v[None] for v in (gain_one, shift_one, gain_two, shift_two))
    mixed, context, middle, lse, send, grads = attend(
        n_exp, n_hid, lc, cap, lengths, slot[None], tokens, gain1, shift1, w_qkv, w_out, gain2, shift2, cotangent
    )
    back, x, hid, gp, f_part, gb_in, gb_back = experts(
        n_exp, n_hid, send, grads, w_in, bias_in, w_back
    )
    output, g_tokens, mats, norms = attend_back(
        n_exp, n_hid, lengths, slot[:, None], tokens, middle, cotangent, mixed, context, lse, back,
        gain1, shift1, w_qkv, w_out, gain2, bias_back, f_part,
    )
    mats, norms = reduce_all(n_exp, n_hid, mats, norms)
    n_rows = n_exp * n_hid * cap
    g_in, g_back, g_qkv, g_out = finish(
        x.reshape(lc, n_rows, width), gp.reshape(lc, n_rows, ff),
        hid.reshape(lc, n_rows, ff), grads.reshape(lc, n_rows, width), mats,
    )
    return (
        output, g_tokens, norms[0], norms[1], g_qkv, g_out, norms[2], norms[3],
        g_in, gb_in, g_back, gb_back,
    )


def solution(mesh):
    both = P(("exp", "hid"))
    rows = P(("exp", "hid"), None)
    placed = (
        rows, both, rows, P(), P(), P(), P(), P(), P(), P(), P(),
        P("exp", None, "hid"), P("exp", "hid"), P("exp", "hid", None), P("exp", None), rows,
    )
    return jax.shard_map(
        per_device,
        mesh=mesh,
        in_specs=placed,
        out_specs=(
            rows, rows, P(), P(), P(), P(), P(), P(),
            P("exp", None, "hid"), P("exp", "hid"), P("exp", "hid", None), P("exp", None),
        ),
        check_vma=False,
    )
```

```python
import functools

import jax
import jax.numpy as jnp
from jax import lax
from jax.experimental import pallas as pl
from jax.experimental.pallas import tpu as pltpu
from jax.sharding import PartitionSpec as P

HEADS = 16
MESH = pl.DeviceIdType.MESH
BF = jnp.bfloat16
F32 = jnp.float32
epsilon = 1e-05
masked_score = -1e30
DMA = pltpu.SemaphoreType.DMA
VM = pl.BlockSpec(memory_space=pltpu.VMEM)
SM = pl.BlockSpec(memory_space=pltpu.SMEM)
HB = pl.BlockSpec(memory_space=pl.ANY)
MIB = 1 << 20


def mm(a, b):
    return lax.dot_general(a, b, (((1,), (0,)), ((), ())), preferred_element_type=F32)


def mm_nt(a, b):
    return lax.dot_general(a, b, (((1,), (1,)), ((), ())), preferred_element_type=F32)


def mm_tn(a, b):
    return lax.dot_general(a, b, (((0,), (0,)), ((), ())), preferred_element_type=F32)


def place():
    e = lax.axis_index("exp")
    h = lax.axis_index("hid")
    return e, h, lax.div(h, 2), lax.rem(h, 2)


def rcopy(src, dst, send, recv, dev):
    return pltpu.make_async_remote_copy(
        src_ref=src, dst_ref=dst, send_sem=send, recv_sem=recv, device_id=dev, device_id_type=MESH
    )


def greet(n_exp, n_y):
    e, h, y, c = place()
    sem = pltpu.get_barrier_semaphore()
    for k in range(1, n_exp):
        pl.semaphore_signal(sem, inc=1, device_id=(e ^ k, h), device_id_type=MESH)
    for d in range(1, n_y):
        pl.semaphore_signal(
            sem, inc=1, device_id=(e, lax.rem(y + d, n_y) * 2 + c), device_id_type=MESH
        )
    pl.semaphore_signal(sem, inc=1, device_id=(e, y * 2 + 1 - c), device_id_type=MESH)
    pl.semaphore_wait(sem, n_exp - 1 + n_y)


class Spread:
    def __init__(self, n_exp, n_y, rows, land, sems):
        self.n_exp, self.n_y, self.rows, self.land = n_exp, n_y, rows, land
        self.es, self.er, self.ys, self.yr, self.cs, self.cr = sems
        self.e, self.h, self.y, self.c = place()

    @staticmethod
    def sems(n_exp, n_y):
        return [DMA((n_exp,)), DMA((n_exp,))] + [DMA((n_exp, n_y))] * 4

    def over_exp(self, k):
        return rcopy(
            self.rows.at[self.e ^ k], self.land.at[:, self.e, self.h],
            self.es.at[k], self.er.at[k], (self.e ^ k, self.h),
        )

    def start(self):
        @pl.loop(1, self.n_exp)
        def _(i):
            low, high = lax.div(i + 1, 2), self.n_exp // 2 + lax.div(i, 2) - 1
            k = jnp.where(i == self.n_exp - 1, self.n_exp - 1, jnp.where(lax.rem(i, 2) == 1, low, high))
            self.over_exp(k).start()

    def block(self, k, hid):
        return self.land.at[:, self.e ^ k, hid]

    def over_y(self, k, d):
        blk = self.block(k, self.h)
        dev = (self.e, lax.rem(self.y + d, self.n_y) * 2 + self.c)
        return rcopy(blk, blk, self.ys.at[k, d], self.yr.at[k, d], dev)

    def over_core(self, k, d):
        blk = self.block(k, lax.rem(self.y + self.n_y - d, self.n_y) * 2 + self.c)
        dev = (self.e, self.y * 2 + 1 - self.c)
        return rcopy(blk, blk, self.cs.at[k, d], self.cr.at[k, d], dev)

    def pass_on(self, k):
        @pl.when(k > 0)
        def _():
            self.over_exp(k).wait_recv()

        for d in range(1, self.n_y):
            self.over_y(k, d).start()
        self.over_core(k, 0).start()

    def pass_y(self, k):
        for d in range(1, self.n_y):
            self.over_y(k, d).wait_recv()
            self.over_core(k, d).start()

    def landed(self, k):
        for d in range(self.n_y):
            self.over_core(k, d).wait_recv()

    def sent(self, k):
        @pl.when(k > 0)
        def _():
            self.over_exp(k).wait_send()

        for d in range(1, self.n_y):
            self.over_y(k, d).wait_send()
        for d in range(self.n_y):
            self.over_core(k, d).wait_send()


class Gather:
    def __init__(self, n_exp, n_y, other, mine, pairs, from_y, back, sems):
        self.n_exp, self.n_y, self.other, self.mine = n_exp, n_y, other, mine
        self.pairs, self.from_y, self.back = pairs, from_y, back
        self.es, self.er, self.ys, self.yr, self.cs, self.cr = sems
        self.e, self.h, self.y, self.c = place()

    @staticmethod
    def sems(n_exp, n_y):
        return [DMA((n_exp,)), DMA((n_exp,)), DMA((n_exp, n_y)), DMA((n_exp, n_y)), DMA((n_exp,)), DMA((n_exp,))]

    @staticmethod
    def scratch(n_exp, n_y, lc, cap, d):
        return [
            pltpu.VMEM((n_exp, lc, n_y, cap, d), BF),
            pltpu.VMEM((n_exp, n_y - 1, lc, cap, d), BF),
        ]

    def over_core(self, k):
        t = self.e ^ k
        dev = (self.e, self.y * 2 + 1 - self.c)
        return rcopy(self.other(k), self.pairs.at[t], self.cs.at[k], self.cr.at[k], dev)

    def over_y(self, k, d):
        t = self.e ^ k
        dev = (self.e, lax.rem(self.y + d, self.n_y) * 2 + self.c)
        yy = lax.rem(self.y + d, self.n_y)
        return rcopy(self.pairs.at[t, :, yy], self.from_y.at[t, d - 1], self.ys.at[k, d], self.yr.at[k, d], dev)

    def over_exp(self, k):
        t = self.e ^ k
        return rcopy(self.pairs.at[t, :, self.y], self.back.at[self.e], self.es.at[k], self.er.at[k], (t, self.h))

    def step_core(self, k):
        self.over_core(k).start()

    def fold(self, at, k):
        t = self.e ^ k
        self.over_core(k).wait_recv()
        for yy in range(self.n_y):
            pair = self.pairs[t, :, yy].astype(F32) + self.mine(at, yy).astype(F32)
            self.pairs[t, :, yy] = pair.astype(BF)

    def send_y(self, k):
        for d in range(1, self.n_y):
            self.over_y(k, d).start()

    def step_exp(self, k, extra=None):
        t = self.e ^ k
        total = self.pairs[t, :, self.y].astype(F32)
        for d in range(1, self.n_y):
            self.over_y(k, d).wait_recv()
            total = total + self.from_y[t, d - 1].astype(F32)
        if extra is not None:
            total = total + extra
        total = total.astype(BF)

        @pl.when(k == 0)
        def _():
            self.back[t] = total

        @pl.when(k > 0)
        def _():
            self.pairs[t, :, self.y] = total
            self.over_exp(k).start()

    def finish(self, k):
        for d in range(1, self.n_y):
            self.over_y(k, d).wait_send()

        @pl.when(k > 0)
        def _():
            self.over_exp(k).wait_send()
            self.over_exp(k).wait_recv()


def norm_rows(rows, gain, shift):
    mean = jnp.mean(rows, axis=-1, keepdims=True)
    centred = rows - mean
    var = jnp.mean(centred * centred, axis=-1, keepdims=True)
    inverse = lax.rsqrt(var + epsilon)
    unit = centred * inverse
    return unit * gain + shift, unit, inverse


def norm_back(upstream, unit, inverse, gain):
    scaled = upstream * gain
    inner = (
        scaled
        - jnp.mean(scaled, axis=-1, keepdims=True)
        - unit * jnp.mean(scaled * unit, axis=-1, keepdims=True)
    )
    return inner * inverse


def slot_block(slot_row, first, count):
    tok = slot_row.shape[1]
    ids = lax.broadcasted_iota(jnp.int32, (count, tok), 0) + first
    return jnp.where(slot_row == ids, 1.0, 0.0).astype(BF)


def tok_block(slot_col, first, count):
    ids = lax.broadcasted_iota(jnp.int32, (slot_col.shape[0], count), 1) + first
    return jnp.where(slot_col == ids, 1.0, 0.0).astype(BF)


def doc_bias(lens, tok):
    q = lax.broadcasted_iota(jnp.int32, (tok, tok), 0)
    k = lax.broadcasted_iota(jnp.int32, (tok, tok), 1)
    dq = jnp.zeros((tok, tok), jnp.int32)
    dk = jnp.zeros((tok, tok), jnp.int32)
    end = 0
    for j in range(lens.shape[1]):
        end = end + lens[0, j]
        dq = dq + jnp.where(q >= end, 1, 0)
        dk = dk + jnp.where(k >= end, 1, 0)
    return jnp.where((dq == dk) & (q >= k), 0.0, masked_score)


def attend_kernel(
    n_exp, n_y, lens, slot_row, tokens, gain1, shift1, w_qkv, w_out, gain2, shift2, cot,
    mixed_h, context_h, middle_h, lse, send_h, land,
    mixed, context, middle, send, cot_rows, normed, bias, wq_v, wo_v, in_sem, out_sem, own_sem, *sems,
):
    tok, width = tokens.shape
    e, h, y, c = place()
    lc, cap = send.shape[1], send.shape[2]
    per = lc * cap
    hd = width // HEADS
    spread = Spread(n_exp, n_y, cot_rows, land, sems)
    loads = [
        pltpu.make_async_copy(w_qkv, wq_v, in_sem.at[0]),
        pltpu.make_async_copy(w_out, wo_v, in_sem.at[1]),
    ]
    stores = [
        pltpu.make_async_copy(a, b, out_sem.at[i])
        for i, (a, b) in enumerate(
            ((mixed, mixed_h), (context, context_h), (middle, middle_h), (send, send_h))
        )
    ]
    for cp in loads:
        cp.start()

    def pick(source, dst):
        rows = mm(slot_block(slot_row[...], dst * per, per), source)
        return rows.astype(BF).reshape(lc, cap, width)

    def advance(k):
        spread.pass_on(k)

        @pl.when(k > 0)
        def _():
            spread.pass_y(k - 1)

    @pl.loop(0, n_exp)
    def _(k):
        cot_rows[k] = pick(cot[...], k)

    own = pltpu.make_async_copy(cot_rows.at[e], land.at[:, e, h], own_sem)
    own.start()
    greet(n_exp, n_y)
    spread.start()
    own.wait()
    spread.pass_on(0)

    @pl.loop(0, tok // 128)
    def _(i):
        rows = pl.ds(i * 128, 128)
        out, _, _ = norm_rows(tokens[rows].astype(F32), gain1[...], shift1[...])
        normed[rows] = out.astype(BF)

    bias[...] = doc_bias(lens, tok)
    loads[0].wait()

    @pl.loop(0, 3)
    def _(i):
        @pl.when(i > 0)
        def _():
            advance(i)

        for j in range(width // 512):
            cols = pl.ds(pl.multiple_of(i * width + j * 512, 512), 512)
            mixed[:, cols] = mm(normed[...], wq_v[:, cols]).astype(BF)

    stores[0].start()
    advance(3)
    lse[...] = jnp.zeros_like(lse)
    lane = lax.broadcasted_iota(jnp.int32, (1, 128), 1)
    n_pairs = width // 128
    half = tok // 2
    heads_in = 128 // hd

    @pl.loop(0, n_pairs)
    def _(p):
        @pl.when((lax.rem(p, 2) == 1) & (p < 6))
        def _():
            advance(4 + lax.div(p, 2))

        def cols(part):
            return pl.ds(pl.multiple_of(part * width + p * 128, 128), 128)

        q, key, val = mixed[:, cols(0)], mixed[:, cols(1)], mixed[:, cols(2)]
        for blk in range(2):
            rows = slice(blk * half, (blk + 1) * half)
            n_keys = (blk + 1) * half
            total = jnp.zeros((half, 128), F32)
            lses = lse[rows, :]
            for hh in range(heads_in):
                own_lanes = (lane >= hh * hd) & (lane < (hh + 1) * hd)
                qh = jnp.where(own_lanes, q[rows] * BF(hd**-0.5), BF(0))
                vh = jnp.where(own_lanes, val[:n_keys], BF(0))
                s = mm_nt(qh, key[:n_keys]) + bias[rows, :n_keys]
                top = jnp.max(s, axis=-1, keepdims=True)
                ex = jnp.exp(s - top)
                tot = jnp.sum(ex, axis=-1, keepdims=True)
                probs = (ex * (1.0 / tot)).astype(BF)
                total = total + mm(probs, vh)
                lses = jnp.where(lane == p * heads_in + hh, top + jnp.log(tot), lses)
            lse[rows, :] = lses
            context[rows, pl.ds(pl.multiple_of(p * 128, 128), 128)] = total.astype(BF)

    stores[1].start()
    loads[1].wait()

    @pl.loop(0, tok // 256)
    def _(i):
        rows = pl.ds(pl.multiple_of(i * 256, 256), 256)
        mid = tokens[rows].astype(F32) + mm(context[rows], wo_v[...])
        middle[rows] = mid
        out, _, _ = norm_rows(mid, gain2[...], shift2[...])
        normed[rows] = out.astype(BF)

    stores[2].start()

    @pl.loop(0, n_exp)
    def _(k):
        send[k] = pick(normed[...], k)

    stores[3].start()

    @pl.loop(7, n_exp)
    def _(k):
        advance(k)

    spread.pass_y(n_exp - 1)
    for cp in stores:
        cp.wait()

    @pl.loop(0, n_exp)
    def _(k):
        spread.landed(k)
        spread.sent(k)


def attend(n_exp, n_hid, lc, cap, lens, slot_row, tokens, gain1, shift1, w_qkv, w_out, gain2, shift2, cot):
    n_y = n_hid // 2
    tok, width = tokens.shape
    shape = jax.ShapeDtypeStruct
    return pl.pallas_call(
        functools.partial(attend_kernel, n_exp, n_y),
        name="attend",
        out_shape=(
            shape((tok, 3 * width), BF),
            shape((tok, width), BF),
            shape((tok, width), F32),
            shape((tok, 128), F32),
            shape((n_exp, lc, cap, width), BF),
            shape((lc, n_exp, n_hid, cap, width), BF),
        ),
        in_specs=[SM, VM, VM, VM, VM, HB, HB, VM, VM, VM],
        out_specs=[HB, HB, HB, VM, HB, HB],
        scratch_shapes=[
            pltpu.VMEM((tok, 3 * width), BF),
            pltpu.VMEM((tok, width), BF),
            pltpu.VMEM((tok, width), F32),
            pltpu.VMEM((n_exp, lc, cap, width), BF),
            pltpu.VMEM((n_exp, lc, cap, width), BF),
            pltpu.VMEM((tok, width), BF),
            pltpu.VMEM((tok, tok), F32),
            pltpu.VMEM(w_qkv.shape, BF),
            pltpu.VMEM(w_out.shape, BF),
            DMA((2,)),
            DMA((4,)),
            DMA,
            *Spread.sems(n_exp, n_y),
        ],
        compiler_params=pltpu.CompilerParams(
            collective_id=0, has_side_effects=True, vmem_limit_bytes=56 * MIB
        ),
    )(lens, slot_row, tokens, gain1, shift1, w_qkv, w_out, gain2, shift2, cot)


def expert_kernel(
    n_exp, n_y, rows, grads, w_in, bias_in, w_back,
    back, x_out, h_out, gp_out, f_out, gb_in, gb_back,
    land, part, win_v, wback_v, g_v, h_v, gp_v, f_v,
    w_sem, g_sem, o_sem, x_sem, own_sem, *rest,
):
    e, h, y, c = place()
    n_gather = len(Gather.scratch(1, 2, 1, 1, 1))
    n_spread = len(Spread.sems(1, 1))
    scr, sp_sems, ga_sems = rest[:n_gather], rest[n_gather : n_gather + n_spread], rest[n_gather + n_spread :]
    spread = Spread(n_exp, n_y, rows, land, sp_sems)


    def part_of(k):
        return part.at[lax.rem(lax.div(k, 2), 2), :, lax.rem(e ^ k, 2)]

    gather = Gather(
        n_exp, n_y, lambda k: part_of(k).at[:, :, 1 - c], lambda k, yy: part_of(k)[:, yy, c],
        *scr, back, ga_sems,
    )
    n_hid = 2 * n_y
    lc, cap, width = rows.shape[1:]
    ff = w_in.shape[2]
    count = 2 * n_hid * cap
    n_chunks = n_exp // 2
    step_f = min(512, ff)

    def weights(ex):
        return (
            pltpu.make_async_copy(w_in.at[ex], win_v.at[ex], w_sem.at[0, ex]),
            pltpu.make_async_copy(w_back.at[ex], wback_v.at[ex], w_sem.at[1, ex]),
        )

    for ex in range(lc):
        for cp in weights(ex):
            cp.start()

    def base_of(i):
        t = e ^ (2 * lax.div(i, lc))
        return t - lax.rem(t, 2)

    def g_copy(i):
        src = grads.at[lax.rem(i, lc), pl.ds(base_of(i), 2)]
        return pltpu.make_async_copy(src, g_v.at[lax.rem(i, 2)], g_sem.at[lax.rem(i, 2)])

    def out_copies(i):
        ex, slot, to = lax.rem(i, lc), lax.rem(i, 2), pl.ds(base_of(i), 2)
        return (
            pltpu.make_async_copy(h_v.at[slot], h_out.at[ex, to], o_sem.at[0, slot]),
            pltpu.make_async_copy(gp_v.at[slot], gp_out.at[ex, to], o_sem.at[1, slot]),
            pltpu.make_async_copy(f_v.at[slot], f_out.at[ex, to], o_sem.at[2, slot]),
        )

    def x_copy(i):
        ex, to = lax.rem(i, lc), pl.ds(base_of(i), 2)
        return pltpu.make_async_copy(land.at[ex, to], x_out.at[ex, to], x_sem.at[i])

    g_copy(0).start()
    own = pltpu.make_async_copy(rows.at[e], land.at[:, e, h], own_sem)
    own.start()
    greet(n_exp, n_y)

    spread.start()
    gb_in[...] = jnp.zeros_like(gb_in)
    gb_back[...] = jnp.zeros_like(gb_back)
    own.wait()
    spread.pass_on(0)
    spread.pass_on(1)
    spread.pass_y(0)
    spread.pass_on(2)
    spread.pass_y(1)

    n_steps = n_chunks * lc

    @pl.loop(0, n_steps)
    def _(i):
        j, ex = lax.div(i, lc), lax.rem(i, lc)
        slot = lax.rem(i, 2)
        base = base_of(i)

        @pl.when(i + 1 < n_steps)
        def _():
            g_copy(i + 1).start()

        @pl.when(ex == 0)
        def _():
            spread.landed(2 * j)
            spread.landed(2 * j + 1)

            @pl.when(j >= 2)
            def _():
                gather.over_core(2 * j - 4).wait_send()
                gather.over_core(2 * j - 3).wait_send()

        @pl.when(j == 0)
        def _():
            for cp in weights(ex):
                cp.wait()

        x_copy(i).start()
        g_copy(i).wait()

        @pl.when(i >= 2)
        def _():
            for cp in out_copies(i - 2):
                cp.wait()

        x = land[ex, pl.ds(base, 2)].reshape(count, width)
        g = g_v[slot].reshape(count, width)
        gb_back[pl.ds(ex, 1)] += jnp.sum(g.astype(F32), axis=0, keepdims=True)
        hs, gps = [], []
        for f in range(ff // step_f):
            cols = slice(f * step_f, (f + 1) * step_f)
            pre = mm(x, win_v[ex, :, cols]) + bias_in[pl.ds(ex, 1), cols]
            sig = jax.nn.sigmoid(pre)
            hid = (pre * sig).astype(BF)
            gh = mm_nt(g, wback_v[ex, cols, :])
            gp = (gh * sig * (1.0 + pre * (1.0 - sig))).astype(BF)
            gb_in[pl.ds(ex, 1), cols] += jnp.sum(gp.astype(F32), axis=0, keepdims=True)
            h_v[slot, :, :, cols] = hid.reshape(2, n_hid * cap, step_f)
            gp_v[slot, :, :, cols] = gp.reshape(2, n_hid * cap, step_f)
        gpv = gp_v[slot].reshape(count, ff)
        gd = mm_nt(gpv, win_v[ex])
        part[lax.rem(j, 2), ex] = gd.astype(BF).reshape(2, n_y, 2, cap, width)
        hv = h_v[slot].reshape(count, ff)
        f_v[slot] = mm(hv, wback_v[ex]).astype(BF).reshape(2, n_y, 2, cap, width)
        for cp in out_copies(i):
            cp.start()

        @pl.when(i == 0)
        def _():
            spread.pass_y(2)
            spread.pass_on(3)

        @pl.when(i == 1)
        def _():
            spread.pass_y(3)

        @pl.when((i >= 2) & (lax.rem(i, 2) == 0) & (lax.div(i, 2) + 3 < n_exp))
        def _():
            spread.pass_on(lax.div(i, 2) + 3)

            @pl.when(i == 2 * (n_exp - 4))
            def _():
                gather.send_y(0)
                gather.send_y(1)

        @pl.when((i >= 3) & (lax.rem(i, 2) == 1) & (lax.div(i, 2) + 3 < n_exp))
        def _():
            spread.pass_y(lax.div(i, 2) + 3)

        @pl.when((j >= 1) & (ex == 0))
        def _():
            gather.fold(2 * j - 2, 2 * j - 2)

        @pl.when((j >= 1) & (ex == 1))
        def _():
            gather.fold(2 * j - 1, 2 * j - 1)

            @pl.when(j >= 2)
            def _():
                gather.send_y(2 * j - 2)
                gather.send_y(2 * j - 1)

        @pl.when((j >= 3) & (ex == 2))
        def _():
            gather.step_exp(2 * j - 4)

        @pl.when(ex == lc - 1)
        def _():
            @pl.when(j >= 3)
            def _():
                gather.step_exp(2 * j - 3)

            gather.step_core(2 * j)
            gather.step_core(2 * j + 1)

    for k in (n_exp - 2, n_exp - 1):
        gather.fold(k, k)
        gather.send_y(k)
    for k in (*range(n_exp - 4, n_exp), 0, 1):
        gather.step_exp(k)

    for k in range(n_exp - 4, n_exp):
        gather.over_core(k).wait_send()
    for i in (n_steps - 2, n_steps - 1):
        for cp in out_copies(i):
            cp.wait()

    @pl.loop(0, n_steps)
    def _(i):
        x_copy(i).wait()

    @pl.loop(0, n_exp)
    def _(k):
        spread.sent(k)
        gather.finish(k)


def experts(n_exp, n_hid, rows, grads, w_in, bias_in, w_back):
    n_y = n_hid // 2
    _, lc, cap, width = rows.shape
    ff = w_in.shape[2]
    shape = jax.ShapeDtypeStruct
    per = n_hid * cap
    n_steps = n_exp // 2 * lc
    return pl.pallas_call(
        functools.partial(expert_kernel, n_exp, n_y),
        name="experts",
        out_shape=(
            shape((n_exp, lc, cap, width), BF),
            shape((lc, n_exp, n_hid, cap, width), BF),
            shape((lc, n_exp, per, ff), BF),
            shape((lc, n_exp, per, ff), BF),
            shape((lc, n_exp, n_y, 2, cap, width), BF),
            shape((lc, ff), F32),
            shape((lc, width), F32),
        ),
        in_specs=[VM, HB, HB, VM, HB],
        out_specs=[VM, HB, HB, HB, HB, VM, VM],
        scratch_shapes=[
            pltpu.VMEM((lc, n_exp, n_hid, cap, width), BF),
            pltpu.VMEM((2, lc, 2, n_y, 2, cap, width), BF),
            pltpu.VMEM(w_in.shape, BF),
            pltpu.VMEM(w_back.shape, BF),
            pltpu.VMEM((2, 2, n_hid, cap, width), BF),
            pltpu.VMEM((2, 2, per, ff), BF),
            pltpu.VMEM((2, 2, per, ff), BF),
            pltpu.VMEM((2, 2, n_y, 2, cap, width), BF),
            DMA((2, lc)), DMA((2,)), DMA((3, 2)), DMA((n_steps,)), DMA,
            *Gather.scratch(n_exp, n_y, lc, cap, width),
            *Spread.sems(n_exp, n_y),
            *Gather.sems(n_exp, n_y),
        ],
        compiler_params=pltpu.CompilerParams(
            collective_id=1, has_side_effects=True, vmem_limit_bytes=62 * MIB
        ),
    )(rows, grads, w_in, bias_in, w_back)


def finish_kernel(x, gp, h, g, mats, g_in, g_back, g_qkv, g_out):
    g_in[0] = mm_tn(x[0], gp[0])
    g_back[0] = mm_tn(h[0], g[0])
    rows, width = g_out.shape
    for part in range(3):
        g_qkv[:, part * width : (part + 1) * width] = mats[part].reshape(rows, width).astype(F32)
    g_out[...] = mats[3].reshape(rows, width).astype(F32)


def finish(x, gp, h, g, mats):
    lc, n, width = x.shape
    ff = gp.shape[2]
    cut = 2
    rows = width // (lc * cut)
    mats = mats.reshape(4, width // 16, 16, width)
    shape = jax.ShapeDtypeStruct
    return pl.pallas_call(
        finish_kernel,
        name="finish",
        grid=(lc, cut),
        out_shape=(
            shape((lc, width, ff), F32), shape((lc, ff, width), F32),
            shape((width, 3 * width), F32), shape((width, width), F32),
        ),
        in_specs=[
            pl.BlockSpec((1, n, width), lambda i, j: (i, 0, 0)),
            pl.BlockSpec((1, n, ff // cut), lambda i, j: (i, 0, j)),
            pl.BlockSpec((1, n, ff), lambda i, j: (i, 0, 0)),
            pl.BlockSpec((1, n, width // cut), lambda i, j: (i, 0, j)),
            pl.BlockSpec((4, rows // 16, 16, width), lambda i, j: (0, i * cut + j, 0, 0)),
        ],
        out_specs=[
            pl.BlockSpec((1, width, ff // cut), lambda i, j: (i, 0, j)),
            pl.BlockSpec((1, ff, width // cut), lambda i, j: (i, 0, j)),
            pl.BlockSpec((rows, 3 * width), lambda i, j: (i * cut + j, 0)),
            pl.BlockSpec((rows, width), lambda i, j: (i * cut + j, 0)),
        ],
        compiler_params=pltpu.CompilerParams(vmem_limit_bytes=56 * MIB),
    )(x, gp, h, g, mats)


def attend_back_kernel(
    n_exp, n_y, lens, slot_col, tokens_h, middle_h, cot_h, mixed_h, context_h, lse, back_h,
    gain1, shift1, w_qkv_h, w_out_h, gain2, bias_back, f_part,
    output, g_tokens, g_mats, g_norms,
    tokens, middle, cot, mixed, context, back, w_qkv, w_out,
    bias, gm, gattn, gctx, gmixed, n1t, lse_t, mine_v, f_back, mine_sem, in_sem, *rest,
):
    tok, width = tokens.shape
    hd = width // HEADS
    e, h, y, c = place()
    n_gather = len(Gather.scratch(1, 2, 1, 1, 1))
    lc, cap = f_back.shape[1:3]
    gather = Gather(
        n_exp, n_y, lambda k: f_part.at[:, e ^ k, :, 1 - c], lambda m, yy: mine_v[lax.rem(m, 4), :, yy],
        *rest[:n_gather], f_back, rest[n_gather:],
    )

    def order(m):
        return jnp.where(m < n_exp // 2, m + n_exp // 2, n_exp - 1 - m)

    def fetch(m):
        slot = lax.rem(m, 4)
        return pltpu.make_async_copy(
            f_part.at[:, e ^ order(m), :, c], mine_v.at[slot], mine_sem.at[slot]
        )

    loads = [
        pltpu.make_async_copy(a, b, in_sem.at[i])
        for i, (a, b) in enumerate((
            (back_h, back), (middle_h, middle), (cot_h, cot), (w_out_h, w_out), (tokens_h, tokens),
            (context_h, context), (mixed_h, mixed), (w_qkv_h, w_qkv),
        ))
    ]
    greet(n_exp, n_y)

    @pl.loop(0, n_exp)
    def _(m):
        gather.step_core(order(m))

    for m in range(4):
        fetch(m).start()
    for cp in loads:
        cp.start()

    def leave(m):
        fetch(m).wait()
        gather.fold(m, order(m))
        gather.send_y(order(m))

        @pl.when(m + 4 < n_exp)
        def _():
            fetch(m + 4).start()

    leave(0)
    leave(1)
    for cp in loads[:5]:
        cp.wait()

    g_norms[...] = jnp.zeros_like(g_norms)
    n_slots = n_exp * lc * cap

    def fold(values):
        return jnp.sum(values, axis=0, keepdims=True)

    @pl.loop(0, tok // 256)
    def _(i):
        rows = pl.ds(pl.multiple_of(i * 256, 256), 256)
        table = tok_block(slot_col[rows], 0, n_slots)
        up = mm(table, back[...].reshape(n_slots, width))
        _, unit, inverse = norm_rows(middle[rows], gain2[...], 0.0)
        g_norms[2:3] += fold(up * unit)
        g_norms[3:4] += fold(up)
        g_mid = cot[rows].astype(F32) + norm_back(up, unit, inverse, gain2[...])
        gm[rows] = g_mid
        gattn[rows] = g_mid.astype(BF)
        gctx[rows] = mm_nt(gattn[rows], w_out[...]).astype(BF)
        out, _, _ = norm_rows(tokens[rows].astype(F32), gain1[...], shift1[...])
        n1t[:, rows] = out.astype(BF).T

    leave(2)
    leave(3)
    for cp in loads[5:]:
        cp.wait()

    @pl.loop(0, width // 256)
    def _(i):
        cols = pl.ds(pl.multiple_of(i * 256, 256), 256)
        part = mm_tn(context[:, cols], gattn[...]).astype(BF)
        g_mats[3, pl.ds(i * 16, 16)] = part.reshape(16, 16, width)

    key_i = lax.broadcasted_iota(jnp.int32, (tok, tok), 0)
    qry_i = lax.broadcasted_iota(jnp.int32, (tok, tok), 1)
    dk_, dq_ = jnp.zeros((tok, tok), jnp.int32), jnp.zeros((tok, tok), jnp.int32)
    end = 0
    for j in range(lens.shape[1]):
        end = end + lens[0, j]
        dk_ = dk_ + jnp.where(key_i >= end, 1, 0)
        dq_ = dq_ + jnp.where(qry_i >= end, 1, 0)
    bias[...] = jnp.where((dk_ == dq_) & (qry_i >= key_i), 0.0, masked_score)
    lse_t[...] = lse[...].T

    lane = lax.broadcasted_iota(jnp.int32, (1, 128), 1)
    n_pairs = width // 128
    half = tok // 2
    heads_in = 128 // hd

    @pl.loop(0, n_pairs)
    def _(p):
        @pl.when(p + 4 < n_exp)
        def _():
            leave(p + 4)

        @pl.when((p >= 2) & (lax.rem(p, 2) == 0))
        def _():
            gather.step_exp(order(lax.div(p, 2) - 1), bias_back[...].reshape(lc, 1, width))

        def cols(part):
            return pl.ds(pl.multiple_of(part * width + p * 128, 128), 128)

        q, key, val, do = mixed[:, cols(0)], mixed[:, cols(1)], mixed[:, cols(2)], gctx[:, cols(0)]
        dq = [jnp.zeros((half, 128), F32) for _ in range(2)]
        dkey = [jnp.zeros((half, 128), F32) for _ in range(2)]
        dval = [jnp.zeros((half, 128), F32) for _ in range(2)]
        for hh in range(heads_in):
            own_lanes = (lane >= hh * hd) & (lane < (hh + 1) * hd)
            qh = jnp.where(own_lanes, q * BF(hd**-0.5), BF(0))
            kh = jnp.where(own_lanes, key * BF(hd**-0.5), BF(0))
            doh = jnp.where(own_lanes, do, BF(0))
            lrow = lse_t[pl.ds(p * heads_in + hh, 1), :]
            for qb in range(2):
                rows = slice(qb * half, (qb + 1) * half)
                n = (qb + 1) * half
                s = mm_nt(key[:n], qh[rows]) + (bias[:n, rows] - lrow[:, rows])
                pt = jnp.exp(s)
                dp = mm_nt(val[:n], doh[rows])
                inner = jnp.sum(dp * pt, axis=0, keepdims=True)
                ds = (pt * (dp - inner)).astype(BF)
                ptb = pt.astype(BF)
                dv_, dk2 = mm(ptb, doh[rows]), mm(ds, qh[rows])
                for kb in range(qb + 1):
                    part = slice(kb * half, (kb + 1) * half)
                    dval[kb] = dval[kb] + dv_[part]
                    dkey[kb] = dkey[kb] + dk2[part]
                dq[qb] = dq[qb] + mm_tn(ds, kh[:n])
        for b in range(2):
            rows = slice(b * half, (b + 1) * half)
            gmixed[rows, cols(0)] = dq[b].astype(BF)
            gmixed[rows, cols(1)] = dkey[b].astype(BF)
            gmixed[rows, cols(2)] = dval[b].astype(BF)

    gather.step_exp(order(3), bias_back[...].reshape(lc, 1, width))

    @pl.loop(0, tok // 256)
    def _(i):
        rows = pl.ds(pl.multiple_of(i * 256, 256), 256)
        up = mm_nt(gmixed[rows], w_qkv[...])
        _, unit, inverse = norm_rows(tokens[rows].astype(F32), gain1[...], 0.0)
        g_norms[0:1] += fold(up * unit)
        g_norms[1:2] += fold(up)
        g_tokens[rows] = gm[rows] + norm_back(up, unit, inverse, gain1[...])

    gather.step_exp(order(4), bias_back[...].reshape(lc, 1, width))

    for part in range(3):

        @pl.loop(0, width // 256)
        def _(i):
            rows = pl.ds(pl.multiple_of(i * 256, 256), 256)
            piece = mm(n1t[rows], gmixed[:, part * width : (part + 1) * width])
            g_mats[part, pl.ds(i * 16, 16)] = piece.astype(BF).reshape(16, 16, width)

    @pl.loop(n_pairs + 4, max(n_exp, n_pairs + 4))
    def _(m):
        leave(m)

    @pl.loop(5, n_exp)
    def _(m):
        gather.step_exp(order(m), bias_back[...].reshape(lc, 1, width))

    @pl.loop(0, n_exp)
    def _(k):
        gather.over_core(k).wait_send()
        gather.finish(k)

    @pl.loop(0, tok // 256)
    def _(i):
        rows = pl.ds(pl.multiple_of(i * 256, 256), 256)
        table = tok_block(slot_col[rows], 0, n_slots)
        output[rows] = (middle[rows] + mm(table, f_back[...].reshape(n_slots, width))).astype(BF)


def attend_back(
    n_exp, n_hid, lens, slot_col, tokens, middle, cot, mixed, context, lse, back,
    gain1, shift1, w_qkv, w_out, gain2, bias_back, f_part,
):
    n_y = n_hid // 2
    tok, width = tokens.shape
    _, lc, cap, _ = back.shape
    shape = jax.ShapeDtypeStruct
    return pl.pallas_call(
        functools.partial(attend_back_kernel, n_exp, n_y),
        name="attend_back",
        out_shape=(
            shape((tok, width), BF),
            shape((tok, width), F32),
            shape((4, width // 16, 16, width), BF),
            shape((8, width), F32),
        ),
        in_specs=[SM, VM, HB, HB, HB, HB, HB, VM, HB, VM, VM, HB, HB, VM, VM, HB],
        out_specs=[VM] * 4,
        scratch_shapes=[
            *[pltpu.VMEM(a.shape, a.dtype) for a in (tokens, middle, cot, mixed, context, back, w_qkv, w_out)],
            pltpu.VMEM((tok, tok), F32),
            pltpu.VMEM((tok, width), F32),
            pltpu.VMEM((tok, width), BF),
            pltpu.VMEM((tok, width), BF),
            pltpu.VMEM((tok, 3 * width), BF),
            pltpu.VMEM((width, tok), BF),
            pltpu.VMEM((128, tok), F32),
            pltpu.VMEM((4, lc, n_y, cap, width), BF),
            pltpu.VMEM((n_exp, lc, cap, width), BF),
            DMA((4,)),
            DMA((8,)),
            *Gather.scratch(n_exp, n_y, lc, cap, width),
            *Gather.sems(n_exp, n_y),
        ],
        compiler_params=pltpu.CompilerParams(
            collective_id=2, has_side_effects=True, vmem_limit_bytes=62 * MIB
        ),
    )(
        lens, slot_col, tokens, middle, cot, mixed, context, lse, back,
        gain1, shift1, w_qkv, w_out, gain2, bias_back, f_part,
    )


def reduce_kernel(
    n_x, n_y, n_z, mats, norms, out, norms_out,
    acc, core_in, in1, in2, in3, n_acc, n_in,
    c_s, c_r, s1, r1, s2, r2, s3, r3, t3, u3, t2, u2, t1, u1, d_s, d_r, n_s, n_r,
):
    e, h, y, c = place()
    x, z = lax.rem(e, n_x), lax.div(e, n_x)
    sub = n_x * n_y * n_z
    half = mats.shape[0] // 2
    piece = half // 2
    n_sub = piece // sub
    at = {"x": (n_x, x), "y": (n_y, y), "z": (n_z, z)}
    orders = (("y", "x", "z"), ("x", "y", "z"))
    sibling = (e, y * 2 + 1 - c)

    def device(axis, o):
        return {"x": (z * n_x + o, h), "y": (e, o * 2 + c), "z": (o * n_x + x, h)}[axis]

    sem = pltpu.get_barrier_semaphore()
    for axis in "xyz":
        n, i = at[axis]
        for d in range(1, n):
            pl.semaphore_signal(sem, inc=1, device_id=device(axis, lax.rem(i + d, n)), device_id_type=MESH)
    pl.semaphore_signal(sem, inc=1, device_id=sibling, device_id_type=MESH)
    pl.semaphore_wait(sem, n_x + n_y + n_z - 2)

    def units(p, b, depth):
        first, count = p * piece + b * sub, sub
        for axis in orders[p][:depth]:
            n, i = at[axis]
            count = count // n
            first = first + i * count
        return first, count

    def core_copy(p, b):
        first = p * piece + b * sub
        return rcopy(
            mats.at[pl.ds((1 - c) * half + first, sub)], core_in.at[pl.ds(first, sub)],
            c_s.at[p, b], c_r.at[p, b], sibling,
        )

    lands = (in1, in2, in3)
    sends, recvs = (s1, s2, s3), (r1, r2, r3)

    def down(p, b, stage, d):
        n, i = at[orders[p][stage]]
        first, count = units(p, b, stage)
        count = count // n
        o = lax.rem(i + d, n)
        return rcopy(
            acc.at[pl.ds(first + o * count, count)], lands[stage].at[p, b, d - 1, pl.ds(0, count)],
            sends[stage].at[p, b, d - 1], recvs[stage].at[p, b, d - 1], device(orders[p][stage], o),
        )

    ups, upr = (t1, t2, t3), (u1, u2, u3)

    def up(p, b, stage, d):
        n, i = at[orders[p][stage]]
        first, count = units(p, b, stage + 1)
        region = out.at[pl.ds(c * half + first, count)]
        o = lax.rem(i + d, n)
        return rcopy(
            region, region, ups[stage].at[p, b, d - 1], upr[stage].at[p, b, d - 1], device(orders[p][stage], o)
        )

    def core_up(p, b):
        region = out.at[pl.ds(c * half + p * piece + b * sub, sub)]
        return rcopy(region, region, d_s.at[p, b], d_r.at[p, b], sibling)

    def peers(p, stage):
        return range(1, at[orders[p][stage]][0])

    def event(p, b, q):
        if q == 0:
            core_copy(p, b).wait_recv()
            first = p * piece + b * sub
            mine = mats[pl.ds(c * half + first, sub)].astype(F32)
            acc[pl.ds(first, sub)] = (mine + core_in[pl.ds(first, sub)].astype(F32)).astype(BF)
        elif q <= 3:
            first, count = units(p, b, q)
            total = acc[pl.ds(first, count)].astype(F32)
            for d in peers(p, q - 1):
                down(p, b, q - 1, d).wait_recv()
                total = total + lands[q - 1][p, b, d - 1, :count].astype(F32)
            if q < 3:
                acc[pl.ds(first, count)] = total.astype(BF)
            else:
                out[pl.ds(c * half + first, count)] = total.astype(BF)
        else:
            for d in peers(p, 6 - q):
                up(p, b, 6 - q, d).wait_recv()
        if q < 3:
            for d in peers(p, q):
                down(p, b, q, d).start()
        elif q < 6:
            for d in peers(p, 5 - q):
                up(p, b, 5 - q, d).start()
        else:
            core_up(p, b).start()

    for b in range(n_sub):
        for p in range(2):
            core_copy(p, b).start()

    n_axes = (None, "y", "x", "z")

    def n_copy(stage, d):
        if stage == 0:
            dev = sibling
        else:
            n, i = at[n_axes[stage]]
            dev = device(n_axes[stage], lax.rem(i + d, n))
        return rcopy(n_acc.at[stage], n_in.at[stage, d - 1], n_s.at[stage, d - 1], n_r.at[stage, d - 1], dev)

    def n_peers(stage):
        return range(1, 2 if stage == 0 else at[n_axes[stage]][0])

    def n_total(stage):
        for d in n_peers(stage):
            n_copy(stage, d).wait_recv()
        own = n_acc[stage]
        if stage == 0:
            return own + n_in[0, 0]
        n, i = at[n_axes[stage]]
        total = jnp.zeros_like(own)
        for m in range(n):
            term = own
            for d in range(1, n):
                term = jnp.where(lax.rem(i + n - d, n) == m, n_in[stage, d - 1], term)
            total = total + term
        return total

    n_acc[0] = norms[...]
    n_copy(0, 1).start()

    @pl.loop(0, n_sub + 6)
    def _(s):
        for q in range(7):

            @pl.when((s >= q) & (s - q < n_sub))
            def _():
                for p in range(2):
                    event(p, s - q, q)

        for stage in range(1, 4):

            @pl.when(s == stage)
            def _():
                n_acc[stage] = n_total(stage - 1)
                for d in n_peers(stage):
                    n_copy(stage, d).start()

    norms_out[...] = n_total(3)
    for stage in range(4):
        for d in n_peers(stage):
            n_copy(stage, d).wait_send()

    @pl.loop(0, n_sub)
    def _(b):
        for p in range(2):
            core_up(p, b).wait_recv()
            core_copy(p, b).wait_send()
            core_up(p, b).wait_send()
            for stage in range(3):
                for d in peers(p, stage):
                    down(p, b, stage, d).wait_send()
                    up(p, b, stage, d).wait_send()


def reduce_all(n_exp, n_hid, mats, norms):
    n_y = n_hid // 2
    n_x = n_y
    n_z = n_exp // n_x
    sub = n_x * n_y * n_z
    width = norms.shape[1]
    flat = mats.reshape(-1, 16, width)
    half = flat.shape[0] // 2
    n_sub = half // 2 // sub
    most = max(n_x, n_y)
    shape = jax.ShapeDtypeStruct

    def land(n, count):
        return pltpu.VMEM((2, n_sub, n - 1, count, 16, width), BF)

    def sems(n):
        return [DMA((2, n_sub, n - 1))] * 2

    mats, norms = pl.pallas_call(
        functools.partial(reduce_kernel, n_x, n_y, n_z),
        name="reduce_all",
        out_shape=(shape(flat.shape, BF), shape(norms.shape, F32)),
        in_specs=[VM] * 2,
        out_specs=[VM] * 2,
        scratch_shapes=[
            pltpu.VMEM((half, 16, width), BF),
            pltpu.VMEM((half, 16, width), BF),
            land(most, sub // min(n_x, n_y)),
            land(most, sub // (n_x * n_y)),
            land(n_z, 1),
            pltpu.VMEM((4, *norms.shape), F32),
            pltpu.VMEM((4, max(most, n_z) - 1, *norms.shape), F32),
            DMA((2, n_sub)), DMA((2, n_sub)),
            *sems(most), *sems(most), *sems(n_z), *sems(n_z), *sems(most), *sems(most),
            DMA((2, n_sub)), DMA((2, n_sub)),
            *[DMA((4, max(most, n_z) - 1))] * 2,
        ],
        compiler_params=pltpu.CompilerParams(
            collective_id=3, has_side_effects=True, vmem_limit_bytes=50 * MIB
        ),
    )(flat, norms)
    return mats, norms


def token_slots(token_ids, hash_table, capacity, cap):
    chosen = jnp.take(hash_table, token_ids, mode="clip")
    places = jnp.arange(chosen.shape[0], dtype=jnp.int32)
    earlier = (chosen[:, None] == chosen[None, :]) & (places[:, None] > places[None, :])
    rank = jnp.sum(earlier.astype(jnp.int32), axis=1)
    experts_ids = jnp.arange(capacity.shape[0], dtype=jnp.int32)
    limit = jnp.sum(jnp.where(chosen[:, None] == experts_ids[None, :], capacity[None, :], 0), axis=1)
    return jnp.where(rank < limit, chosen * cap + rank, -1)


def per_device(
    tokens, token_ids, lengths, hash_table, capacity, gain_one, shift_one, w_qkv, w_out,
    gain_two, shift_two, w_in, bias_in, w_back, bias_back, cotangent,
):
    n_exp, n_hid = lax.axis_size("exp"), lax.axis_size("hid")
    tok, width = tokens.shape
    lc, _, ff = w_in.shape
    cap = 2 * tok // capacity.shape[0]
    slot = token_slots(token_ids, hash_table, capacity, cap)
    gain1, shift1, gain2, shift2 = (v[None] for v in (gain_one, shift_one, gain_two, shift_two))
    mixed, context, middle, lse, send, grads = attend(
        n_exp, n_hid, lc, cap, lengths, slot[None], tokens, gain1, shift1, w_qkv, w_out, gain2, shift2, cotangent
    )
    back, x, hid, gp, f_part, gb_in, gb_back = experts(
        n_exp, n_hid, send, grads, w_in, bias_in, w_back
    )
    output, g_tokens, mats, norms = attend_back(
        n_exp, n_hid, lengths, slot[:, None], tokens, middle, cotangent, mixed, context, lse, back,
        gain1, shift1, w_qkv, w_out, gain2, bias_back, f_part,
    )
    mats, norms = reduce_all(n_exp, n_hid, mats, norms)
    n_rows = n_exp * n_hid * cap
    g_in, g_back, g_qkv, g_out = finish(
        x.reshape(lc, n_rows, width), gp.reshape(lc, n_rows, ff),
        hid.reshape(lc, n_rows, ff), grads.reshape(lc, n_rows, width), mats,
    )
    return (
        output, g_tokens, norms[0], norms[1], g_qkv, g_out, norms[2], norms[3],
        g_in, gb_in, g_back, gb_back,
    )


def solution(mesh):
    both = P(("exp", "hid"))
    rows = P(("exp", "hid"), None)
    placed = (
        rows, both, rows, P(), P(), P(), P(), P(), P(), P(), P(),
        P("exp", None, "hid"), P("exp", "hid"), P("exp", "hid", None), P("exp", None), rows,
    )
    return jax.shard_map(
        per_device,
        mesh=mesh,
        in_specs=placed,
        out_specs=(
            rows, rows, P(), P(), P(), P(), P(), P(),
            P("exp", None, "hid"), P("exp", "hid"), P("exp", "hid", None), P("exp", None),
        ),
        check_vma=False,
    )
```

```python
import functools

import jax
import jax.numpy as jnp
from jax import lax
from jax.experimental import pallas as pl
from jax.experimental.pallas import tpu as pltpu
from jax.sharding import PartitionSpec as P

HEADS = 16
MESH = pl.DeviceIdType.MESH
BF = jnp.bfloat16
F32 = jnp.float32
epsilon = 1e-05
masked_score = -1e30
DMA = pltpu.SemaphoreType.DMA
VM = pl.BlockSpec(memory_space=pltpu.VMEM)
SM = pl.BlockSpec(memory_space=pltpu.SMEM)
HB = pl.BlockSpec(memory_space=pl.ANY)
MIB = 1 << 20


def mm(a, b):
    return lax.dot_general(a, b, (((1,), (0,)), ((), ())), preferred_element_type=F32)


def mm_nt(a, b):
    return lax.dot_general(a, b, (((1,), (1,)), ((), ())), preferred_element_type=F32)


def mm_tn(a, b):
    return lax.dot_general(a, b, (((0,), (0,)), ((), ())), preferred_element_type=F32)


def place():
    e = lax.axis_index("exp")
    h = lax.axis_index("hid")
    return e, h, lax.div(h, 2), lax.rem(h, 2)


def rcopy(src, dst, send, recv, dev):
    return pltpu.make_async_remote_copy(
        src_ref=src, dst_ref=dst, send_sem=send, recv_sem=recv, device_id=dev, device_id_type=MESH
    )


def greet(n_exp, n_y):
    e, h, y, c = place()
    sem = pltpu.get_barrier_semaphore()
    for k in range(1, n_exp):
        pl.semaphore_signal(sem, inc=1, device_id=(e ^ k, h), device_id_type=MESH)
    for d in range(1, n_y):
        pl.semaphore_signal(
            sem, inc=1, device_id=(e, lax.rem(y + d, n_y) * 2 + c), device_id_type=MESH
        )
    pl.semaphore_signal(sem, inc=1, device_id=(e, y * 2 + 1 - c), device_id_type=MESH)
    pl.semaphore_wait(sem, n_exp - 1 + n_y)


class Spread:
    def __init__(self, n_exp, n_y, rows, land, sems):
        self.n_exp, self.n_y, self.rows, self.land = n_exp, n_y, rows, land
        self.es, self.er, self.ys, self.yr, self.cs, self.cr = sems
        self.e, self.h, self.y, self.c = place()

    @staticmethod
    def sems(n_exp, n_y):
        return [DMA((n_exp,)), DMA((n_exp,))] + [DMA((n_exp, n_y))] * 4

    def over_exp(self, k):
        return rcopy(
            self.rows.at[self.e ^ k], self.land.at[:, self.e, self.h],
            self.es.at[k], self.er.at[k], (self.e ^ k, self.h),
        )

    def start(self):
        @pl.loop(1, self.n_exp)
        def _(i):
            low, high = lax.div(i + 1, 2), self.n_exp // 2 + lax.div(i, 2) - 1
            k = jnp.where(i == self.n_exp - 1, self.n_exp - 1, jnp.where(lax.rem(i, 2) == 1, low, high))
            self.over_exp(k).start()

    def block(self, k, hid):
        return self.land.at[:, self.e ^ k, hid]

    def over_y(self, k, d):
        blk = self.block(k, self.h)
        dev = (self.e, lax.rem(self.y + d, self.n_y) * 2 + self.c)
        return rcopy(blk, blk, self.ys.at[k, d], self.yr.at[k, d], dev)

    def over_core(self, k, d):
        blk = self.block(k, lax.rem(self.y + self.n_y - d, self.n_y) * 2 + self.c)
        dev = (self.e, self.y * 2 + 1 - self.c)
        return rcopy(blk, blk, self.cs.at[k, d], self.cr.at[k, d], dev)

    def pass_on(self, k):
        @pl.when(k > 0)
        def _():
            self.over_exp(k).wait_recv()

        for d in range(1, self.n_y):
            self.over_y(k, d).start()
        self.over_core(k, 0).start()

    def pass_y(self, k):
        for d in range(1, self.n_y):
            self.over_y(k, d).wait_recv()
            self.over_core(k, d).start()

    def landed(self, k):
        for d in range(self.n_y):
            self.over_core(k, d).wait_recv()

    def sent(self, k):
        @pl.when(k > 0)
        def _():
            self.over_exp(k).wait_send()

        for d in range(1, self.n_y):
            self.over_y(k, d).wait_send()
        for d in range(self.n_y):
            self.over_core(k, d).wait_send()


class Gather:
    def __init__(self, n_exp, n_y, other, mine, pairs, from_y, back, sems):
        self.n_exp, self.n_y, self.other, self.mine = n_exp, n_y, other, mine
        self.pairs, self.from_y, self.back = pairs, from_y, back
        self.es, self.er, self.ys, self.yr, self.cs, self.cr = sems
        self.e, self.h, self.y, self.c = place()

    @staticmethod
    def sems(n_exp, n_y):
        return [DMA((n_exp,)), DMA((n_exp,)), DMA((n_exp, n_y)), DMA((n_exp, n_y)), DMA((n_exp,)), DMA((n_exp,))]

    @staticmethod
    def scratch(n_exp, n_y, lc, cap, d):
        return [
            pltpu.VMEM((n_exp, lc, n_y, cap, d), BF),
            pltpu.VMEM((n_exp, n_y - 1, lc, cap, d), BF),
        ]

    def over_core(self, k):
        t = self.e ^ k
        dev = (self.e, self.y * 2 + 1 - self.c)
        return rcopy(self.other(k), self.pairs.at[t], self.cs.at[k], self.cr.at[k], dev)

    def over_y(self, k, d):
        t = self.e ^ k
        dev = (self.e, lax.rem(self.y + d, self.n_y) * 2 + self.c)
        yy = lax.rem(self.y + d, self.n_y)
        return rcopy(self.pairs.at[t, :, yy], self.from_y.at[t, d - 1], self.ys.at[k, d], self.yr.at[k, d], dev)

    def over_exp(self, k):
        t = self.e ^ k
        return rcopy(self.pairs.at[t, :, self.y], self.back.at[self.e], self.es.at[k], self.er.at[k], (t, self.h))

    def step_core(self, k):
        self.over_core(k).start()

    def fold(self, at, k):
        t = self.e ^ k
        self.over_core(k).wait_recv()
        for yy in range(self.n_y):
            pair = self.pairs[t, :, yy].astype(F32) + self.mine(at, yy).astype(F32)
            self.pairs[t, :, yy] = pair.astype(BF)

    def send_y(self, k):
        for d in range(1, self.n_y):
            self.over_y(k, d).start()

    def step_exp(self, k, extra=None):
        t = self.e ^ k
        total = self.pairs[t, :, self.y].astype(F32)
        for d in range(1, self.n_y):
            self.over_y(k, d).wait_recv()
            total = total + self.from_y[t, d - 1].astype(F32)
        if extra is not None:
            total = total + extra
        total = total.astype(BF)

        @pl.when(k == 0)
        def _():
            self.back[t] = total

        @pl.when(k > 0)
        def _():
            self.pairs[t, :, self.y] = total
            self.over_exp(k).start()

    def finish(self, k):
        for d in range(1, self.n_y):
            self.over_y(k, d).wait_send()

        @pl.when(k > 0)
        def _():
            self.over_exp(k).wait_send()
            self.over_exp(k).wait_recv()


def norm_rows(rows, gain, shift):
    mean = jnp.mean(rows, axis=-1, keepdims=True)
    centred = rows - mean
    var = jnp.mean(centred * centred, axis=-1, keepdims=True)
    inverse = lax.rsqrt(var + epsilon)
    unit = centred * inverse
    return unit * gain + shift, unit, inverse


def norm_back(upstream, unit, inverse, gain):
    scaled = upstream * gain
    inner = (
        scaled
        - jnp.mean(scaled, axis=-1, keepdims=True)
        - unit * jnp.mean(scaled * unit, axis=-1, keepdims=True)
    )
    return inner * inverse


def slot_block(slot_row, first, count):
    tok = slot_row.shape[1]
    ids = lax.broadcasted_iota(jnp.int32, (count, tok), 0) + first
    return jnp.where(slot_row == ids, 1.0, 0.0).astype(BF)


def tok_block(slot_col, first, count):
    ids = lax.broadcasted_iota(jnp.int32, (slot_col.shape[0], count), 1) + first
    return jnp.where(slot_col == ids, 1.0, 0.0).astype(BF)


def doc_bias(lens, tok):
    q = lax.broadcasted_iota(jnp.int32, (tok, tok), 0)
    k = lax.broadcasted_iota(jnp.int32, (tok, tok), 1)
    dq = jnp.zeros((tok, tok), jnp.int32)
    dk = jnp.zeros((tok, tok), jnp.int32)
    end = 0
    for j in range(lens.shape[1]):
        end = end + lens[0, j]
        dq = dq + jnp.where(q >= end, 1, 0)
        dk = dk + jnp.where(k >= end, 1, 0)
    return jnp.where((dq == dk) & (q >= k), 0.0, masked_score)


def attend_kernel(
    n_exp, n_y, lens, slot_row, tokens, gain1, shift1, w_qkv, w_out, gain2, shift2, cot,
    mixed_h, context_h, middle_h, lse, send_h, land,
    mixed, context, middle, send, cot_rows, normed, bias, wq_v, wo_v, in_sem, out_sem, own_sem, *sems,
):
    tok, width = tokens.shape
    e, h, y, c = place()
    lc, cap = send.shape[1], send.shape[2]
    per = lc * cap
    hd = width // HEADS
    spread = Spread(n_exp, n_y, cot_rows, land, sems)
    loads = [
        pltpu.make_async_copy(w_qkv, wq_v, in_sem.at[0]),
        pltpu.make_async_copy(w_out, wo_v, in_sem.at[1]),
    ]
    stores = [
        pltpu.make_async_copy(a, b, out_sem.at[i])
        for i, (a, b) in enumerate(
            ((mixed, mixed_h), (context, context_h), (middle, middle_h), (send, send_h))
        )
    ]
    for cp in loads:
        cp.start()

    def pick(source, dst):
        rows = mm(slot_block(slot_row[...], dst * per, per), source)
        return rows.astype(BF).reshape(lc, cap, width)

    def advance(k):
        spread.pass_on(k)

        @pl.when(k > 0)
        def _():
            spread.pass_y(k - 1)

    @pl.loop(0, n_exp)
    def _(k):
        cot_rows[k] = pick(cot[...], k)

    own = pltpu.make_async_copy(cot_rows.at[e], land.at[:, e, h], own_sem)
    own.start()
    greet(n_exp, n_y)
    spread.start()
    own.wait()
    spread.pass_on(0)

    @pl.loop(0, tok // 128)
    def _(i):
        rows = pl.ds(i * 128, 128)
        out, _, _ = norm_rows(tokens[rows].astype(F32), gain1[...], shift1[...])
        normed[rows] = out.astype(BF)

    bias[...] = doc_bias(lens, tok)
    loads[0].wait()

    @pl.loop(0, 3)
    def _(i):
        @pl.when(i > 0)
        def _():
            advance(i)

        for j in range(width // 512):
            cols = pl.ds(pl.multiple_of(i * width + j * 512, 512), 512)
            mixed[:, cols] = mm(normed[...], wq_v[:, cols]).astype(BF)

    stores[0].start()
    advance(3)
    lse[...] = jnp.zeros_like(lse)
    lane = lax.broadcasted_iota(jnp.int32, (1, 128), 1)
    n_pairs = width // 128
    half = tok // 2
    heads_in = 128 // hd

    @pl.loop(0, n_pairs)
    def _(p):
        @pl.when((lax.rem(p, 2) == 1) & (p < 6))
        def _():
            advance(4 + lax.div(p, 2))

        def cols(part):
            return pl.ds(pl.multiple_of(part * width + p * 128, 128), 128)

        q, key, val = mixed[:, cols(0)], mixed[:, cols(1)], mixed[:, cols(2)]
        for blk in range(2):
            rows = slice(blk * half, (blk + 1) * half)
            n_keys = (blk + 1) * half
            total = jnp.zeros((half, 128), F32)
            lses = lse[rows, :]
            for hh in range(heads_in):
                own_lanes = (lane >= hh * hd) & (lane < (hh + 1) * hd)
                qh = jnp.where(own_lanes, q[rows] * BF(hd**-0.5), BF(0))
                vh = jnp.where(own_lanes, val[:n_keys], BF(0))
                s = mm_nt(qh, key[:n_keys]) + bias[rows, :n_keys]
                top = jnp.max(s, axis=-1, keepdims=True)
                ex = jnp.exp(s - top)
                tot = jnp.sum(ex, axis=-1, keepdims=True)
                probs = (ex * (1.0 / tot)).astype(BF)
                total = total + mm(probs, vh)
                lses = jnp.where(lane == p * heads_in + hh, top + jnp.log(tot), lses)
            lse[rows, :] = lses
            context[rows, pl.ds(pl.multiple_of(p * 128, 128), 128)] = total.astype(BF)

    stores[1].start()
    loads[1].wait()

    @pl.loop(0, tok // 256)
    def _(i):
        rows = pl.ds(pl.multiple_of(i * 256, 256), 256)
        mid = tokens[rows].astype(F32) + mm(context[rows], wo_v[...])
        middle[rows] = mid
        out, _, _ = norm_rows(mid, gain2[...], shift2[...])
        normed[rows] = out.astype(BF)

    stores[2].start()

    @pl.loop(0, n_exp)
    def _(k):
        send[k] = pick(normed[...], k)

    stores[3].start()

    @pl.loop(7, n_exp)
    def _(k):
        advance(k)

    spread.pass_y(n_exp - 1)
    for cp in stores:
        cp.wait()

    @pl.loop(0, n_exp)
    def _(k):
        spread.landed(k)
        spread.sent(k)


def attend(n_exp, n_hid, lc, cap, lens, slot_row, tokens, gain1, shift1, w_qkv, w_out, gain2, shift2, cot):
    n_y = n_hid // 2
    tok, width = tokens.shape
    shape = jax.ShapeDtypeStruct
    return pl.pallas_call(
        functools.partial(attend_kernel, n_exp, n_y),
        name="attend",
        out_shape=(
            shape((tok, 3 * width), BF),
            shape((tok, width), BF),
            shape((tok, width), F32),
            shape((tok, 128), F32),
            shape((n_exp, lc, cap, width), BF),
            shape((lc, n_exp, n_hid, cap, width), BF),
        ),
        in_specs=[SM, VM, VM, VM, VM, HB, HB, VM, VM, VM],
        out_specs=[HB, HB, HB, VM, HB, HB],
        scratch_shapes=[
            pltpu.VMEM((tok, 3 * width), BF),
            pltpu.VMEM((tok, width), BF),
            pltpu.VMEM((tok, width), F32),
            pltpu.VMEM((n_exp, lc, cap, width), BF),
            pltpu.VMEM((n_exp, lc, cap, width), BF),
            pltpu.VMEM((tok, width), BF),
            pltpu.VMEM((tok, tok), F32),
            pltpu.VMEM(w_qkv.shape, BF),
            pltpu.VMEM(w_out.shape, BF),
            DMA((2,)),
            DMA((4,)),
            DMA,
            *Spread.sems(n_exp, n_y),
        ],
        compiler_params=pltpu.CompilerParams(
            collective_id=0, has_side_effects=True, vmem_limit_bytes=56 * MIB
        ),
    )(lens, slot_row, tokens, gain1, shift1, w_qkv, w_out, gain2, shift2, cot)


STEP_W = 512


class Halves:
    def __init__(self, n_exp, n_y):
        self.n_exp, self.n_y, self.half = n_exp, n_y, n_exp // 2
        self.e, self.h, self.y, self.c = place()
        self.sibling = (self.e, self.y * 2 + 1 - self.c)

    def range(self, g):
        first = lax.div(self.e, self.half) * self.half
        return pl.ds(pl.multiple_of(first if g == 0 else self.half - first, self.half), self.half)

    def y_peer(self, d):
        return (self.e, lax.rem(self.y + d, self.n_y) * 2 + self.c)


class SpreadExpert(Halves):
    def __init__(self, n_exp, n_y, rows, land, sems):
        super().__init__(n_exp, n_y)
        self.rows, self.land = rows, land
        self.es, self.er, self.ys, self.yr, self.cs, self.cr = sems

    @staticmethod
    def sems(lc, n_exp, n_y):
        return [DMA((lc, n_exp))] * 2 + [DMA((lc, 2, n_y))] * 4

    def over_exp(self, ex, k):
        return rcopy(
            self.rows.at[self.e ^ k, ex], self.land.at[ex, self.e, self.h],
            self.es.at[ex, k], self.er.at[ex, k], (self.e ^ k, self.h),
        )

    def start(self, ex):
        half = self.half
        for i in range(1, self.n_exp):
            self.over_exp(ex, half + i // 2 - 1 if i % 2 == 0 else ((i + 1) // 2 if i < self.n_exp - 1 else i)).start()

    def over_y(self, ex, g, d):
        blk = self.land.at[ex, self.range(g), self.h]
        return rcopy(blk, blk, self.ys.at[ex, g, d], self.yr.at[ex, g, d], self.y_peer(d))

    def over_core(self, ex, g, d):
        hid = lax.rem(self.y + self.n_y - d, self.n_y) * 2 + self.c
        blk = self.land.at[ex, self.range(g), hid]
        return rcopy(blk, blk, self.cs.at[ex, g, d], self.cr.at[ex, g, d], self.sibling)

    def pass_on(self, ex, g):
        for k in range(max(1, g * self.half), (g + 1) * self.half):
            self.over_exp(ex, k).wait_recv()
        for d in range(1, self.n_y):
            self.over_y(ex, g, d).start()
        self.over_core(ex, g, 0).start()

    def pass_y(self, ex, g):
        for d in range(1, self.n_y):
            self.over_y(ex, g, d).wait_recv()
            self.over_core(ex, g, d).start()

    def landed(self, ex, g):
        for d in range(self.n_y):
            self.over_core(ex, g, d).wait_recv()

    def sent(self, ex):
        for k in range(1, self.n_exp):
            self.over_exp(ex, k).wait_send()
        for g in range(2):
            for d in range(1, self.n_y):
                self.over_y(ex, g, d).wait_send()
            for d in range(self.n_y):
                self.over_core(ex, g, d).wait_send()


class GatherExpert(Halves):
    def __init__(self, n_exp, n_y, part, pairs, from_y, back, sems):
        super().__init__(n_exp, n_y)
        self.part, self.pairs, self.from_y, self.back = part, pairs, from_y, back
        self.es, self.er, self.ys, self.yr, self.cs, self.cr = sems

    @staticmethod
    def sems(lc, n_exp, n_y):
        return [DMA((lc, n_exp))] * 2 + [DMA((lc, 2, n_y))] * 2 + [DMA((lc, 2))] * 2

    def over_core(self, ex, b):
        return rcopy(
            self.part.at[self.range(b), :, 1 - self.c], self.pairs.at[ex, self.range(b)],
            self.cs.at[ex, b], self.cr.at[ex, b], self.sibling,
        )

    def over_y(self, ex, b, d):
        yy = lax.rem(self.y + d, self.n_y)
        return rcopy(
            self.pairs.at[ex, self.range(b), yy], self.from_y.at[d - 1, ex, self.range(b)],
            self.ys.at[ex, b, d], self.yr.at[ex, b, d], self.y_peer(d),
        )

    def over_exp(self, ex, k):
        t = self.e ^ k
        return rcopy(
            self.pairs.at[ex, t, self.y], self.back.at[self.e, ex], self.es.at[ex, k], self.er.at[ex, k], (t, self.h)
        )

    def stay(self, ex):
        return pltpu.make_async_copy(self.pairs.at[ex, self.e, self.y], self.back.at[self.e, ex], self.es.at[ex, 0])

    def fold(self, ex, b):
        self.over_core(ex, b).wait_recv()
        rows = self.range(b)
        for yy in range(self.n_y):
            pair = self.pairs[ex, rows, yy].astype(F32) + self.part[rows, yy, self.c].astype(F32)
            self.pairs[ex, rows, yy] = pair.astype(BF)
        for d in range(1, self.n_y):
            self.over_y(ex, b, d).start()
        self.over_core(ex, b).wait_send()

    def step_exp(self, ex, b):
        rows = self.range(b)
        total = self.pairs[ex, rows, self.y].astype(F32)
        for d in range(1, self.n_y):
            self.over_y(ex, b, d).wait_recv()
            total = total + self.from_y[d - 1, ex, rows].astype(F32)
        self.pairs[ex, rows, self.y] = total.astype(BF)
        for i in range(self.half):
            k = b * self.half + i
            if k == 0:
                self.stay(ex).start()
            else:
                self.over_exp(ex, k).start()

    def finish(self, ex):
        self.stay(ex).wait()
        for b in range(2):
            for d in range(1, self.n_y):
                self.over_y(ex, b, d).wait_send()
        for k in range(1, self.n_exp):
            self.over_exp(ex, k).wait_send()
            self.over_exp(ex, k).wait_recv()


def expert_kernel(
    n_exp, n_y, rows, grads, w_in, bias_in, w_back,
    back, f_out, wi_out, wb_out, gb_in, gb_back,
    land, part, pairs, from_y, wi_v, wb_v, g_v, h_v, gp_v, f_v, wi_st, wb_st,
    w_sem, g_sem, f_sem, o_sem, own_sem, *rest,
):
    e, h, y, c = place()
    n_spread = len(SpreadExpert.sems(1, 1, 1))
    spread = SpreadExpert(n_exp, n_y, rows, land, rest[:n_spread])
    gather = GatherExpert(n_exp, n_y, part, pairs, from_y, back, rest[n_spread:])
    n_hid = 2 * n_y
    lc, cap, width = rows.shape[1:]
    ff = w_in.shape[2]
    n_src = 4
    block = n_src * n_hid * cap
    n_rb = n_exp // n_src
    step_f = min(512, ff)
    step_w = STEP_W

    def weights(ex):
        slot = lax.rem(ex, 2)
        return (
            pltpu.make_async_copy(w_in.at[ex], wi_v.at[slot], w_sem.at[0, slot]),
            pltpu.make_async_copy(w_back.at[ex], wb_v.at[slot], w_sem.at[1, slot]),
        )

    def g_copy(ex):
        slot = lax.rem(ex, 2)
        return pltpu.make_async_copy(grads.at[ex], g_v.at[slot], g_sem.at[slot])

    def f_copy(ex, rb):
        return pltpu.make_async_copy(f_v, f_out.at[ex, sources(rb)], f_sem)

    def wi_copy(ex, i):
        return pltpu.make_async_copy(wi_st, wi_out.at[ex, pl.ds(i * step_w, step_w)], o_sem.at[0])

    def wb_copy(ex, i):
        return pltpu.make_async_copy(wb_st, wb_out.at[ex, pl.ds(i * step_w, step_w)], o_sem.at[1])

    def sources(rb):
        return pl.ds(lax.rem(lax.div(e, n_exp // 2) * (n_rb // 2) + rb, n_rb) * n_src, n_src)

    own = pltpu.make_async_copy(rows.at[e], land.at[:, e, h], own_sem)
    own.start()
    greet(n_exp, n_y)

    spread.start(0)
    for ex in range(2):
        for cp in weights(ex):
            cp.start()
    g_copy(0).start()
    gb_in[...] = jnp.zeros_like(gb_in)
    gb_back[...] = jnp.zeros_like(gb_back)
    own.wait()
    spread.pass_on(0, 0)
    spread.start(1)
    spread.pass_on(0, 1)
    spread.pass_y(0, 0)

    def weight_grads(ex, after):
        slot = lax.rem(ex, 2)

        @pl.loop(0, width // step_w)
        def _(i):
            cols = pl.ds(pl.multiple_of(i * step_w, step_w), step_w)
            x = land[ex, :, :, :, cols].reshape(n_exp * n_hid * cap, step_w)
            piece = mm_tn(x, gp_v[slot].reshape(n_exp * n_hid * cap, ff)).astype(BF)

            @pl.when(i > 0)
            def _():
                wi_copy(ex, i).wait()

            wi_st[...] = piece
            wi_copy(ex, i).start()
            after(i)

        @pl.loop(0, ff // step_w)
        def _(i):
            cols = pl.ds(pl.multiple_of(i * step_w, step_w), step_w)
            hid = h_v[slot, :, :, cols].reshape(n_exp * n_hid * cap, step_w)
            piece = mm_tn(hid, g_v[slot].reshape(n_exp * n_hid * cap, width)).astype(BF)

            @pl.when(i > 0)
            def _():
                wb_copy(ex, i).wait()

            wb_st[...] = piece
            wb_copy(ex, i).start()

        wi_copy(ex, 0).wait()
        wb_copy(ex, 0).wait()

    @pl.loop(0, lc)
    def _(ex):
        slot = lax.rem(ex, 2)
        g_copy(ex).wait()
        for cp in weights(ex):
            cp.wait()

        @pl.loop(0, n_rb)
        def _(rb):
            at = sources(rb)
            for b in range(2):

                @pl.when(rb == b * (n_rb // 2))
                def _():
                    spread.landed(ex, b)

            x = land[ex, at].reshape(block, width)
            g = g_v[slot, at].reshape(block, width)
            gb_back[pl.ds(ex, 1)] += jnp.sum(g.astype(F32), axis=0, keepdims=True)
            for f in range(ff // step_f):
                cols = slice(f * step_f, (f + 1) * step_f)
                pre = mm(x, wi_v[slot, :, cols]) + bias_in[pl.ds(ex, 1), cols]
                sig = jax.nn.sigmoid(pre)
                hid = (pre * sig).astype(BF)
                gh = mm_nt(g, wb_v[slot, cols, :])
                gp = (gh * sig * (1.0 + pre * (1.0 - sig))).astype(BF)
                gb_in[pl.ds(ex, 1), cols] += jnp.sum(gp.astype(F32), axis=0, keepdims=True)
                h_v[slot, at, :, cols] = hid.reshape(n_src, n_hid * cap, step_f)
                gp_v[slot, at, :, cols] = gp.reshape(n_src, n_hid * cap, step_f)
            gd = mm_nt(gp_v[slot, at].reshape(block, ff), wi_v[slot])
            part[at] = gd.astype(BF).reshape(n_src, n_y, 2, cap, width)

            for b in range(2):

                @pl.when(rb == (b + 1) * (n_rb // 2) - 1)
                def _():
                    gather.over_core(ex, b).start()

                    if b == 0:

                        @pl.when(ex == 0)
                        def _():
                            spread.pass_y(0, 1)

                        @pl.when(ex + 2 < lc)
                        def _():
                            spread.start(ex + 2)

                    @pl.when(ex + 1 < lc)
                    def _():
                        spread.pass_on(ex + 1, b)

                    @pl.when(ex > 0)
                    def _():
                        gather.step_exp(ex - 1, b)

        @pl.loop(0, n_rb)
        def _(rb):
            hv = h_v[slot, sources(rb)].reshape(block, ff)
            f = mm(hv, wb_v[slot]).astype(BF).reshape(n_src, n_y, 2, cap, width)

            @pl.when((ex > 0) | (rb > 0))
            def _():
                f_copy(ex, rb).wait()

            f_v[...] = f
            f_copy(ex, rb).start()

            for b in range(2):

                @pl.when(rb == (b + 1) * (n_rb // 2) - 1)
                def _():
                    gather.fold(ex, b)

                    @pl.when(ex + 1 < lc)
                    def _():
                        spread.pass_y(ex + 1, b)

        @pl.when(ex + 2 < lc)
        def _():
            for cp in weights(ex + 2):
                cp.start()

        @pl.when(ex > 0)
        def _():
            weight_grads(ex - 1, lambda i: None)

        @pl.when(ex + 1 < lc)
        def _():
            g_copy(ex + 1).start()

    def last(i):
        @pl.when(i == 0)
        def _():
            gather.step_exp(lc - 1, 0)

    weight_grads(lc - 1, last)
    gather.step_exp(lc - 1, 1)
    f_copy(lc - 1, 0).wait()

    @pl.loop(0, lc)
    def _(ex):
        spread.sent(ex)
        gather.finish(ex)


def experts(n_exp, n_hid, rows, grads, w_in, bias_in, w_back):
    n_y = n_hid // 2
    _, lc, cap, width = rows.shape
    ff = w_in.shape[2]
    shape = jax.ShapeDtypeStruct
    per = n_hid * cap
    return pl.pallas_call(
        functools.partial(expert_kernel, n_exp, n_y),
        name="experts",
        out_shape=(
            shape((n_exp, lc, cap, width), BF),
            shape((lc, n_exp, n_y, 2, cap, width), BF),
            shape(w_in.shape, BF),
            shape(w_back.shape, BF),
            shape((lc, ff), F32),
            shape((lc, width), F32),
        ),
        in_specs=[HB, HB, HB, VM, HB],
        out_specs=[HB, HB, HB, HB, VM, VM],
        scratch_shapes=[
            pltpu.VMEM((lc, n_exp, n_hid, cap, width), BF),
            pltpu.VMEM((n_exp, n_y, 2, cap, width), BF),
            pltpu.VMEM((lc, n_exp, n_y, cap, width), BF),
            pltpu.VMEM((n_y - 1, lc, n_exp, cap, width), BF),
            pltpu.VMEM((2, *w_in.shape[1:]), BF),
            pltpu.VMEM((2, *w_back.shape[1:]), BF),
            pltpu.VMEM((2, n_exp, n_hid, cap, width), BF),
            pltpu.VMEM((2, n_exp, per, ff), BF),
            pltpu.VMEM((2, n_exp, per, ff), BF),
            pltpu.VMEM((4, n_y, 2, cap, width), BF),
            pltpu.VMEM((STEP_W, ff), BF),
            pltpu.VMEM((STEP_W, width), BF),
            DMA((2, 2)), DMA((2,)), DMA, DMA((2,)), DMA,
            *SpreadExpert.sems(lc, n_exp, n_y),
            *GatherExpert.sems(lc, n_exp, n_y),
        ],
        compiler_params=pltpu.CompilerParams(
            collective_id=1, has_side_effects=True, vmem_limit_bytes=63 * MIB
        ),
    )(rows, grads, w_in, bias_in, w_back)


def finish_kernel(wi, wb, mats, g_in, g_back, g_qkv, g_out):
    g_in[...] = wi[...].astype(F32)
    g_back[...] = wb[...].astype(F32)
    rows, width = g_out.shape
    for part in range(3):
        g_qkv[:, part * width : (part + 1) * width] = mats[part].reshape(rows, width).astype(F32)
    g_out[...] = mats[3].reshape(rows, width).astype(F32)


def finish(wi, wb, mats):
    lc, width, ff = wi.shape
    cut = 2
    rows = width // (lc * cut)
    mats = mats.reshape(4, width // 16, 16, width)
    shape = jax.ShapeDtypeStruct
    wi_spec = pl.BlockSpec((1, width // cut, ff), lambda i, j: (i, j, 0))
    wb_spec = pl.BlockSpec((1, ff // cut, width), lambda i, j: (i, j, 0))
    return pl.pallas_call(
        finish_kernel,
        name="finish",
        grid=(lc, cut),
        out_shape=(
            shape(wi.shape, F32), shape(wb.shape, F32),
            shape((width, 3 * width), F32), shape((width, width), F32),
        ),
        in_specs=[
            wi_spec, wb_spec,
            pl.BlockSpec((4, rows // 16, 16, width), lambda i, j: (0, i * cut + j, 0, 0)),
        ],
        out_specs=[
            wi_spec, wb_spec,
            pl.BlockSpec((rows, 3 * width), lambda i, j: (i * cut + j, 0)),
            pl.BlockSpec((rows, width), lambda i, j: (i * cut + j, 0)),
        ],
        compiler_params=pltpu.CompilerParams(vmem_limit_bytes=56 * MIB),
    )(wi, wb, mats)


def attend_back_kernel(
    n_exp, n_y, lens, slot_col, tokens_h, middle_h, cot_h, mixed_h, context_h, lse, back_h,
    gain1, shift1, w_qkv_h, w_out_h, gain2, bias_back, f_part,
    output, g_tokens, g_mats, g_norms,
    tokens, middle, cot, mixed, context, back, w_qkv, w_out,
    bias, gm, gattn, gctx, gmixed, n1t, lse_t, mine_v, f_back, mine_sem, in_sem, *rest,
):
    tok, width = tokens.shape
    hd = width // HEADS
    e, h, y, c = place()
    n_gather = len(Gather.scratch(1, 2, 1, 1, 1))
    lc, cap = f_back.shape[1:3]
    gather = Gather(
        n_exp, n_y, lambda k: f_part.at[:, e ^ k, :, 1 - c], lambda m, yy: mine_v[lax.rem(m, 4), :, yy],
        *rest[:n_gather], f_back, rest[n_gather:],
    )

    def order(m):
        return jnp.where(m < n_exp // 2, m + n_exp // 2, n_exp - 1 - m)

    def fetch(m):
        slot = lax.rem(m, 4)
        return pltpu.make_async_copy(
            f_part.at[:, e ^ order(m), :, c], mine_v.at[slot], mine_sem.at[slot]
        )

    loads = [
        pltpu.make_async_copy(a, b, in_sem.at[i])
        for i, (a, b) in enumerate((
            (back_h, back), (middle_h, middle), (cot_h, cot), (w_out_h, w_out), (tokens_h, tokens),
            (context_h, context), (mixed_h, mixed), (w_qkv_h, w_qkv),
        ))
    ]
    greet(n_exp, n_y)

    @pl.loop(0, n_exp)
    def _(m):
        gather.step_core(order(m))

    for m in range(4):
        fetch(m).start()
    for cp in loads:
        cp.start()

    def leave(m):
        fetch(m).wait()
        gather.fold(m, order(m))
        gather.send_y(order(m))

        @pl.when(m + 4 < n_exp)
        def _():
            fetch(m + 4).start()

    leave(0)
    leave(1)
    for cp in loads[:5]:
        cp.wait()

    g_norms[...] = jnp.zeros_like(g_norms)
    n_slots = n_exp * lc * cap

    def fold(values):
        return jnp.sum(values, axis=0, keepdims=True)

    @pl.loop(0, tok // 256)
    def _(i):
        rows = pl.ds(pl.multiple_of(i * 256, 256), 256)
        table = tok_block(slot_col[rows], 0, n_slots)
        up = mm(table, back[...].reshape(n_slots, width))
        _, unit, inverse = norm_rows(middle[rows], gain2[...], 0.0)
        g_norms[2:3] += fold(up * unit)
        g_norms[3:4] += fold(up)
        g_mid = cot[rows].astype(F32) + norm_back(up, unit, inverse, gain2[...])
        gm[rows] = g_mid
        gattn[rows] = g_mid.astype(BF)
        gctx[rows] = mm_nt(gattn[rows], w_out[...]).astype(BF)
        out, _, _ = norm_rows(tokens[rows].astype(F32), gain1[...], shift1[...])
        n1t[:, rows] = out.astype(BF).T

    leave(2)
    leave(3)
    for cp in loads[5:]:
        cp.wait()

    @pl.loop(0, width // 256)
    def _(i):
        cols = pl.ds(pl.multiple_of(i * 256, 256), 256)
        part = mm_tn(context[:, cols], gattn[...]).astype(BF)
        g_mats[3, pl.ds(i * 16, 16)] = part.reshape(16, 16, width)

    key_i = lax.broadcasted_iota(jnp.int32, (tok, tok), 0)
    qry_i = lax.broadcasted_iota(jnp.int32, (tok, tok), 1)
    dk_, dq_ = jnp.zeros((tok, tok), jnp.int32), jnp.zeros((tok, tok), jnp.int32)
    end = 0
    for j in range(lens.shape[1]):
        end = end + lens[0, j]
        dk_ = dk_ + jnp.where(key_i >= end, 1, 0)
        dq_ = dq_ + jnp.where(qry_i >= end, 1, 0)
    bias[...] = jnp.where((dk_ == dq_) & (qry_i >= key_i), 0.0, masked_score)
    lse_t[...] = lse[...].T

    lane = lax.broadcasted_iota(jnp.int32, (1, 128), 1)
    n_pairs = width // 128
    half = tok // 2
    heads_in = 128 // hd

    @pl.loop(0, n_pairs)
    def _(p):
        @pl.when(p + 4 < n_exp)
        def _():
            leave(p + 4)

        @pl.when((p >= 2) & (lax.rem(p, 2) == 0))
        def _():
            gather.step_exp(order(lax.div(p, 2) - 1), bias_back[...].reshape(lc, 1, width))

        def cols(part):
            return pl.ds(pl.multiple_of(part * width + p * 128, 128), 128)

        q, key, val, do = mixed[:, cols(0)], mixed[:, cols(1)], mixed[:, cols(2)], gctx[:, cols(0)]
        dq = [jnp.zeros((half, 128), F32) for _ in range(2)]
        dkey = [jnp.zeros((half, 128), F32) for _ in range(2)]
        dval = [jnp.zeros((half, 128), F32) for _ in range(2)]
        for hh in range(heads_in):
            own_lanes = (lane >= hh * hd) & (lane < (hh + 1) * hd)
            qh = jnp.where(own_lanes, q * BF(hd**-0.5), BF(0))
            kh = jnp.where(own_lanes, key * BF(hd**-0.5), BF(0))
            doh = jnp.where(own_lanes, do, BF(0))
            lrow = lse_t[pl.ds(p * heads_in + hh, 1), :]
            for qb in range(2):
                rows = slice(qb * half, (qb + 1) * half)
                n = (qb + 1) * half
                s = mm_nt(key[:n], qh[rows]) + (bias[:n, rows] - lrow[:, rows])
                pt = jnp.exp(s)
                dp = mm_nt(val[:n], doh[rows])
                inner = jnp.sum(dp * pt, axis=0, keepdims=True)
                ds = (pt * (dp - inner)).astype(BF)
                ptb = pt.astype(BF)
                dv_, dk2 = mm(ptb, doh[rows]), mm(ds, qh[rows])
                for kb in range(qb + 1):
                    part = slice(kb * half, (kb + 1) * half)
                    dval[kb] = dval[kb] + dv_[part]
                    dkey[kb] = dkey[kb] + dk2[part]
                dq[qb] = dq[qb] + mm_tn(ds, kh[:n])
        for b in range(2):
            rows = slice(b * half, (b + 1) * half)
            gmixed[rows, cols(0)] = dq[b].astype(BF)
            gmixed[rows, cols(1)] = dkey[b].astype(BF)
            gmixed[rows, cols(2)] = dval[b].astype(BF)

    gather.step_exp(order(3), bias_back[...].reshape(lc, 1, width))

    @pl.loop(0, tok // 256)
    def _(i):
        rows = pl.ds(pl.multiple_of(i * 256, 256), 256)
        up = mm_nt(gmixed[rows], w_qkv[...])
        _, unit, inverse = norm_rows(tokens[rows].astype(F32), gain1[...], 0.0)
        g_norms[0:1] += fold(up * unit)
        g_norms[1:2] += fold(up)
        g_tokens[rows] = gm[rows] + norm_back(up, unit, inverse, gain1[...])

    gather.step_exp(order(4), bias_back[...].reshape(lc, 1, width))

    for part in range(3):

        @pl.loop(0, width // 256)
        def _(i):
            rows = pl.ds(pl.multiple_of(i * 256, 256), 256)
            piece = mm(n1t[rows], gmixed[:, part * width : (part + 1) * width])
            g_mats[part, pl.ds(i * 16, 16)] = piece.astype(BF).reshape(16, 16, width)

    @pl.loop(n_pairs + 4, max(n_exp, n_pairs + 4))
    def _(m):
        leave(m)

    @pl.loop(5, n_exp)
    def _(m):
        gather.step_exp(order(m), bias_back[...].reshape(lc, 1, width))

    @pl.loop(0, n_exp)
    def _(k):
        gather.over_core(k).wait_send()
        gather.finish(k)

    @pl.loop(0, tok // 256)
    def _(i):
        rows = pl.ds(pl.multiple_of(i * 256, 256), 256)
        table = tok_block(slot_col[rows], 0, n_slots)
        output[rows] = (middle[rows] + mm(table, f_back[...].reshape(n_slots, width))).astype(BF)


def attend_back(
    n_exp, n_hid, lens, slot_col, tokens, middle, cot, mixed, context, lse, back,
    gain1, shift1, w_qkv, w_out, gain2, bias_back, f_part,
):
    n_y = n_hid // 2
    tok, width = tokens.shape
    _, lc, cap, _ = back.shape
    shape = jax.ShapeDtypeStruct
    return pl.pallas_call(
        functools.partial(attend_back_kernel, n_exp, n_y),
        name="attend_back",
        out_shape=(
            shape((tok, width), BF),
            shape((tok, width), F32),
            shape((4, width // 16, 16, width), BF),
            shape((8, width), F32),
        ),
        in_specs=[SM, VM, HB, HB, HB, HB, HB, VM, HB, VM, VM, HB, HB, VM, VM, HB],
        out_specs=[VM] * 4,
        scratch_shapes=[
            *[pltpu.VMEM(a.shape, a.dtype) for a in (tokens, middle, cot, mixed, context, back, w_qkv, w_out)],
            pltpu.VMEM((tok, tok), F32),
            pltpu.VMEM((tok, width), F32),
            pltpu.VMEM((tok, width), BF),
            pltpu.VMEM((tok, width), BF),
            pltpu.VMEM((tok, 3 * width), BF),
            pltpu.VMEM((width, tok), BF),
            pltpu.VMEM((128, tok), F32),
            pltpu.VMEM((4, lc, n_y, cap, width), BF),
            pltpu.VMEM((n_exp, lc, cap, width), BF),
            DMA((4,)),
            DMA((8,)),
            *Gather.scratch(n_exp, n_y, lc, cap, width),
            *Gather.sems(n_exp, n_y),
        ],
        compiler_params=pltpu.CompilerParams(
            collective_id=2, has_side_effects=True, vmem_limit_bytes=62 * MIB
        ),
    )(
        lens, slot_col, tokens, middle, cot, mixed, context, lse, back,
        gain1, shift1, w_qkv, w_out, gain2, bias_back, f_part,
    )


def reduce_kernel(
    n_x, n_y, n_z, mats, norms, out, norms_out,
    acc, core_in, in1, in2, in3, n_acc, n_in,
    c_s, c_r, s1, r1, s2, r2, s3, r3, t3, u3, t2, u2, t1, u1, d_s, d_r, n_s, n_r,
):
    e, h, y, c = place()
    x, z = lax.rem(e, n_x), lax.div(e, n_x)
    sub = n_x * n_y * n_z
    half = mats.shape[0] // 2
    piece = half // 2
    n_sub = piece // sub
    at = {"x": (n_x, x), "y": (n_y, y), "z": (n_z, z)}
    orders = (("y", "x", "z"), ("x", "y", "z"))
    sibling = (e, y * 2 + 1 - c)

    def device(axis, o):
        return {"x": (z * n_x + o, h), "y": (e, o * 2 + c), "z": (o * n_x + x, h)}[axis]

    sem = pltpu.get_barrier_semaphore()
    for axis in "xyz":
        n, i = at[axis]
        for d in range(1, n):
            pl.semaphore_signal(sem, inc=1, device_id=device(axis, lax.rem(i + d, n)), device_id_type=MESH)
    pl.semaphore_signal(sem, inc=1, device_id=sibling, device_id_type=MESH)
    pl.semaphore_wait(sem, n_x + n_y + n_z - 2)

    def units(p, b, depth):
        first, count = p * piece + b * sub, sub
        for axis in orders[p][:depth]:
            n, i = at[axis]
            count = count // n
            first = first + i * count
        return first, count

    def core_copy(p, b):
        first = p * piece + b * sub
        return rcopy(
            mats.at[pl.ds((1 - c) * half + first, sub)], core_in.at[pl.ds(first, sub)],
            c_s.at[p, b], c_r.at[p, b], sibling,
        )

    lands = (in1, in2, in3)
    sends, recvs = (s1, s2, s3), (r1, r2, r3)

    def down(p, b, stage, d):
        n, i = at[orders[p][stage]]
        first, count = units(p, b, stage)
        count = count // n
        o = lax.rem(i + d, n)
        return rcopy(
            acc.at[pl.ds(first + o * count, count)], lands[stage].at[p, b, d - 1, pl.ds(0, count)],
            sends[stage].at[p, b, d - 1], recvs[stage].at[p, b, d - 1], device(orders[p][stage], o),
        )

    ups, upr = (t1, t2, t3), (u1, u2, u3)

    def up(p, b, stage, d):
        n, i = at[orders[p][stage]]
        first, count = units(p, b, stage + 1)
        region = out.at[pl.ds(c * half + first, count)]
        o = lax.rem(i + d, n)
        return rcopy(
            region, region, ups[stage].at[p, b, d - 1], upr[stage].at[p, b, d - 1], device(orders[p][stage], o)
        )

    def core_up(p, b):
        region = out.at[pl.ds(c * half + p * piece + b * sub, sub)]
        return rcopy(region, region, d_s.at[p, b], d_r.at[p, b], sibling)

    def peers(p, stage):
        return range(1, at[orders[p][stage]][0])

    def event(p, b, q):
        if q == 0:
            core_copy(p, b).wait_recv()
            first = p * piece + b * sub
            mine = mats[pl.ds(c * half + first, sub)].astype(F32)
            acc[pl.ds(first, sub)] = (mine + core_in[pl.ds(first, sub)].astype(F32)).astype(BF)
        elif q <= 3:
            first, count = units(p, b, q)
            total = acc[pl.ds(first, count)].astype(F32)
            for d in peers(p, q - 1):
                down(p, b, q - 1, d).wait_recv()
                total = total + lands[q - 1][p, b, d - 1, :count].astype(F32)
            if q < 3:
                acc[pl.ds(first, count)] = total.astype(BF)
            else:
                out[pl.ds(c * half + first, count)] = total.astype(BF)
        else:
            for d in peers(p, 6 - q):
                up(p, b, 6 - q, d).wait_recv()
        if q < 3:
            for d in peers(p, q):
                down(p, b, q, d).start()
        elif q < 6:
            for d in peers(p, 5 - q):
                up(p, b, 5 - q, d).start()
        else:
            core_up(p, b).start()

    for b in range(n_sub):
        for p in range(2):
            core_copy(p, b).start()

    n_axes = (None, "y", "x", "z")

    def n_copy(stage, d):
        if stage == 0:
            dev = sibling
        else:
            n, i = at[n_axes[stage]]
            dev = device(n_axes[stage], lax.rem(i + d, n))
        return rcopy(n_acc.at[stage], n_in.at[stage, d - 1], n_s.at[stage, d - 1], n_r.at[stage, d - 1], dev)

    def n_peers(stage):
        return range(1, 2 if stage == 0 else at[n_axes[stage]][0])

    def n_total(stage):
        for d in n_peers(stage):
            n_copy(stage, d).wait_recv()
        own = n_acc[stage]
        if stage == 0:
            return own + n_in[0, 0]
        n, i = at[n_axes[stage]]
        total = jnp.zeros_like(own)
        for m in range(n):
            term = own
            for d in range(1, n):
                term = jnp.where(lax.rem(i + n - d, n) == m, n_in[stage, d - 1], term)
            total = total + term
        return total

    n_acc[0] = norms[...]
    n_copy(0, 1).start()

    @pl.loop(0, n_sub + 6)
    def _(s):
        for q in range(7):

            @pl.when((s >= q) & (s - q < n_sub))
            def _():
                for p in range(2):
                    event(p, s - q, q)

        for stage in range(1, 4):

            @pl.when(s == stage)
            def _():
                n_acc[stage] = n_total(stage - 1)
                for d in n_peers(stage):
                    n_copy(stage, d).start()

    norms_out[...] = n_total(3)
    for stage in range(4):
        for d in n_peers(stage):
            n_copy(stage, d).wait_send()

    @pl.loop(0, n_sub)
    def _(b):
        for p in range(2):
            core_up(p, b).wait_recv()
            core_copy(p, b).wait_send()
            core_up(p, b).wait_send()
            for stage in range(3):
                for d in peers(p, stage):
                    down(p, b, stage, d).wait_send()
                    up(p, b, stage, d).wait_send()


def reduce_all(n_exp, n_hid, mats, norms):
    n_y = n_hid // 2
    n_x = n_y
    n_z = n_exp // n_x
    sub = n_x * n_y * n_z
    width = norms.shape[1]
    flat = mats.reshape(-1, 16, width)
    half = flat.shape[0] // 2
    n_sub = half // 2 // sub
    most = max(n_x, n_y)
    shape = jax.ShapeDtypeStruct

    def land(n, count):
        return pltpu.VMEM((2, n_sub, n - 1, count, 16, width), BF)

    def sems(n):
        return [DMA((2, n_sub, n - 1))] * 2

    mats, norms = pl.pallas_call(
        functools.partial(reduce_kernel, n_x, n_y, n_z),
        name="reduce_all",
        out_shape=(shape(flat.shape, BF), shape(norms.shape, F32)),
        in_specs=[VM] * 2,
        out_specs=[VM] * 2,
        scratch_shapes=[
            pltpu.VMEM((half, 16, width), BF),
            pltpu.VMEM((half, 16, width), BF),
            land(most, sub // min(n_x, n_y)),
            land(most, sub // (n_x * n_y)),
            land(n_z, 1),
            pltpu.VMEM((4, *norms.shape), F32),
            pltpu.VMEM((4, max(most, n_z) - 1, *norms.shape), F32),
            DMA((2, n_sub)), DMA((2, n_sub)),
            *sems(most), *sems(most), *sems(n_z), *sems(n_z), *sems(most), *sems(most),
            DMA((2, n_sub)), DMA((2, n_sub)),
            *[DMA((4, max(most, n_z) - 1))] * 2,
        ],
        compiler_params=pltpu.CompilerParams(
            collective_id=3, has_side_effects=True, vmem_limit_bytes=50 * MIB
        ),
    )(flat, norms)
    return mats, norms


def token_slots(token_ids, hash_table, capacity, cap):
    chosen = jnp.take(hash_table, token_ids, mode="clip")
    places = jnp.arange(chosen.shape[0], dtype=jnp.int32)
    earlier = (chosen[:, None] == chosen[None, :]) & (places[:, None] > places[None, :])
    rank = jnp.sum(earlier.astype(jnp.int32), axis=1)
    experts_ids = jnp.arange(capacity.shape[0], dtype=jnp.int32)
    limit = jnp.sum(jnp.where(chosen[:, None] == experts_ids[None, :], capacity[None, :], 0), axis=1)
    return jnp.where(rank < limit, chosen * cap + rank, -1)


def per_device(
    tokens, token_ids, lengths, hash_table, capacity, gain_one, shift_one, w_qkv, w_out,
    gain_two, shift_two, w_in, bias_in, w_back, bias_back, cotangent,
):
    n_exp, n_hid = lax.axis_size("exp"), lax.axis_size("hid")
    tok, width = tokens.shape
    lc, _, ff = w_in.shape
    cap = 2 * tok // capacity.shape[0]
    slot = token_slots(token_ids, hash_table, capacity, cap)
    gain1, shift1, gain2, shift2 = (v[None] for v in (gain_one, shift_one, gain_two, shift_two))
    mixed, context, middle, lse, send, grads = attend(
        n_exp, n_hid, lc, cap, lengths, slot[None], tokens, gain1, shift1, w_qkv, w_out, gain2, shift2, cotangent
    )
    back, f_part, wi, wb, gb_in, gb_back = experts(
        n_exp, n_hid, send, grads, w_in, bias_in, w_back
    )
    output, g_tokens, mats, norms = attend_back(
        n_exp, n_hid, lengths, slot[:, None], tokens, middle, cotangent, mixed, context, lse, back,
        gain1, shift1, w_qkv, w_out, gain2, bias_back, f_part,
    )
    mats, norms = reduce_all(n_exp, n_hid, mats, norms)
    g_in, g_back, g_qkv, g_out = finish(wi, wb, mats)
    return (
        output, g_tokens, norms[0], norms[1], g_qkv, g_out, norms[2], norms[3],
        g_in, gb_in, g_back, gb_back,
    )


def solution(mesh):
    both = P(("exp", "hid"))
    rows = P(("exp", "hid"), None)
    placed = (
        rows, both, rows, P(), P(), P(), P(), P(), P(), P(), P(),
        P("exp", None, "hid"), P("exp", "hid"), P("exp", "hid", None), P("exp", None), rows,
    )
    return jax.shard_map(
        per_device,
        mesh=mesh,
        in_specs=placed,
        out_specs=(
            rows, rows, P(), P(), P(), P(), P(), P(),
            P("exp", None, "hid"), P("exp", "hid"), P("exp", "hid", None), P("exp", None),
        ),
        check_vma=False,
    )
```

```python
import functools

import jax
import jax.numpy as jnp
from jax import lax
from jax.experimental import pallas as pl
from jax.experimental.pallas import tpu as pltpu
from jax.sharding import PartitionSpec as P

HEADS = 16
MESH = pl.DeviceIdType.MESH
BF = jnp.bfloat16
F32 = jnp.float32
epsilon = 1e-05
masked_score = -1e30
DMA = pltpu.SemaphoreType.DMA
VM = pl.BlockSpec(memory_space=pltpu.VMEM)
SM = pl.BlockSpec(memory_space=pltpu.SMEM)
HB = pl.BlockSpec(memory_space=pl.ANY)
MIB = 1 << 20


def mm(a, b):
    return lax.dot_general(a, b, (((1,), (0,)), ((), ())), preferred_element_type=F32)


def mm_nt(a, b):
    return lax.dot_general(a, b, (((1,), (1,)), ((), ())), preferred_element_type=F32)


def mm_tn(a, b):
    return lax.dot_general(a, b, (((0,), (0,)), ((), ())), preferred_element_type=F32)


def place():
    e = lax.axis_index("exp")
    h = lax.axis_index("hid")
    return e, h, lax.div(h, 2), lax.rem(h, 2)


def rcopy(src, dst, send, recv, dev):
    return pltpu.make_async_remote_copy(
        src_ref=src, dst_ref=dst, send_sem=send, recv_sem=recv, device_id=dev, device_id_type=MESH
    )


def greet(n_exp, n_y):
    e, h, y, c = place()
    sem = pltpu.get_barrier_semaphore()
    for k in range(1, n_exp):
        pl.semaphore_signal(sem, inc=1, device_id=(e ^ k, h), device_id_type=MESH)
    for d in range(1, n_y):
        pl.semaphore_signal(
            sem, inc=1, device_id=(e, lax.rem(y + d, n_y) * 2 + c), device_id_type=MESH
        )
    pl.semaphore_signal(sem, inc=1, device_id=(e, y * 2 + 1 - c), device_id_type=MESH)
    pl.semaphore_wait(sem, n_exp - 1 + n_y)


class Spread:
    def __init__(self, n_exp, n_y, rows, land, sems):
        self.n_exp, self.n_y, self.rows, self.land = n_exp, n_y, rows, land
        self.es, self.er, self.ys, self.yr, self.cs, self.cr = sems
        self.e, self.h, self.y, self.c = place()

    @staticmethod
    def sems(n_exp, n_y):
        return [DMA((n_exp,)), DMA((n_exp,))] + [DMA((n_exp, n_y))] * 4

    def over_exp(self, k):
        return rcopy(
            self.rows.at[self.e ^ k], self.land.at[:, self.e, self.h],
            self.es.at[k], self.er.at[k], (self.e ^ k, self.h),
        )

    def start(self):
        @pl.loop(1, self.n_exp)
        def _(i):
            low, high = lax.div(i + 1, 2), self.n_exp // 2 + lax.div(i, 2) - 1
            k = jnp.where(i == self.n_exp - 1, self.n_exp - 1, jnp.where(lax.rem(i, 2) == 1, low, high))
            self.over_exp(k).start()

    def block(self, k, hid):
        return self.land.at[:, self.e ^ k, hid]

    def over_y(self, k, d):
        blk = self.block(k, self.h)
        dev = (self.e, lax.rem(self.y + d, self.n_y) * 2 + self.c)
        return rcopy(blk, blk, self.ys.at[k, d], self.yr.at[k, d], dev)

    def over_core(self, k, d):
        blk = self.block(k, lax.rem(self.y + self.n_y - d, self.n_y) * 2 + self.c)
        dev = (self.e, self.y * 2 + 1 - self.c)
        return rcopy(blk, blk, self.cs.at[k, d], self.cr.at[k, d], dev)

    def pass_on(self, k):
        @pl.when(k > 0)
        def _():
            self.over_exp(k).wait_recv()

        for d in range(1, self.n_y):
            self.over_y(k, d).start()
        self.over_core(k, 0).start()

    def pass_y(self, k):
        for d in range(1, self.n_y):
            self.over_y(k, d).wait_recv()
            self.over_core(k, d).start()

    def landed(self, k):
        for d in range(self.n_y):
            self.over_core(k, d).wait_recv()

    def sent(self, k):
        @pl.when(k > 0)
        def _():
            self.over_exp(k).wait_send()

        for d in range(1, self.n_y):
            self.over_y(k, d).wait_send()
        for d in range(self.n_y):
            self.over_core(k, d).wait_send()


class Gather:
    def __init__(self, n_exp, n_y, other, mine, pairs, from_y, back, sems):
        self.n_exp, self.n_y, self.other, self.mine = n_exp, n_y, other, mine
        self.pairs, self.from_y, self.back = pairs, from_y, back
        self.es, self.er, self.ys, self.yr, self.cs, self.cr = sems
        self.e, self.h, self.y, self.c = place()

    @staticmethod
    def sems(n_exp, n_y):
        return [DMA((n_exp,)), DMA((n_exp,)), DMA((n_exp, n_y)), DMA((n_exp, n_y)), DMA((n_exp,)), DMA((n_exp,))]

    @staticmethod
    def scratch(n_exp, n_y, lc, cap, d):
        return [
            pltpu.VMEM((n_exp, lc, n_y, cap, d), BF),
            pltpu.VMEM((n_exp, n_y - 1, lc, cap, d), BF),
        ]

    def over_core(self, k):
        t = self.e ^ k
        dev = (self.e, self.y * 2 + 1 - self.c)
        return rcopy(self.other(k), self.pairs.at[t], self.cs.at[k], self.cr.at[k], dev)

    def over_y(self, k, d):
        t = self.e ^ k
        dev = (self.e, lax.rem(self.y + d, self.n_y) * 2 + self.c)
        yy = lax.rem(self.y + d, self.n_y)
        return rcopy(self.pairs.at[t, :, yy], self.from_y.at[t, d - 1], self.ys.at[k, d], self.yr.at[k, d], dev)

    def over_exp(self, k):
        t = self.e ^ k
        return rcopy(self.pairs.at[t, :, self.y], self.back.at[self.e], self.es.at[k], self.er.at[k], (t, self.h))

    def step_core(self, k):
        self.over_core(k).start()

    def fold(self, at, k):
        t = self.e ^ k
        self.over_core(k).wait_recv()
        for yy in range(self.n_y):
            pair = self.pairs[t, :, yy].astype(F32) + self.mine(at, yy).astype(F32)
            self.pairs[t, :, yy] = pair.astype(BF)

    def send_y(self, k):
        for d in range(1, self.n_y):
            self.over_y(k, d).start()

    def step_exp(self, k, extra=None):
        t = self.e ^ k
        total = self.pairs[t, :, self.y].astype(F32)
        for d in range(1, self.n_y):
            self.over_y(k, d).wait_recv()
            total = total + self.from_y[t, d - 1].astype(F32)
        if extra is not None:
            total = total + extra
        total = total.astype(BF)

        @pl.when(k == 0)
        def _():
            self.back[t] = total

        @pl.when(k > 0)
        def _():
            self.pairs[t, :, self.y] = total
            self.over_exp(k).start()

    def sent(self, k):
        for d in range(1, self.n_y):
            self.over_y(k, d).wait_send()

        @pl.when(k > 0)
        def _():
            self.over_exp(k).wait_send()


def norm_rows(rows, gain, shift):
    mean = jnp.mean(rows, axis=-1, keepdims=True)
    centred = rows - mean
    var = jnp.mean(centred * centred, axis=-1, keepdims=True)
    inverse = lax.rsqrt(var + epsilon)
    unit = centred * inverse
    return unit * gain + shift, unit, inverse


def norm_back(upstream, unit, inverse, gain):
    scaled = upstream * gain
    inner = (
        scaled
        - jnp.mean(scaled, axis=-1, keepdims=True)
        - unit * jnp.mean(scaled * unit, axis=-1, keepdims=True)
    )
    return inner * inverse


def slot_block(slot_row, first, count):
    tok = slot_row.shape[1]
    ids = lax.broadcasted_iota(jnp.int32, (count, tok), 0) + first
    return jnp.where(slot_row == ids, 1.0, 0.0).astype(BF)


def tok_block(slot_col, first, count):
    ids = lax.broadcasted_iota(jnp.int32, (slot_col.shape[0], count), 1) + first
    return jnp.where(slot_col == ids, 1.0, 0.0).astype(BF)


def doc_bias(lens, tok):
    q = lax.broadcasted_iota(jnp.int32, (tok, tok), 0)
    k = lax.broadcasted_iota(jnp.int32, (tok, tok), 1)
    dq = jnp.zeros((tok, tok), jnp.int32)
    dk = jnp.zeros((tok, tok), jnp.int32)
    end = 0
    for j in range(lens.shape[1]):
        end = end + lens[0, j]
        dq = dq + jnp.where(q >= end, 1, 0)
        dk = dk + jnp.where(k >= end, 1, 0)
    return jnp.where((dq == dk) & (q >= k), 0.0, masked_score)


def attend_kernel(
    n_exp, n_y, lens, slot_row, tokens, gain1, shift1, w_qkv, w_out, gain2, shift2, cot,
    mixed_h, context_h, middle_h, lse, send_h, land,
    mixed, context, middle, send, cot_rows, normed, bias, wq_v, wo_v, in_sem, out_sem, own_sem, *sems,
):
    tok, width = tokens.shape
    e, h, y, c = place()
    lc, cap = send.shape[1], send.shape[2]
    per = lc * cap
    hd = width // HEADS
    spread = Spread(n_exp, n_y, cot_rows, land, sems)
    loads = [
        pltpu.make_async_copy(w_qkv, wq_v, in_sem.at[0]),
        pltpu.make_async_copy(w_out, wo_v, in_sem.at[1]),
    ]
    stores = [
        pltpu.make_async_copy(a, b, out_sem.at[i])
        for i, (a, b) in enumerate(
            ((mixed, mixed_h), (context, context_h), (middle, middle_h), (send, send_h))
        )
    ]
    for cp in loads:
        cp.start()

    def pick(source, dst):
        rows = mm(slot_block(slot_row[...], dst * per, per), source)
        return rows.astype(BF).reshape(lc, cap, width)

    def advance(k):
        spread.pass_on(k)

        @pl.when(k > 0)
        def _():
            spread.pass_y(k - 1)

    @pl.loop(0, n_exp)
    def _(k):
        cot_rows[k] = pick(cot[...], k)

    own = pltpu.make_async_copy(cot_rows.at[e], land.at[:, e, h], own_sem)
    own.start()
    greet(n_exp, n_y)
    spread.start()
    own.wait()
    spread.pass_on(0)

    @pl.loop(0, tok // 128)
    def _(i):
        rows = pl.ds(i * 128, 128)
        out, _, _ = norm_rows(tokens[rows].astype(F32), gain1[...], shift1[...])
        normed[rows] = out.astype(BF)

    bias[...] = doc_bias(lens, tok)
    loads[0].wait()

    @pl.loop(0, 3)
    def _(i):
        @pl.when(i > 0)
        def _():
            advance(i)

        for j in range(width // 512):
            cols = pl.ds(pl.multiple_of(i * width + j * 512, 512), 512)
            mixed[:, cols] = mm(normed[...], wq_v[:, cols]).astype(BF)

    stores[0].start()
    advance(3)
    lse[...] = jnp.zeros_like(lse)
    lane = lax.broadcasted_iota(jnp.int32, (1, 128), 1)
    n_pairs = width // 128
    half = tok // 2
    heads_in = 128 // hd

    @pl.loop(0, n_pairs)
    def _(p):
        @pl.when((lax.rem(p, 2) == 1) & (p < 6))
        def _():
            advance(4 + lax.div(p, 2))

        def cols(part):
            return pl.ds(pl.multiple_of(part * width + p * 128, 128), 128)

        q, key, val = mixed[:, cols(0)], mixed[:, cols(1)], mixed[:, cols(2)]
        for blk in range(2):
            rows = slice(blk * half, (blk + 1) * half)
            n_keys = (blk + 1) * half
            total = jnp.zeros((half, 128), F32)
            lses = lse[rows, :]
            for hh in range(heads_in):
                own_lanes = (lane >= hh * hd) & (lane < (hh + 1) * hd)
                qh = jnp.where(own_lanes, q[rows] * BF(hd**-0.5), BF(0))
                vh = jnp.where(own_lanes, val[:n_keys], BF(0))
                s = mm_nt(qh, key[:n_keys]) + bias[rows, :n_keys]
                top = jnp.max(s, axis=-1, keepdims=True)
                ex = jnp.exp(s - top)
                tot = jnp.sum(ex, axis=-1, keepdims=True)
                probs = (ex * (1.0 / tot)).astype(BF)
                total = total + mm(probs, vh)
                lses = jnp.where(lane == p * heads_in + hh, top + jnp.log(tot), lses)
            lse[rows, :] = lses
            context[rows, pl.ds(pl.multiple_of(p * 128, 128), 128)] = total.astype(BF)

    stores[1].start()
    loads[1].wait()

    @pl.loop(0, tok // 256)
    def _(i):
        rows = pl.ds(pl.multiple_of(i * 256, 256), 256)
        mid = tokens[rows].astype(F32) + mm(context[rows], wo_v[...])
        middle[rows] = mid
        out, _, _ = norm_rows(mid, gain2[...], shift2[...])
        normed[rows] = out.astype(BF)

    stores[2].start()

    @pl.loop(0, n_exp)
    def _(k):
        send[k] = pick(normed[...], k)

    stores[3].start()

    @pl.loop(7, n_exp)
    def _(k):
        advance(k)

    spread.pass_y(n_exp - 1)
    for cp in stores:
        cp.wait()

    @pl.loop(0, n_exp)
    def _(k):
        spread.landed(k)
        spread.sent(k)


def attend(n_exp, n_hid, lc, cap, lens, slot_row, tokens, gain1, shift1, w_qkv, w_out, gain2, shift2, cot):
    n_y = n_hid // 2
    tok, width = tokens.shape
    shape = jax.ShapeDtypeStruct
    return pl.pallas_call(
        functools.partial(attend_kernel, n_exp, n_y),
        name="attend",
        out_shape=(
            shape((tok, 3 * width), BF),
            shape((tok, width), BF),
            shape((tok, width), F32),
            shape((tok, 128), F32),
            shape((n_exp, lc, cap, width), BF),
            shape((lc, n_exp, n_hid, cap, width), BF),
        ),
        in_specs=[SM, VM, VM, VM, VM, HB, HB, VM, VM, VM],
        out_specs=[HB, HB, HB, VM, HB, HB],
        scratch_shapes=[
            pltpu.VMEM((tok, 3 * width), BF),
            pltpu.VMEM((tok, width), BF),
            pltpu.VMEM((tok, width), F32),
            pltpu.VMEM((n_exp, lc, cap, width), BF),
            pltpu.VMEM((n_exp, lc, cap, width), BF),
            pltpu.VMEM((tok, width), BF),
            pltpu.VMEM((tok, tok), F32),
            pltpu.VMEM(w_qkv.shape, BF),
            pltpu.VMEM(w_out.shape, BF),
            DMA((2,)),
            DMA((4,)),
            DMA,
            *Spread.sems(n_exp, n_y),
        ],
        compiler_params=pltpu.CompilerParams(
            collective_id=0, has_side_effects=True, vmem_limit_bytes=56 * MIB
        ),
    )(lens, slot_row, tokens, gain1, shift1, w_qkv, w_out, gain2, shift2, cot)


STEP_W = 512


class Halves:
    def __init__(self, n_exp, n_y):
        self.n_exp, self.n_y, self.half = n_exp, n_y, n_exp // 2
        self.e, self.h, self.y, self.c = place()
        self.sibling = (self.e, self.y * 2 + 1 - self.c)

    def range(self, g):
        first = lax.div(self.e, self.half) * self.half
        return pl.ds(pl.multiple_of(first if g == 0 else self.half - first, self.half), self.half)

    def y_peer(self, d):
        return (self.e, lax.rem(self.y + d, self.n_y) * 2 + self.c)


class SpreadExpert(Halves):
    def __init__(self, n_exp, n_y, rows, land, sems):
        super().__init__(n_exp, n_y)
        self.rows, self.land = rows, land
        self.es, self.er, self.ys, self.yr, self.cs, self.cr = sems

    @staticmethod
    def sems(lc, n_exp, n_y):
        return [DMA((lc, n_exp))] * 2 + [DMA((lc, 2, n_y))] * 4

    def over_exp(self, ex, k):
        return rcopy(
            self.rows.at[self.e ^ k, ex], self.land.at[ex, self.e, self.h],
            self.es.at[ex, k], self.er.at[ex, k], (self.e ^ k, self.h),
        )

    def start(self, ex):
        half = self.half
        for i in range(1, self.n_exp):
            self.over_exp(ex, half + i // 2 - 1 if i % 2 == 0 else ((i + 1) // 2 if i < self.n_exp - 1 else i)).start()

    def over_y(self, ex, g, d):
        blk = self.land.at[ex, self.range(g), self.h]
        return rcopy(blk, blk, self.ys.at[ex, g, d], self.yr.at[ex, g, d], self.y_peer(d))

    def over_core(self, ex, g, d):
        hid = lax.rem(self.y + self.n_y - d, self.n_y) * 2 + self.c
        blk = self.land.at[ex, self.range(g), hid]
        return rcopy(blk, blk, self.cs.at[ex, g, d], self.cr.at[ex, g, d], self.sibling)

    def pass_on(self, ex, g):
        for k in range(max(1, g * self.half), (g + 1) * self.half):
            self.over_exp(ex, k).wait_recv()
        for d in range(1, self.n_y):
            self.over_y(ex, g, d).start()
        self.over_core(ex, g, 0).start()

    def pass_y(self, ex, g):
        for d in range(1, self.n_y):
            self.over_y(ex, g, d).wait_recv()
            self.over_core(ex, g, d).start()

    def landed(self, ex, g):
        for d in range(self.n_y):
            self.over_core(ex, g, d).wait_recv()

    def sent(self, ex):
        for k in range(1, self.n_exp):
            self.over_exp(ex, k).wait_send()
        for g in range(2):
            for d in range(1, self.n_y):
                self.over_y(ex, g, d).wait_send()
            for d in range(self.n_y):
                self.over_core(ex, g, d).wait_send()


class GatherExpert(Halves):
    def __init__(self, n_exp, n_y, part, pairs, from_y, back, sems):
        super().__init__(n_exp, n_y)
        self.part, self.pairs, self.from_y, self.back = part, pairs, from_y, back
        self.es, self.er, self.ys, self.yr, self.cs, self.cr = sems

    @staticmethod
    def sems(lc, n_exp, n_y):
        return [DMA((lc, n_exp))] * 2 + [DMA((lc, 2, n_y))] * 2 + [DMA((lc, 2))] * 2

    def over_core(self, ex, b):
        return rcopy(
            self.part.at[self.range(b), :, 1 - self.c], self.pairs.at[ex, self.range(b)],
            self.cs.at[ex, b], self.cr.at[ex, b], self.sibling,
        )

    def over_y(self, ex, b, d):
        yy = lax.rem(self.y + d, self.n_y)
        return rcopy(
            self.pairs.at[ex, self.range(b), yy], self.from_y.at[d - 1, ex, self.range(b)],
            self.ys.at[ex, b, d], self.yr.at[ex, b, d], self.y_peer(d),
        )

    def over_exp(self, ex, k):
        t = self.e ^ k
        return rcopy(
            self.pairs.at[ex, t, self.y], self.back.at[self.e, ex], self.es.at[ex, k], self.er.at[ex, k], (t, self.h)
        )

    def stay(self, ex):
        return pltpu.make_async_copy(self.pairs.at[ex, self.e, self.y], self.back.at[self.e, ex], self.es.at[ex, 0])

    def fold(self, ex, b):
        self.over_core(ex, b).wait_recv()
        rows = self.range(b)
        for yy in range(self.n_y):
            pair = self.pairs[ex, rows, yy].astype(F32) + self.part[rows, yy, self.c].astype(F32)
            self.pairs[ex, rows, yy] = pair.astype(BF)
        for d in range(1, self.n_y):
            self.over_y(ex, b, d).start()
        self.over_core(ex, b).wait_send()

    def step_exp(self, ex, b):
        rows = self.range(b)
        total = self.pairs[ex, rows, self.y].astype(F32)
        for d in range(1, self.n_y):
            self.over_y(ex, b, d).wait_recv()
            total = total + self.from_y[d - 1, ex, rows].astype(F32)
        self.pairs[ex, rows, self.y] = total.astype(BF)
        for i in range(self.half):
            k = b * self.half + i
            if k == 0:
                self.stay(ex).start()
            else:
                self.over_exp(ex, k).start()

    def finish(self, ex):
        self.stay(ex).wait()
        for b in range(2):
            for d in range(1, self.n_y):
                self.over_y(ex, b, d).wait_send()
        for k in range(1, self.n_exp):
            self.over_exp(ex, k).wait_send()
            self.over_exp(ex, k).wait_recv()


def expert_kernel(
    n_exp, n_y, rows, grads, w_in, bias_in, w_back,
    back, f_out, wi_out, wb_out, gb_in, gb_back,
    land, part, pairs, from_y, wi_v, wb_v, g_v, h_v, gp_v, f_v, wi_st, wb_st,
    w_sem, g_sem, f_sem, o_sem, own_sem, *rest,
):
    e, h, y, c = place()
    n_spread = len(SpreadExpert.sems(1, 1, 1))
    spread = SpreadExpert(n_exp, n_y, rows, land, rest[:n_spread])
    gather = GatherExpert(n_exp, n_y, part, pairs, from_y, back, rest[n_spread:])
    n_hid = 2 * n_y
    lc, cap, width = rows.shape[1:]
    ff = w_in.shape[2]
    n_src = 4
    block = n_src * n_hid * cap
    n_rb = n_exp // n_src
    step_f = min(512, ff)
    step_w = STEP_W

    def weights(ex):
        slot = lax.rem(ex, 2)
        return (
            pltpu.make_async_copy(w_in.at[ex], wi_v.at[slot], w_sem.at[0, slot]),
            pltpu.make_async_copy(w_back.at[ex], wb_v.at[slot], w_sem.at[1, slot]),
        )

    def g_copy(ex):
        slot = lax.rem(ex, 2)
        return pltpu.make_async_copy(grads.at[ex], g_v.at[slot], g_sem.at[slot])

    def f_copy(ex, rb):
        return pltpu.make_async_copy(f_v, f_out.at[ex, sources(rb)], f_sem)

    def wi_copy(ex, i):
        return pltpu.make_async_copy(wi_st, wi_out.at[ex, pl.ds(i * step_w, step_w)], o_sem.at[0])

    def wb_copy(ex, i):
        return pltpu.make_async_copy(wb_st, wb_out.at[ex, pl.ds(i * step_w, step_w)], o_sem.at[1])

    def sources(rb):
        return pl.ds(lax.rem(lax.div(e, n_exp // 2) * (n_rb // 2) + rb, n_rb) * n_src, n_src)

    own = pltpu.make_async_copy(rows.at[e], land.at[:, e, h], own_sem)
    own.start()
    greet(n_exp, n_y)

    spread.start(0)
    for ex in range(2):
        for cp in weights(ex):
            cp.start()
    g_copy(0).start()
    gb_in[...] = jnp.zeros_like(gb_in)
    gb_back[...] = jnp.zeros_like(gb_back)
    own.wait()
    spread.pass_on(0, 0)
    spread.start(1)
    spread.pass_on(0, 1)
    spread.pass_y(0, 0)

    def weight_grads(ex, after):
        slot = lax.rem(ex, 2)

        @pl.loop(0, width // step_w)
        def _(i):
            cols = pl.ds(pl.multiple_of(i * step_w, step_w), step_w)
            x = land[ex, :, :, :, cols].reshape(n_exp * n_hid * cap, step_w)
            piece = mm_tn(x, gp_v[slot].reshape(n_exp * n_hid * cap, ff)).astype(BF)

            @pl.when(i > 0)
            def _():
                wi_copy(ex, i).wait()

            wi_st[...] = piece
            wi_copy(ex, i).start()
            after(i)

        @pl.loop(0, ff // step_w)
        def _(i):
            cols = pl.ds(pl.multiple_of(i * step_w, step_w), step_w)
            hid = h_v[slot, :, :, cols].reshape(n_exp * n_hid * cap, step_w)
            piece = mm_tn(hid, g_v[slot].reshape(n_exp * n_hid * cap, width)).astype(BF)

            @pl.when(i > 0)
            def _():
                wb_copy(ex, i).wait()

            wb_st[...] = piece
            wb_copy(ex, i).start()

        wi_copy(ex, 0).wait()
        wb_copy(ex, 0).wait()

    @pl.loop(0, lc)
    def _(ex):
        slot = lax.rem(ex, 2)
        g_copy(ex).wait()
        for cp in weights(ex):
            cp.wait()

        @pl.loop(0, n_rb)
        def _(rb):
            at = sources(rb)
            for b in range(2):

                @pl.when(rb == b * (n_rb // 2))
                def _():
                    spread.landed(ex, b)

            x = land[ex, at].reshape(block, width)
            g = g_v[slot, at].reshape(block, width)
            gb_back[pl.ds(ex, 1)] += jnp.sum(g.astype(F32), axis=0, keepdims=True)
            for f in range(ff // step_f):
                cols = slice(f * step_f, (f + 1) * step_f)
                pre = mm(x, wi_v[slot, :, cols]) + bias_in[pl.ds(ex, 1), cols]
                sig = jax.nn.sigmoid(pre)
                hid = (pre * sig).astype(BF)
                gh = mm_nt(g, wb_v[slot, cols, :])
                gp = (gh * sig * (1.0 + pre * (1.0 - sig))).astype(BF)
                gb_in[pl.ds(ex, 1), cols] += jnp.sum(gp.astype(F32), axis=0, keepdims=True)
                h_v[slot, at, :, cols] = hid.reshape(n_src, n_hid * cap, step_f)
                gp_v[slot, at, :, cols] = gp.reshape(n_src, n_hid * cap, step_f)
            gd = mm_nt(gp_v[slot, at].reshape(block, ff), wi_v[slot])
            part[at] = gd.astype(BF).reshape(n_src, n_y, 2, cap, width)

            for b in range(2):

                @pl.when(rb == (b + 1) * (n_rb // 2) - 1)
                def _():
                    gather.over_core(ex, b).start()

                    if b == 0:

                        @pl.when(ex == 0)
                        def _():
                            spread.pass_y(0, 1)

                        @pl.when(ex + 2 < lc)
                        def _():
                            spread.start(ex + 2)

                    @pl.when(ex + 1 < lc)
                    def _():
                        spread.pass_on(ex + 1, b)

                    @pl.when(ex > 0)
                    def _():
                        gather.step_exp(ex - 1, b)

        @pl.loop(0, n_rb)
        def _(rb):
            hv = h_v[slot, sources(rb)].reshape(block, ff)
            f = mm(hv, wb_v[slot]).astype(BF).reshape(n_src, n_y, 2, cap, width)

            @pl.when((ex > 0) | (rb > 0))
            def _():
                f_copy(ex, rb).wait()

            f_v[...] = f
            f_copy(ex, rb).start()

            for b in range(2):

                @pl.when(rb == (b + 1) * (n_rb // 2) - 1)
                def _():
                    gather.fold(ex, b)

                    @pl.when(ex + 1 < lc)
                    def _():
                        spread.pass_y(ex + 1, b)

        @pl.when(ex + 2 < lc)
        def _():
            for cp in weights(ex + 2):
                cp.start()

        @pl.when(ex > 0)
        def _():
            weight_grads(ex - 1, lambda i: None)

        @pl.when(ex + 1 < lc)
        def _():
            g_copy(ex + 1).start()

    def last(i):
        @pl.when(i == 0)
        def _():
            gather.step_exp(lc - 1, 0)

    weight_grads(lc - 1, last)
    gather.step_exp(lc - 1, 1)
    f_copy(lc - 1, 0).wait()

    @pl.loop(0, lc)
    def _(ex):
        spread.sent(ex)
        gather.finish(ex)


def experts(n_exp, n_hid, rows, grads, w_in, bias_in, w_back):
    n_y = n_hid // 2
    _, lc, cap, width = rows.shape
    ff = w_in.shape[2]
    shape = jax.ShapeDtypeStruct
    per = n_hid * cap
    return pl.pallas_call(
        functools.partial(expert_kernel, n_exp, n_y),
        name="experts",
        out_shape=(
            shape((n_exp, lc, cap, width), BF),
            shape((lc, n_exp, n_y, 2, cap, width), BF),
            shape(w_in.shape, BF),
            shape(w_back.shape, BF),
            shape((lc, ff), F32),
            shape((lc, width), F32),
        ),
        in_specs=[HB, HB, HB, VM, HB],
        out_specs=[HB, HB, HB, HB, VM, VM],
        scratch_shapes=[
            pltpu.VMEM((lc, n_exp, n_hid, cap, width), BF),
            pltpu.VMEM((n_exp, n_y, 2, cap, width), BF),
            pltpu.VMEM((lc, n_exp, n_y, cap, width), BF),
            pltpu.VMEM((n_y - 1, lc, n_exp, cap, width), BF),
            pltpu.VMEM((2, *w_in.shape[1:]), BF),
            pltpu.VMEM((2, *w_back.shape[1:]), BF),
            pltpu.VMEM((2, n_exp, n_hid, cap, width), BF),
            pltpu.VMEM((2, n_exp, per, ff), BF),
            pltpu.VMEM((2, n_exp, per, ff), BF),
            pltpu.VMEM((4, n_y, 2, cap, width), BF),
            pltpu.VMEM((STEP_W, ff), BF),
            pltpu.VMEM((STEP_W, width), BF),
            DMA((2, 2)), DMA((2,)), DMA, DMA((2,)), DMA,
            *SpreadExpert.sems(lc, n_exp, n_y),
            *GatherExpert.sems(lc, n_exp, n_y),
        ],
        compiler_params=pltpu.CompilerParams(
            collective_id=1, has_side_effects=True, vmem_limit_bytes=63 * MIB
        ),
    )(rows, grads, w_in, bias_in, w_back)


def finish_kernel(wi, wb, mats, g_in, g_back, g_qkv, g_out):
    g_in[...] = wi[...].astype(F32)
    g_back[...] = wb[...].astype(F32)
    rows, width = g_out.shape
    for part in range(3):
        g_qkv[:, part * width : (part + 1) * width] = mats[part].reshape(rows, width).astype(F32)
    g_out[...] = mats[3].reshape(rows, width).astype(F32)


def finish(wi, wb, mats):
    lc, width, ff = wi.shape
    cut = 2
    rows = width // (lc * cut)
    mats = mats.reshape(4, width // 16, 16, width)
    shape = jax.ShapeDtypeStruct
    wi_spec = pl.BlockSpec((1, width // cut, ff), lambda i, j: (i, j, 0))
    wb_spec = pl.BlockSpec((1, ff // cut, width), lambda i, j: (i, j, 0))
    return pl.pallas_call(
        finish_kernel,
        name="finish",
        grid=(lc, cut),
        out_shape=(
            shape(wi.shape, F32), shape(wb.shape, F32),
            shape((width, 3 * width), F32), shape((width, width), F32),
        ),
        in_specs=[
            wi_spec, wb_spec,
            pl.BlockSpec((4, rows // 16, 16, width), lambda i, j: (0, i * cut + j, 0, 0)),
        ],
        out_specs=[
            wi_spec, wb_spec,
            pl.BlockSpec((rows, 3 * width), lambda i, j: (i * cut + j, 0)),
            pl.BlockSpec((rows, width), lambda i, j: (i * cut + j, 0)),
        ],
        compiler_params=pltpu.CompilerParams(vmem_limit_bytes=56 * MIB),
    )(wi, wb, mats)


class Reduce:
    def __init__(self, n_exp, n_y, mats, out, norms, scratch):
        (self.core_in, in1, in2, in3, self.n_acc, self.n_in, self.c_s, self.c_r,
         s1, r1, s2, r2, s3, r3, t3, u3, t2, u2, t1, u1, self.d_s, self.d_r, self.n_s, self.n_r, self.l_s) = scratch
        self.mats, self.out, self.norms = mats, out, norms
        self.e, self.h, self.y, self.c = place()
        self.n_x, self.n_z, self.sub, self.half, self.n_sub = self.sizes(n_exp, n_y, mats.shape[0])
        x, z = lax.rem(self.e, self.n_x), lax.div(self.e, self.n_x)
        self.x, self.z = x, z
        self.piece = self.half // 2
        self.at = {"x": (self.n_x, x), "y": (n_y, self.y), "z": (self.n_z, z)}
        self.orders = (("y", "x", "z"), ("x", "y", "z"))
        self.n_axes = (None, "y", "x", "z")
        self.sibling = (self.e, self.y * 2 + 1 - self.c)
        self.lands = (in1, in2, in3)
        self.sends, self.recvs = (s1, s2, s3), (r1, r2, r3)
        self.ups, self.upr = (t1, t2, t3), (u1, u2, u3)

    @staticmethod
    def sizes(n_exp, n_y, n_units):
        n_x = n_y
        n_z = n_exp // n_x
        sub = n_x * n_y * n_z
        half = n_units // 2
        return n_x, n_z, sub, half, half // 2 // sub

    @classmethod
    def scratch(cls, n_exp, n_y, n_units, norms_shape):
        n_x, n_z, sub, half, n_sub = cls.sizes(n_exp, n_y, n_units)
        most = max(n_x, n_y)
        width = norms_shape[1]

        def land(n, count):
            return pltpu.VMEM((2, n_sub, n - 1, count, 16, width), BF)

        def sems(n):
            return [DMA((2, n_sub, n - 1))] * 2

        return [
            pltpu.VMEM((half, 16, width), BF),
            land(most, sub // min(n_x, n_y)),
            land(most, sub // (n_x * n_y)),
            land(n_z, 1),
            pltpu.VMEM((4, *norms_shape), F32),
            pltpu.VMEM((4, max(most, n_z) - 1, *norms_shape), F32),
            DMA((2, n_sub)), DMA((2, n_sub)),
            *sems(most), *sems(most), *sems(n_z), *sems(n_z), *sems(most), *sems(most),
            DMA((2, n_sub)), DMA((2, n_sub)),
            *[DMA((4, max(most, n_z) - 1))] * 2,
            DMA((2, n_sub)),
        ]

    def device(self, axis, o):
        return {
            "x": (self.z * self.n_x + o, self.h), "y": (self.e, o * 2 + self.c), "z": (o * self.n_x + self.x, self.h)
        }[axis]

    def own(self, first, count):
        return pl.ds(self.c * self.half + first, count)

    def units(self, p, b, depth):
        first, count = p * self.piece + b * self.sub, self.sub
        for axis in self.orders[p][:depth]:
            n, i = self.at[axis]
            count = count // n
            first = first + i * count
        return first, count

    def core_copy(self, p, b):
        first = p * self.piece + b * self.sub
        return rcopy(
            self.mats.at[pl.ds((1 - self.c) * self.half + first, self.sub)], self.core_in.at[pl.ds(first, self.sub)],
            self.c_s.at[p, b], self.c_r.at[p, b], self.sibling,
        )

    def down(self, p, b, stage, d):
        n, i = self.at[self.orders[p][stage]]
        first, count = self.units(p, b, stage)
        count = count // n
        o = lax.rem(i + d, n)
        return rcopy(
            self.mats.at[self.own(first + o * count, count)], self.lands[stage].at[p, b, d - 1, pl.ds(0, count)],
            self.sends[stage].at[p, b, d - 1], self.recvs[stage].at[p, b, d - 1],
            self.device(self.orders[p][stage], o),
        )

    def up(self, p, b, stage, d):
        n, i = self.at[self.orders[p][stage]]
        at = self.own(*self.units(p, b, stage + 1))
        source = self.mats if stage == 2 else self.out
        o = lax.rem(i + d, n)
        return rcopy(
            source.at[at], self.out.at[at], self.ups[stage].at[p, b, d - 1], self.upr[stage].at[p, b, d - 1],
            self.device(self.orders[p][stage], o),
        )

    def stay(self, p, b):
        at = self.own(*self.units(p, b, 3))
        return pltpu.make_async_copy(self.mats.at[at], self.out.at[at], self.l_s.at[p, b])

    def core_up(self, p, b):
        region = self.out.at[self.own(p * self.piece + b * self.sub, self.sub)]
        return rcopy(region, region, self.d_s.at[p, b], self.d_r.at[p, b], self.sibling)

    def peers(self, p, stage):
        return range(1, self.at[self.orders[p][stage]][0])

    def event(self, p, b, q):
        mats = self.mats
        if q == 0:
            self.core_copy(p, b).wait_recv()
            first = p * self.piece + b * self.sub
            at = self.own(first, self.sub)
            mats[at] = (mats[at].astype(F32) + self.core_in[pl.ds(first, self.sub)].astype(F32)).astype(BF)
        elif q <= 3:
            first, count = self.units(p, b, q)
            at = self.own(first, count)
            total = mats[at].astype(F32)
            for d in self.peers(p, q - 1):
                self.down(p, b, q - 1, d).wait_recv()
                total = total + self.lands[q - 1][p, b, d - 1, :count].astype(F32)
            mats[at] = total.astype(BF)
            if q == 3:
                self.stay(p, b).start()
        else:
            if q == 4:
                self.stay(p, b).wait()
            for d in self.peers(p, 6 - q):
                self.up(p, b, 6 - q, d).wait_recv()
        if q < 3:
            for d in self.peers(p, q):
                self.down(p, b, q, d).start()
        elif q < 6:
            for d in self.peers(p, 5 - q):
                self.up(p, b, 5 - q, d).start()
        else:
            self.core_up(p, b).start()

    def begin(self, part):
        @pl.when(self.c == 1 - part // 2)
        def _():
            @pl.loop(0, self.n_sub)
            def _(b):
                self.core_copy(part % 2, b).start()

    def n_copy(self, stage, d):
        if stage == 0:
            dev = self.sibling
        else:
            n, i = self.at[self.n_axes[stage]]
            dev = self.device(self.n_axes[stage], lax.rem(i + d, n))
        return rcopy(
            self.n_acc.at[stage], self.n_in.at[stage, d - 1], self.n_s.at[stage, d - 1], self.n_r.at[stage, d - 1], dev
        )

    def n_peers(self, stage):
        return range(1, 2 if stage == 0 else self.at[self.n_axes[stage]][0])

    def n_total(self, stage):
        for d in self.n_peers(stage):
            self.n_copy(stage, d).wait_recv()
        own = self.n_acc[stage]
        if stage == 0:
            return own + self.n_in[0, 0]
        n, i = self.at[self.n_axes[stage]]
        total = jnp.zeros_like(own)
        for m in range(n):
            term = own
            for d in range(1, n):
                term = jnp.where(lax.rem(i + n - d, n) == m, self.n_in[stage, d - 1], term)
            total = total + term
        return total

    def run(self, aside):
        self.n_acc[0] = self.norms[...]
        self.n_copy(0, 1).start()

        @pl.loop(0, self.n_sub + 6)
        def _(s):
            for q in range(7):

                @pl.when((s >= q) & (s - q < self.n_sub))
                def _():
                    for p in range(2):
                        self.event(p, s - q, q)

            for stage in range(1, 4):

                @pl.when(s == stage)
                def _():
                    self.n_acc[stage] = self.n_total(stage - 1)
                    for d in self.n_peers(stage):
                        self.n_copy(stage, d).start()

            aside(s)

        self.norms[...] = self.n_total(3)
        for stage in range(4):
            for d in self.n_peers(stage):
                self.n_copy(stage, d).wait_send()

        @pl.loop(0, self.n_sub)
        def _(b):
            for p in range(2):
                self.core_up(p, b).wait_recv()
                self.core_copy(p, b).wait_send()
                self.core_up(p, b).wait_send()
                for stage in range(3):
                    for d in self.peers(p, stage):
                        self.down(p, b, stage, d).wait_send()
                        self.up(p, b, stage, d).wait_send()


def attend_back_kernel(
    n_exp, n_y, lens, slot_col, tokens_h, middle_h, cot_h, mixed_h, context_h, lse, back_h,
    gain1, shift1, w_qkv_h, w_out_h, gain2, bias_back, f_part,
    output, g_tokens, mats_out, g_norms,
    tokens, middle, cot, mixed, context, back, w_qkv, w_out, g_mats,
    bias, gattn, gctx, n1t, lse_t, mine_v, f_back, mine_sem, in_sem, *rest,
):
    tok, width = tokens.shape
    hd = width // HEADS
    e, h, y, c = place()
    n_gather, n_sems = len(Gather.scratch(1, 2, 1, 1, 1)), len(Gather.sems(1, 1))
    lc, cap = f_back.shape[1:3]
    gather = Gather(
        n_exp, n_y, lambda k: f_part.at[:, e ^ k, :, 1 - c], lambda m, yy: mine_v[lax.rem(m, 4), :, yy],
        *rest[:n_gather], f_back, rest[n_gather : n_gather + n_sems],
    )
    total = Reduce(n_exp, n_y, g_mats, mats_out, g_norms, rest[n_gather + n_sems :])

    def order(m):
        return jnp.where(m < n_exp // 2, m + n_exp // 2, n_exp - 1 - m)

    def fetch(m):
        slot = lax.rem(m, 4)
        return pltpu.make_async_copy(
            f_part.at[:, e ^ order(m), :, c], mine_v.at[slot], mine_sem.at[slot]
        )

    loads = [
        pltpu.make_async_copy(a, b, in_sem.at[i])
        for i, (a, b) in enumerate((
            (back_h, back), (middle_h, middle), (cot_h, cot), (w_out_h, w_out), (tokens_h, tokens),
            (context_h, context), (mixed_h, mixed), (w_qkv_h, w_qkv),
        ))
    ]
    greet(n_exp, n_y)

    @pl.loop(0, n_exp)
    def _(m):
        gather.step_core(order(m))

    for m in range(4):
        fetch(m).start()
    for cp in loads:
        cp.start()

    def leave(m):
        fetch(m).wait()
        gather.fold(m, order(m))
        gather.send_y(order(m))

        @pl.when(m + 4 < n_exp)
        def _():
            fetch(m + 4).start()

    leave(0)
    leave(1)
    for cp in loads[:5]:
        cp.wait()

    g_norms[...] = jnp.zeros_like(g_norms)
    n_slots = n_exp * lc * cap
    n_quarter = width // 16

    def fold(values):
        return jnp.sum(values, axis=0, keepdims=True)

    @pl.loop(0, tok // 256)
    def _(i):
        rows = pl.ds(pl.multiple_of(i * 256, 256), 256)
        table = tok_block(slot_col[rows], 0, n_slots)
        up = mm(table, back[...].reshape(n_slots, width))
        _, unit, inverse = norm_rows(middle[rows], gain2[...], 0.0)
        g_norms[2:3] += fold(up * unit)
        g_norms[3:4] += fold(up)
        g_mid = cot[rows].astype(F32) + norm_back(up, unit, inverse, gain2[...])
        g_tokens[rows] = g_mid
        gattn[rows] = g_mid.astype(BF)
        gctx[rows] = mm_nt(gattn[rows], w_out[...]).astype(BF)
        out, _, _ = norm_rows(tokens[rows].astype(F32), gain1[...], shift1[...])
        n1t[:, rows] = out.astype(BF).T

    leave(2)
    leave(3)
    for cp in loads[5:]:
        cp.wait()

    @pl.loop(0, width // 256)
    def _(i):
        cols = pl.ds(pl.multiple_of(i * 256, 256), 256)
        part = mm_tn(context[:, cols], gattn[...]).astype(BF)
        g_mats[pl.ds(3 * n_quarter + i * 16, 16)] = part.reshape(16, 16, width)

    total.begin(3)
    key_i = lax.broadcasted_iota(jnp.int32, (tok, tok), 0)
    qry_i = lax.broadcasted_iota(jnp.int32, (tok, tok), 1)
    dk_, dq_ = jnp.zeros((tok, tok), jnp.int32), jnp.zeros((tok, tok), jnp.int32)
    end = 0
    for j in range(lens.shape[1]):
        end = end + lens[0, j]
        dk_ = dk_ + jnp.where(key_i >= end, 1, 0)
        dq_ = dq_ + jnp.where(qry_i >= end, 1, 0)
    bias[...] = jnp.where((dk_ == dq_) & (qry_i >= key_i), 0.0, masked_score)
    lse_t[...] = lse[...].T

    lane = lax.broadcasted_iota(jnp.int32, (1, 128), 1)
    n_pairs = width // 128
    half = tok // 2
    heads_in = 128 // hd

    @pl.loop(0, n_pairs)
    def _(p):
        @pl.when(p + 4 < n_exp)
        def _():
            leave(p + 4)

        @pl.when((p >= 2) & (lax.rem(p, 2) == 0))
        def _():
            gather.step_exp(order(lax.div(p, 2) - 1), bias_back[...].reshape(lc, 1, width))

        def cols(part):
            return pl.ds(pl.multiple_of(part * width + p * 128, 128), 128)

        q, key, val, do = mixed[:, cols(0)], mixed[:, cols(1)], mixed[:, cols(2)], gctx[:, cols(0)]
        dq = [jnp.zeros((half, 128), F32) for _ in range(2)]
        dkey = [jnp.zeros((half, 128), F32) for _ in range(2)]
        dval = [jnp.zeros((half, 128), F32) for _ in range(2)]
        for hh in range(heads_in):
            own_lanes = (lane >= hh * hd) & (lane < (hh + 1) * hd)
            qh = jnp.where(own_lanes, q * BF(hd**-0.5), BF(0))
            kh = jnp.where(own_lanes, key * BF(hd**-0.5), BF(0))
            doh = jnp.where(own_lanes, do, BF(0))
            lrow = lse_t[pl.ds(p * heads_in + hh, 1), :]
            for qb in range(2):
                rows = slice(qb * half, (qb + 1) * half)
                n = (qb + 1) * half
                s = mm_nt(key[:n], qh[rows]) + (bias[:n, rows] - lrow[:, rows])
                pt = jnp.exp(s)
                dp = mm_nt(val[:n], doh[rows])
                inner = jnp.sum(dp * pt, axis=0, keepdims=True)
                ds = (pt * (dp - inner)).astype(BF)
                ptb = pt.astype(BF)
                dv_, dk2 = mm(ptb, doh[rows]), mm(ds, qh[rows])
                for kb in range(qb + 1):
                    part = slice(kb * half, (kb + 1) * half)
                    dval[kb] = dval[kb] + dv_[part]
                    dkey[kb] = dkey[kb] + dk2[part]
                dq[qb] = dq[qb] + mm_tn(ds, kh[:n])
        for b in range(2):
            rows = slice(b * half, (b + 1) * half)
            mixed[rows, cols(0)] = dq[b].astype(BF)
            mixed[rows, cols(1)] = dkey[b].astype(BF)
            mixed[rows, cols(2)] = dval[b].astype(BF)

    def step_exp(m):
        gather.step_exp(order(m), bias_back[...].reshape(lc, 1, width))

    step_exp(3)
    for part in range(3):

        @pl.loop(0, width // 256)
        def _(i):
            rows = pl.ds(pl.multiple_of(i * 256, 256), 256)
            piece = mm(n1t[rows], mixed[:, part * width : (part + 1) * width])
            g_mats[pl.ds(part * n_quarter + i * 16, 16)] = piece.astype(BF).reshape(16, 16, width)

        total.begin(part)

    @pl.loop(n_pairs + 4, max(n_exp, n_pairs + 4))
    def _(m):
        leave(m)

    step_exp(4)

    @pl.loop(0, tok // 256)
    def _(i):
        rows = pl.ds(pl.multiple_of(i * 256, 256), 256)
        up = mm_nt(mixed[rows], w_qkv[...])
        _, unit, inverse = norm_rows(tokens[rows].astype(F32), gain1[...], 0.0)
        g_norms[0:1] += fold(up * unit)
        g_norms[1:2] += fold(up)
        g_tokens[rows] += norm_back(up, unit, inverse, gain1[...])

    def aside(s):
        @pl.when(s == 0)
        def _():
            @pl.loop(5, n_exp - 2)
            def _(m):
                step_exp(m)

        for j in (1, 2):

            @pl.when(s == j)
            def _():
                step_exp(n_exp - 3 + j)

        @pl.when(s == 5)
        def _():
            @pl.loop(1, n_exp)
            def _(k):
                gather.over_exp(k).wait_recv()

            @pl.loop(0, tok // 256)
            def _(i):
                rows = pl.ds(pl.multiple_of(i * 256, 256), 256)
                table = tok_block(slot_col[rows], 0, n_slots)
                whole = middle[rows] + mm(table, f_back[...].reshape(n_slots, width))
                output[rows] = whole.astype(BF)

    total.run(aside)

    @pl.loop(0, n_exp)
    def _(k):
        gather.over_core(k).wait_send()
        gather.sent(k)


def attend_back(
    n_exp, n_hid, lens, slot_col, tokens, middle, cot, mixed, context, lse, back,
    gain1, shift1, w_qkv, w_out, gain2, bias_back, f_part,
):
    n_y = n_hid // 2
    tok, width = tokens.shape
    _, lc, cap, _ = back.shape
    n_units = 4 * width // 16
    shape = jax.ShapeDtypeStruct
    return pl.pallas_call(
        functools.partial(attend_back_kernel, n_exp, n_y),
        name="attend_back",
        out_shape=(
            shape((tok, width), BF),
            shape((tok, width), F32),
            shape((n_units, 16, width), BF),
            shape((8, width), F32),
        ),
        in_specs=[SM, VM, HB, HB, HB, HB, HB, VM, HB, VM, VM, HB, HB, VM, VM, HB],
        out_specs=[VM, VM, HB, VM],
        scratch_shapes=[
            *[pltpu.VMEM(a.shape, a.dtype) for a in (tokens, middle, cot, mixed, context, back, w_qkv, w_out)],
            pltpu.VMEM((n_units, 16, width), BF),
            pltpu.VMEM((tok, tok), F32),
            pltpu.VMEM((tok, width), BF),
            pltpu.VMEM((tok, width), BF),
            pltpu.VMEM((width, tok), BF),
            pltpu.VMEM((128, tok), F32),
            pltpu.VMEM((4, lc, n_y, cap, width), BF),
            pltpu.VMEM((n_exp, lc, cap, width), BF),
            DMA((4,)),
            DMA((8,)),
            *Gather.scratch(n_exp, n_y, lc, cap, width),
            *Gather.sems(n_exp, n_y),
            *Reduce.scratch(n_exp, n_y, n_units, (8, width)),
        ],
        compiler_params=pltpu.CompilerParams(
            collective_id=2, has_side_effects=True, vmem_limit_bytes=63 * MIB
        ),
    )(
        lens, slot_col, tokens, middle, cot, mixed, context, lse, back,
        gain1, shift1, w_qkv, w_out, gain2, bias_back, f_part,
    )


def token_slots(token_ids, hash_table, capacity, cap):
    chosen = jnp.take(hash_table, token_ids, mode="clip")
    places = jnp.arange(chosen.shape[0], dtype=jnp.int32)
    earlier = (chosen[:, None] == chosen[None, :]) & (places[:, None] > places[None, :])
    rank = jnp.sum(earlier.astype(jnp.int32), axis=1)
    experts_ids = jnp.arange(capacity.shape[0], dtype=jnp.int32)
    limit = jnp.sum(jnp.where(chosen[:, None] == experts_ids[None, :], capacity[None, :], 0), axis=1)
    return jnp.where(rank < limit, chosen * cap + rank, -1)


def per_device(
    tokens, token_ids, lengths, hash_table, capacity, gain_one, shift_one, w_qkv, w_out,
    gain_two, shift_two, w_in, bias_in, w_back, bias_back, cotangent,
):
    n_exp, n_hid = lax.axis_size("exp"), lax.axis_size("hid")
    tok, width = tokens.shape
    lc, _, ff = w_in.shape
    cap = 2 * tok // capacity.shape[0]
    slot = token_slots(token_ids, hash_table, capacity, cap)
    gain1, shift1, gain2, shift2 = (v[None] for v in (gain_one, shift_one, gain_two, shift_two))
    mixed, context, middle, lse, send, grads = attend(
        n_exp, n_hid, lc, cap, lengths, slot[None], tokens, gain1, shift1, w_qkv, w_out, gain2, shift2, cotangent
    )
    back, f_part, wi, wb, gb_in, gb_back = experts(
        n_exp, n_hid, send, grads, w_in, bias_in, w_back
    )
    output, g_tokens, mats, norms = attend_back(
        n_exp, n_hid, lengths, slot[:, None], tokens, middle, cotangent, mixed, context, lse, back,
        gain1, shift1, w_qkv, w_out, gain2, bias_back, f_part,
    )
    g_in, g_back, g_qkv, g_out = finish(wi, wb, mats)
    return (
        output, g_tokens, norms[0], norms[1], g_qkv, g_out, norms[2], norms[3],
        g_in, gb_in, g_back, gb_back,
    )


def solution(mesh):
    both = P(("exp", "hid"))
    rows = P(("exp", "hid"), None)
    placed = (
        rows, both, rows, P(), P(), P(), P(), P(), P(), P(), P(),
        P("exp", None, "hid"), P("exp", "hid"), P("exp", "hid", None), P("exp", None), rows,
    )
    return jax.shard_map(
        per_device,
        mesh=mesh,
        in_specs=placed,
        out_specs=(
            rows, rows, P(), P(), P(), P(), P(), P(),
            P("exp", None, "hid"), P("exp", "hid"), P("exp", "hid", None), P("exp", None),
        ),
        check_vma=False,
    )
```

```python
import functools

import jax
import jax.numpy as jnp
from jax import lax
from jax.experimental import pallas as pl
from jax.experimental.pallas import tpu as pltpu
from jax.sharding import PartitionSpec as P

HEADS = 16
MESH = pl.DeviceIdType.MESH
BF = jnp.bfloat16
F32 = jnp.float32
epsilon = 1e-05
masked_score = -1e30
DMA = pltpu.SemaphoreType.DMA
VM = pl.BlockSpec(memory_space=pltpu.VMEM)
SM = pl.BlockSpec(memory_space=pltpu.SMEM)
HB = pl.BlockSpec(memory_space=pl.ANY)
MIB = 1 << 20


def mm(a, b):
    return lax.dot_general(a, b, (((1,), (0,)), ((), ())), preferred_element_type=F32)


def mm_nt(a, b):
    return lax.dot_general(a, b, (((1,), (1,)), ((), ())), preferred_element_type=F32)


def mm_tn(a, b):
    return lax.dot_general(a, b, (((0,), (0,)), ((), ())), preferred_element_type=F32)


def place():
    e = lax.axis_index("exp")
    h = lax.axis_index("hid")
    return e, h, lax.div(h, 2), lax.rem(h, 2)


def rcopy(src, dst, send, recv, dev):
    return pltpu.make_async_remote_copy(
        src_ref=src, dst_ref=dst, send_sem=send, recv_sem=recv, device_id=dev, device_id_type=MESH
    )


def greet(n_exp, n_y):
    e, h, y, c = place()
    sem = pltpu.get_barrier_semaphore()
    for k in range(1, n_exp):
        pl.semaphore_signal(sem, inc=1, device_id=(e ^ k, h), device_id_type=MESH)
    for d in range(1, n_y):
        pl.semaphore_signal(
            sem, inc=1, device_id=(e, lax.rem(y + d, n_y) * 2 + c), device_id_type=MESH
        )
    pl.semaphore_signal(sem, inc=1, device_id=(e, y * 2 + 1 - c), device_id_type=MESH)
    pl.semaphore_wait(sem, n_exp - 1 + n_y)


class Spread:
    def __init__(self, n_exp, n_y, rows, land, sems):
        self.n_exp, self.n_y, self.rows, self.land = n_exp, n_y, rows, land
        self.es, self.er, self.ys, self.yr, self.cs, self.cr = sems
        self.e, self.h, self.y, self.c = place()

    @staticmethod
    def sems(n_exp, n_y):
        return [DMA((n_exp,)), DMA((n_exp,))] + [DMA((n_exp, n_y))] * 4

    def over_exp(self, k):
        return rcopy(
            self.rows.at[self.e ^ k], self.land.at[:, self.e, self.h],
            self.es.at[k], self.er.at[k], (self.e ^ k, self.h),
        )

    def turn(self, i):
        low, high = lax.div(i + 1, 2), self.n_exp // 2 + lax.div(i, 2) - 1
        return jnp.where(i == self.n_exp - 1, self.n_exp - 1, jnp.where(lax.rem(i, 2) == 1, low, high))

    def block(self, k, hid):
        return self.land.at[:, self.e ^ k, hid]

    def over_y(self, k, d):
        blk = self.block(k, self.h)
        dev = (self.e, lax.rem(self.y + d, self.n_y) * 2 + self.c)
        return rcopy(blk, blk, self.ys.at[k, d], self.yr.at[k, d], dev)

    def over_core(self, k, d):
        blk = self.block(k, lax.rem(self.y + self.n_y - d, self.n_y) * 2 + self.c)
        dev = (self.e, self.y * 2 + 1 - self.c)
        return rcopy(blk, blk, self.cs.at[k, d], self.cr.at[k, d], dev)

    def pass_on(self, k):
        @pl.when(k > 0)
        def _():
            self.over_exp(k).wait_recv()

        for d in range(1, self.n_y):
            self.over_y(k, d).start()
        self.over_core(k, 0).start()

    def pass_y(self, k):
        for d in range(1, self.n_y):
            self.over_y(k, d).wait_recv()
            self.over_core(k, d).start()

    def landed(self, k):
        for d in range(self.n_y):
            self.over_core(k, d).wait_recv()

    def sent(self, k):
        @pl.when(k > 0)
        def _():
            self.over_exp(k).wait_send()

        for d in range(1, self.n_y):
            self.over_y(k, d).wait_send()
        for d in range(self.n_y):
            self.over_core(k, d).wait_send()


class Gather:
    def __init__(self, n_exp, n_y, other, mine, pairs, from_y, back, sems):
        self.n_exp, self.n_y, self.other, self.mine = n_exp, n_y, other, mine
        self.pairs, self.from_y, self.back = pairs, from_y, back
        self.es, self.er, self.ys, self.yr, self.cs, self.cr = sems
        self.e, self.h, self.y, self.c = place()

    @staticmethod
    def sems(n_exp, n_y):
        return [DMA((n_exp,)), DMA((n_exp,)), DMA((n_exp, n_y)), DMA((n_exp, n_y)), DMA((n_exp,)), DMA((n_exp,))]

    @staticmethod
    def scratch(n_exp, n_y, lc, cap, d):
        return [
            pltpu.VMEM((n_exp, lc, n_y, cap, d), BF),
            pltpu.VMEM((n_exp, n_y - 1, lc, cap, d), BF),
        ]

    def over_core(self, k):
        t = self.e ^ k
        dev = (self.e, self.y * 2 + 1 - self.c)
        return rcopy(self.other(k), self.pairs.at[t], self.cs.at[k], self.cr.at[k], dev)

    def over_y(self, k, d):
        t = self.e ^ k
        dev = (self.e, lax.rem(self.y + d, self.n_y) * 2 + self.c)
        yy = lax.rem(self.y + d, self.n_y)
        return rcopy(self.pairs.at[t, :, yy], self.from_y.at[t, d - 1], self.ys.at[k, d], self.yr.at[k, d], dev)

    def over_exp(self, k):
        t = self.e ^ k
        return rcopy(self.pairs.at[t, :, self.y], self.back.at[self.e], self.es.at[k], self.er.at[k], (t, self.h))

    def step_core(self, k):
        self.over_core(k).start()

    def fold(self, at, k):
        t = self.e ^ k
        self.over_core(k).wait_recv()
        for yy in range(self.n_y):
            pair = self.pairs[t, :, yy].astype(F32) + self.mine(at, yy).astype(F32)
            self.pairs[t, :, yy] = pair.astype(BF)

    def send_y(self, k):
        for d in range(1, self.n_y):
            self.over_y(k, d).start()

    def step_exp(self, k, extra=None):
        t = self.e ^ k
        total = self.pairs[t, :, self.y].astype(F32)
        for d in range(1, self.n_y):
            self.over_y(k, d).wait_recv()
            total = total + self.from_y[t, d - 1].astype(F32)
        if extra is not None:
            total = total + extra
        total = total.astype(BF)

        @pl.when(k == 0)
        def _():
            self.back[t] = total

        @pl.when(k > 0)
        def _():
            self.pairs[t, :, self.y] = total
            self.over_exp(k).start()

    def sent(self, k):
        for d in range(1, self.n_y):
            self.over_y(k, d).wait_send()

        @pl.when(k > 0)
        def _():
            self.over_exp(k).wait_send()


def norm_rows(rows, gain, shift):
    mean = jnp.mean(rows, axis=-1, keepdims=True)
    centred = rows - mean
    var = jnp.mean(centred * centred, axis=-1, keepdims=True)
    inverse = lax.rsqrt(var + epsilon)
    unit = centred * inverse
    return unit * gain + shift, unit, inverse


def norm_back(upstream, unit, inverse, gain):
    scaled = upstream * gain
    inner = (
        scaled
        - jnp.mean(scaled, axis=-1, keepdims=True)
        - unit * jnp.mean(scaled * unit, axis=-1, keepdims=True)
    )
    return inner * inverse


def turned(values):
    if values.shape[1] == 1:
        return jnp.broadcast_to(values, (values.shape[0], 128)).T
    return jnp.broadcast_to(values, (128, values.shape[1])).T


def token_slots(token_ids, hash_table, capacity, cap):
    tok = token_ids.shape[1]
    ids = turned(token_ids.astype(F32)).astype(jnp.int32)
    row, col = lax.shift_right_logical(ids, 7), ids & 127
    n_rows = hash_table.shape[0]
    lanes = lax.broadcasted_iota(jnp.int32, (tok, 128), 1)
    is_row = jnp.where(lanes[:, :n_rows] == row[:, :n_rows], 1.0, 0.0).astype(BF)
    found = mm(is_row, hash_table.astype(F32).astype(BF))
    chosen = jnp.sum(jnp.where(lanes == col, found, 0.0), axis=1, keepdims=True)
    n_experts = capacity.shape[1]
    ids_e = lax.broadcasted_iota(jnp.int32, (tok, n_experts), 1)
    onehot = jnp.where(ids_e == chosen.astype(jnp.int32), 1.0, 0.0)
    here = lax.broadcasted_iota(jnp.int32, (tok, tok), 0)
    there = lax.broadcasted_iota(jnp.int32, (tok, tok), 1)
    before = mm(jnp.where(here > there, 1.0, 0.0).astype(BF), onehot.astype(BF))
    rank = jnp.sum(before * onehot, axis=1, keepdims=True)
    limit = jnp.sum(capacity.astype(F32) * onehot, axis=1, keepdims=True)
    return jnp.where(rank < limit, chosen * cap + rank, -1.0)


def slot_block(slot_row, first, count):
    tok = slot_row.shape[1]
    ids = lax.broadcasted_iota(jnp.int32, (count, tok), 0) + first
    return jnp.where(slot_row == ids, 1.0, 0.0).astype(BF)


def tok_block(slot_col, first, count):
    ids = lax.broadcasted_iota(jnp.int32, (slot_col.shape[0], count), 1) + first
    return jnp.where(slot_col == ids, 1.0, 0.0).astype(BF)


def doc_bias(lens, tok):
    q = lax.broadcasted_iota(jnp.int32, (tok, tok), 0)
    k = lax.broadcasted_iota(jnp.int32, (tok, tok), 1)
    dq = jnp.zeros((tok, tok), jnp.int32)
    dk = jnp.zeros((tok, tok), jnp.int32)
    end = 0
    for j in range(lens.shape[1]):
        end = end + lens[0, j]
        dq = dq + jnp.where(q >= end, 1, 0)
        dk = dk + jnp.where(k >= end, 1, 0)
    return jnp.where((dq == dk) & (q >= k), 0.0, masked_score)


def attend_kernel(
    n_exp, n_y, lens, token_ids, hash_table, capacity, tokens, gain1, shift1, w_qkv, w_out, gain2, shift2, cot,
    mixed_h, context_h, middle_h, lse, slot_col, send_h, land, first_rows,
    slot_row, mixed, context, middle, send, cot_rows, normed, bias, wq_v, wo_v, in_sem, out_sem, own_sem, first_s, first_r, *sems,
):
    tok, width = tokens.shape
    e, h, y, c = place()
    lc, cap = send.shape[1], send.shape[2]
    per = lc * cap
    hd = width // HEADS
    spread = Spread(n_exp, n_y, cot_rows, land, sems)
    loads = [
        pltpu.make_async_copy(w_qkv, wq_v, in_sem.at[0]),
        pltpu.make_async_copy(w_out, wo_v, in_sem.at[1]),
    ]
    stores = [
        pltpu.make_async_copy(a, b, out_sem.at[i])
        for i, (a, b) in enumerate(
            ((mixed, mixed_h), (context, context_h), (middle, middle_h), (send, send_h))
        )
    ]
    for cp in loads:
        cp.start()

    slots = token_slots(token_ids[...], hash_table[...], capacity[...], cap)
    slot_col[...] = slots.astype(jnp.int32)
    slot_row[...] = turned(slots)[:1].astype(jnp.int32)

    def pick(source, dst):
        rows = mm(slot_block(slot_row[...], dst * per, per), source)
        return rows.astype(BF).reshape(lc, cap, width)

    def advance(k):
        spread.pass_on(k)

        @pl.when(k > 0)
        def _():
            spread.pass_y(k - 1)

    def first(k):
        return rcopy(
            send.at[e ^ k, 0], first_rows.at[e], first_s.at[k], first_r.at[k], (e ^ k, h)
        )

    cot_rows[e] = pick(cot[...], e)
    own = pltpu.make_async_copy(cot_rows.at[e], land.at[:, e, h], own_sem)
    own.start()
    greet(n_exp, n_y)

    @pl.loop(1, n_exp)
    def _(i):
        k = spread.turn(i)
        cot_rows[e ^ k] = pick(cot[...], e ^ k)
        spread.over_exp(k).start()

    own.wait()
    spread.pass_on(0)

    @pl.loop(0, tok // 128)
    def _(i):
        rows = pl.ds(i * 128, 128)
        out, _, _ = norm_rows(tokens[rows].astype(F32), gain1[...], shift1[...])
        normed[rows] = out.astype(BF)

    bias[...] = doc_bias(lens, tok)
    loads[0].wait()

    @pl.loop(0, 3)
    def _(i):
        @pl.when(i > 0)
        def _():
            advance(i)

        for j in range(width // 512):
            cols = pl.ds(pl.multiple_of(i * width + j * 512, 512), 512)
            mixed[:, cols] = mm(normed[...], wq_v[:, cols]).astype(BF)

    stores[0].start()
    advance(3)
    lse[...] = jnp.zeros_like(lse)
    lane = lax.broadcasted_iota(jnp.int32, (1, 128), 1)
    n_pairs = width // 128
    half = tok // 2
    heads_in = 128 // hd

    @pl.loop(0, n_pairs)
    def _(p):
        @pl.when((lax.rem(p, 2) == 1) & (p < 6))
        def _():
            advance(4 + lax.div(p, 2))

        def cols(part):
            return pl.ds(pl.multiple_of(part * width + p * 128, 128), 128)

        q, key, val = mixed[:, cols(0)], mixed[:, cols(1)], mixed[:, cols(2)]
        for blk in range(2):
            rows = slice(blk * half, (blk + 1) * half)
            n_keys = (blk + 1) * half
            total = jnp.zeros((half, 128), F32)
            lses = lse[rows, :]
            for hh in range(heads_in):
                own_lanes = (lane >= hh * hd) & (lane < (hh + 1) * hd)
                qh = jnp.where(own_lanes, q[rows] * BF(hd**-0.5), BF(0))
                vh = jnp.where(own_lanes, val[:n_keys], BF(0))
                s = mm_nt(qh, key[:n_keys]) + bias[rows, :n_keys]
                top = jnp.max(s, axis=-1, keepdims=True)
                ex = jnp.exp(s - top)
                tot = jnp.sum(ex, axis=-1, keepdims=True)
                probs = (ex * (1.0 / tot)).astype(BF)
                total = total + mm(probs, vh)
                lses = jnp.where(lane == p * heads_in + hh, top + jnp.log(tot), lses)
            lse[rows, :] = lses
            context[rows, pl.ds(pl.multiple_of(p * 128, 128), 128)] = total.astype(BF)

    stores[1].start()
    loads[1].wait()

    @pl.loop(0, tok // 256)
    def _(i):
        rows = pl.ds(pl.multiple_of(i * 256, 256), 256)
        mid = tokens[rows].astype(F32) + mm(context[rows], wo_v[...])
        middle[rows] = mid
        out, _, _ = norm_rows(mid, gain2[...], shift2[...])
        normed[rows] = out.astype(BF)

    stores[2].start()

    @pl.loop(0, n_exp)
    def _(k):
        send[k] = pick(normed[...], k)

    stores[3].start()
    own_first = pltpu.make_async_copy(send.at[e, 0], first_rows.at[e], own_sem)
    own_first.start()

    @pl.loop(1, n_exp)
    def _(k):
        first(k).start()

    @pl.loop(7, n_exp)
    def _(k):
        advance(k)

    spread.pass_y(n_exp - 1)
    for cp in stores:
        cp.wait()
    own_first.wait()

    @pl.loop(1, n_exp)
    def _(k):
        first(k).wait_send()
        first(k).wait_recv()

    @pl.loop(0, n_exp)
    def _(k):
        spread.landed(k)
        spread.sent(k)


def attend(n_exp, n_hid, lc, cap, lens, token_ids, hash_table, capacity, tokens, gain1, shift1, w_qkv, w_out, gain2, shift2, cot):
    n_y = n_hid // 2
    tok, width = tokens.shape
    shape = jax.ShapeDtypeStruct
    return pl.pallas_call(
        functools.partial(attend_kernel, n_exp, n_y),
        name="attend",
        out_shape=(
            shape((tok, 3 * width), BF),
            shape((tok, width), BF),
            shape((tok, width), F32),
            shape((tok, 128), F32),
            shape((tok, 1), jnp.int32),
            shape((n_exp, lc, cap, width), BF),
            shape((lc, n_exp, n_hid, cap, width), BF),
            shape((n_exp, cap, width), BF),
        ),
        in_specs=[SM, VM, VM, VM, VM, VM, VM, HB, HB, VM, VM, VM],
        out_specs=[HB, HB, HB, VM, VM, HB, HB, HB],
        scratch_shapes=[
            pltpu.VMEM((1, tok), jnp.int32),
            pltpu.VMEM((tok, 3 * width), BF),
            pltpu.VMEM((tok, width), BF),
            pltpu.VMEM((tok, width), F32),
            pltpu.VMEM((n_exp, lc, cap, width), BF),
            pltpu.VMEM((n_exp, lc, cap, width), BF),
            pltpu.VMEM((tok, width), BF),
            pltpu.VMEM((tok, tok), F32),
            pltpu.VMEM(w_qkv.shape, BF),
            pltpu.VMEM(w_out.shape, BF),
            DMA((2,)),
            DMA((4,)),
            DMA,
            DMA((n_exp,)),
            DMA((n_exp,)),
            *Spread.sems(n_exp, n_y),
        ],
        compiler_params=pltpu.CompilerParams(
            collective_id=0, has_side_effects=True, vmem_limit_bytes=56 * MIB
        ),
    )(lens, token_ids, hash_table, capacity, tokens, gain1, shift1, w_qkv, w_out, gain2, shift2, cot)


STEP_W = 512


class Halves:
    def __init__(self, n_exp, n_y):
        self.n_exp, self.n_y, self.half = n_exp, n_y, n_exp // 2
        self.e, self.h, self.y, self.c = place()
        self.sibling = (self.e, self.y * 2 + 1 - self.c)

    def range(self, g):
        first = lax.div(self.e, self.half) * self.half
        return pl.ds(pl.multiple_of(first if g == 0 else self.half - first, self.half), self.half)

    def y_peer(self, d):
        return (self.e, lax.rem(self.y + d, self.n_y) * 2 + self.c)


class SpreadExpert(Halves):
    def __init__(self, n_exp, n_y, rows, land, sems):
        super().__init__(n_exp, n_y)
        self.rows, self.land = rows, land
        self.es, self.er, self.ys, self.yr, self.cs, self.cr = sems

    @staticmethod
    def sems(lc, n_exp, n_y):
        return [DMA((lc, n_exp))] * 2 + [DMA((lc, 2, n_y))] * 4

    def over_exp(self, ex, k):
        return rcopy(
            self.rows.at[self.e ^ k, ex], self.land.at[ex, self.e, self.h],
            self.es.at[ex, k], self.er.at[ex, k], (self.e ^ k, self.h),
        )

    def start(self, ex):
        half = self.half
        for i in range(1, self.n_exp):
            self.over_exp(ex, half + i // 2 - 1 if i % 2 == 0 else ((i + 1) // 2 if i < self.n_exp - 1 else i)).start()

    def over_y(self, ex, g, d):
        blk = self.land.at[ex, self.range(g), self.h]
        return rcopy(blk, blk, self.ys.at[ex, g, d], self.yr.at[ex, g, d], self.y_peer(d))

    def over_core(self, ex, g, d):
        hid = lax.rem(self.y + self.n_y - d, self.n_y) * 2 + self.c
        blk = self.land.at[ex, self.range(g), hid]
        return rcopy(blk, blk, self.cs.at[ex, g, d], self.cr.at[ex, g, d], self.sibling)

    def pass_on(self, ex, g, came=False):
        if not came:
            for k in range(max(1, g * self.half), (g + 1) * self.half):
                self.over_exp(ex, k).wait_recv()
        for d in range(1, self.n_y):
            self.over_y(ex, g, d).start()
        self.over_core(ex, g, 0).start()

    def pass_y(self, ex, g):
        for d in range(1, self.n_y):
            self.over_y(ex, g, d).wait_recv()
            self.over_core(ex, g, d).start()

    def landed(self, ex, g):
        for d in range(self.n_y):
            self.over_core(ex, g, d).wait_recv()

    def sent(self, ex):
        @pl.when(ex > 0)
        def _():
            for k in range(1, self.n_exp):
                self.over_exp(ex, k).wait_send()

        for g in range(2):
            for d in range(1, self.n_y):
                self.over_y(ex, g, d).wait_send()
            for d in range(self.n_y):
                self.over_core(ex, g, d).wait_send()


class GatherExpert(Halves):
    def __init__(self, n_exp, n_y, part, pairs, from_y, back, sems):
        super().__init__(n_exp, n_y)
        self.part, self.pairs, self.from_y, self.back = part, pairs, from_y, back
        self.es, self.er, self.ys, self.yr, self.cs, self.cr = sems

    @staticmethod
    def sems(lc, n_exp, n_y):
        return [DMA((lc, n_exp))] * 2 + [DMA((lc, 2, n_y))] * 2 + [DMA((lc, 2))] * 2

    def over_core(self, ex, b):
        return rcopy(
            self.part.at[self.range(b), :, 1 - self.c], self.pairs.at[ex, self.range(b)],
            self.cs.at[ex, b], self.cr.at[ex, b], self.sibling,
        )

    def over_y(self, ex, b, d):
        yy = lax.rem(self.y + d, self.n_y)
        return rcopy(
            self.pairs.at[ex, self.range(b), yy], self.from_y.at[d - 1, ex, self.range(b)],
            self.ys.at[ex, b, d], self.yr.at[ex, b, d], self.y_peer(d),
        )

    def over_exp(self, ex, k):
        t = self.e ^ k
        return rcopy(
            self.pairs.at[ex, t, self.y], self.back.at[self.e, ex], self.es.at[ex, k], self.er.at[ex, k], (t, self.h)
        )

    def stay(self, ex):
        return pltpu.make_async_copy(self.pairs.at[ex, self.e, self.y], self.back.at[self.e, ex], self.es.at[ex, 0])

    def fold(self, ex, b):
        self.over_core(ex, b).wait_recv()
        rows = self.range(b)
        for yy in range(self.n_y):
            pair = self.pairs[ex, rows, yy].astype(F32) + self.part[rows, yy, self.c].astype(F32)
            self.pairs[ex, rows, yy] = pair.astype(BF)
        for d in range(1, self.n_y):
            self.over_y(ex, b, d).start()
        self.over_core(ex, b).wait_send()

    def step_exp(self, ex, b):
        rows = self.range(b)
        total = self.pairs[ex, rows, self.y].astype(F32)
        for d in range(1, self.n_y):
            self.over_y(ex, b, d).wait_recv()
            total = total + self.from_y[d - 1, ex, rows].astype(F32)
        self.pairs[ex, rows, self.y] = total.astype(BF)
        for i in range(self.half):
            k = b * self.half + i
            if k == 0:
                self.stay(ex).start()
            else:
                self.over_exp(ex, k).start()

    def finish(self, ex):
        self.stay(ex).wait()
        for b in range(2):
            for d in range(1, self.n_y):
                self.over_y(ex, b, d).wait_send()
        for k in range(1, self.n_exp):
            self.over_exp(ex, k).wait_send()
            self.over_exp(ex, k).wait_recv()


def expert_kernel(
    n_exp, n_y, first_rows, rows, grads, w_in, bias_in, w_back,
    back, f_out, wi_out, wb_out, gb_in, gb_back,
    land, part, pairs, from_y, wi_v, wb_v, g_v, h_v, gp_v, f_v, wi_st, wb_st,
    w_sem, g_sem, f_sem, o_sem, own_sem, *rest,
):
    e, h, y, c = place()
    n_spread = len(SpreadExpert.sems(1, 1, 1))
    spread = SpreadExpert(n_exp, n_y, rows, land, rest[:n_spread])
    gather = GatherExpert(n_exp, n_y, part, pairs, from_y, back, rest[n_spread:])
    n_hid = 2 * n_y
    lc, cap, width = rows.shape[1:]
    ff = w_in.shape[2]
    n_src = 4
    block = n_src * n_hid * cap
    n_rb = n_exp // n_src
    step_f = min(512, ff)
    step_w = STEP_W

    def weights(ex):
        slot = lax.rem(ex, 2)
        return (
            pltpu.make_async_copy(w_in.at[ex], wi_v.at[slot], w_sem.at[0, slot]),
            pltpu.make_async_copy(w_back.at[ex], wb_v.at[slot], w_sem.at[1, slot]),
        )

    def g_copy(ex):
        slot = lax.rem(ex, 2)
        return pltpu.make_async_copy(grads.at[ex], g_v.at[slot], g_sem.at[slot])

    def f_copy(ex, rb):
        return pltpu.make_async_copy(f_v, f_out.at[ex, sources(rb)], f_sem)

    def wi_copy(ex, i):
        return pltpu.make_async_copy(wi_st, wi_out.at[ex, pl.ds(i * step_w, step_w)], o_sem.at[0])

    def wb_copy(ex, i):
        return pltpu.make_async_copy(wb_st, wb_out.at[ex, pl.ds(i * step_w, step_w)], o_sem.at[1])

    def sources(rb):
        return pl.ds(lax.rem(lax.div(e, n_exp // 2) * (n_rb // 2) + rb, n_rb) * n_src, n_src)

    own = pltpu.make_async_copy(rows.at[e, pl.ds(1, lc - 1)], land.at[pl.ds(1, lc - 1), e, h], own_sem.at[0])
    own_first = pltpu.make_async_copy(first_rows, land.at[0, :, h], own_sem.at[1])
    own_first.start()
    own.start()
    greet(n_exp, n_y)
    own_first.wait()
    spread.pass_on(0, 0, came=True)
    spread.pass_on(0, 1, came=True)
    spread.start(1)
    for ex in range(2):
        for cp in weights(ex):
            cp.start()
    g_copy(0).start()
    gb_in[...] = jnp.zeros_like(gb_in)
    gb_back[...] = jnp.zeros_like(gb_back)
    own.wait()
    spread.pass_y(0, 0)
    spread.start(2)

    def weight_grads(ex, after):
        slot = lax.rem(ex, 2)

        @pl.loop(0, width // step_w)
        def _(i):
            cols = pl.ds(pl.multiple_of(i * step_w, step_w), step_w)
            x = land[ex, :, :, :, cols].reshape(n_exp * n_hid * cap, step_w)
            piece = mm_tn(x, gp_v[slot].reshape(n_exp * n_hid * cap, ff)).astype(BF)

            @pl.when(i > 0)
            def _():
                wi_copy(ex, i).wait()

            wi_st[...] = piece
            wi_copy(ex, i).start()
            after(i)

        @pl.loop(0, ff // step_w)
        def _(i):
            cols = pl.ds(pl.multiple_of(i * step_w, step_w), step_w)
            hid = h_v[slot, :, :, cols].reshape(n_exp * n_hid * cap, step_w)
            piece = mm_tn(hid, g_v[slot].reshape(n_exp * n_hid * cap, width)).astype(BF)

            @pl.when(i > 0)
            def _():
                wb_copy(ex, i).wait()

            wb_st[...] = piece
            wb_copy(ex, i).start()

        wi_copy(ex, 0).wait()
        wb_copy(ex, 0).wait()

    @pl.loop(0, lc)
    def _(ex):
        slot = lax.rem(ex, 2)
        g_copy(ex).wait()
        for cp in weights(ex):
            cp.wait()

        @pl.loop(0, n_rb)
        def _(rb):
            at = sources(rb)
            for b in range(2):

                @pl.when(rb == b * (n_rb // 2))
                def _():
                    spread.landed(ex, b)

            x = land[ex, at].reshape(block, width)
            g = g_v[slot, at].reshape(block, width)
            gb_back[pl.ds(ex, 1)] += jnp.sum(g.astype(F32), axis=0, keepdims=True)
            for f in range(ff // step_f):
                cols = slice(f * step_f, (f + 1) * step_f)
                pre = mm(x, wi_v[slot, :, cols]) + bias_in[pl.ds(ex, 1), cols]
                sig = jax.nn.sigmoid(pre)
                hid = (pre * sig).astype(BF)
                gh = mm_nt(g, wb_v[slot, cols, :])
                gp = (gh * sig * (1.0 + pre * (1.0 - sig))).astype(BF)
                gb_in[pl.ds(ex, 1), cols] += jnp.sum(gp.astype(F32), axis=0, keepdims=True)
                h_v[slot, at, :, cols] = hid.reshape(n_src, n_hid * cap, step_f)
                gp_v[slot, at, :, cols] = gp.reshape(n_src, n_hid * cap, step_f)
            gd = mm_nt(gp_v[slot, at].reshape(block, ff), wi_v[slot])
            part[at] = gd.astype(BF).reshape(n_src, n_y, 2, cap, width)

            for b in range(2):

                @pl.when(rb == (b + 1) * (n_rb // 2) - 1)
                def _():
                    gather.over_core(ex, b).start()

                    if b == 0:

                        @pl.when(ex == 0)
                        def _():
                            spread.pass_y(0, 1)

                        @pl.when(ex + 3 < lc)
                        def _():
                            spread.start(ex + 3)

                    @pl.when(ex + 1 < lc)
                    def _():
                        spread.pass_on(ex + 1, b)

                    @pl.when(ex > 0)
                    def _():
                        gather.step_exp(ex - 1, b)

        @pl.loop(0, n_rb)
        def _(rb):
            hv = h_v[slot, sources(rb)].reshape(block, ff)
            f = mm(hv, wb_v[slot]).astype(BF).reshape(n_src, n_y, 2, cap, width)

            @pl.when((ex > 0) | (rb > 0))
            def _():
                f_copy(ex, rb).wait()

            f_v[...] = f
            f_copy(ex, rb).start()

            for b in range(2):

                @pl.when(rb == (b + 1) * (n_rb // 2) - 1)
                def _():
                    gather.fold(ex, b)

                    @pl.when(ex + 1 < lc)
                    def _():
                        spread.pass_y(ex + 1, b)

        @pl.when(ex + 2 < lc)
        def _():
            for cp in weights(ex + 2):
                cp.start()

        @pl.when(ex > 0)
        def _():
            weight_grads(ex - 1, lambda i: None)

        @pl.when(ex + 1 < lc)
        def _():
            g_copy(ex + 1).start()

    def last(i):
        @pl.when(i == 0)
        def _():
            gather.step_exp(lc - 1, 0)

    weight_grads(lc - 1, last)
    gather.step_exp(lc - 1, 1)
    f_copy(lc - 1, 0).wait()

    @pl.loop(0, lc)
    def _(ex):
        spread.sent(ex)
        gather.finish(ex)


def experts(n_exp, n_hid, first_rows, rows, grads, w_in, bias_in, w_back):
    n_y = n_hid // 2
    _, lc, cap, width = rows.shape
    ff = w_in.shape[2]
    shape = jax.ShapeDtypeStruct
    per = n_hid * cap
    return pl.pallas_call(
        functools.partial(expert_kernel, n_exp, n_y),
        name="experts",
        out_shape=(
            shape((n_exp, lc, cap, width), BF),
            shape((lc, n_exp, n_y, 2, cap, width), BF),
            shape(w_in.shape, BF),
            shape(w_back.shape, BF),
            shape((lc, ff), F32),
            shape((lc, width), F32),
        ),
        in_specs=[HB, HB, HB, HB, VM, HB],
        out_specs=[HB, HB, HB, HB, VM, VM],
        scratch_shapes=[
            pltpu.VMEM((lc, n_exp, n_hid, cap, width), BF),
            pltpu.VMEM((n_exp, n_y, 2, cap, width), BF),
            pltpu.VMEM((lc, n_exp, n_y, cap, width), BF),
            pltpu.VMEM((n_y - 1, lc, n_exp, cap, width), BF),
            pltpu.VMEM((2, *w_in.shape[1:]), BF),
            pltpu.VMEM((2, *w_back.shape[1:]), BF),
            pltpu.VMEM((2, n_exp, n_hid, cap, width), BF),
            pltpu.VMEM((2, n_exp, per, ff), BF),
            pltpu.VMEM((2, n_exp, per, ff), BF),
            pltpu.VMEM((4, n_y, 2, cap, width), BF),
            pltpu.VMEM((STEP_W, ff), BF),
            pltpu.VMEM((STEP_W, width), BF),
            DMA((2, 2)), DMA((2,)), DMA, DMA((2,)), DMA((2,)),
            *SpreadExpert.sems(lc, n_exp, n_y),
            *GatherExpert.sems(lc, n_exp, n_y),
        ],
        compiler_params=pltpu.CompilerParams(
            collective_id=1, has_side_effects=True, vmem_limit_bytes=63 * MIB
        ),
    )(first_rows, rows, grads, w_in, bias_in, w_back)


def finish_kernel(wi, wb, mats, norms, bi, bb, g_in, g_back, g_qkv, g_out, n0, n1, n2, n3, g_bi, g_bb):
    @pl.when((pl.program_id(0) == 0) & (pl.program_id(1) == 0))
    def _():
        for i, n in enumerate((n0, n1, n2, n3)):
            n[...] = norms[i]
        g_bi[...] = bi[...]
        g_bb[...] = bb[...]

    g_in[...] = wi[...].astype(F32)
    g_back[...] = wb[...].astype(F32)
    rows, width = g_out.shape
    for part in range(3):
        g_qkv[:, part * width : (part + 1) * width] = mats[part].reshape(rows, width).astype(F32)
    g_out[...] = mats[3].reshape(rows, width).astype(F32)


def finish(wi, wb, mats, norms, bi, bb):
    lc, width, ff = wi.shape
    cut = 4
    rows = width // (lc * cut)
    mats = mats.reshape(4, width // 16, 16, width)
    shape = jax.ShapeDtypeStruct
    wi_spec = pl.BlockSpec((1, width // cut, ff), lambda i, j: (i, j, 0))
    wb_spec = pl.BlockSpec((1, ff // cut, width), lambda i, j: (i, j, 0))
    small = [pl.BlockSpec(a.shape, lambda i, j: (0, 0)) for a in (norms, bi, bb)]
    return pl.pallas_call(
        finish_kernel,
        name="finish",
        grid=(lc, cut),
        out_shape=(
            shape(wi.shape, F32), shape(wb.shape, F32),
            shape((width, 3 * width), F32), shape((width, width), F32),
            *[shape((width,), F32)] * 4, shape(bi.shape, F32), shape(bb.shape, F32),
        ),
        in_specs=[
            wi_spec, wb_spec,
            pl.BlockSpec((4, rows // 16, 16, width), lambda i, j: (0, i * cut + j, 0, 0)),
            *small,
        ],
        out_specs=[
            wi_spec, wb_spec,
            pl.BlockSpec((rows, 3 * width), lambda i, j: (i * cut + j, 0)),
            pl.BlockSpec((rows, width), lambda i, j: (i * cut + j, 0)),
            *[pl.BlockSpec((width,), lambda i, j: (0,))] * 4,
            *small[1:],
        ],
        compiler_params=pltpu.CompilerParams(vmem_limit_bytes=56 * MIB),
    )(wi, wb, mats, norms, bi, bb)


class Reduce:
    def __init__(self, n_exp, n_y, mats, out, norms, scratch):
        (self.core_in, in1, in2, in3, self.n_acc, self.n_in, self.c_s, self.c_r,
         s1, r1, s2, r2, s3, r3, t3, u3, t2, u2, t1, u1, self.d_s, self.d_r, self.n_s, self.n_r, self.l_s) = scratch
        self.mats, self.out, self.norms = mats, out, norms
        self.e, self.h, self.y, self.c = place()
        self.n_x, self.n_z, self.sub, self.half, self.n_sub = self.sizes(n_exp, n_y, mats.shape[0])
        x, z = lax.rem(self.e, self.n_x), lax.div(self.e, self.n_x)
        self.x, self.z = x, z
        self.piece = self.half // 2
        self.at = {"x": (self.n_x, x), "y": (n_y, self.y), "z": (self.n_z, z)}
        self.orders = (("y", "x", "z"), ("x", "y", "z"))
        self.n_axes = (None, "y", "x", "z")
        self.sibling = (self.e, self.y * 2 + 1 - self.c)
        self.lands = (in1, in2, in3)
        self.sends, self.recvs = (s1, s2, s3), (r1, r2, r3)
        self.ups, self.upr = (t1, t2, t3), (u1, u2, u3)

    @staticmethod
    def sizes(n_exp, n_y, n_units):
        n_x = n_y
        n_z = n_exp // n_x
        sub = n_x * n_y * n_z
        half = n_units // 2
        return n_x, n_z, sub, half, half // 2 // sub

    @classmethod
    def scratch(cls, n_exp, n_y, n_units, norms_shape):
        n_x, n_z, sub, half, n_sub = cls.sizes(n_exp, n_y, n_units)
        most = max(n_x, n_y)
        width = norms_shape[1]

        def land(n, count):
            return pltpu.VMEM((2, n_sub, n - 1, count, 16, width), BF)

        def sems(n):
            return [DMA((2, n_sub, n - 1))] * 2

        return [
            pltpu.VMEM((half, 16, width), BF),
            land(most, sub // min(n_x, n_y)),
            land(most, sub // (n_x * n_y)),
            land(n_z, 1),
            pltpu.VMEM((4, *norms_shape), F32),
            pltpu.VMEM((4, max(most, n_z) - 1, *norms_shape), F32),
            DMA((2, n_sub)), DMA((2, n_sub)),
            *sems(most), *sems(most), *sems(n_z), *sems(n_z), *sems(most), *sems(most),
            DMA((2, n_sub)), DMA((2, n_sub)),
            *[DMA((4, max(most, n_z) - 1))] * 2,
            DMA((2, n_sub)),
        ]

    def device(self, axis, o):
        return {
            "x": (self.z * self.n_x + o, self.h), "y": (self.e, o * 2 + self.c), "z": (o * self.n_x + self.x, self.h)
        }[axis]

    def own(self, first, count):
        return pl.ds(self.c * self.half + first, count)

    def units(self, p, b, depth):
        first, count = p * self.piece + b * self.sub, self.sub
        for axis in self.orders[p][:depth]:
            n, i = self.at[axis]
            count = count // n
            first = first + i * count
        return first, count

    def core_copy(self, p, b):
        first = p * self.piece + b * self.sub
        return rcopy(
            self.mats.at[pl.ds((1 - self.c) * self.half + first, self.sub)], self.core_in.at[pl.ds(first, self.sub)],
            self.c_s.at[p, b], self.c_r.at[p, b], self.sibling,
        )

    def down(self, p, b, stage, d):
        n, i = self.at[self.orders[p][stage]]
        first, count = self.units(p, b, stage)
        count = count // n
        o = lax.rem(i + d, n)
        return rcopy(
            self.mats.at[self.own(first + o * count, count)], self.lands[stage].at[p, b, d - 1, pl.ds(0, count)],
            self.sends[stage].at[p, b, d - 1], self.recvs[stage].at[p, b, d - 1],
            self.device(self.orders[p][stage], o),
        )

    def up(self, p, b, stage, d):
        n, i = self.at[self.orders[p][stage]]
        at = self.own(*self.units(p, b, stage + 1))
        source = self.mats if stage == 2 else self.out
        o = lax.rem(i + d, n)
        return rcopy(
            source.at[at], self.out.at[at], self.ups[stage].at[p, b, d - 1], self.upr[stage].at[p, b, d - 1],
            self.device(self.orders[p][stage], o),
        )

    def stay(self, p, b):
        at = self.own(*self.units(p, b, 3))
        return pltpu.make_async_copy(self.mats.at[at], self.out.at[at], self.l_s.at[p, b])

    def core_up(self, p, b):
        region = self.out.at[self.own(p * self.piece + b * self.sub, self.sub)]
        return rcopy(region, region, self.d_s.at[p, b], self.d_r.at[p, b], self.sibling)

    def peers(self, p, stage):
        return range(1, self.at[self.orders[p][stage]][0])

    def event(self, p, b, q):
        mats = self.mats
        if q == 0:
            self.core_copy(p, b).wait_recv()
            first = p * self.piece + b * self.sub
            at = self.own(first, self.sub)
            mats[at] = (mats[at].astype(F32) + self.core_in[pl.ds(first, self.sub)].astype(F32)).astype(BF)
        elif q <= 3:
            first, count = self.units(p, b, q)
            at = self.own(first, count)
            total = mats[at].astype(F32)
            for d in self.peers(p, q - 1):
                self.down(p, b, q - 1, d).wait_recv()
                total = total + self.lands[q - 1][p, b, d - 1, :count].astype(F32)
            mats[at] = total.astype(BF)
            if q == 3:
                self.stay(p, b).start()
        else:
            if q == 4:
                self.stay(p, b).wait()
            for d in self.peers(p, 6 - q):
                self.up(p, b, 6 - q, d).wait_recv()
        if q < 3:
            for d in self.peers(p, q):
                self.down(p, b, q, d).start()
        elif q < 6:
            for d in self.peers(p, 5 - q):
                self.up(p, b, 5 - q, d).start()
        else:
            self.core_up(p, b).start()

    def begin(self, part):
        @pl.when(self.c == 1 - part // 2)
        def _():
            @pl.loop(0, self.n_sub)
            def _(b):
                self.core_copy(part % 2, b).start()

    def n_copy(self, stage, d):
        if stage == 0:
            dev = self.sibling
        else:
            n, i = self.at[self.n_axes[stage]]
            dev = self.device(self.n_axes[stage], lax.rem(i + d, n))
        return rcopy(
            self.n_acc.at[stage], self.n_in.at[stage, d - 1], self.n_s.at[stage, d - 1], self.n_r.at[stage, d - 1], dev
        )

    def n_peers(self, stage):
        return range(1, 2 if stage == 0 else self.at[self.n_axes[stage]][0])

    def n_total(self, stage):
        for d in self.n_peers(stage):
            self.n_copy(stage, d).wait_recv()
        own = self.n_acc[stage]
        if stage == 0:
            return own + self.n_in[0, 0]
        n, i = self.at[self.n_axes[stage]]
        total = jnp.zeros_like(own)
        for m in range(n):
            term = own
            for d in range(1, n):
                term = jnp.where(lax.rem(i + n - d, n) == m, self.n_in[stage, d - 1], term)
            total = total + term
        return total

    def run(self, aside):
        self.n_acc[0] = self.norms[...]
        self.n_copy(0, 1).start()

        @pl.loop(0, self.n_sub + 6)
        def _(s):
            for q in range(7):

                @pl.when((s >= q) & (s - q < self.n_sub))
                def _():
                    for p in range(2):
                        self.event(p, s - q, q)

            for stage in range(1, 4):

                @pl.when(s == stage)
                def _():
                    self.n_acc[stage] = self.n_total(stage - 1)
                    for d in self.n_peers(stage):
                        self.n_copy(stage, d).start()

            aside(s)

        self.norms[...] = self.n_total(3)
        for stage in range(4):
            for d in self.n_peers(stage):
                self.n_copy(stage, d).wait_send()

        @pl.loop(0, self.n_sub)
        def _(b):
            for p in range(2):
                self.core_up(p, b).wait_recv()
                self.core_copy(p, b).wait_send()
                self.core_up(p, b).wait_send()
                for stage in range(3):
                    for d in self.peers(p, stage):
                        self.down(p, b, stage, d).wait_send()
                        self.up(p, b, stage, d).wait_send()


def attend_back_kernel(
    n_exp, n_y, lens, slot_col, tokens_h, middle_h, cot_h, mixed_h, context_h, lse, back_h,
    gain1, shift1, w_qkv_h, w_out_h, gain2, bias_back, f_part,
    output, g_tokens, mats_out, g_norms,
    tokens, middle, cot, mixed, context, back, w_qkv, w_out, g_mats,
    bias, gattn, gctx, n1t, lse_t, mine_v, f_back, mine_sem, in_sem, *rest,
):
    tok, width = tokens.shape
    hd = width // HEADS
    e, h, y, c = place()
    n_gather, n_sems = len(Gather.scratch(1, 2, 1, 1, 1)), len(Gather.sems(1, 1))
    lc, cap = f_back.shape[1:3]
    gather = Gather(
        n_exp, n_y, lambda k: f_part.at[:, e ^ k, :, 1 - c], lambda m, yy: mine_v[lax.rem(m, 4), :, yy],
        *rest[:n_gather], f_back, rest[n_gather : n_gather + n_sems],
    )
    total = Reduce(n_exp, n_y, g_mats, mats_out, g_norms, rest[n_gather + n_sems :])

    def order(m):
        return jnp.where(m < n_exp // 2, m + n_exp // 2, n_exp - 1 - m)

    def fetch(m):
        slot = lax.rem(m, 4)
        return pltpu.make_async_copy(
            f_part.at[:, e ^ order(m), :, c], mine_v.at[slot], mine_sem.at[slot]
        )

    loads = [
        pltpu.make_async_copy(a, b, in_sem.at[i])
        for i, (a, b) in enumerate((
            (back_h, back), (middle_h, middle), (cot_h, cot), (w_out_h, w_out), (tokens_h, tokens),
            (context_h, context), (mixed_h, mixed), (w_qkv_h, w_qkv),
        ))
    ]
    greet(n_exp, n_y)

    @pl.loop(0, n_exp)
    def _(m):
        gather.step_core(order(m))

    for m in range(4):
        fetch(m).start()
    for cp in loads:
        cp.start()

    def leave(m):
        fetch(m).wait()
        gather.fold(m, order(m))
        gather.send_y(order(m))

        @pl.when(m + 4 < n_exp)
        def _():
            fetch(m + 4).start()

    leave(0)
    leave(1)
    for cp in loads[:5]:
        cp.wait()

    g_norms[...] = jnp.zeros_like(g_norms)
    n_slots = n_exp * lc * cap
    n_quarter = width // 16

    def fold(values):
        return jnp.sum(values, axis=0, keepdims=True)

    @pl.loop(0, tok // 256)
    def _(i):
        rows = pl.ds(pl.multiple_of(i * 256, 256), 256)
        table = tok_block(slot_col[rows], 0, n_slots)
        up = mm(table, back[...].reshape(n_slots, width))
        _, unit, inverse = norm_rows(middle[rows], gain2[...], 0.0)
        g_norms[2:3] += fold(up * unit)
        g_norms[3:4] += fold(up)
        g_mid = cot[rows].astype(F32) + norm_back(up, unit, inverse, gain2[...])
        g_tokens[rows] = g_mid
        gattn[rows] = g_mid.astype(BF)
        gctx[rows] = mm_nt(gattn[rows], w_out[...]).astype(BF)
        out, _, _ = norm_rows(tokens[rows].astype(F32), gain1[...], shift1[...])
        n1t[:, rows] = out.astype(BF).T

    leave(2)
    leave(3)
    for cp in loads[5:]:
        cp.wait()

    @pl.loop(0, width // 256)
    def _(i):
        cols = pl.ds(pl.multiple_of(i * 256, 256), 256)
        part = mm_tn(context[:, cols], gattn[...]).astype(BF)
        g_mats[pl.ds(3 * n_quarter + i * 16, 16)] = part.reshape(16, 16, width)

    total.begin(3)
    key_i = lax.broadcasted_iota(jnp.int32, (tok, tok), 0)
    qry_i = lax.broadcasted_iota(jnp.int32, (tok, tok), 1)
    dk_, dq_ = jnp.zeros((tok, tok), jnp.int32), jnp.zeros((tok, tok), jnp.int32)
    end = 0
    for j in range(lens.shape[1]):
        end = end + lens[0, j]
        dk_ = dk_ + jnp.where(key_i >= end, 1, 0)
        dq_ = dq_ + jnp.where(qry_i >= end, 1, 0)
    bias[...] = jnp.where((dk_ == dq_) & (qry_i >= key_i), 0.0, masked_score)
    lse_t[...] = lse[...].T

    lane = lax.broadcasted_iota(jnp.int32, (1, 128), 1)
    n_pairs = width // 128
    half = tok // 2
    heads_in = 128 // hd

    @pl.loop(0, n_pairs)
    def _(p):
        @pl.when(p + 4 < n_exp)
        def _():
            leave(p + 4)

        @pl.when((p >= 2) & (lax.rem(p, 2) == 0))
        def _():
            gather.step_exp(order(lax.div(p, 2) - 1), bias_back[...].reshape(lc, 1, width))

        def cols(part):
            return pl.ds(pl.multiple_of(part * width + p * 128, 128), 128)

        q, key, val, do = mixed[:, cols(0)], mixed[:, cols(1)], mixed[:, cols(2)], gctx[:, cols(0)]
        dq = [jnp.zeros((half, 128), F32) for _ in range(2)]
        dkey = [jnp.zeros((half, 128), F32) for _ in range(2)]
        dval = [jnp.zeros((half, 128), F32) for _ in range(2)]
        for hh in range(heads_in):
            own_lanes = (lane >= hh * hd) & (lane < (hh + 1) * hd)
            qh = jnp.where(own_lanes, q * BF(hd**-0.5), BF(0))
            kh = jnp.where(own_lanes, key * BF(hd**-0.5), BF(0))
            doh = jnp.where(own_lanes, do, BF(0))
            lrow = lse_t[pl.ds(p * heads_in + hh, 1), :]
            for qb in range(2):
                rows = slice(qb * half, (qb + 1) * half)
                n = (qb + 1) * half
                s = mm_nt(key[:n], qh[rows]) + (bias[:n, rows] - lrow[:, rows])
                pt = jnp.exp(s)
                dp = mm_nt(val[:n], doh[rows])
                inner = jnp.sum(dp * pt, axis=0, keepdims=True)
                ds = (pt * (dp - inner)).astype(BF)
                ptb = pt.astype(BF)
                dv_, dk2 = mm(ptb, doh[rows]), mm(ds, qh[rows])
                for kb in range(qb + 1):
                    part = slice(kb * half, (kb + 1) * half)
                    dval[kb] = dval[kb] + dv_[part]
                    dkey[kb] = dkey[kb] + dk2[part]
                dq[qb] = dq[qb] + mm_tn(ds, kh[:n])
        for b in range(2):
            rows = slice(b * half, (b + 1) * half)
            mixed[rows, cols(0)] = dq[b].astype(BF)
            mixed[rows, cols(1)] = dkey[b].astype(BF)
            mixed[rows, cols(2)] = dval[b].astype(BF)

    def step_exp(m):
        gather.step_exp(order(m), bias_back[...].reshape(lc, 1, width))

    step_exp(3)
    for part in range(3):

        @pl.loop(0, width // 256)
        def _(i):
            rows = pl.ds(pl.multiple_of(i * 256, 256), 256)
            piece = mm(n1t[rows], mixed[:, part * width : (part + 1) * width])
            g_mats[pl.ds(part * n_quarter + i * 16, 16)] = piece.astype(BF).reshape(16, 16, width)

        total.begin(part)

    @pl.loop(n_pairs + 4, max(n_exp, n_pairs + 4))
    def _(m):
        leave(m)

    step_exp(4)

    @pl.loop(0, tok // 256)
    def _(i):
        rows = pl.ds(pl.multiple_of(i * 256, 256), 256)
        up = mm_nt(mixed[rows], w_qkv[...])
        _, unit, inverse = norm_rows(tokens[rows].astype(F32), gain1[...], 0.0)
        g_norms[0:1] += fold(up * unit)
        g_norms[1:2] += fold(up)
        g_tokens[rows] += norm_back(up, unit, inverse, gain1[...])

    def aside(s):
        @pl.when(s == 0)
        def _():
            @pl.loop(5, n_exp - 2)
            def _(m):
                step_exp(m)

        for j in (1, 2):

            @pl.when(s == j)
            def _():
                step_exp(n_exp - 3 + j)

        @pl.when(s == 5)
        def _():
            @pl.loop(1, n_exp)
            def _(k):
                gather.over_exp(k).wait_recv()

            @pl.loop(0, tok // 256)
            def _(i):
                rows = pl.ds(pl.multiple_of(i * 256, 256), 256)
                table = tok_block(slot_col[rows], 0, n_slots)
                whole = middle[rows] + mm(table, f_back[...].reshape(n_slots, width))
                output[rows] = whole.astype(BF)

    total.run(aside)

    @pl.loop(0, n_exp)
    def _(k):
        gather.over_core(k).wait_send()
        gather.sent(k)


def attend_back(
    n_exp, n_hid, lens, slot_col, tokens, middle, cot, mixed, context, lse, back,
    gain1, shift1, w_qkv, w_out, gain2, bias_back, f_part,
):
    n_y = n_hid // 2
    tok, width = tokens.shape
    _, lc, cap, _ = back.shape
    n_units = 4 * width // 16
    shape = jax.ShapeDtypeStruct
    return pl.pallas_call(
        functools.partial(attend_back_kernel, n_exp, n_y),
        name="attend_back",
        out_shape=(
            shape((tok, width), BF),
            shape((tok, width), F32),
            shape((n_units, 16, width), BF),
            shape((8, width), F32),
        ),
        in_specs=[SM, VM, HB, HB, HB, HB, HB, VM, HB, VM, VM, HB, HB, VM, VM, HB],
        out_specs=[VM, VM, HB, VM],
        scratch_shapes=[
            *[pltpu.VMEM(a.shape, a.dtype) for a in (tokens, middle, cot, mixed, context, back, w_qkv, w_out)],
            pltpu.VMEM((n_units, 16, width), BF),
            pltpu.VMEM((tok, tok), F32),
            pltpu.VMEM((tok, width), BF),
            pltpu.VMEM((tok, width), BF),
            pltpu.VMEM((width, tok), BF),
            pltpu.VMEM((128, tok), F32),
            pltpu.VMEM((4, lc, n_y, cap, width), BF),
            pltpu.VMEM((n_exp, lc, cap, width), BF),
            DMA((4,)),
            DMA((8,)),
            *Gather.scratch(n_exp, n_y, lc, cap, width),
            *Gather.sems(n_exp, n_y),
            *Reduce.scratch(n_exp, n_y, n_units, (8, width)),
        ],
        compiler_params=pltpu.CompilerParams(
            collective_id=2, has_side_effects=True, vmem_limit_bytes=63 * MIB
        ),
    )(
        lens, slot_col, tokens, middle, cot, mixed, context, lse, back,
        gain1, shift1, w_qkv, w_out, gain2, bias_back, f_part,
    )


def per_device(
    tokens, token_ids, lengths, hash_table, capacity, gain_one, shift_one, w_qkv, w_out,
    gain_two, shift_two, w_in, bias_in, w_back, bias_back, cotangent,
):
    n_exp, n_hid = lax.axis_size("exp"), lax.axis_size("hid")
    tok, width = tokens.shape
    lc, _, ff = w_in.shape
    cap = 2 * tok // capacity.shape[0]
    table_rows = -(-hash_table.shape[0] // 1024) * 8
    table = jnp.pad(hash_table, (0, table_rows * 128 - hash_table.shape[0])).reshape(table_rows, 128)
    gain1, shift1, gain2, shift2 = (v[None] for v in (gain_one, shift_one, gain_two, shift_two))
    mixed, context, middle, lse, slot, send, grads, first_rows = attend(
        n_exp, n_hid, lc, cap, lengths, token_ids[None], table, capacity[None], tokens, gain1, shift1, w_qkv, w_out, gain2, shift2, cotangent
    )
    back, f_part, wi, wb, gb_in, gb_back = experts(
        n_exp, n_hid, first_rows, send, grads, w_in, bias_in, w_back
    )
    output, g_tokens, mats, norms = attend_back(
        n_exp, n_hid, lengths, slot, tokens, middle, cotangent, mixed, context, lse, back,
        gain1, shift1, w_qkv, w_out, gain2, bias_back, f_part,
    )
    g_in, g_back, g_qkv, g_out, *norms, gb_in, gb_back = finish(wi, wb, mats, norms, gb_in, gb_back)
    return (
        output, g_tokens, norms[0], norms[1], g_qkv, g_out, norms[2], norms[3], g_in, gb_in, g_back, gb_back,
    )


def solution(mesh):
    both = P(("exp", "hid"))
    rows = P(("exp", "hid"), None)
    placed = (
        rows, both, rows, P(), P(), P(), P(), P(), P(), P(), P(),
        P("exp", None, "hid"), P("exp", "hid"), P("exp", "hid", None), P("exp", None), rows,
    )
    return jax.shard_map(
        per_device,
        mesh=mesh,
        in_specs=placed,
        out_specs=(
            rows, rows, P(), P(), P(), P(), P(), P(),
            P("exp", None, "hid"), P("exp", "hid"), P("exp", "hid", None), P("exp", None),
        ),
        check_vma=False,
    )
```

```python
import functools

import jax
import jax.numpy as jnp
from jax import lax
from jax.experimental import pallas as pl
from jax.experimental.pallas import tpu as pltpu
from jax.sharding import PartitionSpec as P

HEADS = 16
MESH = pl.DeviceIdType.MESH
BF = jnp.bfloat16
F32 = jnp.float32
epsilon = 1e-05
masked_score = -1e30
DMA = pltpu.SemaphoreType.DMA
VM = pl.BlockSpec(memory_space=pltpu.VMEM)
SM = pl.BlockSpec(memory_space=pltpu.SMEM)
HB = pl.BlockSpec(memory_space=pl.ANY)
MIB = 1 << 20


def mm(a, b):
    return lax.dot_general(a, b, (((1,), (0,)), ((), ())), preferred_element_type=F32)


def mm_nt(a, b):
    return lax.dot_general(a, b, (((1,), (1,)), ((), ())), preferred_element_type=F32)


def mm_tn(a, b):
    return lax.dot_general(a, b, (((0,), (0,)), ((), ())), preferred_element_type=F32)


def place():
    e = lax.axis_index("exp")
    h = lax.axis_index("hid")
    return e, h, lax.div(h, 2), lax.rem(h, 2)


def rcopy(src, dst, send, recv, dev):
    return pltpu.make_async_remote_copy(
        src_ref=src, dst_ref=dst, send_sem=send, recv_sem=recv, device_id=dev, device_id_type=MESH
    )


def greet(n_exp, n_y):
    e, h, y, c = place()
    sem = pltpu.get_barrier_semaphore()
    for k in range(1, n_exp):
        pl.semaphore_signal(sem, inc=1, device_id=(e ^ k, h), device_id_type=MESH)
    for d in range(1, n_y):
        pl.semaphore_signal(
            sem, inc=1, device_id=(e, lax.rem(y + d, n_y) * 2 + c), device_id_type=MESH
        )
    pl.semaphore_signal(sem, inc=1, device_id=(e, y * 2 + 1 - c), device_id_type=MESH)
    pl.semaphore_wait(sem, n_exp - 1 + n_y)


class Spread:
    def __init__(self, n_exp, n_y, rows, land, sems):
        self.n_exp, self.n_y, self.rows, self.land = n_exp, n_y, rows, land
        self.es, self.er, self.ys, self.yr, self.cs, self.cr = sems
        self.e, self.h, self.y, self.c = place()

    @staticmethod
    def sems(n_exp, n_y):
        return [DMA((n_exp,)), DMA((n_exp,))] + [DMA((n_exp, n_y))] * 4

    def over_exp(self, k):
        return rcopy(
            self.rows.at[self.e ^ k], self.land.at[:, self.e, self.h],
            self.es.at[k], self.er.at[k], (self.e ^ k, self.h),
        )

    def turn(self, i):
        low, high = lax.div(i + 1, 2), self.n_exp // 2 + lax.div(i, 2) - 1
        return jnp.where(i == self.n_exp - 1, self.n_exp - 1, jnp.where(lax.rem(i, 2) == 1, low, high))

    def block(self, k, hid):
        return self.land.at[:, self.e ^ k, hid]

    def over_y(self, k, d):
        blk = self.block(k, self.h)
        dev = (self.e, lax.rem(self.y + d, self.n_y) * 2 + self.c)
        return rcopy(blk, blk, self.ys.at[k, d], self.yr.at[k, d], dev)

    def over_core(self, k, d):
        blk = self.block(k, lax.rem(self.y + self.n_y - d, self.n_y) * 2 + self.c)
        dev = (self.e, self.y * 2 + 1 - self.c)
        return rcopy(blk, blk, self.cs.at[k, d], self.cr.at[k, d], dev)

    def pass_on(self, k):
        @pl.when(k > 0)
        def _():
            self.over_exp(k).wait_recv()

        for d in range(1, self.n_y):
            self.over_y(k, d).start()
        self.over_core(k, 0).start()

    def pass_y(self, k):
        for d in range(1, self.n_y):
            self.over_y(k, d).wait_recv()
            self.over_core(k, d).start()

    def landed(self, k):
        for d in range(self.n_y):
            self.over_core(k, d).wait_recv()

    def sent(self, k):
        @pl.when(k > 0)
        def _():
            self.over_exp(k).wait_send()

        for d in range(1, self.n_y):
            self.over_y(k, d).wait_send()
        for d in range(self.n_y):
            self.over_core(k, d).wait_send()


class Gather:
    def __init__(self, n_exp, n_y, other, mine, pairs, from_y, back, sems):
        self.n_exp, self.n_y, self.other, self.mine = n_exp, n_y, other, mine
        self.pairs, self.from_y, self.back = pairs, from_y, back
        self.es, self.er, self.ys, self.yr, self.cs, self.cr = sems
        self.e, self.h, self.y, self.c = place()

    @staticmethod
    def sems(n_exp, n_y):
        return [DMA((n_exp,)), DMA((n_exp,)), DMA((n_exp, n_y)), DMA((n_exp, n_y)), DMA((n_exp,)), DMA((n_exp,))]

    @staticmethod
    def scratch(n_exp, n_y, lc, cap, d):
        return [
            pltpu.VMEM((n_exp, lc, n_y, cap, d), BF),
            pltpu.VMEM((n_exp, n_y - 1, lc, cap, d), BF),
        ]

    def over_core(self, k):
        t = self.e ^ k
        dev = (self.e, self.y * 2 + 1 - self.c)
        return rcopy(self.other(k), self.pairs.at[t], self.cs.at[k], self.cr.at[k], dev)

    def over_y(self, k, d):
        t = self.e ^ k
        dev = (self.e, lax.rem(self.y + d, self.n_y) * 2 + self.c)
        yy = lax.rem(self.y + d, self.n_y)
        return rcopy(self.pairs.at[t, :, yy], self.from_y.at[t, d - 1], self.ys.at[k, d], self.yr.at[k, d], dev)

    def over_exp(self, k):
        t = self.e ^ k
        return rcopy(self.pairs.at[t, :, self.y], self.back.at[self.e], self.es.at[k], self.er.at[k], (t, self.h))

    def step_core(self, k):
        self.over_core(k).start()

    def fold(self, at, k):
        t = self.e ^ k
        self.over_core(k).wait_recv()
        for yy in range(self.n_y):
            pair = self.pairs[t, :, yy].astype(F32) + self.mine(at, yy).astype(F32)
            self.pairs[t, :, yy] = pair.astype(BF)

    def send_y(self, k):
        for d in range(1, self.n_y):
            self.over_y(k, d).start()

    def step_exp(self, k, extra=None):
        t = self.e ^ k
        total = self.pairs[t, :, self.y].astype(F32)
        for d in range(1, self.n_y):
            self.over_y(k, d).wait_recv()
            total = total + self.from_y[t, d - 1].astype(F32)
        if extra is not None:
            total = total + extra
        total = total.astype(BF)

        @pl.when(k == 0)
        def _():
            self.back[t] = total

        @pl.when(k > 0)
        def _():
            self.pairs[t, :, self.y] = total
            self.over_exp(k).start()

    def sent(self, k):
        for d in range(1, self.n_y):
            self.over_y(k, d).wait_send()

        @pl.when(k > 0)
        def _():
            self.over_exp(k).wait_send()


def norm_rows(rows, gain, shift):
    mean = jnp.mean(rows, axis=-1, keepdims=True)
    centred = rows - mean
    var = jnp.mean(centred * centred, axis=-1, keepdims=True)
    inverse = lax.rsqrt(var + epsilon)
    unit = centred * inverse
    return unit * gain + shift, unit, inverse


def norm_back(upstream, unit, inverse, gain):
    scaled = upstream * gain
    inner = (
        scaled
        - jnp.mean(scaled, axis=-1, keepdims=True)
        - unit * jnp.mean(scaled * unit, axis=-1, keepdims=True)
    )
    return inner * inverse


def turned(values):
    if values.shape[1] == 1:
        return jnp.broadcast_to(values, (values.shape[0], 128)).T
    return jnp.broadcast_to(values, (128, values.shape[1])).T


def token_slots(token_ids, hash_table, capacity, cap):
    tok = token_ids.shape[1]
    ids = turned(token_ids.astype(F32)).astype(jnp.int32)
    row, col = lax.shift_right_logical(ids, 7), ids & 127
    n_rows = hash_table.shape[0]
    lanes = lax.broadcasted_iota(jnp.int32, (tok, 128), 1)
    is_row = jnp.where(lanes[:, :n_rows] == row[:, :n_rows], 1.0, 0.0).astype(BF)
    found = mm(is_row, hash_table.astype(F32).astype(BF))
    chosen = jnp.sum(jnp.where(lanes == col, found, 0.0), axis=1, keepdims=True)
    n_experts = capacity.shape[1]
    ids_e = lax.broadcasted_iota(jnp.int32, (tok, n_experts), 1)
    onehot = jnp.where(ids_e == chosen.astype(jnp.int32), 1.0, 0.0)
    here = lax.broadcasted_iota(jnp.int32, (tok, tok), 0)
    there = lax.broadcasted_iota(jnp.int32, (tok, tok), 1)
    before = mm(jnp.where(here > there, 1.0, 0.0).astype(BF), onehot.astype(BF))
    rank = jnp.sum(before * onehot, axis=1, keepdims=True)
    limit = jnp.sum(capacity.astype(F32) * onehot, axis=1, keepdims=True)
    return jnp.where(rank < limit, chosen * cap + rank, -1.0)


def slot_block(slot_row, first, count):
    tok = slot_row.shape[1]
    ids = lax.broadcasted_iota(jnp.int32, (count, tok), 0) + first
    return jnp.where(slot_row == ids, 1.0, 0.0).astype(BF)


def tok_block(slot_col, first, count):
    ids = lax.broadcasted_iota(jnp.int32, (slot_col.shape[0], count), 1) + first
    return jnp.where(slot_col == ids, 1.0, 0.0).astype(BF)


def doc_bias(lens, tok):
    q = lax.broadcasted_iota(jnp.int32, (tok, tok), 0)
    k = lax.broadcasted_iota(jnp.int32, (tok, tok), 1)
    dq = jnp.zeros((tok, tok), jnp.int32)
    dk = jnp.zeros((tok, tok), jnp.int32)
    end = 0
    for j in range(lens.shape[1]):
        end = end + lens[0, j]
        dq = dq + jnp.where(q >= end, 1, 0)
        dk = dk + jnp.where(k >= end, 1, 0)
    return jnp.where((dq == dk) & (q >= k), 0.0, masked_score)


def attend_kernel(
    n_exp, n_y, lens, token_ids, hash_table, capacity, tokens, gain1, shift1, w_qkv, w_out, gain2, shift2, cot,
    mixed_h, context_h, middle_h, lse, slot_col, send_h, land, first_rows,
    slot_row, mixed, context, middle, send, cot_rows, normed, bias, wq_v, wo_v, in_sem, out_sem, own_sem, first_s, first_r, *sems,
):
    tok, width = tokens.shape
    e, h, y, c = place()
    lc, cap = send.shape[1], send.shape[2]
    per = lc * cap
    hd = width // HEADS
    spread = Spread(n_exp, n_y, cot_rows, land, sems)
    loads = [
        pltpu.make_async_copy(w_qkv, wq_v, in_sem.at[0]),
        pltpu.make_async_copy(w_out, wo_v, in_sem.at[1]),
    ]
    stores = [
        pltpu.make_async_copy(a, b, out_sem.at[i])
        for i, (a, b) in enumerate(
            ((mixed, mixed_h), (context, context_h), (middle, middle_h), (send, send_h))
        )
    ]
    for cp in loads:
        cp.start()

    slots = token_slots(token_ids[...], hash_table[...], capacity[...], cap)
    slot_col[...] = slots.astype(jnp.int32)
    slot_row[...] = turned(slots)[:1].astype(jnp.int32)

    def pick(source, dst):
        rows = mm(slot_block(slot_row[...], dst * per, per), source)
        return rows.astype(BF).reshape(lc, cap, width)

    def advance(k):
        spread.pass_on(k)

        @pl.when(k > 0)
        def _():
            spread.pass_y(k - 1)

    def first(k):
        return rcopy(
            send.at[e ^ k, 0], first_rows.at[e], first_s.at[k], first_r.at[k], (e ^ k, h)
        )

    cot_rows[e] = pick(cot[...], e)
    own = pltpu.make_async_copy(cot_rows.at[e], land.at[:, e, h], own_sem)
    own.start()
    greet(n_exp, n_y)

    @pl.loop(1, n_exp)
    def _(i):
        k = spread.turn(i)
        cot_rows[e ^ k] = pick(cot[...], e ^ k)
        spread.over_exp(k).start()

    own.wait()
    spread.pass_on(0)

    @pl.loop(0, tok // 128)
    def _(i):
        rows = pl.ds(i * 128, 128)
        out, _, _ = norm_rows(tokens[rows].astype(F32), gain1[...], shift1[...])
        normed[rows] = out.astype(BF)

    bias[...] = doc_bias(lens, tok)
    loads[0].wait()

    @pl.loop(0, 3)
    def _(i):
        @pl.when(i > 0)
        def _():
            advance(i)

        for j in range(width // 512):
            cols = pl.ds(pl.multiple_of(i * width + j * 512, 512), 512)
            mixed[:, cols] = mm(normed[...], wq_v[:, cols]).astype(BF)

    stores[0].start()
    advance(3)
    lse[...] = jnp.zeros_like(lse)
    lane = lax.broadcasted_iota(jnp.int32, (1, 128), 1)
    n_pairs = width // 128
    half = tok // 2
    heads_in = 128 // hd

    @pl.loop(0, n_pairs)
    def _(p):
        @pl.when((lax.rem(p, 2) == 1) & (p < 6))
        def _():
            advance(4 + lax.div(p, 2))

        def cols(part):
            return pl.ds(pl.multiple_of(part * width + p * 128, 128), 128)

        q, key, val = mixed[:, cols(0)], mixed[:, cols(1)], mixed[:, cols(2)]
        for blk in range(2):
            rows = slice(blk * half, (blk + 1) * half)
            n_keys = (blk + 1) * half
            total = jnp.zeros((half, 128), F32)
            lses = lse[rows, :]
            for hh in range(heads_in):
                own_lanes = (lane >= hh * hd) & (lane < (hh + 1) * hd)
                qh = jnp.where(own_lanes, q[rows] * BF(hd**-0.5), BF(0))
                vh = jnp.where(own_lanes, val[:n_keys], BF(0))
                s = mm_nt(qh, key[:n_keys]) + bias[rows, :n_keys]
                top = jnp.max(s, axis=-1, keepdims=True)
                ex = jnp.exp(s - top)
                tot = jnp.sum(ex, axis=-1, keepdims=True)
                probs = (ex * (1.0 / tot)).astype(BF)
                total = total + mm(probs, vh)
                lses = jnp.where(lane == p * heads_in + hh, top + jnp.log(tot), lses)
            lse[rows, :] = lses
            context[rows, pl.ds(pl.multiple_of(p * 128, 128), 128)] = total.astype(BF)

    stores[1].start()
    loads[1].wait()

    @pl.loop(0, tok // 256)
    def _(i):
        rows = pl.ds(pl.multiple_of(i * 256, 256), 256)
        mid = tokens[rows].astype(F32) + mm(context[rows], wo_v[...])
        middle[rows] = mid
        out, _, _ = norm_rows(mid, gain2[...], shift2[...])
        normed[rows] = out.astype(BF)

    stores[2].start()

    @pl.loop(0, n_exp)
    def _(k):
        send[k] = pick(normed[...], k)

    stores[3].start()
    own_first = pltpu.make_async_copy(send.at[e, 0], first_rows.at[e], own_sem)
    own_first.start()

    @pl.loop(1, n_exp)
    def _(k):
        first(k).start()

    @pl.loop(7, n_exp)
    def _(k):
        advance(k)

    spread.pass_y(n_exp - 1)
    for cp in stores:
        cp.wait()
    own_first.wait()

    @pl.loop(1, n_exp)
    def _(k):
        first(k).wait_send()
        first(k).wait_recv()

    @pl.loop(0, n_exp)
    def _(k):
        spread.landed(k)
        spread.sent(k)


def attend(n_exp, n_hid, lc, cap, lens, token_ids, hash_table, capacity, tokens, gain1, shift1, w_qkv, w_out, gain2, shift2, cot):
    n_y = n_hid // 2
    tok, width = tokens.shape
    shape = jax.ShapeDtypeStruct
    return pl.pallas_call(
        functools.partial(attend_kernel, n_exp, n_y),
        name="attend",
        out_shape=(
            shape((tok, 3 * width), BF),
            shape((tok, width), BF),
            shape((tok, width), F32),
            shape((tok, 128), F32),
            shape((tok, 1), jnp.int32),
            shape((n_exp, lc, cap, width), BF),
            shape((lc, n_exp, n_hid, cap, width), BF),
            shape((n_exp, cap, width), BF),
        ),
        in_specs=[SM, VM, VM, VM, VM, VM, VM, HB, HB, VM, VM, VM],
        out_specs=[HB, HB, HB, VM, VM, HB, HB, HB],
        scratch_shapes=[
            pltpu.VMEM((1, tok), jnp.int32),
            pltpu.VMEM((tok, 3 * width), BF),
            pltpu.VMEM((tok, width), BF),
            pltpu.VMEM((tok, width), F32),
            pltpu.VMEM((n_exp, lc, cap, width), BF),
            pltpu.VMEM((n_exp, lc, cap, width), BF),
            pltpu.VMEM((tok, width), BF),
            pltpu.VMEM((tok, tok), F32),
            pltpu.VMEM(w_qkv.shape, BF),
            pltpu.VMEM(w_out.shape, BF),
            DMA((2,)),
            DMA((4,)),
            DMA,
            DMA((n_exp,)),
            DMA((n_exp,)),
            *Spread.sems(n_exp, n_y),
        ],
        compiler_params=pltpu.CompilerParams(
            collective_id=0, has_side_effects=True, vmem_limit_bytes=56 * MIB
        ),
    )(lens, token_ids, hash_table, capacity, tokens, gain1, shift1, w_qkv, w_out, gain2, shift2, cot)


STEP_W = 512


class Halves:
    def __init__(self, n_exp, n_y):
        self.n_exp, self.n_y, self.half = n_exp, n_y, n_exp // 2
        self.e, self.h, self.y, self.c = place()
        self.sibling = (self.e, self.y * 2 + 1 - self.c)

    def range(self, g):
        first = lax.div(self.e, self.half) * self.half
        return pl.ds(pl.multiple_of(first if g == 0 else self.half - first, self.half), self.half)

    def y_peer(self, d):
        return (self.e, lax.rem(self.y + d, self.n_y) * 2 + self.c)


class SpreadExpert(Halves):
    def __init__(self, n_exp, n_y, rows, land, sems):
        super().__init__(n_exp, n_y)
        self.rows, self.land = rows, land
        self.es, self.er, self.ys, self.yr, self.cs, self.cr = sems

    @staticmethod
    def sems(lc, n_exp, n_y):
        return [DMA((lc, n_exp))] * 2 + [DMA((lc, 2, n_y))] * 4

    def over_exp(self, ex, k):
        return rcopy(
            self.rows.at[self.e ^ k, ex], self.land.at[ex, self.e, self.h],
            self.es.at[ex, k], self.er.at[ex, k], (self.e ^ k, self.h),
        )

    def start(self, ex):
        half = self.half
        for i in range(1, self.n_exp):
            self.over_exp(ex, half + i // 2 - 1 if i % 2 == 0 else ((i + 1) // 2 if i < self.n_exp - 1 else i)).start()

    def over_y(self, ex, g, d):
        blk = self.land.at[ex, self.range(g), self.h]
        return rcopy(blk, blk, self.ys.at[ex, g, d], self.yr.at[ex, g, d], self.y_peer(d))

    def over_core(self, ex, g, d):
        hid = lax.rem(self.y + self.n_y - d, self.n_y) * 2 + self.c
        blk = self.land.at[ex, self.range(g), hid]
        return rcopy(blk, blk, self.cs.at[ex, g, d], self.cr.at[ex, g, d], self.sibling)

    def pass_on(self, ex, g, came=False):
        if not came:
            for k in range(max(1, g * self.half), (g + 1) * self.half):
                self.over_exp(ex, k).wait_recv()
        for d in range(1, self.n_y):
            self.over_y(ex, g, d).start()
        self.over_core(ex, g, 0).start()

    def pass_y(self, ex, g):
        for d in range(1, self.n_y):
            self.over_y(ex, g, d).wait_recv()
            self.over_core(ex, g, d).start()

    def landed(self, ex, g):
        for d in range(self.n_y):
            self.over_core(ex, g, d).wait_recv()

    def sent(self, ex):
        @pl.when(ex > 0)
        def _():
            for k in range(1, self.n_exp):
                self.over_exp(ex, k).wait_send()

        for g in range(2):
            for d in range(1, self.n_y):
                self.over_y(ex, g, d).wait_send()
            for d in range(self.n_y):
                self.over_core(ex, g, d).wait_send()


class GatherExpert(Halves):
    def __init__(self, n_exp, n_y, part, pairs, from_y, back, sems):
        super().__init__(n_exp, n_y)
        self.part, self.pairs, self.from_y, self.back = part, pairs, from_y, back
        self.es, self.er, self.ys, self.yr, self.cs, self.cr = sems

    @staticmethod
    def sems(lc, n_exp, n_y):
        return [DMA((lc, n_exp))] * 2 + [DMA((lc, 2, n_y))] * 2 + [DMA((lc, 2))] * 2

    def over_core(self, ex, b):
        return rcopy(
            self.part.at[self.range(b), :, 1 - self.c], self.pairs.at[ex, self.range(b)],
            self.cs.at[ex, b], self.cr.at[ex, b], self.sibling,
        )

    def over_y(self, ex, b, d):
        yy = lax.rem(self.y + d, self.n_y)
        return rcopy(
            self.pairs.at[ex, self.range(b), yy], self.from_y.at[d - 1, ex, self.range(b)],
            self.ys.at[ex, b, d], self.yr.at[ex, b, d], self.y_peer(d),
        )

    def over_exp(self, ex, k):
        t = self.e ^ k
        return rcopy(
            self.pairs.at[ex, t, self.y], self.back.at[self.e, ex], self.es.at[ex, k], self.er.at[ex, k], (t, self.h)
        )

    def stay(self, ex):
        return pltpu.make_async_copy(self.pairs.at[ex, self.e, self.y], self.back.at[self.e, ex], self.es.at[ex, 0])

    def fold(self, ex, b):
        self.over_core(ex, b).wait_recv()
        rows = self.range(b)
        for yy in range(self.n_y):
            pair = self.pairs[ex, rows, yy].astype(F32) + self.part[rows, yy, self.c].astype(F32)
            self.pairs[ex, rows, yy] = pair.astype(BF)
        for d in range(1, self.n_y):
            self.over_y(ex, b, d).start()
        self.over_core(ex, b).wait_send()

    def step_exp(self, ex, b):
        rows = self.range(b)
        total = self.pairs[ex, rows, self.y].astype(F32)
        for d in range(1, self.n_y):
            self.over_y(ex, b, d).wait_recv()
            total = total + self.from_y[d - 1, ex, rows].astype(F32)
        self.pairs[ex, rows, self.y] = total.astype(BF)
        for i in range(self.half):
            k = b * self.half + i
            if k == 0:
                self.stay(ex).start()
            else:
                self.over_exp(ex, k).start()

    def finish(self, ex):
        self.stay(ex).wait()
        for b in range(2):
            for d in range(1, self.n_y):
                self.over_y(ex, b, d).wait_send()
        for k in range(1, self.n_exp):
            self.over_exp(ex, k).wait_send()
            self.over_exp(ex, k).wait_recv()


def expert_kernel(
    n_exp, n_y, first_rows, rows, grads, w_in, bias_in, w_back,
    back, f_out, wi_out, wb_out, gb_in, gb_back,
    land, part, pairs, from_y, wi_v, wb_v, g_v, h_v, gp_v, f_v, wi_st, wb_st,
    w_sem, g_sem, f_sem, o_sem, own_sem, *rest,
):
    e, h, y, c = place()
    n_spread = len(SpreadExpert.sems(1, 1, 1))
    spread = SpreadExpert(n_exp, n_y, rows, land, rest[:n_spread])
    gather = GatherExpert(n_exp, n_y, part, pairs, from_y, back, rest[n_spread:])
    n_hid = 2 * n_y
    lc, cap, width = rows.shape[1:]
    ff = w_in.shape[2]
    n_src = 4
    block = n_src * n_hid * cap
    n_rb = n_exp // n_src
    step_f = min(512, ff)
    step_w = STEP_W

    def weights(ex):
        slot = lax.rem(ex, 2)
        return (
            pltpu.make_async_copy(w_in.at[ex], wi_v.at[slot], w_sem.at[0, slot]),
            pltpu.make_async_copy(w_back.at[ex], wb_v.at[slot], w_sem.at[1, slot]),
        )

    def g_copy(ex):
        slot = lax.rem(ex, 2)
        return pltpu.make_async_copy(grads.at[ex], g_v.at[slot], g_sem.at[slot])

    def f_copy(ex, rb):
        return pltpu.make_async_copy(f_v, f_out.at[ex, sources(rb)], f_sem)

    def wi_copy(ex, i):
        return pltpu.make_async_copy(wi_st, wi_out.at[ex, pl.ds(i * step_w, step_w)], o_sem.at[0])

    def wb_copy(ex, i):
        return pltpu.make_async_copy(wb_st, wb_out.at[ex, pl.ds(i * step_w, step_w)], o_sem.at[1])

    def sources(rb):
        return pl.ds(lax.rem(lax.div(e, n_exp // 2) * (n_rb // 2) + rb, n_rb) * n_src, n_src)

    own = pltpu.make_async_copy(rows.at[e, pl.ds(1, lc - 1)], land.at[pl.ds(1, lc - 1), e, h], own_sem.at[0])
    own_first = pltpu.make_async_copy(first_rows, land.at[0, :, h], own_sem.at[1])
    own_first.start()
    own.start()
    greet(n_exp, n_y)
    own_first.wait()
    spread.pass_on(0, 0, came=True)
    spread.pass_on(0, 1, came=True)
    spread.start(1)
    for ex in range(2):
        for cp in weights(ex):
            cp.start()
    g_copy(0).start()
    gb_in[...] = jnp.zeros_like(gb_in)
    gb_back[...] = jnp.zeros_like(gb_back)
    own.wait()
    spread.pass_y(0, 0)
    spread.start(2)

    def weight_grads(ex, after):
        slot = lax.rem(ex, 2)

        @pl.loop(0, width // step_w)
        def _(i):
            cols = pl.ds(pl.multiple_of(i * step_w, step_w), step_w)
            x = land[ex, :, :, :, cols].reshape(n_exp * n_hid * cap, step_w)
            piece = mm_tn(x, gp_v[slot].reshape(n_exp * n_hid * cap, ff)).astype(BF)

            @pl.when(i > 0)
            def _():
                wi_copy(ex, i).wait()

            wi_st[...] = piece
            wi_copy(ex, i).start()
            after(i)

        @pl.loop(0, ff // step_w)
        def _(i):
            cols = pl.ds(pl.multiple_of(i * step_w, step_w), step_w)
            hid = h_v[slot, :, :, cols].reshape(n_exp * n_hid * cap, step_w)
            piece = mm_tn(hid, g_v[slot].reshape(n_exp * n_hid * cap, width)).astype(BF)

            @pl.when(i > 0)
            def _():
                wb_copy(ex, i).wait()

            wb_st[...] = piece
            wb_copy(ex, i).start()

        wi_copy(ex, 0).wait()
        wb_copy(ex, 0).wait()

    @pl.loop(0, lc)
    def _(ex):
        slot = lax.rem(ex, 2)
        g_copy(ex).wait()
        for cp in weights(ex):
            cp.wait()

        @pl.loop(0, n_rb)
        def _(rb):
            at = sources(rb)
            for b in range(2):

                @pl.when(rb == b * (n_rb // 2))
                def _():
                    spread.landed(ex, b)

            x = land[ex, at].reshape(block, width)
            g = g_v[slot, at].reshape(block, width)
            gb_back[pl.ds(ex, 1)] += jnp.sum(g.astype(F32), axis=0, keepdims=True)
            for f in range(ff // step_f):
                cols = slice(f * step_f, (f + 1) * step_f)
                pre = mm(x, wi_v[slot, :, cols]) + bias_in[pl.ds(ex, 1), cols]
                sig = jax.nn.sigmoid(pre)
                hid = (pre * sig).astype(BF)
                gh = mm_nt(g, wb_v[slot, cols, :])
                gp = (gh * sig * (1.0 + pre * (1.0 - sig))).astype(BF)
                gb_in[pl.ds(ex, 1), cols] += jnp.sum(gp.astype(F32), axis=0, keepdims=True)
                h_v[slot, at, :, cols] = hid.reshape(n_src, n_hid * cap, step_f)
                gp_v[slot, at, :, cols] = gp.reshape(n_src, n_hid * cap, step_f)
            gd = mm_nt(gp_v[slot, at].reshape(block, ff), wi_v[slot])
            part[at] = gd.astype(BF).reshape(n_src, n_y, 2, cap, width)

            for b in range(2):

                @pl.when(rb == (b + 1) * (n_rb // 2) - 1)
                def _():
                    gather.over_core(ex, b).start()

                    if b == 0:

                        @pl.when(ex == 0)
                        def _():
                            spread.pass_y(0, 1)

                        @pl.when(ex + 3 < lc)
                        def _():
                            spread.start(ex + 3)

                    @pl.when(ex + 1 < lc)
                    def _():
                        spread.pass_on(ex + 1, b)

                    @pl.when(ex > 0)
                    def _():
                        gather.step_exp(ex - 1, b)

        @pl.loop(0, n_rb)
        def _(rb):
            hv = h_v[slot, sources(rb)].reshape(block, ff)
            f = mm(hv, wb_v[slot]).astype(BF).reshape(n_src, n_y, 2, cap, width)

            @pl.when((ex > 0) | (rb > 0))
            def _():
                f_copy(ex, rb).wait()

            f_v[...] = f
            f_copy(ex, rb).start()

            for b in range(2):

                @pl.when(rb == (b + 1) * (n_rb // 2) - 1)
                def _():
                    gather.fold(ex, b)

                    @pl.when(ex + 1 < lc)
                    def _():
                        spread.pass_y(ex + 1, b)

        @pl.when(ex + 2 < lc)
        def _():
            for cp in weights(ex + 2):
                cp.start()

        @pl.when(ex > 0)
        def _():
            weight_grads(ex - 1, lambda i: None)

        @pl.when(ex + 1 < lc)
        def _():
            g_copy(ex + 1).start()

    def last(i):
        @pl.when(i == 0)
        def _():
            gather.step_exp(lc - 1, 0)

    weight_grads(lc - 1, last)
    gather.step_exp(lc - 1, 1)
    f_copy(lc - 1, 0).wait()

    @pl.loop(0, lc)
    def _(ex):
        spread.sent(ex)
        gather.finish(ex)


def experts(n_exp, n_hid, first_rows, rows, grads, w_in, bias_in, w_back):
    n_y = n_hid // 2
    _, lc, cap, width = rows.shape
    ff = w_in.shape[2]
    shape = jax.ShapeDtypeStruct
    per = n_hid * cap
    return pl.pallas_call(
        functools.partial(expert_kernel, n_exp, n_y),
        name="experts",
        out_shape=(
            shape((n_exp, lc, cap, width), BF),
            shape((lc, n_exp, n_y, 2, cap, width), BF),
            shape(w_in.shape, BF),
            shape(w_back.shape, BF),
            shape((lc, ff), F32),
            shape((lc, width), F32),
        ),
        in_specs=[HB, HB, HB, HB, VM, HB],
        out_specs=[HB, HB, HB, HB, VM, VM],
        scratch_shapes=[
            pltpu.VMEM((lc, n_exp, n_hid, cap, width), BF),
            pltpu.VMEM((n_exp, n_y, 2, cap, width), BF),
            pltpu.VMEM((lc, n_exp, n_y, cap, width), BF),
            pltpu.VMEM((n_y - 1, lc, n_exp, cap, width), BF),
            pltpu.VMEM((2, *w_in.shape[1:]), BF),
            pltpu.VMEM((2, *w_back.shape[1:]), BF),
            pltpu.VMEM((2, n_exp, n_hid, cap, width), BF),
            pltpu.VMEM((2, n_exp, per, ff), BF),
            pltpu.VMEM((2, n_exp, per, ff), BF),
            pltpu.VMEM((4, n_y, 2, cap, width), BF),
            pltpu.VMEM((STEP_W, ff), BF),
            pltpu.VMEM((STEP_W, width), BF),
            DMA((2, 2)), DMA((2,)), DMA, DMA((2,)), DMA((2,)),
            *SpreadExpert.sems(lc, n_exp, n_y),
            *GatherExpert.sems(lc, n_exp, n_y),
        ],
        compiler_params=pltpu.CompilerParams(
            collective_id=1, has_side_effects=True, vmem_limit_bytes=63 * MIB
        ),
    )(first_rows, rows, grads, w_in, bias_in, w_back)


def finish_kernel(wi, wb, mats, norms, bi, bb, g_in, g_back, g_qkv, g_out, n0, n1, n2, n3, g_bi, g_bb):
    @pl.when((pl.program_id(0) == 0) & (pl.program_id(1) == 0))
    def _():
        for i, n in enumerate((n0, n1, n2, n3)):
            n[...] = norms[i]
        g_bi[...] = bi[...]
        g_bb[...] = bb[...]

    g_in[...] = wi[...].astype(F32)
    g_back[...] = wb[...].astype(F32)
    rows, width = g_out.shape
    for part in range(3):
        g_qkv[:, part * width : (part + 1) * width] = mats[part + 1].reshape(rows, width).astype(F32)
    g_out[...] = mats[0].reshape(rows, width).astype(F32)


def finish(wi, wb, mats, norms, bi, bb):
    lc, width, ff = wi.shape
    cut = 4
    rows = width // (lc * cut)
    mats = mats.reshape(4, width // 16, 16, width)
    shape = jax.ShapeDtypeStruct
    wi_spec = pl.BlockSpec((1, width // cut, ff), lambda i, j: (i, j, 0))
    wb_spec = pl.BlockSpec((1, ff // cut, width), lambda i, j: (i, j, 0))
    small = [pl.BlockSpec(a.shape, lambda i, j: (0, 0)) for a in (norms, bi, bb)]
    return pl.pallas_call(
        finish_kernel,
        name="finish",
        grid=(lc, cut),
        out_shape=(
            shape(wi.shape, F32), shape(wb.shape, F32),
            shape((width, 3 * width), F32), shape((width, width), F32),
            *[shape((width,), F32)] * 4, shape(bi.shape, F32), shape(bb.shape, F32),
        ),
        in_specs=[
            wi_spec, wb_spec,
            pl.BlockSpec((4, rows // 16, 16, width), lambda i, j: (0, i * cut + j, 0, 0)),
            *small,
        ],
        out_specs=[
            wi_spec, wb_spec,
            pl.BlockSpec((rows, 3 * width), lambda i, j: (i * cut + j, 0)),
            pl.BlockSpec((rows, width), lambda i, j: (i * cut + j, 0)),
            *[pl.BlockSpec((width,), lambda i, j: (0,))] * 4,
            *small[1:],
        ],
        compiler_params=pltpu.CompilerParams(vmem_limit_bytes=56 * MIB),
    )(wi, wb, mats, norms, bi, bb)


EARLY = (2,)


class Reduce:
    lead = 1

    def __init__(self, n_exp, n_y, mats, out, norms, scratch):
        (self.core_in, in1, in2, in3, self.n_acc, self.n_in, self.c_s, self.c_r,
         s1, r1, s2, r2, s3, r3, t3, u3, t2, u2, t1, u1, self.d_s, self.d_r, self.n_s, self.n_r, self.l_s) = scratch
        self.mats, self.out, self.norms = mats, out, norms
        self.e, self.h, self.y, self.c = place()
        self.n_x, self.n_z, self.sub, self.half, self.n_sub = self.sizes(n_exp, n_y, mats.shape[0])
        x, z = lax.rem(self.e, self.n_x), lax.div(self.e, self.n_x)
        self.x, self.z = x, z
        self.at = {"x": (self.n_x, x), "y": (n_y, self.y), "z": (self.n_z, z)}
        self.orders = (("y", "x", "z"), ("x", "y", "z"))
        self.n_axes = (None, "y", "x", "z")
        self.sibling = (self.e, self.y * 2 + 1 - self.c)
        self.lands = (in1, in2, in3)
        self.sends, self.recvs = (s1, s2, s3), (r1, r2, r3)
        self.ups, self.upr = (t1, t2, t3), (u1, u2, u3)

    @staticmethod
    def sizes(n_exp, n_y, n_units):
        n_x = n_y
        n_z = n_exp // n_x
        sub = n_x * n_y * n_z
        half = n_units // 2
        return n_x, n_z, sub, half, half // 2 // sub

    @classmethod
    def scratch(cls, n_exp, n_y, n_units, norms_shape):
        n_x, n_z, sub, half, n_sub = cls.sizes(n_exp, n_y, n_units)
        most = max(n_x, n_y)
        width = norms_shape[1]

        def land(n, count):
            return pltpu.VMEM((2, n_sub, n - 1, count, 16, width), BF)

        def sems(n):
            return [DMA((2, n_sub, n - 1))] * 2

        return [
            pltpu.VMEM((half, 16, width), BF),
            land(most, sub // min(n_x, n_y)),
            land(most, sub // (n_x * n_y)),
            land(n_z, 1),
            pltpu.VMEM((4, *norms_shape), F32),
            pltpu.VMEM((4, max(most, n_z) - 1, *norms_shape), F32),
            DMA((2, n_sub)), DMA((2, n_sub)),
            *sems(most), *sems(most), *sems(n_z), *sems(n_z), *sems(most), *sems(most),
            DMA((2, n_sub)), DMA((2, n_sub)),
            *[DMA((4, max(most, n_z) - 1))] * 2,
            DMA((2, n_sub)),
        ]

    def device(self, axis, o):
        return {
            "x": (self.z * self.n_x + o, self.h), "y": (self.e, o * 2 + self.c), "z": (o * self.n_x + self.x, self.h)
        }[axis]

    def first(self, p, b, core):
        return (b * 4 + core * 2 + p) * self.sub

    def units(self, p, b, depth):
        first, count = self.first(p, b, self.c), self.sub
        for axis in self.orders[p][:depth]:
            n, i = self.at[axis]
            count = count // n
            first = first + i * count
        return first, count

    def core_copy(self, p, b):
        return rcopy(
            self.mats.at[pl.ds(self.first(p, b, 1 - self.c), self.sub)],
            self.core_in.at[pl.ds((b * 2 + p) * self.sub, self.sub)],
            self.c_s.at[p, b], self.c_r.at[p, b], self.sibling,
        )

    def down(self, p, b, stage, d):
        n, i = self.at[self.orders[p][stage]]
        first, count = self.units(p, b, stage)
        count = count // n
        o = lax.rem(i + d, n)
        return rcopy(
            self.mats.at[pl.ds(first + o * count, count)], self.lands[stage].at[p, b, d - 1, pl.ds(0, count)],
            self.sends[stage].at[p, b, d - 1], self.recvs[stage].at[p, b, d - 1],
            self.device(self.orders[p][stage], o),
        )

    def up(self, p, b, stage, d):
        n, i = self.at[self.orders[p][stage]]
        at = pl.ds(*self.units(p, b, stage + 1))
        source = self.mats if stage == 2 else self.out
        o = lax.rem(i + d, n)
        return rcopy(
            source.at[at], self.out.at[at], self.ups[stage].at[p, b, d - 1], self.upr[stage].at[p, b, d - 1],
            self.device(self.orders[p][stage], o),
        )

    def stay(self, p, b):
        at = pl.ds(*self.units(p, b, 3))
        return pltpu.make_async_copy(self.mats.at[at], self.out.at[at], self.l_s.at[p, b])

    def core_up(self, p, b):
        region = self.out.at[pl.ds(*self.units(p, b, 0))]
        return rcopy(region, region, self.d_s.at[p, b], self.d_r.at[p, b], self.sibling)

    def peers(self, p, stage):
        return range(1, self.at[self.orders[p][stage]][0])

    def event(self, p, b, q):
        mats = self.mats
        if q == 0:
            self.core_copy(p, b).wait_recv()
            at = pl.ds(*self.units(p, b, 0))
            other = self.core_in[pl.ds((b * 2 + p) * self.sub, self.sub)]
            mats[at] = (mats[at].astype(F32) + other.astype(F32)).astype(BF)
        elif q <= 3:
            first, count = self.units(p, b, q)
            at = pl.ds(first, count)
            total = mats[at].astype(F32)
            for d in self.peers(p, q - 1):
                self.down(p, b, q - 1, d).wait_recv()
                total = total + self.lands[q - 1][p, b, d - 1, :count].astype(F32)
            mats[at] = total.astype(BF)
            if q == 3:
                self.stay(p, b).start()
        else:
            if q == 4:
                self.stay(p, b).wait()
            for d in self.peers(p, 6 - q):
                self.up(p, b, 6 - q, d).wait_recv()
        if q < 3:
            for d in self.peers(p, q):
                self.down(p, b, q, d).start()
        elif q < 6:
            for d in self.peers(p, 5 - q):
                self.up(p, b, 5 - q, d).start()
        else:
            self.core_up(p, b).start()

    def begin(self, quarter):
        if self.n_sub == 4:
            for p in range(2):
                self.core_copy(p, quarter).start()
        elif quarter == 3:
            for b in range(self.n_sub):
                for p in range(2):
                    self.core_copy(p, b).start()

    def early(self, q):
        if self.n_sub == 4:
            for p in range(2):
                self.event(p, 0, q)

    def n_copy(self, stage, d):
        if stage == 0:
            dev = self.sibling
        else:
            n, i = self.at[self.n_axes[stage]]
            dev = self.device(self.n_axes[stage], lax.rem(i + d, n))
        return rcopy(
            self.n_acc.at[stage], self.n_in.at[stage, d - 1], self.n_s.at[stage, d - 1], self.n_r.at[stage, d - 1], dev
        )

    def n_peers(self, stage):
        return range(1, 2 if stage == 0 else self.at[self.n_axes[stage]][0])

    def n_total(self, stage):
        for d in self.n_peers(stage):
            self.n_copy(stage, d).wait_recv()
        own = self.n_acc[stage]
        if stage == 0:
            return own + self.n_in[0, 0]
        n, i = self.at[self.n_axes[stage]]
        total = jnp.zeros_like(own)
        for m in range(n):
            term = own
            for d in range(1, n):
                term = jnp.where(lax.rem(i + n - d, n) == m, self.n_in[stage, d - 1], term)
            total = total + term
        return total

    def run(self, aside):
        self.n_acc[0] = self.norms[...]
        self.n_copy(0, 1).start()

        ahead = self.n_sub == 4

        @pl.loop(0, self.n_sub - 1 + 6 + (not ahead))
        def _(s):
            for q in range(7):
                if ahead and q >= self.lead:

                    @pl.when(s == q - self.lead)
                    def _():
                        for p in range(2):
                            self.event(p, 0, q)

                b = s - q + (1 if ahead else 0)

                @pl.when((b >= (1 if ahead else 0)) & (b < self.n_sub))
                def _():
                    for p in range(2):
                        self.event(p, b, q)

            for stage in range(1, 4):

                @pl.when(s == stage)
                def _():
                    self.n_acc[stage] = self.n_total(stage - 1)
                    for d in self.n_peers(stage):
                        self.n_copy(stage, d).start()

            aside(s)

        self.norms[...] = self.n_total(3)
        for stage in range(4):
            for d in self.n_peers(stage):
                self.n_copy(stage, d).wait_send()

        @pl.loop(0, self.n_sub)
        def _(b):
            for p in range(2):
                self.core_up(p, b).wait_recv()
                self.core_copy(p, b).wait_send()
                self.core_up(p, b).wait_send()
                for stage in range(3):
                    for d in self.peers(p, stage):
                        self.down(p, b, stage, d).wait_send()
                        self.up(p, b, stage, d).wait_send()


def attend_back_kernel(
    n_exp, n_y, lens, slot_col, tokens_h, middle_h, cot_h, mixed_h, context_h, lse, back_h,
    gain1, shift1, w_qkv_h, w_out_h, gain2, bias_back, f_part,
    output, g_tokens, mats_out, g_norms,
    tokens, middle, cot, mixed, context, back, w_qkv, w_out, g_mats,
    bias, gattn, gctx, n1t, lse_t, mine_v, f_back, mine_sem, in_sem, *rest,
):
    tok, width = tokens.shape
    hd = width // HEADS
    e, h, y, c = place()
    n_gather, n_sems = len(Gather.scratch(1, 2, 1, 1, 1)), len(Gather.sems(1, 1))
    lc, cap = f_back.shape[1:3]
    gather = Gather(
        n_exp, n_y, lambda k: f_part.at[:, e ^ k, :, 1 - c], lambda m, yy: mine_v[lax.rem(m, 4), :, yy],
        *rest[:n_gather], f_back, rest[n_gather : n_gather + n_sems],
    )
    total = Reduce(n_exp, n_y, g_mats, mats_out, g_norms, rest[n_gather + n_sems :])

    def order(m):
        return jnp.where(m < n_exp // 2, m + n_exp // 2, n_exp - 1 - m)

    def fetch(m):
        slot = lax.rem(m, 4)
        return pltpu.make_async_copy(
            f_part.at[:, e ^ order(m), :, c], mine_v.at[slot], mine_sem.at[slot]
        )

    loads = [
        pltpu.make_async_copy(a, b, in_sem.at[i])
        for i, (a, b) in enumerate((
            (back_h, back), (middle_h, middle), (cot_h, cot), (w_out_h, w_out), (tokens_h, tokens),
            (context_h, context), (mixed_h, mixed), (w_qkv_h, w_qkv),
        ))
    ]
    greet(n_exp, n_y)

    @pl.loop(0, n_exp)
    def _(m):
        gather.step_core(order(m))

    for m in range(4):
        fetch(m).start()
    for cp in loads:
        cp.start()

    def leave(m):
        fetch(m).wait()
        gather.fold(m, order(m))
        gather.send_y(order(m))

        @pl.when(m + 4 < n_exp)
        def _():
            fetch(m + 4).start()

    leave(0)
    leave(1)
    for cp in loads[:5]:
        cp.wait()

    g_norms[...] = jnp.zeros_like(g_norms)
    n_slots = n_exp * lc * cap
    n_quarter = width // 16

    def fold(values):
        return jnp.sum(values, axis=0, keepdims=True)

    @pl.loop(0, tok // 256)
    def _(i):
        rows = pl.ds(pl.multiple_of(i * 256, 256), 256)
        table = tok_block(slot_col[rows], 0, n_slots)
        up = mm(table, back[...].reshape(n_slots, width))
        _, unit, inverse = norm_rows(middle[rows], gain2[...], 0.0)
        g_norms[2:3] += fold(up * unit)
        g_norms[3:4] += fold(up)
        g_mid = cot[rows].astype(F32) + norm_back(up, unit, inverse, gain2[...])
        g_tokens[rows] = g_mid
        gattn[rows] = g_mid.astype(BF)
        gctx[rows] = mm_nt(gattn[rows], w_out[...]).astype(BF)
        out, _, _ = norm_rows(tokens[rows].astype(F32), gain1[...], shift1[...])
        n1t[:, rows] = out.astype(BF).T

    leave(2)
    leave(3)
    for cp in loads[5:]:
        cp.wait()

    @pl.loop(0, width // 256)
    def _(i):
        cols = pl.ds(pl.multiple_of(i * 256, 256), 256)
        part = mm_tn(context[:, cols], gattn[...]).astype(BF)
        g_mats[pl.ds(i * 16, 16)] = part.reshape(16, 16, width)

    total.begin(0)
    key_i = lax.broadcasted_iota(jnp.int32, (tok, tok), 0)
    qry_i = lax.broadcasted_iota(jnp.int32, (tok, tok), 1)
    dk_, dq_ = jnp.zeros((tok, tok), jnp.int32), jnp.zeros((tok, tok), jnp.int32)
    end = 0
    for j in range(lens.shape[1]):
        end = end + lens[0, j]
        dk_ = dk_ + jnp.where(key_i >= end, 1, 0)
        dq_ = dq_ + jnp.where(qry_i >= end, 1, 0)
    bias[...] = jnp.where((dk_ == dq_) & (qry_i >= key_i), 0.0, masked_score)
    lse_t[...] = lse[...].T

    lane = lax.broadcasted_iota(jnp.int32, (1, 128), 1)
    n_pairs = width // 128
    half = tok // 2
    heads_in = 128 // hd

    @pl.loop(0, n_pairs)
    def _(p):
        @pl.when(p + 4 < n_exp)
        def _():
            leave(p + 4)

        @pl.when((p >= 2) & (lax.rem(p, 2) == 0))
        def _():
            gather.step_exp(order(lax.div(p, 2) - 1), bias_back[...].reshape(lc, 1, width))

        for q_step, at in enumerate(EARLY):

            @pl.when(p == at)
            def _():
                total.early(q_step)

        def cols(part):
            return pl.ds(pl.multiple_of(part * width + p * 128, 128), 128)

        q, key, val, do = mixed[:, cols(0)], mixed[:, cols(1)], mixed[:, cols(2)], gctx[:, cols(0)]
        dq = [jnp.zeros((half, 128), F32) for _ in range(2)]
        dkey = [jnp.zeros((half, 128), F32) for _ in range(2)]
        dval = [jnp.zeros((half, 128), F32) for _ in range(2)]
        for hh in range(heads_in):
            own_lanes = (lane >= hh * hd) & (lane < (hh + 1) * hd)
            qh = jnp.where(own_lanes, q * BF(hd**-0.5), BF(0))
            kh = jnp.where(own_lanes, key * BF(hd**-0.5), BF(0))
            doh = jnp.where(own_lanes, do, BF(0))
            lrow = lse_t[pl.ds(p * heads_in + hh, 1), :]
            for qb in range(2):
                rows = slice(qb * half, (qb + 1) * half)
                n = (qb + 1) * half
                s = mm_nt(key[:n], qh[rows]) + (bias[:n, rows] - lrow[:, rows])
                pt = jnp.exp(s)
                dp = mm_nt(val[:n], doh[rows])
                inner = jnp.sum(dp * pt, axis=0, keepdims=True)
                ds = (pt * (dp - inner)).astype(BF)
                ptb = pt.astype(BF)
                dv_, dk2 = mm(ptb, doh[rows]), mm(ds, qh[rows])
                for kb in range(qb + 1):
                    part = slice(kb * half, (kb + 1) * half)
                    dval[kb] = dval[kb] + dv_[part]
                    dkey[kb] = dkey[kb] + dk2[part]
                dq[qb] = dq[qb] + mm_tn(ds, kh[:n])
        for b in range(2):
            rows = slice(b * half, (b + 1) * half)
            mixed[rows, cols(0)] = dq[b].astype(BF)
            mixed[rows, cols(1)] = dkey[b].astype(BF)
            mixed[rows, cols(2)] = dval[b].astype(BF)

    def step_exp(m):
        gather.step_exp(order(m), bias_back[...].reshape(lc, 1, width))

    step_exp(3)
    for part in range(3):

        @pl.loop(0, width // 256)
        def _(i):
            rows = pl.ds(pl.multiple_of(i * 256, 256), 256)
            piece = mm(n1t[rows], mixed[:, part * width : (part + 1) * width])
            g_mats[pl.ds((part + 1) * n_quarter + i * 16, 16)] = piece.astype(BF).reshape(16, 16, width)

        total.begin(part + 1)

    @pl.loop(n_pairs + 4, max(n_exp, n_pairs + 4))
    def _(m):
        leave(m)

    step_exp(4)

    @pl.loop(0, tok // 256)
    def _(i):
        rows = pl.ds(pl.multiple_of(i * 256, 256), 256)
        up = mm_nt(mixed[rows], w_qkv[...])
        _, unit, inverse = norm_rows(tokens[rows].astype(F32), gain1[...], 0.0)
        g_norms[0:1] += fold(up * unit)
        g_norms[1:2] += fold(up)
        g_tokens[rows] += norm_back(up, unit, inverse, gain1[...])

    def aside(s):
        @pl.when(s == 0)
        def _():
            @pl.loop(5, n_exp - 2)
            def _(m):
                step_exp(m)

        for j in (1, 2):

            @pl.when(s == j)
            def _():
                step_exp(n_exp - 3 + j)

        @pl.when(s == 5)
        def _():
            @pl.loop(1, n_exp)
            def _(k):
                gather.over_exp(k).wait_recv()

            @pl.loop(0, tok // 256)
            def _(i):
                rows = pl.ds(pl.multiple_of(i * 256, 256), 256)
                table = tok_block(slot_col[rows], 0, n_slots)
                whole = middle[rows] + mm(table, f_back[...].reshape(n_slots, width))
                output[rows] = whole.astype(BF)

    total.run(aside)

    @pl.loop(0, n_exp)
    def _(k):
        gather.over_core(k).wait_send()
        gather.sent(k)


def attend_back(
    n_exp, n_hid, lens, slot_col, tokens, middle, cot, mixed, context, lse, back,
    gain1, shift1, w_qkv, w_out, gain2, bias_back, f_part,
):
    n_y = n_hid // 2
    tok, width = tokens.shape
    _, lc, cap, _ = back.shape
    n_units = 4 * width // 16
    shape = jax.ShapeDtypeStruct
    return pl.pallas_call(
        functools.partial(attend_back_kernel, n_exp, n_y),
        name="attend_back",
        out_shape=(
            shape((tok, width), BF),
            shape((tok, width), F32),
            shape((n_units, 16, width), BF),
            shape((8, width), F32),
        ),
        in_specs=[SM, VM, HB, HB, HB, HB, HB, VM, HB, VM, VM, HB, HB, VM, VM, HB],
        out_specs=[VM, VM, HB, VM],
        scratch_shapes=[
            *[pltpu.VMEM(a.shape, a.dtype) for a in (tokens, middle, cot, mixed, context, back, w_qkv, w_out)],
            pltpu.VMEM((n_units, 16, width), BF),
            pltpu.VMEM((tok, tok), F32),
            pltpu.VMEM((tok, width), BF),
            pltpu.VMEM((tok, width), BF),
            pltpu.VMEM((width, tok), BF),
            pltpu.VMEM((128, tok), F32),
            pltpu.VMEM((4, lc, n_y, cap, width), BF),
            pltpu.VMEM((n_exp, lc, cap, width), BF),
            DMA((4,)),
            DMA((8,)),
            *Gather.scratch(n_exp, n_y, lc, cap, width),
            *Gather.sems(n_exp, n_y),
            *Reduce.scratch(n_exp, n_y, n_units, (8, width)),
        ],
        compiler_params=pltpu.CompilerParams(
            collective_id=2, has_side_effects=True, vmem_limit_bytes=63 * MIB
        ),
    )(
        lens, slot_col, tokens, middle, cot, mixed, context, lse, back,
        gain1, shift1, w_qkv, w_out, gain2, bias_back, f_part,
    )


def per_device(
    tokens, token_ids, lengths, hash_table, capacity, gain_one, shift_one, w_qkv, w_out,
    gain_two, shift_two, w_in, bias_in, w_back, bias_back, cotangent,
):
    n_exp, n_hid = lax.axis_size("exp"), lax.axis_size("hid")
    tok, width = tokens.shape
    lc, _, ff = w_in.shape
    cap = 2 * tok // capacity.shape[0]
    table_rows = -(-hash_table.shape[0] // 1024) * 8
    table = jnp.pad(hash_table, (0, table_rows * 128 - hash_table.shape[0])).reshape(table_rows, 128)
    gain1, shift1, gain2, shift2 = (v[None] for v in (gain_one, shift_one, gain_two, shift_two))
    mixed, context, middle, lse, slot, send, grads, first_rows = attend(
        n_exp, n_hid, lc, cap, lengths, token_ids[None], table, capacity[None], tokens, gain1, shift1, w_qkv, w_out, gain2, shift2, cotangent
    )
    back, f_part, wi, wb, gb_in, gb_back = experts(
        n_exp, n_hid, first_rows, send, grads, w_in, bias_in, w_back
    )
    output, g_tokens, mats, norms = attend_back(
        n_exp, n_hid, lengths, slot, tokens, middle, cotangent, mixed, context, lse, back,
        gain1, shift1, w_qkv, w_out, gain2, bias_back, f_part,
    )
    g_in, g_back, g_qkv, g_out, *norms, gb_in, gb_back = finish(wi, wb, mats, norms, gb_in, gb_back)
    return (
        output, g_tokens, norms[0], norms[1], g_qkv, g_out, norms[2], norms[3], g_in, gb_in, g_back, gb_back,
    )


def solution(mesh):
    both = P(("exp", "hid"))
    rows = P(("exp", "hid"), None)
    placed = (
        rows, both, rows, P(), P(), P(), P(), P(), P(), P(), P(),
        P("exp", None, "hid"), P("exp", "hid"), P("exp", "hid", None), P("exp", None), rows,
    )
    return jax.shard_map(
        per_device,
        mesh=mesh,
        in_specs=placed,
        out_specs=(
            rows, rows, P(), P(), P(), P(), P(), P(),
            P("exp", None, "hid"), P("exp", "hid"), P("exp", "hid", None), P("exp", None),
        ),
        check_vma=False,
    )
```

```python
import functools

import jax
import jax.numpy as jnp
from jax import lax
from jax.experimental import pallas as pl
from jax.experimental.pallas import tpu as pltpu
from jax.sharding import PartitionSpec as P

HEADS = 16
MESH = pl.DeviceIdType.MESH
BF = jnp.bfloat16
F32 = jnp.float32
epsilon = 1e-05
masked_score = -1e30
DMA = pltpu.SemaphoreType.DMA
VM = pl.BlockSpec(memory_space=pltpu.VMEM)
SM = pl.BlockSpec(memory_space=pltpu.SMEM)
HB = pl.BlockSpec(memory_space=pl.ANY)
MIB = 1 << 20


def mm(a, b):
    return lax.dot_general(a, b, (((1,), (0,)), ((), ())), preferred_element_type=F32)


def mm_nt(a, b):
    return lax.dot_general(a, b, (((1,), (1,)), ((), ())), preferred_element_type=F32)


def mm_tn(a, b):
    return lax.dot_general(a, b, (((0,), (0,)), ((), ())), preferred_element_type=F32)


def place():
    e = lax.axis_index("exp")
    h = lax.axis_index("hid")
    return e, h, lax.div(h, 2), lax.rem(h, 2)


def rcopy(src, dst, send, recv, dev):
    return pltpu.make_async_remote_copy(
        src_ref=src, dst_ref=dst, send_sem=send, recv_sem=recv, device_id=dev, device_id_type=MESH
    )


def greet(n_exp, n_y):
    e, h, y, c = place()
    sem = pltpu.get_barrier_semaphore()
    for k in range(1, n_exp):
        pl.semaphore_signal(sem, inc=1, device_id=(e ^ k, h), device_id_type=MESH)
    for d in range(1, n_y):
        pl.semaphore_signal(
            sem, inc=1, device_id=(e, lax.rem(y + d, n_y) * 2 + c), device_id_type=MESH
        )
    pl.semaphore_signal(sem, inc=1, device_id=(e, y * 2 + 1 - c), device_id_type=MESH)
    pl.semaphore_wait(sem, n_exp - 1 + n_y)


class Spread:
    def __init__(self, n_exp, n_y, rows, land, sems):
        self.n_exp, self.n_y, self.rows, self.land = n_exp, n_y, rows, land
        self.es, self.er, self.ys, self.yr, self.cs, self.cr = sems
        self.e, self.h, self.y, self.c = place()

    @staticmethod
    def sems(n_exp, n_y):
        return [DMA((n_exp,)), DMA((n_exp,))] + [DMA((n_exp, n_y))] * 4

    def over_exp(self, k):
        return rcopy(
            self.rows.at[self.e ^ k], self.land.at[:, self.e, self.h],
            self.es.at[k], self.er.at[k], (self.e ^ k, self.h),
        )

    def turn(self, i):
        low, high = lax.div(i + 1, 2), self.n_exp // 2 + lax.div(i, 2) - 1
        return jnp.where(i == self.n_exp - 1, self.n_exp - 1, jnp.where(lax.rem(i, 2) == 1, low, high))

    def block(self, k, hid):
        return self.land.at[:, self.e ^ k, hid]

    def over_y(self, k, d):
        blk = self.block(k, self.h)
        dev = (self.e, lax.rem(self.y + d, self.n_y) * 2 + self.c)
        return rcopy(blk, blk, self.ys.at[k, d], self.yr.at[k, d], dev)

    def over_core(self, k, d):
        blk = self.block(k, lax.rem(self.y + self.n_y - d, self.n_y) * 2 + self.c)
        dev = (self.e, self.y * 2 + 1 - self.c)
        return rcopy(blk, blk, self.cs.at[k, d], self.cr.at[k, d], dev)

    def pass_on(self, k):
        @pl.when(k > 0)
        def _():
            self.over_exp(k).wait_recv()

        for d in range(1, self.n_y):
            self.over_y(k, d).start()
        self.over_core(k, 0).start()

    def pass_y(self, k):
        for d in range(1, self.n_y):
            self.over_y(k, d).wait_recv()
            self.over_core(k, d).start()

    def landed(self, k):
        for d in range(self.n_y):
            self.over_core(k, d).wait_recv()

    def sent(self, k):
        @pl.when(k > 0)
        def _():
            self.over_exp(k).wait_send()

        for d in range(1, self.n_y):
            self.over_y(k, d).wait_send()
        for d in range(self.n_y):
            self.over_core(k, d).wait_send()


class Gather:
    def __init__(self, n_exp, n_y, other, mine, pairs, from_y, back, sems):
        self.n_exp, self.n_y, self.other, self.mine = n_exp, n_y, other, mine
        self.pairs, self.from_y, self.back = pairs, from_y, back
        self.es, self.er, self.ys, self.yr, self.cs, self.cr = sems
        self.e, self.h, self.y, self.c = place()

    @staticmethod
    def sems(n_exp, n_y):
        return [DMA((n_exp,)), DMA((n_exp,)), DMA((n_exp, n_y)), DMA((n_exp, n_y)), DMA((n_exp,)), DMA((n_exp,))]

    @staticmethod
    def scratch(n_exp, n_y, lc, cap, d):
        return [
            pltpu.VMEM((n_exp, lc, n_y, cap, d), BF),
            pltpu.VMEM((n_exp, n_y - 1, lc, cap, d), BF),
        ]

    def over_core(self, k):
        t = self.e ^ k
        dev = (self.e, self.y * 2 + 1 - self.c)
        return rcopy(self.other(k), self.pairs.at[t], self.cs.at[k], self.cr.at[k], dev)

    def over_y(self, k, d):
        t = self.e ^ k
        dev = (self.e, lax.rem(self.y + d, self.n_y) * 2 + self.c)
        yy = lax.rem(self.y + d, self.n_y)
        return rcopy(self.pairs.at[t, :, yy], self.from_y.at[t, d - 1], self.ys.at[k, d], self.yr.at[k, d], dev)

    def over_exp(self, k):
        t = self.e ^ k
        return rcopy(self.pairs.at[t, :, self.y], self.back.at[self.e], self.es.at[k], self.er.at[k], (t, self.h))

    def step_core(self, k):
        self.over_core(k).start()

    def fold(self, at, k):
        t = self.e ^ k
        self.over_core(k).wait_recv()
        for yy in range(self.n_y):
            pair = self.pairs[t, :, yy].astype(F32) + self.mine(at, yy).astype(F32)
            self.pairs[t, :, yy] = pair.astype(BF)

    def send_y(self, k):
        for d in range(1, self.n_y):
            self.over_y(k, d).start()

    def step_exp(self, k, extra=None):
        t = self.e ^ k
        total = self.pairs[t, :, self.y].astype(F32)
        for d in range(1, self.n_y):
            self.over_y(k, d).wait_recv()
            total = total + self.from_y[t, d - 1].astype(F32)
        if extra is not None:
            total = total + extra
        total = total.astype(BF)

        @pl.when(k == 0)
        def _():
            self.back[t] = total

        @pl.when(k > 0)
        def _():
            self.pairs[t, :, self.y] = total
            self.over_exp(k).start()

    def sent(self, k):
        for d in range(1, self.n_y):
            self.over_y(k, d).wait_send()

        @pl.when(k > 0)
        def _():
            self.over_exp(k).wait_send()


def norm_rows(rows, gain, shift):
    mean = jnp.mean(rows, axis=-1, keepdims=True)
    centred = rows - mean
    var = jnp.mean(centred * centred, axis=-1, keepdims=True)
    inverse = lax.rsqrt(var + epsilon)
    unit = centred * inverse
    return unit * gain + shift, unit, inverse


def norm_back(upstream, unit, inverse, gain):
    scaled = upstream * gain
    inner = (
        scaled
        - jnp.mean(scaled, axis=-1, keepdims=True)
        - unit * jnp.mean(scaled * unit, axis=-1, keepdims=True)
    )
    return inner * inverse


def turned(values):
    if values.shape[1] == 1:
        return jnp.broadcast_to(values, (values.shape[0], 128)).T
    return jnp.broadcast_to(values, (128, values.shape[1])).T


def token_slots(token_ids, hash_table, capacity, cap):
    tok = token_ids.shape[1]
    ids = turned(token_ids.astype(F32)).astype(jnp.int32)
    row, col = lax.shift_right_logical(ids, 7), ids & 127
    n_rows = hash_table.shape[0]
    lanes = lax.broadcasted_iota(jnp.int32, (tok, 128), 1)
    is_row = jnp.where(lanes[:, :n_rows] == row[:, :n_rows], 1.0, 0.0).astype(BF)
    found = mm(is_row, hash_table.astype(F32).astype(BF))
    chosen = jnp.sum(jnp.where(lanes == col, found, 0.0), axis=1, keepdims=True)
    n_experts = capacity.shape[1]
    ids_e = lax.broadcasted_iota(jnp.int32, (tok, n_experts), 1)
    onehot = jnp.where(ids_e == chosen.astype(jnp.int32), 1.0, 0.0)
    here = lax.broadcasted_iota(jnp.int32, (tok, tok), 0)
    there = lax.broadcasted_iota(jnp.int32, (tok, tok), 1)
    before = mm(jnp.where(here > there, 1.0, 0.0).astype(BF), onehot.astype(BF))
    rank = jnp.sum(before * onehot, axis=1, keepdims=True)
    limit = jnp.sum(capacity.astype(F32) * onehot, axis=1, keepdims=True)
    return jnp.where(rank < limit, chosen * cap + rank, -1.0)


def slot_block(slot_row, first, count):
    tok = slot_row.shape[1]
    ids = lax.broadcasted_iota(jnp.int32, (count, tok), 0) + first
    return jnp.where(slot_row == ids, 1.0, 0.0).astype(BF)


def tok_block(slot_col, first, count):
    ids = lax.broadcasted_iota(jnp.int32, (slot_col.shape[0], count), 1) + first
    return jnp.where(slot_col == ids, 1.0, 0.0).astype(BF)


def doc_bias(lens, tok):
    q = lax.broadcasted_iota(jnp.int32, (tok, tok), 0)
    k = lax.broadcasted_iota(jnp.int32, (tok, tok), 1)
    dq = jnp.zeros((tok, tok), jnp.int32)
    dk = jnp.zeros((tok, tok), jnp.int32)
    end = 0
    for j in range(lens.shape[1]):
        end = end + lens[0, j]
        dq = dq + jnp.where(q >= end, 1, 0)
        dk = dk + jnp.where(k >= end, 1, 0)
    return jnp.where((dq == dk) & (q >= k), 0.0, masked_score)


def attend_kernel(
    n_exp, n_y, lens, token_ids, hash_table, capacity, tokens, gain1, shift1, w_qkv, w_out, gain2, shift2, cot,
    mixed_h, context_h, middle_h, lse, slot_col, send_h, land, first_rows,
    slot_row, mixed, context, middle, send, cot_rows, normed, bias, wq_v, wo_v, in_sem, out_sem, own_sem, first_s, first_r, *sems,
):
    tok, width = tokens.shape
    e, h, y, c = place()
    lc, cap = send.shape[1], send.shape[2]
    per = lc * cap
    hd = width // HEADS
    spread = Spread(n_exp, n_y, cot_rows, land, sems)
    loads = [
        pltpu.make_async_copy(w_qkv, wq_v, in_sem.at[0]),
        pltpu.make_async_copy(w_out, wo_v, in_sem.at[1]),
    ]
    stores = [
        pltpu.make_async_copy(a, b, out_sem.at[i])
        for i, (a, b) in enumerate(
            ((mixed, mixed_h), (context, context_h), (middle, middle_h), (send, send_h))
        )
    ]
    for cp in loads:
        cp.start()

    slots = token_slots(token_ids[...], hash_table[...], capacity[...], cap)
    slot_col[...] = slots.astype(jnp.int32)
    slot_row[...] = turned(slots)[:1].astype(jnp.int32)

    def pick(source, dst):
        rows = mm(slot_block(slot_row[...], dst * per, per), source)
        return rows.astype(BF).reshape(lc, cap, width)

    def advance(k):
        spread.pass_on(k)

        @pl.when(k > 1)
        def _():
            spread.pass_y(k - 2)

    def first(k):
        return rcopy(
            send.at[e ^ k, 0], first_rows.at[e], first_s.at[k], first_r.at[k], (e ^ k, h)
        )

    cot_rows[e] = pick(cot[...], e)
    own = pltpu.make_async_copy(cot_rows.at[e], land.at[:, e, h], own_sem)
    own.start()
    greet(n_exp, n_y)

    @pl.loop(1, n_exp)
    def _(i):
        k = spread.turn(i)
        cot_rows[e ^ k] = pick(cot[...], e ^ k)
        spread.over_exp(k).start()

    own.wait()
    spread.pass_on(0)

    @pl.loop(0, tok // 128)
    def _(i):
        rows = pl.ds(i * 128, 128)
        out, _, _ = norm_rows(tokens[rows].astype(F32), gain1[...], shift1[...])
        normed[rows] = out.astype(BF)

    bias[...] = doc_bias(lens, tok)
    loads[0].wait()

    @pl.loop(0, 3)
    def _(i):
        @pl.when(i > 0)
        def _():
            advance(i)

        for j in range(width // 512):
            cols = pl.ds(pl.multiple_of(i * width + j * 512, 512), 512)
            mixed[:, cols] = mm(normed[...], wq_v[:, cols]).astype(BF)

    stores[0].start()
    advance(3)
    lse[...] = jnp.zeros_like(lse)
    lane = lax.broadcasted_iota(jnp.int32, (1, 128), 1)
    n_pairs = width // 128
    half = tok // 2
    heads_in = 128 // hd

    @pl.loop(0, n_pairs)
    def _(p):
        @pl.when((lax.rem(p, 2) == 1) & (p < 6))
        def _():
            advance(4 + lax.div(p, 2))

        def cols(part):
            return pl.ds(pl.multiple_of(part * width + p * 128, 128), 128)

        q, key, val = mixed[:, cols(0)], mixed[:, cols(1)], mixed[:, cols(2)]
        for blk in range(2):
            rows = slice(blk * half, (blk + 1) * half)
            n_keys = (blk + 1) * half
            total = jnp.zeros((half, 128), F32)
            lses = lse[rows, :]
            for hh in range(heads_in):
                own_lanes = (lane >= hh * hd) & (lane < (hh + 1) * hd)
                qh = jnp.where(own_lanes, q[rows] * BF(hd**-0.5), BF(0))
                vh = jnp.where(own_lanes, val[:n_keys], BF(0))
                s = mm_nt(qh, key[:n_keys]) + bias[rows, :n_keys]
                top = jnp.max(s, axis=-1, keepdims=True)
                ex = jnp.exp(s - top)
                tot = jnp.sum(ex, axis=-1, keepdims=True)
                probs = (ex * (1.0 / tot)).astype(BF)
                total = total + mm(probs, vh)
                lses = jnp.where(lane == p * heads_in + hh, top + jnp.log(tot), lses)
            lse[rows, :] = lses
            context[rows, pl.ds(pl.multiple_of(p * 128, 128), 128)] = total.astype(BF)

    stores[1].start()
    loads[1].wait()

    @pl.loop(0, tok // 256)
    def _(i):
        rows = pl.ds(pl.multiple_of(i * 256, 256), 256)
        mid = tokens[rows].astype(F32) + mm(context[rows], wo_v[...])
        middle[rows] = mid
        out, _, _ = norm_rows(mid, gain2[...], shift2[...])
        normed[rows] = out.astype(BF)

    stores[2].start()

    @pl.loop(0, n_exp)
    def _(k):
        send[k] = pick(normed[...], k)

    stores[3].start()
    own_first = pltpu.make_async_copy(send.at[e, 0], first_rows.at[e], own_sem)
    own_first.start()

    @pl.loop(1, n_exp)
    def _(k):
        first(k).start()

    @pl.loop(7, n_exp)
    def _(k):
        advance(k)

    spread.pass_y(n_exp - 2)
    spread.pass_y(n_exp - 1)
    for cp in stores:
        cp.wait()
    own_first.wait()

    @pl.loop(1, n_exp)
    def _(k):
        first(k).wait_send()
        first(k).wait_recv()

    @pl.loop(0, n_exp)
    def _(k):
        spread.landed(k)
        spread.sent(k)


def attend(n_exp, n_hid, lc, cap, lens, token_ids, hash_table, capacity, tokens, gain1, shift1, w_qkv, w_out, gain2, shift2, cot):
    n_y = n_hid // 2
    tok, width = tokens.shape
    shape = jax.ShapeDtypeStruct
    return pl.pallas_call(
        functools.partial(attend_kernel, n_exp, n_y),
        name="attend",
        out_shape=(
            shape((tok, 3 * width), BF),
            shape((tok, width), BF),
            shape((tok, width), F32),
            shape((tok, 128), F32),
            shape((tok, 1), jnp.int32),
            shape((n_exp, lc, cap, width), BF),
            shape((lc, n_exp, n_hid, cap, width), BF),
            shape((n_exp, cap, width), BF),
        ),
        in_specs=[SM, VM, VM, VM, VM, VM, VM, HB, HB, VM, VM, VM],
        out_specs=[HB, HB, HB, VM, VM, HB, HB, HB],
        scratch_shapes=[
            pltpu.VMEM((1, tok), jnp.int32),
            pltpu.VMEM((tok, 3 * width), BF),
            pltpu.VMEM((tok, width), BF),
            pltpu.VMEM((tok, width), F32),
            pltpu.VMEM((n_exp, lc, cap, width), BF),
            pltpu.VMEM((n_exp, lc, cap, width), BF),
            pltpu.VMEM((tok, width), BF),
            pltpu.VMEM((tok, tok), F32),
            pltpu.VMEM(w_qkv.shape, BF),
            pltpu.VMEM(w_out.shape, BF),
            DMA((2,)),
            DMA((4,)),
            DMA,
            DMA((n_exp,)),
            DMA((n_exp,)),
            *Spread.sems(n_exp, n_y),
        ],
        compiler_params=pltpu.CompilerParams(
            collective_id=0, has_side_effects=True, vmem_limit_bytes=56 * MIB
        ),
    )(lens, token_ids, hash_table, capacity, tokens, gain1, shift1, w_qkv, w_out, gain2, shift2, cot)


STEP_W = 512


class Halves:
    def __init__(self, n_exp, n_y):
        self.n_exp, self.n_y, self.half = n_exp, n_y, n_exp // 2
        self.e, self.h, self.y, self.c = place()
        self.sibling = (self.e, self.y * 2 + 1 - self.c)

    def range(self, g):
        first = lax.div(self.e, self.half) * self.half
        return pl.ds(pl.multiple_of(first if g == 0 else self.half - first, self.half), self.half)

    def y_peer(self, d):
        return (self.e, lax.rem(self.y + d, self.n_y) * 2 + self.c)


class SpreadExpert(Halves):
    def __init__(self, n_exp, n_y, rows, land, sems):
        super().__init__(n_exp, n_y)
        self.rows, self.land = rows, land
        self.es, self.er, self.ys, self.yr, self.cs, self.cr = sems

    @staticmethod
    def sems(lc, n_exp, n_y):
        return [DMA((lc, n_exp))] * 2 + [DMA((lc, 2, n_y))] * 4

    def over_exp(self, ex, k):
        return rcopy(
            self.rows.at[self.e ^ k, ex], self.land.at[ex, self.e, self.h],
            self.es.at[ex, k], self.er.at[ex, k], (self.e ^ k, self.h),
        )

    def start(self, ex):
        half = self.half
        for i in range(1, self.n_exp):
            self.over_exp(ex, half + i // 2 - 1 if i % 2 == 0 else ((i + 1) // 2 if i < self.n_exp - 1 else i)).start()

    def over_y(self, ex, g, d):
        blk = self.land.at[ex, self.range(g), self.h]
        return rcopy(blk, blk, self.ys.at[ex, g, d], self.yr.at[ex, g, d], self.y_peer(d))

    def over_core(self, ex, g, d):
        hid = lax.rem(self.y + self.n_y - d, self.n_y) * 2 + self.c
        blk = self.land.at[ex, self.range(g), hid]
        return rcopy(blk, blk, self.cs.at[ex, g, d], self.cr.at[ex, g, d], self.sibling)

    def pass_on(self, ex, g, came=False):
        if not came:
            for k in range(max(1, g * self.half), (g + 1) * self.half):
                self.over_exp(ex, k).wait_recv()
        for d in range(1, self.n_y):
            self.over_y(ex, g, d).start()
        self.over_core(ex, g, 0).start()

    def pass_y(self, ex, g):
        for d in range(1, self.n_y):
            self.over_y(ex, g, d).wait_recv()
            self.over_core(ex, g, d).start()

    def landed(self, ex, g):
        for d in range(self.n_y):
            self.over_core(ex, g, d).wait_recv()

    def sent(self, ex):
        @pl.when(ex > 0)
        def _():
            for k in range(1, self.n_exp):
                self.over_exp(ex, k).wait_send()

        for g in range(2):
            for d in range(1, self.n_y):
                self.over_y(ex, g, d).wait_send()
            for d in range(self.n_y):
                self.over_core(ex, g, d).wait_send()


class GatherExpert(Halves):
    def __init__(self, n_exp, n_y, part, pairs, from_y, back, sems):
        super().__init__(n_exp, n_y)
        self.part, self.pairs, self.from_y, self.back = part, pairs, from_y, back
        self.es, self.er, self.ys, self.yr, self.cs, self.cr = sems

    @staticmethod
    def sems(lc, n_exp, n_y):
        return [DMA((lc, n_exp))] * 2 + [DMA((lc, 2, n_y))] * 2 + [DMA((lc, 2))] * 2

    def over_core(self, ex, b):
        return rcopy(
            self.part.at[self.range(b), :, 1 - self.c], self.pairs.at[ex, self.range(b)],
            self.cs.at[ex, b], self.cr.at[ex, b], self.sibling,
        )

    def over_y(self, ex, b, d):
        yy = lax.rem(self.y + d, self.n_y)
        return rcopy(
            self.pairs.at[ex, self.range(b), yy], self.from_y.at[d - 1, ex, self.range(b)],
            self.ys.at[ex, b, d], self.yr.at[ex, b, d], self.y_peer(d),
        )

    def over_exp(self, ex, k):
        t = self.e ^ k
        return rcopy(
            self.pairs.at[ex, t, self.y], self.back.at[self.e, ex], self.es.at[ex, k], self.er.at[ex, k], (t, self.h)
        )

    def stay(self, ex):
        return pltpu.make_async_copy(self.pairs.at[ex, self.e, self.y], self.back.at[self.e, ex], self.es.at[ex, 0])

    def fold(self, ex, b):
        self.over_core(ex, b).wait_recv()
        rows = self.range(b)
        for yy in range(self.n_y):
            pair = self.pairs[ex, rows, yy].astype(F32) + self.part[rows, yy, self.c].astype(F32)
            self.pairs[ex, rows, yy] = pair.astype(BF)
        for d in range(1, self.n_y):
            self.over_y(ex, b, d).start()
        self.over_core(ex, b).wait_send()

    def step_exp(self, ex, b):
        rows = self.range(b)
        total = self.pairs[ex, rows, self.y].astype(F32)
        for d in range(1, self.n_y):
            self.over_y(ex, b, d).wait_recv()
            total = total + self.from_y[d - 1, ex, rows].astype(F32)
        self.pairs[ex, rows, self.y] = total.astype(BF)
        for i in range(self.half):
            k = b * self.half + i
            if k == 0:
                self.stay(ex).start()
            else:
                self.over_exp(ex, k).start()

    def finish(self, ex):
        self.stay(ex).wait()
        for b in range(2):
            for d in range(1, self.n_y):
                self.over_y(ex, b, d).wait_send()
        for k in range(1, self.n_exp):
            self.over_exp(ex, k).wait_send()
            self.over_exp(ex, k).wait_recv()


def expert_kernel(
    n_exp, n_y, first_rows, rows, grads, w_in, bias_in, w_back,
    back, f_out, wi_out, wb_out, gb_in, gb_back,
    land, part, pairs, from_y, wi_v, wb_v, g_v, h_v, gp_v, f_v, wi_st, wb_st,
    w_sem, g_sem, f_sem, o_sem, own_sem, *rest,
):
    e, h, y, c = place()
    n_spread = len(SpreadExpert.sems(1, 1, 1))
    spread = SpreadExpert(n_exp, n_y, rows, land, rest[:n_spread])
    gather = GatherExpert(n_exp, n_y, part, pairs, from_y, back, rest[n_spread:])
    n_hid = 2 * n_y
    lc, cap, width = rows.shape[1:]
    ff = w_in.shape[2]
    n_src = 4
    block = n_src * n_hid * cap
    n_rb = n_exp // n_src
    step_f = min(512, ff)
    step_w = STEP_W

    def weights(ex):
        slot = lax.rem(ex, 2)
        return (
            pltpu.make_async_copy(w_in.at[ex], wi_v.at[slot], w_sem.at[0, slot]),
            pltpu.make_async_copy(w_back.at[ex], wb_v.at[slot], w_sem.at[1, slot]),
        )

    def g_copy(ex):
        slot = lax.rem(ex, 2)
        return pltpu.make_async_copy(grads.at[ex], g_v.at[slot], g_sem.at[slot])

    def f_copy(ex, rb):
        return pltpu.make_async_copy(f_v, f_out.at[ex, sources(rb)], f_sem)

    def wi_copy(ex, i):
        return pltpu.make_async_copy(wi_st, wi_out.at[ex, pl.ds(i * step_w, step_w)], o_sem.at[0])

    def wb_copy(ex, i):
        return pltpu.make_async_copy(wb_st, wb_out.at[ex, pl.ds(i * step_w, step_w)], o_sem.at[1])

    def sources(rb):
        return pl.ds(lax.rem(lax.div(e, n_exp // 2) * (n_rb // 2) + rb, n_rb) * n_src, n_src)

    own = pltpu.make_async_copy(rows.at[e, pl.ds(1, lc - 1)], land.at[pl.ds(1, lc - 1), e, h], own_sem.at[0])
    own_first = pltpu.make_async_copy(first_rows, land.at[0, :, h], own_sem.at[1])
    own_first.start()
    own.start()
    greet(n_exp, n_y)
    own_first.wait()
    spread.pass_on(0, 0, came=True)
    spread.pass_on(0, 1, came=True)
    spread.start(1)
    for ex in range(2):
        for cp in weights(ex):
            cp.start()
    g_copy(0).start()
    gb_in[...] = jnp.zeros_like(gb_in)
    gb_back[...] = jnp.zeros_like(gb_back)
    own.wait()
    spread.pass_y(0, 0)
    spread.start(2)

    def weight_grads(ex, after):
        slot = lax.rem(ex, 2)

        @pl.loop(0, width // step_w)
        def _(i):
            cols = pl.ds(pl.multiple_of(i * step_w, step_w), step_w)
            x = land[ex, :, :, :, cols].reshape(n_exp * n_hid * cap, step_w)
            piece = mm_tn(x, gp_v[slot].reshape(n_exp * n_hid * cap, ff)).astype(BF)

            @pl.when(i > 0)
            def _():
                wi_copy(ex, i).wait()

            wi_st[...] = piece
            wi_copy(ex, i).start()
            after(i)

        @pl.loop(0, ff // step_w)
        def _(i):
            cols = pl.ds(pl.multiple_of(i * step_w, step_w), step_w)
            hid = h_v[slot, :, :, cols].reshape(n_exp * n_hid * cap, step_w)
            piece = mm_tn(hid, g_v[slot].reshape(n_exp * n_hid * cap, width)).astype(BF)

            @pl.when(i > 0)
            def _():
                wb_copy(ex, i).wait()

            wb_st[...] = piece
            wb_copy(ex, i).start()

        wi_copy(ex, 0).wait()
        wb_copy(ex, 0).wait()

    @pl.loop(0, lc)
    def _(ex):
        slot = lax.rem(ex, 2)
        g_copy(ex).wait()
        for cp in weights(ex):
            cp.wait()

        @pl.loop(0, n_rb)
        def _(rb):
            at = sources(rb)
            for b in range(2):

                @pl.when(rb == b * (n_rb // 2))
                def _():
                    spread.landed(ex, b)

            x = land[ex, at].reshape(block, width)
            g = g_v[slot, at].reshape(block, width)
            gb_back[pl.ds(ex, 1)] += jnp.sum(g.astype(F32), axis=0, keepdims=True)
            for f in range(ff // step_f):
                cols = slice(f * step_f, (f + 1) * step_f)
                pre = mm(x, wi_v[slot, :, cols]) + bias_in[pl.ds(ex, 1), cols]
                sig = jax.nn.sigmoid(pre)
                hid = (pre * sig).astype(BF)
                gh = mm_nt(g, wb_v[slot, cols, :])
                gp = (gh * sig * (1.0 + pre * (1.0 - sig))).astype(BF)
                gb_in[pl.ds(ex, 1), cols] += jnp.sum(gp.astype(F32), axis=0, keepdims=True)
                h_v[slot, at, :, cols] = hid.reshape(n_src, n_hid * cap, step_f)
                gp_v[slot, at, :, cols] = gp.reshape(n_src, n_hid * cap, step_f)
            gd = mm_nt(gp_v[slot, at].reshape(block, ff), wi_v[slot])
            part[at] = gd.astype(BF).reshape(n_src, n_y, 2, cap, width)

            for b in range(2):

                @pl.when(rb == (b + 1) * (n_rb // 2) - 1)
                def _():
                    gather.over_core(ex, b).start()

                    if b == 0:

                        @pl.when(ex == 0)
                        def _():
                            spread.pass_y(0, 1)

                        @pl.when(ex + 3 < lc)
                        def _():
                            spread.start(ex + 3)

                    @pl.when(ex + 1 < lc)
                    def _():
                        spread.pass_on(ex + 1, b)

                    @pl.when(ex > 0)
                    def _():
                        gather.step_exp(ex - 1, b)

        @pl.loop(0, n_rb)
        def _(rb):
            hv = h_v[slot, sources(rb)].reshape(block, ff)
            f = mm(hv, wb_v[slot]).astype(BF).reshape(n_src, n_y, 2, cap, width)

            @pl.when((ex > 0) | (rb > 0))
            def _():
                f_copy(ex, rb).wait()

            f_v[...] = f
            f_copy(ex, rb).start()

            for b in range(2):

                @pl.when(rb == (b + 1) * (n_rb // 2) - 1)
                def _():
                    gather.fold(ex, b)

                    @pl.when(ex + 1 < lc)
                    def _():
                        spread.pass_y(ex + 1, b)

        @pl.when(ex + 2 < lc)
        def _():
            for cp in weights(ex + 2):
                cp.start()

        @pl.when((ex > 0) & (ex < lc - 1))
        def _():
            weight_grads(ex - 1, lambda i: None)

        @pl.when(ex + 1 < lc)
        def _():
            g_copy(ex + 1).start()

    def nearly(i):
        @pl.when(i == 1)
        def _():
            gather.step_exp(lc - 1, 0)

    def last(i):
        @pl.when(i == 0)
        def _():
            gather.step_exp(lc - 1, 1)

    weight_grads(lc - 2, nearly)
    weight_grads(lc - 1, last)
    f_copy(lc - 1, 0).wait()

    @pl.loop(0, lc)
    def _(ex):
        spread.sent(ex)
        gather.finish(ex)


def experts(n_exp, n_hid, first_rows, rows, grads, w_in, bias_in, w_back):
    n_y = n_hid // 2
    _, lc, cap, width = rows.shape
    ff = w_in.shape[2]
    shape = jax.ShapeDtypeStruct
    per = n_hid * cap
    return pl.pallas_call(
        functools.partial(expert_kernel, n_exp, n_y),
        name="experts",
        out_shape=(
            shape((n_exp, lc, cap, width), BF),
            shape((lc, n_exp, n_y, 2, cap, width), BF),
            shape(w_in.shape, BF),
            shape(w_back.shape, BF),
            shape((lc, ff), F32),
            shape((lc, width), F32),
        ),
        in_specs=[HB, HB, HB, HB, VM, HB],
        out_specs=[HB, HB, HB, HB, VM, VM],
        scratch_shapes=[
            pltpu.VMEM((lc, n_exp, n_hid, cap, width), BF),
            pltpu.VMEM((n_exp, n_y, 2, cap, width), BF),
            pltpu.VMEM((lc, n_exp, n_y, cap, width), BF),
            pltpu.VMEM((n_y - 1, lc, n_exp, cap, width), BF),
            pltpu.VMEM((2, *w_in.shape[1:]), BF),
            pltpu.VMEM((2, *w_back.shape[1:]), BF),
            pltpu.VMEM((2, n_exp, n_hid, cap, width), BF),
            pltpu.VMEM((2, n_exp, per, ff), BF),
            pltpu.VMEM((2, n_exp, per, ff), BF),
            pltpu.VMEM((4, n_y, 2, cap, width), BF),
            pltpu.VMEM((STEP_W, ff), BF),
            pltpu.VMEM((STEP_W, width), BF),
            DMA((2, 2)), DMA((2,)), DMA, DMA((2,)), DMA((2,)),
            *SpreadExpert.sems(lc, n_exp, n_y),
            *GatherExpert.sems(lc, n_exp, n_y),
        ],
        compiler_params=pltpu.CompilerParams(
            collective_id=1, has_side_effects=True, vmem_limit_bytes=63 * MIB
        ),
    )(first_rows, rows, grads, w_in, bias_in, w_back)


def finish_kernel(wi, wb, mats, norms, bi, bb, g_in, g_back, g_qkv, g_out, n0, n1, n2, n3, g_bi, g_bb):
    @pl.when((pl.program_id(0) == 0) & (pl.program_id(1) == 0))
    def _():
        for i, n in enumerate((n0, n1, n2, n3)):
            n[...] = norms[i]
        g_bi[...] = bi[...]
        g_bb[...] = bb[...]

    g_in[...] = wi[...].astype(F32)
    g_back[...] = wb[...].astype(F32)
    rows, width = g_out.shape
    for part in range(3):
        g_qkv[:, part * width : (part + 1) * width] = mats[part + 1].reshape(rows, width).astype(F32)
    g_out[...] = mats[0].reshape(rows, width).astype(F32)


def finish(wi, wb, mats, norms, bi, bb):
    lc, width, ff = wi.shape
    cut = 4
    rows = width // (lc * cut)
    mats = mats.reshape(4, width // 16, 16, width)
    shape = jax.ShapeDtypeStruct
    wi_spec = pl.BlockSpec((1, width // cut, ff), lambda i, j: (i, j, 0))
    wb_spec = pl.BlockSpec((1, ff // cut, width), lambda i, j: (i, j, 0))
    small = [pl.BlockSpec(a.shape, lambda i, j: (0, 0)) for a in (norms, bi, bb)]
    return pl.pallas_call(
        finish_kernel,
        name="finish",
        grid=(lc, cut),
        out_shape=(
            shape(wi.shape, F32), shape(wb.shape, F32),
            shape((width, 3 * width), F32), shape((width, width), F32),
            *[shape((width,), F32)] * 4, shape(bi.shape, F32), shape(bb.shape, F32),
        ),
        in_specs=[
            wi_spec, wb_spec,
            pl.BlockSpec((4, rows // 16, 16, width), lambda i, j: (0, i * cut + j, 0, 0)),
            *small,
        ],
        out_specs=[
            wi_spec, wb_spec,
            pl.BlockSpec((rows, 3 * width), lambda i, j: (i * cut + j, 0)),
            pl.BlockSpec((rows, width), lambda i, j: (i * cut + j, 0)),
            *[pl.BlockSpec((width,), lambda i, j: (0,))] * 4,
            *small[1:],
        ],
        compiler_params=pltpu.CompilerParams(vmem_limit_bytes=56 * MIB),
    )(wi, wb, mats, norms, bi, bb)


EARLY = (2,)


class Reduce:
    lead = 1

    def __init__(self, n_exp, n_y, mats, out, norms, scratch):
        (self.core_in, in1, in2, in3, self.n_acc, self.n_in, self.c_s, self.c_r,
         s1, r1, s2, r2, s3, r3, t3, u3, t2, u2, t1, u1, self.d_s, self.d_r, self.n_s, self.n_r, self.l_s) = scratch
        self.mats, self.out, self.norms = mats, out, norms
        self.e, self.h, self.y, self.c = place()
        self.n_x, self.n_z, self.sub, self.half, self.n_sub = self.sizes(n_exp, n_y, mats.shape[0])
        x, z = lax.rem(self.e, self.n_x), lax.div(self.e, self.n_x)
        self.x, self.z = x, z
        self.at = {"x": (self.n_x, x), "y": (n_y, self.y), "z": (self.n_z, z)}
        self.orders = (("y", "x", "z"), ("x", "y", "z"))
        self.n_axes = (None, "y", "x", "z")
        self.sibling = (self.e, self.y * 2 + 1 - self.c)
        self.lands = (in1, in2, in3)
        self.sends, self.recvs = (s1, s2, s3), (r1, r2, r3)
        self.ups, self.upr = (t1, t2, t3), (u1, u2, u3)

    @staticmethod
    def sizes(n_exp, n_y, n_units):
        n_x = n_y
        n_z = n_exp // n_x
        sub = n_x * n_y * n_z
        half = n_units // 2
        return n_x, n_z, sub, half, half // 2 // sub

    @classmethod
    def scratch(cls, n_exp, n_y, n_units, norms_shape):
        n_x, n_z, sub, half, n_sub = cls.sizes(n_exp, n_y, n_units)
        most = max(n_x, n_y)
        width = norms_shape[1]

        def land(n, count):
            return pltpu.VMEM((2, n_sub, n - 1, count, 16, width), BF)

        def sems(n):
            return [DMA((2, n_sub, n - 1))] * 2

        return [
            pltpu.VMEM((half, 16, width), BF),
            land(most, sub // min(n_x, n_y)),
            land(most, sub // (n_x * n_y)),
            land(n_z, 1),
            pltpu.VMEM((4, *norms_shape), F32),
            pltpu.VMEM((4, max(most, n_z) - 1, *norms_shape), F32),
            DMA((2, n_sub)), DMA((2, n_sub)),
            *sems(most), *sems(most), *sems(n_z), *sems(n_z), *sems(most), *sems(most),
            DMA((2, n_sub)), DMA((2, n_sub)),
            *[DMA((4, max(most, n_z) - 1))] * 2,
            DMA((2, n_sub)),
        ]

    def device(self, axis, o):
        return {
            "x": (self.z * self.n_x + o, self.h), "y": (self.e, o * 2 + self.c), "z": (o * self.n_x + self.x, self.h)
        }[axis]

    def first(self, p, b, core):
        return (b * 4 + core * 2 + p) * self.sub

    def units(self, p, b, depth):
        first, count = self.first(p, b, self.c), self.sub
        for axis in self.orders[p][:depth]:
            n, i = self.at[axis]
            count = count // n
            first = first + i * count
        return first, count

    def core_copy(self, p, b):
        return rcopy(
            self.mats.at[pl.ds(self.first(p, b, 1 - self.c), self.sub)],
            self.core_in.at[pl.ds((b * 2 + p) * self.sub, self.sub)],
            self.c_s.at[p, b], self.c_r.at[p, b], self.sibling,
        )

    def down(self, p, b, stage, d):
        n, i = self.at[self.orders[p][stage]]
        first, count = self.units(p, b, stage)
        count = count // n
        o = lax.rem(i + d, n)
        return rcopy(
            self.mats.at[pl.ds(first + o * count, count)], self.lands[stage].at[p, b, d - 1, pl.ds(0, count)],
            self.sends[stage].at[p, b, d - 1], self.recvs[stage].at[p, b, d - 1],
            self.device(self.orders[p][stage], o),
        )

    def up(self, p, b, stage, d):
        n, i = self.at[self.orders[p][stage]]
        at = pl.ds(*self.units(p, b, stage + 1))
        source = self.mats if stage == 2 else self.out
        o = lax.rem(i + d, n)
        return rcopy(
            source.at[at], self.out.at[at], self.ups[stage].at[p, b, d - 1], self.upr[stage].at[p, b, d - 1],
            self.device(self.orders[p][stage], o),
        )

    def stay(self, p, b):
        at = pl.ds(*self.units(p, b, 3))
        return pltpu.make_async_copy(self.mats.at[at], self.out.at[at], self.l_s.at[p, b])

    def core_up(self, p, b):
        region = self.out.at[pl.ds(*self.units(p, b, 0))]
        return rcopy(region, region, self.d_s.at[p, b], self.d_r.at[p, b], self.sibling)

    def peers(self, p, stage):
        return range(1, self.at[self.orders[p][stage]][0])

    def event(self, p, b, q):
        mats = self.mats
        if q == 0:
            self.core_copy(p, b).wait_recv()
            at = pl.ds(*self.units(p, b, 0))
            other = self.core_in[pl.ds((b * 2 + p) * self.sub, self.sub)]
            mats[at] = (mats[at].astype(F32) + other.astype(F32)).astype(BF)
        elif q <= 3:
            first, count = self.units(p, b, q)
            at = pl.ds(first, count)
            total = mats[at].astype(F32)
            for d in self.peers(p, q - 1):
                self.down(p, b, q - 1, d).wait_recv()
                total = total + self.lands[q - 1][p, b, d - 1, :count].astype(F32)
            mats[at] = total.astype(BF)
            if q == 3:
                self.stay(p, b).start()
        else:
            if q == 4:
                self.stay(p, b).wait()
            for d in self.peers(p, 6 - q):
                self.up(p, b, 6 - q, d).wait_recv()
        if q < 3:
            for d in self.peers(p, q):
                self.down(p, b, q, d).start()
        elif q < 6:
            for d in self.peers(p, 5 - q):
                self.up(p, b, 5 - q, d).start()
        else:
            self.core_up(p, b).start()

    def begin(self, quarter):
        if self.n_sub == 4:
            for p in range(2):
                self.core_copy(p, quarter).start()
        elif quarter == 3:
            for b in range(self.n_sub):
                for p in range(2):
                    self.core_copy(p, b).start()

    def early(self, q):
        if self.n_sub == 4:
            for p in range(2):
                self.event(p, 0, q)

    def n_copy(self, stage, d):
        if stage == 0:
            dev = self.sibling
        else:
            n, i = self.at[self.n_axes[stage]]
            dev = self.device(self.n_axes[stage], lax.rem(i + d, n))
        return rcopy(
            self.n_acc.at[stage], self.n_in.at[stage, d - 1], self.n_s.at[stage, d - 1], self.n_r.at[stage, d - 1], dev
        )

    def n_peers(self, stage):
        return range(1, 2 if stage == 0 else self.at[self.n_axes[stage]][0])

    def n_total(self, stage):
        for d in self.n_peers(stage):
            self.n_copy(stage, d).wait_recv()
        own = self.n_acc[stage]
        if stage == 0:
            return own + self.n_in[0, 0]
        n, i = self.at[self.n_axes[stage]]
        total = jnp.zeros_like(own)
        for m in range(n):
            term = own
            for d in range(1, n):
                term = jnp.where(lax.rem(i + n - d, n) == m, self.n_in[stage, d - 1], term)
            total = total + term
        return total

    def run(self, aside):
        self.n_acc[0] = self.norms[...]
        self.n_copy(0, 1).start()

        ahead = self.n_sub == 4

        @pl.loop(0, self.n_sub - 1 + 6 + (not ahead))
        def _(s):
            for q in range(7):
                if ahead and q >= self.lead:

                    @pl.when(s == q - self.lead)
                    def _():
                        for p in range(2):
                            self.event(p, 0, q)

                b = s - q + (1 if ahead else 0)

                @pl.when((b >= (1 if ahead else 0)) & (b < self.n_sub))
                def _():
                    for p in range(2):
                        self.event(p, b, q)

            for stage in range(1, 4):

                @pl.when(s == stage)
                def _():
                    self.n_acc[stage] = self.n_total(stage - 1)
                    for d in self.n_peers(stage):
                        self.n_copy(stage, d).start()

            aside(s)

        self.norms[...] = self.n_total(3)
        for stage in range(4):
            for d in self.n_peers(stage):
                self.n_copy(stage, d).wait_send()

        @pl.loop(0, self.n_sub)
        def _(b):
            for p in range(2):
                self.core_up(p, b).wait_recv()
                self.core_copy(p, b).wait_send()
                self.core_up(p, b).wait_send()
                for stage in range(3):
                    for d in self.peers(p, stage):
                        self.down(p, b, stage, d).wait_send()
                        self.up(p, b, stage, d).wait_send()


def attend_back_kernel(
    n_exp, n_y, lens, slot_col, tokens_h, middle_h, cot_h, mixed_h, context_h, lse, back_h,
    gain1, shift1, w_qkv_h, w_out_h, gain2, bias_back, f_part,
    output, g_tokens, mats_out, g_norms,
    tokens, middle, cot, mixed, context, back, w_qkv, w_out, g_mats,
    bias, gattn, gctx, n1t, lse_t, mine_v, f_back, mine_sem, in_sem, *rest,
):
    tok, width = tokens.shape
    hd = width // HEADS
    e, h, y, c = place()
    n_gather, n_sems = len(Gather.scratch(1, 2, 1, 1, 1)), len(Gather.sems(1, 1))
    lc, cap = f_back.shape[1:3]
    gather = Gather(
        n_exp, n_y, lambda k: f_part.at[:, e ^ k, :, 1 - c], lambda m, yy: mine_v[lax.rem(m, 4), :, yy],
        *rest[:n_gather], f_back, rest[n_gather : n_gather + n_sems],
    )
    total = Reduce(n_exp, n_y, g_mats, mats_out, g_norms, rest[n_gather + n_sems :])

    def order(m):
        return jnp.where(m < n_exp // 2, m + n_exp // 2, n_exp - 1 - m)

    def fetch(m):
        slot = lax.rem(m, 4)
        return pltpu.make_async_copy(
            f_part.at[:, e ^ order(m), :, c], mine_v.at[slot], mine_sem.at[slot]
        )

    loads = [
        pltpu.make_async_copy(a, b, in_sem.at[i])
        for i, (a, b) in enumerate((
            (back_h, back), (middle_h, middle), (cot_h, cot), (w_out_h, w_out), (tokens_h, tokens),
            (context_h, context), (mixed_h, mixed), (w_qkv_h, w_qkv),
        ))
    ]
    greet(n_exp, n_y)

    @pl.loop(0, n_exp)
    def _(m):
        gather.step_core(order(m))

    for m in range(4):
        fetch(m).start()
    for cp in loads:
        cp.start()

    def leave(m):
        fetch(m).wait()
        gather.fold(m, order(m))
        gather.send_y(order(m))

        @pl.when(m + 4 < n_exp)
        def _():
            fetch(m + 4).start()

    leave(0)
    leave(1)
    for cp in loads[:5]:
        cp.wait()

    g_norms[...] = jnp.zeros_like(g_norms)
    n_slots = n_exp * lc * cap
    n_quarter = width // 16

    def fold(values):
        return jnp.sum(values, axis=0, keepdims=True)

    @pl.loop(0, tok // 256)
    def _(i):
        rows = pl.ds(pl.multiple_of(i * 256, 256), 256)
        table = tok_block(slot_col[rows], 0, n_slots)
        up = mm(table, back[...].reshape(n_slots, width))
        _, unit, inverse = norm_rows(middle[rows], gain2[...], 0.0)
        g_norms[2:3] += fold(up * unit)
        g_norms[3:4] += fold(up)
        g_mid = cot[rows].astype(F32) + norm_back(up, unit, inverse, gain2[...])
        g_tokens[rows] = g_mid
        gattn[rows] = g_mid.astype(BF)
        gctx[rows] = mm_nt(gattn[rows], w_out[...]).astype(BF)
        out, _, _ = norm_rows(tokens[rows].astype(F32), gain1[...], shift1[...])
        n1t[:, rows] = out.astype(BF).T

    leave(2)
    leave(3)
    for cp in loads[5:]:
        cp.wait()

    @pl.loop(0, width // 256)
    def _(i):
        cols = pl.ds(pl.multiple_of(i * 256, 256), 256)
        part = mm_tn(context[:, cols], gattn[...]).astype(BF)
        g_mats[pl.ds(i * 16, 16)] = part.reshape(16, 16, width)

    total.begin(0)
    key_i = lax.broadcasted_iota(jnp.int32, (tok, tok), 0)
    qry_i = lax.broadcasted_iota(jnp.int32, (tok, tok), 1)
    dk_, dq_ = jnp.zeros((tok, tok), jnp.int32), jnp.zeros((tok, tok), jnp.int32)
    end = 0
    for j in range(lens.shape[1]):
        end = end + lens[0, j]
        dk_ = dk_ + jnp.where(key_i >= end, 1, 0)
        dq_ = dq_ + jnp.where(qry_i >= end, 1, 0)
    bias[...] = jnp.where((dk_ == dq_) & (qry_i >= key_i), 0.0, masked_score)
    lse_t[...] = lse[...].T

    lane = lax.broadcasted_iota(jnp.int32, (1, 128), 1)
    n_pairs = width // 128
    half = tok // 2
    heads_in = 128 // hd

    @pl.loop(0, n_pairs)
    def _(p):
        @pl.when(p + 4 < n_exp)
        def _():
            leave(p + 4)

        @pl.when((p >= 2) & (lax.rem(p, 2) == 0))
        def _():
            gather.step_exp(order(lax.div(p, 2) - 1), bias_back[...].reshape(lc, 1, width))

        for q_step, at in enumerate(EARLY):

            @pl.when(p == at)
            def _():
                total.early(q_step)

        def cols(part):
            return pl.ds(pl.multiple_of(part * width + p * 128, 128), 128)

        q, key, val, do = mixed[:, cols(0)], mixed[:, cols(1)], mixed[:, cols(2)], gctx[:, cols(0)]
        dq = [jnp.zeros((half, 128), F32) for _ in range(2)]
        dkey = [jnp.zeros((half, 128), F32) for _ in range(2)]
        dval = [jnp.zeros((half, 128), F32) for _ in range(2)]
        for hh in range(heads_in):
            own_lanes = (lane >= hh * hd) & (lane < (hh + 1) * hd)
            qh = jnp.where(own_lanes, q * BF(hd**-0.5), BF(0))
            kh = jnp.where(own_lanes, key * BF(hd**-0.5), BF(0))
            doh = jnp.where(own_lanes, do, BF(0))
            lrow = lse_t[pl.ds(p * heads_in + hh, 1), :]
            for qb in range(2):
                rows = slice(qb * half, (qb + 1) * half)
                n = (qb + 1) * half
                s = mm_nt(key[:n], qh[rows]) + (bias[:n, rows] - lrow[:, rows])
                pt = jnp.exp(s)
                dp = mm_nt(val[:n], doh[rows])
                inner = jnp.sum(dp * pt, axis=0, keepdims=True)
                ds = (pt * (dp - inner)).astype(BF)
                ptb = pt.astype(BF)
                dv_, dk2 = mm(ptb, doh[rows]), mm(ds, qh[rows])
                for kb in range(qb + 1):
                    part = slice(kb * half, (kb + 1) * half)
                    dval[kb] = dval[kb] + dv_[part]
                    dkey[kb] = dkey[kb] + dk2[part]
                dq[qb] = dq[qb] + mm_tn(ds, kh[:n])
        for b in range(2):
            rows = slice(b * half, (b + 1) * half)
            mixed[rows, cols(0)] = dq[b].astype(BF)
            mixed[rows, cols(1)] = dkey[b].astype(BF)
            mixed[rows, cols(2)] = dval[b].astype(BF)

    def step_exp(m):
        gather.step_exp(order(m), bias_back[...].reshape(lc, 1, width))

    step_exp(3)
    for part in range(3):

        @pl.loop(0, width // 256)
        def _(i):
            rows = pl.ds(pl.multiple_of(i * 256, 256), 256)
            piece = mm(n1t[rows], mixed[:, part * width : (part + 1) * width])
            g_mats[pl.ds((part + 1) * n_quarter + i * 16, 16)] = piece.astype(BF).reshape(16, 16, width)

        total.begin(part + 1)

    @pl.loop(n_pairs + 4, max(n_exp, n_pairs + 4))
    def _(m):
        leave(m)

    step_exp(4)

    @pl.loop(0, tok // 256)
    def _(i):
        rows = pl.ds(pl.multiple_of(i * 256, 256), 256)
        up = mm_nt(mixed[rows], w_qkv[...])
        _, unit, inverse = norm_rows(tokens[rows].astype(F32), gain1[...], 0.0)
        g_norms[0:1] += fold(up * unit)
        g_norms[1:2] += fold(up)
        g_tokens[rows] += norm_back(up, unit, inverse, gain1[...])

    def aside(s):
        @pl.when(s == 0)
        def _():
            @pl.loop(5, n_exp - 2)
            def _(m):
                step_exp(m)

        for j in (1, 2):

            @pl.when(s == j)
            def _():
                step_exp(n_exp - 3 + j)

        @pl.when(s == 5)
        def _():
            @pl.loop(1, n_exp)
            def _(k):
                gather.over_exp(k).wait_recv()

            @pl.loop(0, tok // 256)
            def _(i):
                rows = pl.ds(pl.multiple_of(i * 256, 256), 256)
                table = tok_block(slot_col[rows], 0, n_slots)
                whole = middle[rows] + mm(table, f_back[...].reshape(n_slots, width))
                output[rows] = whole.astype(BF)

    total.run(aside)

    @pl.loop(0, n_exp)
    def _(k):
        gather.over_core(k).wait_send()
        gather.sent(k)


def attend_back(
    n_exp, n_hid, lens, slot_col, tokens, middle, cot, mixed, context, lse, back,
    gain1, shift1, w_qkv, w_out, gain2, bias_back, f_part,
):
    n_y = n_hid // 2
    tok, width = tokens.shape
    _, lc, cap, _ = back.shape
    n_units = 4 * width // 16
    shape = jax.ShapeDtypeStruct
    return pl.pallas_call(
        functools.partial(attend_back_kernel, n_exp, n_y),
        name="attend_back",
        out_shape=(
            shape((tok, width), BF),
            shape((tok, width), F32),
            shape((n_units, 16, width), BF),
            shape((8, width), F32),
        ),
        in_specs=[SM, VM, HB, HB, HB, HB, HB, VM, HB, VM, VM, HB, HB, VM, VM, HB],
        out_specs=[VM, VM, HB, VM],
        scratch_shapes=[
            *[pltpu.VMEM(a.shape, a.dtype) for a in (tokens, middle, cot, mixed, context, back, w_qkv, w_out)],
            pltpu.VMEM((n_units, 16, width), BF),
            pltpu.VMEM((tok, tok), F32),
            pltpu.VMEM((tok, width), BF),
            pltpu.VMEM((tok, width), BF),
            pltpu.VMEM((width, tok), BF),
            pltpu.VMEM((128, tok), F32),
            pltpu.VMEM((4, lc, n_y, cap, width), BF),
            pltpu.VMEM((n_exp, lc, cap, width), BF),
            DMA((4,)),
            DMA((8,)),
            *Gather.scratch(n_exp, n_y, lc, cap, width),
            *Gather.sems(n_exp, n_y),
            *Reduce.scratch(n_exp, n_y, n_units, (8, width)),
        ],
        compiler_params=pltpu.CompilerParams(
            collective_id=2, has_side_effects=True, vmem_limit_bytes=63 * MIB
        ),
    )(
        lens, slot_col, tokens, middle, cot, mixed, context, lse, back,
        gain1, shift1, w_qkv, w_out, gain2, bias_back, f_part,
    )


def per_device(
    tokens, token_ids, lengths, hash_table, capacity, gain_one, shift_one, w_qkv, w_out,
    gain_two, shift_two, w_in, bias_in, w_back, bias_back, cotangent,
):
    n_exp, n_hid = lax.axis_size("exp"), lax.axis_size("hid")
    tok, width = tokens.shape
    lc, _, ff = w_in.shape
    cap = 2 * tok // capacity.shape[0]
    table_rows = -(-hash_table.shape[0] // 1024) * 8
    table = jnp.pad(hash_table, (0, table_rows * 128 - hash_table.shape[0])).reshape(table_rows, 128)
    gain1, shift1, gain2, shift2 = (v[None] for v in (gain_one, shift_one, gain_two, shift_two))
    mixed, context, middle, lse, slot, send, grads, first_rows = attend(
        n_exp, n_hid, lc, cap, lengths, token_ids[None], table, capacity[None], tokens, gain1, shift1, w_qkv, w_out, gain2, shift2, cotangent
    )
    back, f_part, wi, wb, gb_in, gb_back = experts(
        n_exp, n_hid, first_rows, send, grads, w_in, bias_in, w_back
    )
    output, g_tokens, mats, norms = attend_back(
        n_exp, n_hid, lengths, slot, tokens, middle, cotangent, mixed, context, lse, back,
        gain1, shift1, w_qkv, w_out, gain2, bias_back, f_part,
    )
    g_in, g_back, g_qkv, g_out, *norms, gb_in, gb_back = finish(wi, wb, mats, norms, gb_in, gb_back)
    return (
        output, g_tokens, norms[0], norms[1], g_qkv, g_out, norms[2], norms[3], g_in, gb_in, g_back, gb_back,
    )


def solution(mesh):
    both = P(("exp", "hid"))
    rows = P(("exp", "hid"), None)
    placed = (
        rows, both, rows, P(), P(), P(), P(), P(), P(), P(), P(),
        P("exp", None, "hid"), P("exp", "hid"), P("exp", "hid", None), P("exp", None), rows,
    )
    return jax.shard_map(
        per_device,
        mesh=mesh,
        in_specs=placed,
        out_specs=(
            rows, rows, P(), P(), P(), P(), P(), P(),
            P("exp", None, "hid"), P("exp", "hid"), P("exp", "hid", None), P("exp", None),
        ),
        check_vma=False,
    )
```

```python
import functools

import jax
import jax.numpy as jnp
from jax import lax
from jax.experimental import pallas as pl
from jax.experimental.pallas import tpu as pltpu
from jax.sharding import PartitionSpec as P

HEADS = 16
MESH = pl.DeviceIdType.MESH
BF = jnp.bfloat16
F32 = jnp.float32
epsilon = 1e-05
masked_score = -1e30
DMA = pltpu.SemaphoreType.DMA
VM = pl.BlockSpec(memory_space=pltpu.VMEM)
SM = pl.BlockSpec(memory_space=pltpu.SMEM)
HB = pl.BlockSpec(memory_space=pl.ANY)
MIB = 1 << 20


def mm(a, b):
    return lax.dot_general(a, b, (((1,), (0,)), ((), ())), preferred_element_type=F32)


def mm_nt(a, b):
    return lax.dot_general(a, b, (((1,), (1,)), ((), ())), preferred_element_type=F32)


def mm_tn(a, b):
    return lax.dot_general(a, b, (((0,), (0,)), ((), ())), preferred_element_type=F32)


def place():
    e = lax.axis_index("exp")
    h = lax.axis_index("hid")
    return e, h, lax.div(h, 2), lax.rem(h, 2)


def rcopy(src, dst, send, recv, dev):
    return pltpu.make_async_remote_copy(
        src_ref=src, dst_ref=dst, send_sem=send, recv_sem=recv, device_id=dev, device_id_type=MESH
    )


def greet(n_exp, n_y):
    e, h, y, c = place()
    sem = pltpu.get_barrier_semaphore()
    for k in range(1, n_exp):
        pl.semaphore_signal(sem, inc=1, device_id=(e ^ k, h), device_id_type=MESH)
    for d in range(1, n_y):
        pl.semaphore_signal(
            sem, inc=1, device_id=(e, lax.rem(y + d, n_y) * 2 + c), device_id_type=MESH
        )
    pl.semaphore_signal(sem, inc=1, device_id=(e, y * 2 + 1 - c), device_id_type=MESH)
    pl.semaphore_wait(sem, n_exp - 1 + n_y)


class Spread:
    def __init__(self, n_exp, n_y, rows, land, sems):
        self.n_exp, self.n_y, self.rows, self.land = n_exp, n_y, rows, land
        self.es, self.er, self.ys, self.yr, self.cs, self.cr = sems
        self.e, self.h, self.y, self.c = place()

    @staticmethod
    def sems(n_exp, n_y):
        return [DMA((n_exp,)), DMA((n_exp,))] + [DMA((n_exp, n_y))] * 4

    def over_exp(self, k):
        return rcopy(
            self.rows.at[self.e ^ k], self.land.at[:, self.e, self.h],
            self.es.at[k], self.er.at[k], (self.e ^ k, self.h),
        )

    def turn(self, i):
        low, high = lax.div(i + 1, 2), self.n_exp // 2 + lax.div(i, 2) - 1
        return jnp.where(i == self.n_exp - 1, self.n_exp - 1, jnp.where(lax.rem(i, 2) == 1, low, high))

    def block(self, k, hid):
        return self.land.at[:, self.e ^ k, hid]

    def over_y(self, k, d):
        blk = self.block(k, self.h)
        dev = (self.e, lax.rem(self.y + d, self.n_y) * 2 + self.c)
        return rcopy(blk, blk, self.ys.at[k, d], self.yr.at[k, d], dev)

    def over_core(self, k, d):
        blk = self.block(k, lax.rem(self.y + self.n_y - d, self.n_y) * 2 + self.c)
        dev = (self.e, self.y * 2 + 1 - self.c)
        return rcopy(blk, blk, self.cs.at[k, d], self.cr.at[k, d], dev)

    def pass_on(self, k):
        @pl.when(k > 0)
        def _():
            self.over_exp(k).wait_recv()

        for d in range(1, self.n_y):
            self.over_y(k, d).start()
        self.over_core(k, 0).start()

    def pass_y(self, k):
        for d in range(1, self.n_y):
            self.over_y(k, d).wait_recv()
            self.over_core(k, d).start()

    def landed(self, k):
        for d in range(self.n_y):
            self.over_core(k, d).wait_recv()

    def sent(self, k):
        @pl.when(k > 0)
        def _():
            self.over_exp(k).wait_send()

        for d in range(1, self.n_y):
            self.over_y(k, d).wait_send()
        for d in range(self.n_y):
            self.over_core(k, d).wait_send()


class Gather:
    def __init__(self, n_exp, n_y, other, mine, pairs, from_y, back, sems):
        self.n_exp, self.n_y, self.other, self.mine = n_exp, n_y, other, mine
        self.pairs, self.from_y, self.back = pairs, from_y, back
        self.es, self.er, self.ys, self.yr, self.cs, self.cr = sems
        self.e, self.h, self.y, self.c = place()

    @staticmethod
    def sems(n_exp, n_y):
        return [DMA((n_exp,)), DMA((n_exp,)), DMA((n_exp, n_y)), DMA((n_exp, n_y)), DMA((n_exp,)), DMA((n_exp,))]

    @staticmethod
    def scratch(n_exp, n_y, lc, cap, d):
        return [
            pltpu.VMEM((n_exp, lc, n_y, cap, d), BF),
            pltpu.VMEM((n_exp, n_y - 1, lc, cap, d), BF),
        ]

    def over_core(self, k):
        t = self.e ^ k
        dev = (self.e, self.y * 2 + 1 - self.c)
        return rcopy(self.other(k), self.pairs.at[t], self.cs.at[k], self.cr.at[k], dev)

    def over_y(self, k, d):
        t = self.e ^ k
        dev = (self.e, lax.rem(self.y + d, self.n_y) * 2 + self.c)
        yy = lax.rem(self.y + d, self.n_y)
        return rcopy(self.pairs.at[t, :, yy], self.from_y.at[t, d - 1], self.ys.at[k, d], self.yr.at[k, d], dev)

    def over_exp(self, k):
        t = self.e ^ k
        return rcopy(self.pairs.at[t, :, self.y], self.back.at[self.e], self.es.at[k], self.er.at[k], (t, self.h))

    def step_core(self, k):
        self.over_core(k).start()

    def fold(self, at, k):
        t = self.e ^ k
        self.over_core(k).wait_recv()
        for yy in range(self.n_y):
            pair = self.pairs[t, :, yy].astype(F32) + self.mine(at, yy).astype(F32)
            self.pairs[t, :, yy] = pair.astype(BF)

    def send_y(self, k):
        for d in range(1, self.n_y):
            self.over_y(k, d).start()

    def step_exp(self, k, extra=None):
        t = self.e ^ k
        total = self.pairs[t, :, self.y].astype(F32)
        for d in range(1, self.n_y):
            self.over_y(k, d).wait_recv()
            total = total + self.from_y[t, d - 1].astype(F32)
        if extra is not None:
            total = total + extra
        total = total.astype(BF)

        @pl.when(k == 0)
        def _():
            self.back[t] = total

        @pl.when(k > 0)
        def _():
            self.pairs[t, :, self.y] = total
            self.over_exp(k).start()

    def sent(self, k):
        for d in range(1, self.n_y):
            self.over_y(k, d).wait_send()

        @pl.when(k > 0)
        def _():
            self.over_exp(k).wait_send()


def norm_rows(rows, gain, shift):
    mean = jnp.mean(rows, axis=-1, keepdims=True)
    centred = rows - mean
    var = jnp.mean(centred * centred, axis=-1, keepdims=True)
    inverse = lax.rsqrt(var + epsilon)
    unit = centred * inverse
    return unit * gain + shift, unit, inverse


def norm_back(upstream, unit, inverse, gain):
    scaled = upstream * gain
    inner = (
        scaled
        - jnp.mean(scaled, axis=-1, keepdims=True)
        - unit * jnp.mean(scaled * unit, axis=-1, keepdims=True)
    )
    return inner * inverse


def turned(values):
    if values.shape[1] == 1:
        return jnp.broadcast_to(values, (values.shape[0], 128)).T
    return jnp.broadcast_to(values, (128, values.shape[1])).T


def token_slots(token_ids, hash_table, capacity, cap):
    tok = token_ids.shape[1]
    ids = turned(token_ids.astype(F32)).astype(jnp.int32)
    row, col = lax.shift_right_logical(ids, 7), ids & 127
    n_rows = hash_table.shape[0]
    lanes = lax.broadcasted_iota(jnp.int32, (tok, 128), 1)
    is_row = jnp.where(lanes[:, :n_rows] == row[:, :n_rows], 1.0, 0.0).astype(BF)
    found = mm(is_row, hash_table.astype(F32).astype(BF))
    chosen = jnp.sum(jnp.where(lanes == col, found, 0.0), axis=1, keepdims=True)
    n_experts = capacity.shape[1]
    ids_e = lax.broadcasted_iota(jnp.int32, (tok, n_experts), 1)
    onehot = jnp.where(ids_e == chosen.astype(jnp.int32), 1.0, 0.0)
    here = lax.broadcasted_iota(jnp.int32, (tok, tok), 0)
    there = lax.broadcasted_iota(jnp.int32, (tok, tok), 1)
    before = mm(jnp.where(here > there, 1.0, 0.0).astype(BF), onehot.astype(BF))
    rank = jnp.sum(before * onehot, axis=1, keepdims=True)
    limit = jnp.sum(capacity.astype(F32) * onehot, axis=1, keepdims=True)
    return jnp.where(rank < limit, chosen * cap + rank, -1.0)


def slot_block(slot_row, first, count):
    tok = slot_row.shape[1]
    ids = lax.broadcasted_iota(jnp.int32, (count, tok), 0) + first
    return jnp.where(slot_row == ids, 1.0, 0.0).astype(BF)


def tok_block(slot_col, first, count):
    ids = lax.broadcasted_iota(jnp.int32, (slot_col.shape[0], count), 1) + first
    return jnp.where(slot_col == ids, 1.0, 0.0).astype(BF)


def doc_bias(lens, tok):
    q = lax.broadcasted_iota(jnp.int32, (tok, tok), 0)
    k = lax.broadcasted_iota(jnp.int32, (tok, tok), 1)
    dq = jnp.zeros((tok, tok), jnp.int32)
    dk = jnp.zeros((tok, tok), jnp.int32)
    end = 0
    for j in range(lens.shape[1]):
        end = end + lens[0, j]
        dq = dq + jnp.where(q >= end, 1, 0)
        dk = dk + jnp.where(k >= end, 1, 0)
    return jnp.where((dq == dk) & (q >= k), 0.0, masked_score)


def attend_kernel(
    n_exp, n_y, lens, token_ids, hash_table, capacity, tokens, gain1, shift1, w_qkv, w_out, gain2, shift2, cot,
    mixed_h, context_h, middle_h, lse, slot_col, send_h, land, first_rows,
    slot_row, mixed, context, middle, send, cot_rows, normed, bias, wq_v, wo_v, in_sem, out_sem, own_sem, first_s, first_r, *sems,
):
    tok, width = tokens.shape
    e, h, y, c = place()
    lc, cap = send.shape[1], send.shape[2]
    per = lc * cap
    hd = width // HEADS
    spread = Spread(n_exp, n_y, cot_rows, land, sems)
    loads = [
        pltpu.make_async_copy(w_qkv, wq_v, in_sem.at[0]),
        pltpu.make_async_copy(w_out, wo_v, in_sem.at[1]),
    ]
    stores = [
        pltpu.make_async_copy(a, b, out_sem.at[i])
        for i, (a, b) in enumerate(
            ((mixed, mixed_h), (context, context_h), (middle, middle_h), (send, send_h))
        )
    ]
    for cp in loads:
        cp.start()

    slots = token_slots(token_ids[...], hash_table[...], capacity[...], cap)
    slot_col[...] = slots.astype(jnp.int32)
    slot_row[...] = turned(slots)[:1].astype(jnp.int32)

    def pick(source, dst):
        rows = mm(slot_block(slot_row[...], dst * per, per), source)
        return rows.astype(BF).reshape(lc, cap, width)

    def advance(k):
        spread.pass_on(k)

        @pl.when(k > 1)
        def _():
            spread.pass_y(k - 2)

    def first(k):
        return rcopy(
            send.at[e ^ k, 0], first_rows.at[e], first_s.at[k], first_r.at[k], (e ^ k, h)
        )

    cot_rows[e] = pick(cot[...], e)
    own = pltpu.make_async_copy(cot_rows.at[e], land.at[:, e, h], own_sem)
    own.start()
    greet(n_exp, n_y)

    @pl.loop(1, n_exp)
    def _(i):
        k = spread.turn(i)
        cot_rows[e ^ k] = pick(cot[...], e ^ k)
        spread.over_exp(k).start()

    own.wait()
    spread.pass_on(0)

    @pl.loop(0, tok // 128)
    def _(i):
        rows = pl.ds(i * 128, 128)
        out, _, _ = norm_rows(tokens[rows].astype(F32), gain1[...], shift1[...])
        normed[rows] = out.astype(BF)

    bias[...] = doc_bias(lens, tok)
    loads[0].wait()

    @pl.loop(0, 3)
    def _(i):
        @pl.when(i > 0)
        def _():
            advance(i)

        for j in range(width // 512):
            cols = pl.ds(pl.multiple_of(i * width + j * 512, 512), 512)
            mixed[:, cols] = mm(normed[...], wq_v[:, cols]).astype(BF)

    stores[0].start()
    advance(3)
    lse[...] = jnp.zeros_like(lse)
    lane = lax.broadcasted_iota(jnp.int32, (1, 128), 1)
    n_pairs = width // 128
    half = tok // 2
    heads_in = 128 // hd

    @pl.loop(0, n_pairs)
    def _(p):
        @pl.when((lax.rem(p, 2) == 1) & (p < 6))
        def _():
            advance(4 + lax.div(p, 2))

        def cols(part):
            return pl.ds(pl.multiple_of(part * width + p * 128, 128), 128)

        q, key, val = mixed[:, cols(0)], mixed[:, cols(1)], mixed[:, cols(2)]
        for blk in range(2):
            rows = slice(blk * half, (blk + 1) * half)
            n_keys = (blk + 1) * half
            total = jnp.zeros((half, 128), F32)
            lses = lse[rows, :]
            for hh in range(heads_in):
                own_lanes = (lane >= hh * hd) & (lane < (hh + 1) * hd)
                qh = jnp.where(own_lanes, q[rows] * BF(hd**-0.5), BF(0))
                vh = jnp.where(own_lanes, val[:n_keys], BF(0))
                s = mm_nt(qh, key[:n_keys]) + bias[rows, :n_keys]
                top = jnp.max(s, axis=-1, keepdims=True)
                ex = jnp.exp(s - top)
                tot = jnp.sum(ex, axis=-1, keepdims=True)
                probs = (ex * (1.0 / tot)).astype(BF)
                total = total + mm(probs, vh)
                lses = jnp.where(lane == p * heads_in + hh, top + jnp.log(tot), lses)
            lse[rows, :] = lses
            context[rows, pl.ds(pl.multiple_of(p * 128, 128), 128)] = total.astype(BF)

    stores[1].start()
    loads[1].wait()

    @pl.loop(0, tok // 256)
    def _(i):
        rows = pl.ds(pl.multiple_of(i * 256, 256), 256)
        mid = tokens[rows].astype(F32) + mm(context[rows], wo_v[...])
        middle[rows] = mid
        out, _, _ = norm_rows(mid, gain2[...], shift2[...])
        normed[rows] = out.astype(BF)

    stores[2].start()

    @pl.loop(0, n_exp)
    def _(k):
        send[k] = pick(normed[...], k)

    stores[3].start()
    own_first = pltpu.make_async_copy(send.at[e, 0], first_rows.at[e], own_sem)
    own_first.start()

    @pl.loop(1, n_exp)
    def _(k):
        first(k).start()

    @pl.loop(7, n_exp)
    def _(k):
        advance(k)

    spread.pass_y(n_exp - 2)
    spread.pass_y(n_exp - 1)
    for cp in stores:
        cp.wait()
    own_first.wait()

    @pl.loop(1, n_exp)
    def _(k):
        first(k).wait_send()
        first(k).wait_recv()

    @pl.loop(0, n_exp)
    def _(k):
        spread.landed(k)
        spread.sent(k)


def attend(n_exp, n_hid, lc, cap, lens, token_ids, hash_table, capacity, tokens, gain1, shift1, w_qkv, w_out, gain2, shift2, cot):
    n_y = n_hid // 2
    tok, width = tokens.shape
    shape = jax.ShapeDtypeStruct
    return pl.pallas_call(
        functools.partial(attend_kernel, n_exp, n_y),
        name="attend",
        out_shape=(
            shape((tok, 3 * width), BF),
            shape((tok, width), BF),
            shape((tok, width), F32),
            shape((tok, 128), F32),
            shape((tok, 1), jnp.int32),
            shape((n_exp, lc, cap, width), BF),
            shape((lc, n_exp, n_hid, cap, width), BF),
            shape((n_exp, cap, width), BF),
        ),
        in_specs=[SM, VM, VM, VM, VM, VM, VM, HB, HB, VM, VM, VM],
        out_specs=[HB, HB, HB, VM, VM, HB, HB, HB],
        scratch_shapes=[
            pltpu.VMEM((1, tok), jnp.int32),
            pltpu.VMEM((tok, 3 * width), BF),
            pltpu.VMEM((tok, width), BF),
            pltpu.VMEM((tok, width), F32),
            pltpu.VMEM((n_exp, lc, cap, width), BF),
            pltpu.VMEM((n_exp, lc, cap, width), BF),
            pltpu.VMEM((tok, width), BF),
            pltpu.VMEM((tok, tok), F32),
            pltpu.VMEM(w_qkv.shape, BF),
            pltpu.VMEM(w_out.shape, BF),
            DMA((2,)),
            DMA((4,)),
            DMA,
            DMA((n_exp,)),
            DMA((n_exp,)),
            *Spread.sems(n_exp, n_y),
        ],
        compiler_params=pltpu.CompilerParams(
            collective_id=0, has_side_effects=True, vmem_limit_bytes=56 * MIB
        ),
    )(lens, token_ids, hash_table, capacity, tokens, gain1, shift1, w_qkv, w_out, gain2, shift2, cot)


STEP_W = 512


class Halves:
    def __init__(self, n_exp, n_y):
        self.n_exp, self.n_y, self.half = n_exp, n_y, n_exp // 2
        self.e, self.h, self.y, self.c = place()
        self.sibling = (self.e, self.y * 2 + 1 - self.c)

    def range(self, g):
        first = lax.div(self.e, self.half) * self.half
        return pl.ds(pl.multiple_of(first if g == 0 else self.half - first, self.half), self.half)

    def y_peer(self, d):
        return (self.e, lax.rem(self.y + d, self.n_y) * 2 + self.c)


class SpreadExpert(Halves):
    def __init__(self, n_exp, n_y, rows, land, sems):
        super().__init__(n_exp, n_y)
        self.rows, self.land = rows, land
        self.es, self.er, self.ys, self.yr, self.cs, self.cr = sems

    @staticmethod
    def sems(lc, n_exp, n_y):
        return [DMA((lc, n_exp))] * 2 + [DMA((lc, 2, n_y))] * 4

    def over_exp(self, ex, k):
        return rcopy(
            self.rows.at[self.e ^ k, ex], self.land.at[ex, self.e, self.h],
            self.es.at[ex, k], self.er.at[ex, k], (self.e ^ k, self.h),
        )

    def start(self, ex):
        half = self.half
        for i in range(1, self.n_exp):
            self.over_exp(ex, half + i // 2 - 1 if i % 2 == 0 else ((i + 1) // 2 if i < self.n_exp - 1 else i)).start()

    def over_y(self, ex, g, d):
        blk = self.land.at[ex, self.range(g), self.h]
        return rcopy(blk, blk, self.ys.at[ex, g, d], self.yr.at[ex, g, d], self.y_peer(d))

    def over_core(self, ex, g, d):
        hid = lax.rem(self.y + self.n_y - d, self.n_y) * 2 + self.c
        blk = self.land.at[ex, self.range(g), hid]
        return rcopy(blk, blk, self.cs.at[ex, g, d], self.cr.at[ex, g, d], self.sibling)

    def pass_on(self, ex, g, came=False):
        if not came:
            for k in range(max(1, g * self.half), (g + 1) * self.half):
                self.over_exp(ex, k).wait_recv()
        for d in range(1, self.n_y):
            self.over_y(ex, g, d).start()
        self.over_core(ex, g, 0).start()

    def pass_y(self, ex, g):
        for d in range(1, self.n_y):
            self.over_y(ex, g, d).wait_recv()
            self.over_core(ex, g, d).start()

    def landed(self, ex, g):
        for d in range(self.n_y):
            self.over_core(ex, g, d).wait_recv()

    def sent(self, ex):
        @pl.when(ex > 0)
        def _():
            for k in range(1, self.n_exp):
                self.over_exp(ex, k).wait_send()

        for g in range(2):
            for d in range(1, self.n_y):
                self.over_y(ex, g, d).wait_send()
            for d in range(self.n_y):
                self.over_core(ex, g, d).wait_send()


class GatherExpert(Halves):
    def __init__(self, n_exp, n_y, part, pairs, from_y, back, sems):
        super().__init__(n_exp, n_y)
        self.part, self.pairs, self.from_y, self.back = part, pairs, from_y, back
        self.es, self.er, self.ys, self.yr, self.cs, self.cr = sems

    @staticmethod
    def sems(lc, n_exp, n_y):
        return [DMA((lc, n_exp))] * 2 + [DMA((lc, 2, n_y))] * 2 + [DMA((lc, 2))] * 2

    def over_core(self, ex, b):
        return rcopy(
            self.part.at[self.range(b), :, 1 - self.c], self.pairs.at[ex, self.range(b)],
            self.cs.at[ex, b], self.cr.at[ex, b], self.sibling,
        )

    def over_y(self, ex, b, d):
        yy = lax.rem(self.y + d, self.n_y)
        return rcopy(
            self.pairs.at[ex, self.range(b), yy], self.from_y.at[d - 1, ex, self.range(b)],
            self.ys.at[ex, b, d], self.yr.at[ex, b, d], self.y_peer(d),
        )

    def over_exp(self, ex, k):
        t = self.e ^ k
        return rcopy(
            self.pairs.at[ex, t, self.y], self.back.at[self.e, ex], self.es.at[ex, k], self.er.at[ex, k], (t, self.h)
        )

    def stay(self, ex):
        return pltpu.make_async_copy(self.pairs.at[ex, self.e, self.y], self.back.at[self.e, ex], self.es.at[ex, 0])

    def fold(self, ex, b):
        self.over_core(ex, b).wait_recv()
        rows = self.range(b)
        for yy in range(self.n_y):
            pair = self.pairs[ex, rows, yy].astype(F32) + self.part[rows, yy, self.c].astype(F32)
            self.pairs[ex, rows, yy] = pair.astype(BF)
        for d in range(1, self.n_y):
            self.over_y(ex, b, d).start()
        self.over_core(ex, b).wait_send()

    def step_exp(self, ex, b):
        rows = self.range(b)
        total = self.pairs[ex, rows, self.y].astype(F32)
        for d in range(1, self.n_y):
            self.over_y(ex, b, d).wait_recv()
            total = total + self.from_y[d - 1, ex, rows].astype(F32)
        self.pairs[ex, rows, self.y] = total.astype(BF)
        for i in range(self.half):
            k = b * self.half + i
            if k == 0:
                self.stay(ex).start()
            else:
                self.over_exp(ex, k).start()

    def finish(self, ex):
        self.stay(ex).wait()
        for b in range(2):
            for d in range(1, self.n_y):
                self.over_y(ex, b, d).wait_send()
        for k in range(1, self.n_exp):
            self.over_exp(ex, k).wait_send()
            self.over_exp(ex, k).wait_recv()


def expert_kernel(
    n_exp, n_y, first_rows, rows, grads, w_in, bias_in, w_back,
    back, f_out, wi_out, wb_out, gb_in, gb_back,
    land, part, pairs, from_y, wi_v, wb_v, g_v, h_v, gp_v, f_v, wi_st, wb_st,
    w_sem, g_sem, f_sem, o_sem, own_sem, *rest,
):
    e, h, y, c = place()
    n_spread = len(SpreadExpert.sems(1, 1, 1))
    spread = SpreadExpert(n_exp, n_y, rows, land, rest[:n_spread])
    gather = GatherExpert(n_exp, n_y, part, pairs, from_y, back, rest[n_spread:])
    n_hid = 2 * n_y
    lc, cap, width = rows.shape[1:]
    ff = w_in.shape[2]
    n_src = 4
    block = n_src * n_hid * cap
    n_rb = n_exp // n_src
    step_f = min(512, ff)
    step_w = STEP_W

    def weights(ex):
        slot = lax.rem(ex, 2)
        return (
            pltpu.make_async_copy(w_in.at[ex], wi_v.at[slot], w_sem.at[0, slot]),
            pltpu.make_async_copy(w_back.at[ex], wb_v.at[slot], w_sem.at[1, slot]),
        )

    def g_copy(ex):
        slot = lax.rem(ex, 2)
        return pltpu.make_async_copy(grads.at[ex], g_v.at[slot], g_sem.at[slot])

    def f_copy(ex, rb):
        return pltpu.make_async_copy(f_v, f_out.at[ex, sources(rb)], f_sem)

    def wi_copy(ex, i):
        return pltpu.make_async_copy(wi_st, wi_out.at[ex, pl.ds(i * step_w, step_w)], o_sem.at[0])

    def wb_copy(ex, i):
        return pltpu.make_async_copy(wb_st, wb_out.at[ex, pl.ds(i * step_w, step_w)], o_sem.at[1])

    def sources(rb):
        return pl.ds(lax.rem(lax.div(e, n_exp // 2) * (n_rb // 2) + rb, n_rb) * n_src, n_src)

    own = pltpu.make_async_copy(rows.at[e, pl.ds(1, lc - 1)], land.at[pl.ds(1, lc - 1), e, h], own_sem.at[0])
    own_first = pltpu.make_async_copy(first_rows, land.at[0, :, h], own_sem.at[1])
    own_first.start()
    own.start()
    greet(n_exp, n_y)
    own_first.wait()
    spread.pass_on(0, 0, came=True)
    spread.pass_on(0, 1, came=True)
    spread.start(1)
    for ex in range(2):
        for cp in weights(ex):
            cp.start()
    g_copy(0).start()
    gb_in[...] = jnp.zeros_like(gb_in)
    gb_back[...] = jnp.zeros_like(gb_back)
    own.wait()
    spread.pass_y(0, 0)
    spread.start(2)

    def weight_grads(ex, after):
        slot = lax.rem(ex, 2)

        @pl.loop(0, width // step_w)
        def _(i):
            cols = pl.ds(pl.multiple_of(i * step_w, step_w), step_w)
            x = land[ex, :, :, :, cols].reshape(n_exp * n_hid * cap, step_w)
            piece = mm_tn(x, gp_v[slot].reshape(n_exp * n_hid * cap, ff)).astype(BF)

            @pl.when(i > 0)
            def _():
                wi_copy(ex, i).wait()

            wi_st[...] = piece
            wi_copy(ex, i).start()
            after(i)

        @pl.loop(0, ff // step_w)
        def _(i):
            cols = pl.ds(pl.multiple_of(i * step_w, step_w), step_w)
            hid = h_v[slot, :, :, cols].reshape(n_exp * n_hid * cap, step_w)
            piece = mm_tn(hid, g_v[slot].reshape(n_exp * n_hid * cap, width)).astype(BF)

            @pl.when(i > 0)
            def _():
                wb_copy(ex, i).wait()

            wb_st[...] = piece
            wb_copy(ex, i).start()

        wi_copy(ex, 0).wait()
        wb_copy(ex, 0).wait()

    @pl.loop(0, lc)
    def _(ex):
        slot = lax.rem(ex, 2)
        g_copy(ex).wait()
        for cp in weights(ex):
            cp.wait()

        @pl.loop(0, n_rb)
        def _(rb):
            at = sources(rb)
            for b in range(2):

                @pl.when(rb == b * (n_rb // 2))
                def _():
                    spread.landed(ex, b)

            x = land[ex, at].reshape(block, width)
            g = g_v[slot, at].reshape(block, width)
            gb_back[pl.ds(ex, 1)] += jnp.sum(g.astype(F32), axis=0, keepdims=True)
            for f in range(ff // step_f):
                cols = slice(f * step_f, (f + 1) * step_f)
                pre = mm(x, wi_v[slot, :, cols]) + bias_in[pl.ds(ex, 1), cols]
                sig = jax.nn.sigmoid(pre)
                hid = (pre * sig).astype(BF)
                gh = mm_nt(g, wb_v[slot, cols, :])
                gp = (gh * sig * (1.0 + pre * (1.0 - sig))).astype(BF)
                gb_in[pl.ds(ex, 1), cols] += jnp.sum(gp.astype(F32), axis=0, keepdims=True)
                h_v[slot, at, :, cols] = hid.reshape(n_src, n_hid * cap, step_f)
                gp_v[slot, at, :, cols] = gp.reshape(n_src, n_hid * cap, step_f)
            gd = mm_nt(gp_v[slot, at].reshape(block, ff), wi_v[slot])
            part[at] = gd.astype(BF).reshape(n_src, n_y, 2, cap, width)

            for b in range(2):

                @pl.when(rb == (b + 1) * (n_rb // 2) - 1)
                def _():
                    gather.over_core(ex, b).start()

                    if b == 0:

                        @pl.when(ex == 0)
                        def _():
                            spread.pass_y(0, 1)

                        @pl.when(ex + 3 < lc)
                        def _():
                            spread.start(ex + 3)

                    @pl.when(ex + 1 < lc)
                    def _():
                        spread.pass_on(ex + 1, b)

                    @pl.when(ex > 0)
                    def _():
                        gather.step_exp(ex - 1, b)

        @pl.loop(0, n_rb)
        def _(rb):
            hv = h_v[slot, sources(rb)].reshape(block, ff)
            f = mm(hv, wb_v[slot]).astype(BF).reshape(n_src, n_y, 2, cap, width)

            @pl.when((ex > 0) | (rb > 0))
            def _():
                f_copy(ex, rb).wait()

            f_v[...] = f
            f_copy(ex, rb).start()

            for b in range(2):

                @pl.when(rb == (b + 1) * (n_rb // 2) - 1)
                def _():
                    gather.fold(ex, b)

                    @pl.when(ex + 1 < lc)
                    def _():
                        spread.pass_y(ex + 1, b)

        @pl.when(ex + 2 < lc)
        def _():
            for cp in weights(ex + 2):
                cp.start()

        @pl.when((ex > 0) & (ex < lc - 1))
        def _():
            weight_grads(ex - 1, lambda i: None)

        @pl.when(ex + 1 < lc)
        def _():
            g_copy(ex + 1).start()

    def nearly(i):
        @pl.when(i == 1)
        def _():
            gather.step_exp(lc - 1, 0)

    def last(i):
        @pl.when(i == 0)
        def _():
            gather.step_exp(lc - 1, 1)

    weight_grads(lc - 2, nearly)
    weight_grads(lc - 1, last)
    f_copy(lc - 1, 0).wait()

    @pl.loop(0, lc)
    def _(ex):
        spread.sent(ex)
        gather.finish(ex)


def experts(n_exp, n_hid, first_rows, rows, grads, w_in, bias_in, w_back):
    n_y = n_hid // 2
    _, lc, cap, width = rows.shape
    ff = w_in.shape[2]
    shape = jax.ShapeDtypeStruct
    per = n_hid * cap
    return pl.pallas_call(
        functools.partial(expert_kernel, n_exp, n_y),
        name="experts",
        out_shape=(
            shape((n_exp, lc, cap, width), BF),
            shape((lc, n_exp, n_y, 2, cap, width), BF),
            shape(w_in.shape, BF),
            shape(w_back.shape, BF),
            shape((lc, ff), F32),
            shape((lc, width), F32),
        ),
        in_specs=[HB, HB, HB, HB, VM, HB],
        out_specs=[HB, HB, HB, HB, VM, VM],
        scratch_shapes=[
            pltpu.VMEM((lc, n_exp, n_hid, cap, width), BF),
            pltpu.VMEM((n_exp, n_y, 2, cap, width), BF),
            pltpu.VMEM((lc, n_exp, n_y, cap, width), BF),
            pltpu.VMEM((n_y - 1, lc, n_exp, cap, width), BF),
            pltpu.VMEM((2, *w_in.shape[1:]), BF),
            pltpu.VMEM((2, *w_back.shape[1:]), BF),
            pltpu.VMEM((2, n_exp, n_hid, cap, width), BF),
            pltpu.VMEM((2, n_exp, per, ff), BF),
            pltpu.VMEM((2, n_exp, per, ff), BF),
            pltpu.VMEM((4, n_y, 2, cap, width), BF),
            pltpu.VMEM((STEP_W, ff), BF),
            pltpu.VMEM((STEP_W, width), BF),
            DMA((2, 2)), DMA((2,)), DMA, DMA((2,)), DMA((2,)),
            *SpreadExpert.sems(lc, n_exp, n_y),
            *GatherExpert.sems(lc, n_exp, n_y),
        ],
        compiler_params=pltpu.CompilerParams(
            collective_id=1, has_side_effects=True, vmem_limit_bytes=63 * MIB
        ),
    )(first_rows, rows, grads, w_in, bias_in, w_back)


def finish_kernel(wi, wb, mats, norms, bi, bb, g_in, g_back, g_qkv, g_out, n0, n1, n2, n3, g_bi, g_bb):
    @pl.when((pl.program_id(0) == 0) & (pl.program_id(1) == 0))
    def _():
        for i, n in enumerate((n0, n1, n2, n3)):
            n[...] = norms[i]
        g_bi[...] = bi[...]
        g_bb[...] = bb[...]

    g_in[...] = wi[...].astype(F32)
    g_back[...] = wb[...].astype(F32)
    rows, width = g_out.shape
    for part in range(3):
        g_qkv[:, part * width : (part + 1) * width] = mats[part + 1].reshape(rows, width).astype(F32)
    g_out[...] = mats[0].reshape(rows, width).astype(F32)


def finish(wi, wb, mats, norms, bi, bb):
    lc, width, ff = wi.shape
    cut = 4
    rows = width // (lc * cut)
    mats = mats.reshape(4, width // 16, 16, width)
    shape = jax.ShapeDtypeStruct
    wi_spec = pl.BlockSpec((1, width // cut, ff), lambda i, j: (i, j, 0))
    wb_spec = pl.BlockSpec((1, ff // cut, width), lambda i, j: (i, j, 0))
    small = [pl.BlockSpec(a.shape, lambda i, j: (0, 0)) for a in (norms, bi, bb)]
    return pl.pallas_call(
        finish_kernel,
        name="finish",
        grid=(lc, cut),
        out_shape=(
            shape(wi.shape, F32), shape(wb.shape, F32),
            shape((width, 3 * width), F32), shape((width, width), F32),
            *[shape((width,), F32)] * 4, shape(bi.shape, F32), shape(bb.shape, F32),
        ),
        in_specs=[
            wi_spec, wb_spec,
            pl.BlockSpec((4, rows // 16, 16, width), lambda i, j: (0, i * cut + j, 0, 0)),
            *small,
        ],
        out_specs=[
            wi_spec, wb_spec,
            pl.BlockSpec((rows, 3 * width), lambda i, j: (i * cut + j, 0)),
            pl.BlockSpec((rows, width), lambda i, j: (i * cut + j, 0)),
            *[pl.BlockSpec((width,), lambda i, j: (0,))] * 4,
            *small[1:],
        ],
        compiler_params=pltpu.CompilerParams(vmem_limit_bytes=56 * MIB),
    )(wi, wb, mats, norms, bi, bb)


EARLY = (1,)


class Reduce:
    lead = 1

    def __init__(self, n_exp, n_y, mats, out, norms, scratch):
        (self.core_in, in1, in2, in3, self.n_acc, self.n_in, self.c_s, self.c_r,
         s1, r1, s2, r2, s3, r3, t3, u3, t2, u2, t1, u1, self.d_s, self.d_r, self.n_s, self.n_r, self.l_s) = scratch
        self.mats, self.out, self.norms = mats, out, norms
        self.e, self.h, self.y, self.c = place()
        self.n_x, self.n_z, self.sub, self.half, self.n_sub = self.sizes(n_exp, n_y, mats.shape[0])
        x, z = lax.rem(self.e, self.n_x), lax.div(self.e, self.n_x)
        self.x, self.z = x, z
        self.at = {"x": (self.n_x, x), "y": (n_y, self.y), "z": (self.n_z, z)}
        self.orders = (("y", "x", "z"), ("x", "y", "z"))
        self.n_axes = (None, "y", "x", "z")
        self.sibling = (self.e, self.y * 2 + 1 - self.c)
        self.lands = (in1, in2, in3)
        self.sends, self.recvs = (s1, s2, s3), (r1, r2, r3)
        self.ups, self.upr = (t1, t2, t3), (u1, u2, u3)

    @staticmethod
    def sizes(n_exp, n_y, n_units):
        n_x = n_y
        n_z = n_exp // n_x
        sub = n_x * n_y * n_z
        half = n_units // 2
        return n_x, n_z, sub, half, half // 2 // sub

    @classmethod
    def scratch(cls, n_exp, n_y, n_units, norms_shape):
        n_x, n_z, sub, half, n_sub = cls.sizes(n_exp, n_y, n_units)
        most = max(n_x, n_y)
        width = norms_shape[1]

        def land(n, count):
            return pltpu.VMEM((2, n_sub, n - 1, count, 16, width), BF)

        def sems(n):
            return [DMA((2, n_sub, n - 1))] * 2

        return [
            pltpu.VMEM((half, 16, width), BF),
            land(most, sub // min(n_x, n_y)),
            land(most, sub // (n_x * n_y)),
            land(n_z, 1),
            pltpu.VMEM((4, *norms_shape), F32),
            pltpu.VMEM((4, max(most, n_z) - 1, *norms_shape), F32),
            DMA((2, n_sub)), DMA((2, n_sub)),
            *sems(most), *sems(most), *sems(n_z), *sems(n_z), *sems(most), *sems(most),
            DMA((2, n_sub)), DMA((2, n_sub)),
            *[DMA((4, max(most, n_z) - 1))] * 2,
            DMA((2, n_sub)),
        ]

    def device(self, axis, o):
        return {
            "x": (self.z * self.n_x + o, self.h), "y": (self.e, o * 2 + self.c), "z": (o * self.n_x + self.x, self.h)
        }[axis]

    def first(self, p, b, core):
        return (b * 4 + core * 2 + p) * self.sub

    def units(self, p, b, depth):
        first, count = self.first(p, b, self.c), self.sub
        for axis in self.orders[p][:depth]:
            n, i = self.at[axis]
            count = count // n
            first = first + i * count
        return first, count

    def core_copy(self, p, b):
        return rcopy(
            self.mats.at[pl.ds(self.first(p, b, 1 - self.c), self.sub)],
            self.core_in.at[pl.ds((b * 2 + p) * self.sub, self.sub)],
            self.c_s.at[p, b], self.c_r.at[p, b], self.sibling,
        )

    def down(self, p, b, stage, d):
        n, i = self.at[self.orders[p][stage]]
        first, count = self.units(p, b, stage)
        count = count // n
        o = lax.rem(i + d, n)
        return rcopy(
            self.mats.at[pl.ds(first + o * count, count)], self.lands[stage].at[p, b, d - 1, pl.ds(0, count)],
            self.sends[stage].at[p, b, d - 1], self.recvs[stage].at[p, b, d - 1],
            self.device(self.orders[p][stage], o),
        )

    def up(self, p, b, stage, d):
        n, i = self.at[self.orders[p][stage]]
        at = pl.ds(*self.units(p, b, stage + 1))
        source = self.mats if stage == 2 else self.out
        o = lax.rem(i + d, n)
        return rcopy(
            source.at[at], self.out.at[at], self.ups[stage].at[p, b, d - 1], self.upr[stage].at[p, b, d - 1],
            self.device(self.orders[p][stage], o),
        )

    def stay(self, p, b):
        at = pl.ds(*self.units(p, b, 3))
        return pltpu.make_async_copy(self.mats.at[at], self.out.at[at], self.l_s.at[p, b])

    def core_up(self, p, b):
        region = self.out.at[pl.ds(*self.units(p, b, 0))]
        return rcopy(region, region, self.d_s.at[p, b], self.d_r.at[p, b], self.sibling)

    def peers(self, p, stage):
        return range(1, self.at[self.orders[p][stage]][0])

    def event(self, p, b, q):
        mats = self.mats
        if q == 0:
            self.core_copy(p, b).wait_recv()
            at = pl.ds(*self.units(p, b, 0))
            other = self.core_in[pl.ds((b * 2 + p) * self.sub, self.sub)]
            mats[at] = (mats[at].astype(F32) + other.astype(F32)).astype(BF)
        elif q <= 3:
            first, count = self.units(p, b, q)
            at = pl.ds(first, count)
            total = mats[at].astype(F32)
            for d in self.peers(p, q - 1):
                self.down(p, b, q - 1, d).wait_recv()
                total = total + self.lands[q - 1][p, b, d - 1, :count].astype(F32)
            mats[at] = total.astype(BF)
            if q == 3:
                self.stay(p, b).start()
        else:
            if q == 4:
                self.stay(p, b).wait()
            for d in self.peers(p, 6 - q):
                self.up(p, b, 6 - q, d).wait_recv()
        if q < 3:
            for d in self.peers(p, q):
                self.down(p, b, q, d).start()
        elif q < 6:
            for d in self.peers(p, 5 - q):
                self.up(p, b, 5 - q, d).start()
        else:
            self.core_up(p, b).start()

    def begin(self, quarter):
        if self.n_sub == 4:
            for p in range(2):
                self.core_copy(p, quarter).start()
        elif quarter == 3:
            for b in range(self.n_sub):
                for p in range(2):
                    self.core_copy(p, b).start()

    def early(self, q):
        if self.n_sub == 4:
            for p in range(2):
                self.event(p, 0, q)

    def n_copy(self, stage, d):
        if stage == 0:
            dev = self.sibling
        else:
            n, i = self.at[self.n_axes[stage]]
            dev = self.device(self.n_axes[stage], lax.rem(i + d, n))
        return rcopy(
            self.n_acc.at[stage], self.n_in.at[stage, d - 1], self.n_s.at[stage, d - 1], self.n_r.at[stage, d - 1], dev
        )

    def n_peers(self, stage):
        return range(1, 2 if stage == 0 else self.at[self.n_axes[stage]][0])

    def n_total(self, stage):
        for d in self.n_peers(stage):
            self.n_copy(stage, d).wait_recv()
        own = self.n_acc[stage]
        if stage == 0:
            return own + self.n_in[0, 0]
        n, i = self.at[self.n_axes[stage]]
        total = jnp.zeros_like(own)
        for m in range(n):
            term = own
            for d in range(1, n):
                term = jnp.where(lax.rem(i + n - d, n) == m, self.n_in[stage, d - 1], term)
            total = total + term
        return total

    def run(self, aside):
        self.n_acc[0] = self.norms[...]
        self.n_copy(0, 1).start()

        ahead = self.n_sub == 4

        @pl.loop(0, self.n_sub - 1 + 6 + (not ahead))
        def _(s):
            for q in range(7):
                if ahead and q >= self.lead:

                    @pl.when(s == q - self.lead)
                    def _():
                        for p in range(2):
                            self.event(p, 0, q)

                b = s - q + (1 if ahead else 0)

                @pl.when((b >= (1 if ahead else 0)) & (b < self.n_sub))
                def _():
                    for p in range(2):
                        self.event(p, b, q)

            for stage in range(1, 4):

                @pl.when(s == stage)
                def _():
                    self.n_acc[stage] = self.n_total(stage - 1)
                    for d in self.n_peers(stage):
                        self.n_copy(stage, d).start()

            aside(s)

        self.norms[...] = self.n_total(3)
        for stage in range(4):
            for d in self.n_peers(stage):
                self.n_copy(stage, d).wait_send()

        @pl.loop(0, self.n_sub)
        def _(b):
            for p in range(2):
                self.core_up(p, b).wait_recv()
                self.core_copy(p, b).wait_send()
                self.core_up(p, b).wait_send()
                for stage in range(3):
                    for d in self.peers(p, stage):
                        self.down(p, b, stage, d).wait_send()
                        self.up(p, b, stage, d).wait_send()


def attend_back_kernel(
    n_exp, n_y, lens, slot_col, tokens_h, middle_h, cot_h, mixed_h, context_h, lse, back_h,
    gain1, shift1, w_qkv_h, w_out_h, gain2, bias_back, f_part,
    output, g_tokens, mats_out, g_norms,
    tokens, middle, cot, mixed, context, back, w_qkv, w_out, g_mats,
    bias, gattn, gctx, n1t, lse_t, mine_v, f_back, mine_sem, in_sem, *rest,
):
    tok, width = tokens.shape
    hd = width // HEADS
    e, h, y, c = place()
    n_gather, n_sems = len(Gather.scratch(1, 2, 1, 1, 1)), len(Gather.sems(1, 1))
    lc, cap = f_back.shape[1:3]
    gather = Gather(
        n_exp, n_y, lambda k: f_part.at[:, e ^ k, :, 1 - c], lambda m, yy: mine_v[lax.rem(m, 4), :, yy],
        *rest[:n_gather], f_back, rest[n_gather : n_gather + n_sems],
    )
    total = Reduce(n_exp, n_y, g_mats, mats_out, g_norms, rest[n_gather + n_sems :])

    def order(m):
        return jnp.where(m < n_exp // 2, m + n_exp // 2, n_exp - 1 - m)

    def fetch(m):
        slot = lax.rem(m, 4)
        return pltpu.make_async_copy(
            f_part.at[:, e ^ order(m), :, c], mine_v.at[slot], mine_sem.at[slot]
        )

    loads = [
        pltpu.make_async_copy(a, b, in_sem.at[i])
        for i, (a, b) in enumerate((
            (back_h, back), (middle_h, middle), (cot_h, cot), (w_out_h, w_out), (tokens_h, tokens),
            (context_h, context), (mixed_h, mixed), (w_qkv_h, w_qkv),
        ))
    ]
    greet(n_exp, n_y)

    @pl.loop(0, n_exp)
    def _(m):
        gather.step_core(order(m))

    for m in range(4):
        fetch(m).start()
    for cp in loads:
        cp.start()

    def leave(m):
        fetch(m).wait()
        gather.fold(m, order(m))
        gather.send_y(order(m))

        @pl.when(m + 4 < n_exp)
        def _():
            fetch(m + 4).start()

    leave(0)
    leave(1)
    for cp in loads[:5]:
        cp.wait()

    g_norms[...] = jnp.zeros_like(g_norms)
    n_slots = n_exp * lc * cap
    n_quarter = width // 16

    def fold(values):
        return jnp.sum(values, axis=0, keepdims=True)

    @pl.loop(0, tok // 256)
    def _(i):
        rows = pl.ds(pl.multiple_of(i * 256, 256), 256)
        table = tok_block(slot_col[rows], 0, n_slots)
        up = mm(table, back[...].reshape(n_slots, width))
        _, unit, inverse = norm_rows(middle[rows], gain2[...], 0.0)
        g_norms[2:3] += fold(up * unit)
        g_norms[3:4] += fold(up)
        g_mid = cot[rows].astype(F32) + norm_back(up, unit, inverse, gain2[...])
        g_tokens[rows] = g_mid
        gattn[rows] = g_mid.astype(BF)
        gctx[rows] = mm_nt(gattn[rows], w_out[...]).astype(BF)
        out, _, _ = norm_rows(tokens[rows].astype(F32), gain1[...], shift1[...])
        n1t[:, rows] = out.astype(BF).T

    leave(2)
    leave(3)
    for cp in loads[5:]:
        cp.wait()

    @pl.loop(0, width // 256)
    def _(i):
        cols = pl.ds(pl.multiple_of(i * 256, 256), 256)
        part = mm_tn(context[:, cols], gattn[...]).astype(BF)
        g_mats[pl.ds(i * 16, 16)] = part.reshape(16, 16, width)

    total.begin(0)
    key_i = lax.broadcasted_iota(jnp.int32, (tok, tok), 0)
    qry_i = lax.broadcasted_iota(jnp.int32, (tok, tok), 1)
    dk_, dq_ = jnp.zeros((tok, tok), jnp.int32), jnp.zeros((tok, tok), jnp.int32)
    end = 0
    for j in range(lens.shape[1]):
        end = end + lens[0, j]
        dk_ = dk_ + jnp.where(key_i >= end, 1, 0)
        dq_ = dq_ + jnp.where(qry_i >= end, 1, 0)
    bias[...] = jnp.where((dk_ == dq_) & (qry_i >= key_i), 0.0, masked_score)
    lse_t[...] = lse[...].T

    lane = lax.broadcasted_iota(jnp.int32, (1, 128), 1)
    n_pairs = width // 128
    half = tok // 2
    heads_in = 128 // hd

    @pl.loop(0, n_pairs)
    def _(p):
        @pl.when((p >= 1) & (p + 3 < n_exp))
        def _():
            leave(p + 3)

        @pl.when((p >= 2) & (lax.rem(p, 2) == 0))
        def _():
            gather.step_exp(order(lax.div(p, 2) - 1), bias_back[...].reshape(lc, 1, width))

        for q_step, at in enumerate(EARLY):

            @pl.when(p == at)
            def _():
                total.early(q_step)

        def cols(part):
            return pl.ds(pl.multiple_of(part * width + p * 128, 128), 128)

        q, key, val, do = mixed[:, cols(0)], mixed[:, cols(1)], mixed[:, cols(2)], gctx[:, cols(0)]
        dq = [jnp.zeros((half, 128), F32) for _ in range(2)]
        dkey = [jnp.zeros((half, 128), F32) for _ in range(2)]
        dval = [jnp.zeros((half, 128), F32) for _ in range(2)]
        for hh in range(heads_in):
            own_lanes = (lane >= hh * hd) & (lane < (hh + 1) * hd)
            qh = jnp.where(own_lanes, q * BF(hd**-0.5), BF(0))
            kh = jnp.where(own_lanes, key * BF(hd**-0.5), BF(0))
            doh = jnp.where(own_lanes, do, BF(0))
            lrow = lse_t[pl.ds(p * heads_in + hh, 1), :]
            for qb in range(2):
                rows = slice(qb * half, (qb + 1) * half)
                n = (qb + 1) * half
                s = mm_nt(key[:n], qh[rows]) + (bias[:n, rows] - lrow[:, rows])
                pt = jnp.exp(s)
                dp = mm_nt(val[:n], doh[rows])
                inner = jnp.sum(dp * pt, axis=0, keepdims=True)
                ds = (pt * (dp - inner)).astype(BF)
                ptb = pt.astype(BF)
                dv_, dk2 = mm(ptb, doh[rows]), mm(ds, qh[rows])
                for kb in range(qb + 1):
                    part = slice(kb * half, (kb + 1) * half)
                    dval[kb] = dval[kb] + dv_[part]
                    dkey[kb] = dkey[kb] + dk2[part]
                dq[qb] = dq[qb] + mm_tn(ds, kh[:n])
        for b in range(2):
            rows = slice(b * half, (b + 1) * half)
            mixed[rows, cols(0)] = dq[b].astype(BF)
            mixed[rows, cols(1)] = dkey[b].astype(BF)
            mixed[rows, cols(2)] = dval[b].astype(BF)

    def step_exp(m):
        gather.step_exp(order(m), bias_back[...].reshape(lc, 1, width))

    step_exp(3)
    for part in range(3):

        @pl.loop(0, width // 256)
        def _(i):
            rows = pl.ds(pl.multiple_of(i * 256, 256), 256)
            piece = mm(n1t[rows], mixed[:, part * width : (part + 1) * width])
            g_mats[pl.ds((part + 1) * n_quarter + i * 16, 16)] = piece.astype(BF).reshape(16, 16, width)

        total.begin(part + 1)

    @pl.loop(n_pairs + 3, max(n_exp, n_pairs + 3))
    def _(m):
        leave(m)

    step_exp(4)

    @pl.loop(0, tok // 256)
    def _(i):
        rows = pl.ds(pl.multiple_of(i * 256, 256), 256)
        up = mm_nt(mixed[rows], w_qkv[...])
        _, unit, inverse = norm_rows(tokens[rows].astype(F32), gain1[...], 0.0)
        g_norms[0:1] += fold(up * unit)
        g_norms[1:2] += fold(up)
        g_tokens[rows] += norm_back(up, unit, inverse, gain1[...])

    def aside(s):
        @pl.when(s == 0)
        def _():
            @pl.loop(5, n_exp - 2)
            def _(m):
                step_exp(m)

        for j in (1, 2):

            @pl.when(s == j)
            def _():
                step_exp(n_exp - 3 + j)

        @pl.when(s == 5)
        def _():
            @pl.loop(1, n_exp)
            def _(k):
                gather.over_exp(k).wait_recv()

            @pl.loop(0, tok // 256)
            def _(i):
                rows = pl.ds(pl.multiple_of(i * 256, 256), 256)
                table = tok_block(slot_col[rows], 0, n_slots)
                whole = middle[rows] + mm(table, f_back[...].reshape(n_slots, width))
                output[rows] = whole.astype(BF)

    total.run(aside)

    @pl.loop(0, n_exp)
    def _(k):
        gather.over_core(k).wait_send()
        gather.sent(k)


def attend_back(
    n_exp, n_hid, lens, slot_col, tokens, middle, cot, mixed, context, lse, back,
    gain1, shift1, w_qkv, w_out, gain2, bias_back, f_part,
):
    n_y = n_hid // 2
    tok, width = tokens.shape
    _, lc, cap, _ = back.shape
    n_units = 4 * width // 16
    shape = jax.ShapeDtypeStruct
    return pl.pallas_call(
        functools.partial(attend_back_kernel, n_exp, n_y),
        name="attend_back",
        out_shape=(
            shape((tok, width), BF),
            shape((tok, width), F32),
            shape((n_units, 16, width), BF),
            shape((8, width), F32),
        ),
        in_specs=[SM, VM, HB, HB, HB, HB, HB, VM, HB, VM, VM, HB, HB, VM, VM, HB],
        out_specs=[VM, VM, HB, VM],
        scratch_shapes=[
            *[pltpu.VMEM(a.shape, a.dtype) for a in (tokens, middle, cot, mixed, context, back, w_qkv, w_out)],
            pltpu.VMEM((n_units, 16, width), BF),
            pltpu.VMEM((tok, tok), F32),
            pltpu.VMEM((tok, width), BF),
            pltpu.VMEM((tok, width), BF),
            pltpu.VMEM((width, tok), BF),
            pltpu.VMEM((128, tok), F32),
            pltpu.VMEM((4, lc, n_y, cap, width), BF),
            pltpu.VMEM((n_exp, lc, cap, width), BF),
            DMA((4,)),
            DMA((8,)),
            *Gather.scratch(n_exp, n_y, lc, cap, width),
            *Gather.sems(n_exp, n_y),
            *Reduce.scratch(n_exp, n_y, n_units, (8, width)),
        ],
        compiler_params=pltpu.CompilerParams(
            collective_id=2, has_side_effects=True, vmem_limit_bytes=63 * MIB
        ),
    )(
        lens, slot_col, tokens, middle, cot, mixed, context, lse, back,
        gain1, shift1, w_qkv, w_out, gain2, bias_back, f_part,
    )


def per_device(
    tokens, token_ids, lengths, hash_table, capacity, gain_one, shift_one, w_qkv, w_out,
    gain_two, shift_two, w_in, bias_in, w_back, bias_back, cotangent,
):
    n_exp, n_hid = lax.axis_size("exp"), lax.axis_size("hid")
    tok, width = tokens.shape
    lc, _, ff = w_in.shape
    cap = 2 * tok // capacity.shape[0]
    table_rows = -(-hash_table.shape[0] // 1024) * 8
    table = jnp.pad(hash_table, (0, table_rows * 128 - hash_table.shape[0])).reshape(table_rows, 128)
    gain1, shift1, gain2, shift2 = (v[None] for v in (gain_one, shift_one, gain_two, shift_two))
    mixed, context, middle, lse, slot, send, grads, first_rows = attend(
        n_exp, n_hid, lc, cap, lengths, token_ids[None], table, capacity[None], tokens, gain1, shift1, w_qkv, w_out, gain2, shift2, cotangent
    )
    back, f_part, wi, wb, gb_in, gb_back = experts(
        n_exp, n_hid, first_rows, send, grads, w_in, bias_in, w_back
    )
    output, g_tokens, mats, norms = attend_back(
        n_exp, n_hid, lengths, slot, tokens, middle, cotangent, mixed, context, lse, back,
        gain1, shift1, w_qkv, w_out, gain2, bias_back, f_part,
    )
    g_in, g_back, g_qkv, g_out, *norms, gb_in, gb_back = finish(wi, wb, mats, norms, gb_in, gb_back)
    return (
        output, g_tokens, norms[0], norms[1], g_qkv, g_out, norms[2], norms[3], g_in, gb_in, g_back, gb_back,
    )


def solution(mesh):
    both = P(("exp", "hid"))
    rows = P(("exp", "hid"), None)
    placed = (
        rows, both, rows, P(), P(), P(), P(), P(), P(), P(), P(),
        P("exp", None, "hid"), P("exp", "hid"), P("exp", "hid", None), P("exp", None), rows,
    )
    return jax.shard_map(
        per_device,
        mesh=mesh,
        in_specs=placed,
        out_specs=(
            rows, rows, P(), P(), P(), P(), P(), P(),
            P("exp", None, "hid"), P("exp", "hid"), P("exp", "hid", None), P("exp", None),
        ),
        check_vma=False,
    )
```
